32 devices in a mesh: shot: 2 (over y), gx: 4 (over x, core), gy: 4 (over z).
Axes of the slice: x: 2, y: 2, z: 4, core: 2. Of those that a mesh axis runs over, the one named last changes fastest.
Arguments:
- src_p_prev: float32 [128, 64, 128], P(('shot', 'gx'), 'gy'), parts along dimension 0, may hold values from -6 to 6
- src_p_now: float32 [128, 64, 128], P(('shot', 'gx'), 'gy'), parts along dimension 0, may hold values from -6 to 6
- src_q_prev: float32 [128, 64, 128], P(('shot', 'gx'), 'gy'), parts along dimension 0, may hold values from -6 to 6
- src_q_now: float32 [128, 64, 128], P(('shot', 'gx'), 'gy'), parts along dimension 0, may hold values from -6 to 6
- rec_p_next: float32 [128, 64, 128], P(('shot', 'gx'), 'gy'), parts along dimension 0, may hold values from -6 to 6
- rec_p_now: float32 [128, 64, 128], P(('shot', 'gx'), 'gy'), parts along dimension 0, may hold values from -6 to 6
- rec_q_next: float32 [128, 64, 128], P(('shot', 'gx'), 'gy'), parts along dimension 0, may hold values from -6 to 6
- rec_q_now: float32 [128, 64, 128], P(('shot', 'gx'), 'gy'), parts along dimension 0, may hold values from -6 to 6
- velocity_term: float32 [64, 64, 128], P('gx', 'gy'), may hold values from 0.12 to 0.16
- epsilon: float32 [64, 64, 128], P('gx', 'gy'), may hold values from 0.2 to 0.4
- delta: float32 [64, 64, 128], P('gx', 'gy'), may hold values from 0 to 0.2
- tilt: float32 [64, 64, 128], P('gx', 'gy'), may hold values from 0 to 1.2
- azimuth: float32 [64, 64, 128], P('gx', 'gy'), may hold values from -3.140625 to 3.140625
- traces: float32 [32, 1024], P('shot', ('gx', 'gy')), parts along dimension 0, may hold values from -6 to 6
- receiver_x: int32 [1024], replicated, may hold values from 0 to 63
- receiver_y: int32 [1024], replicated, may hold values from 0 to 63
- segment_start: int32 [1], replicated, may hold values from 0 to 12
Outputs:
- image: float32 [128, 64, 128], P(('shot', 'gx'), 'gy'), parts along dimension 0
- rec_p_last: float32 [128, 64, 128], P(('shot', 'gx'), 'gy'), parts along dimension 0
- rec_q_last: float32 [128, 64, 128], P(('shot', 'gx'), 'gy'), parts along dimension 0
The draws below stay inside these ranges and needn't reach their ends.
There are 2 independent parts, one for each index of `shot`. The reference program is written for one: setup_inputs(seed, part) draws one part's arguments, and reference() takes and returns one part's arrays. A program takes and returns all parts, laid end to end along the dimension named above; an argument that names none is the same for every part. Nothing has to cross between parts.
All inputs are finite; a program needn't handle non-finite values.
Results may differ from the reference program's by a relative error of at most 0.00021.
Values sent between devices are 32-bit elements; how exact they have to be, the bound alone decides.
No kernel may reach another device: no remote copies, remote signals or barrier semaphores. Data moves between devices by JAX's collectives and lax.ppermute only.
A program may use at most 64 MiB of HBM per device.

```python
import jax
import jax.numpy as jnp
from jax import lax

NZ = 128
STEPS = 4
NT = 16
REC_DEPTH = 4
NX = 64
NY = 64
NREC = 1024


def checker_field(key, salt):
    field_key = jax.random.fold_in(key, salt)
    noise_key = jax.random.fold_in(field_key, 0)
    row_index = lax.broadcasted_iota(jnp.int32, (NX, NY, NZ), 0)
    col_index = lax.broadcasted_iota(jnp.int32, (NX, NY, NZ), 1)
    sign_pattern = (1 - 2 * ((row_index + col_index) % 2)).astype(jnp.float32)
    noise = jax.random.normal(noise_key, (NX, NY, NZ), jnp.float32)
    amplitude = 1.0 + 0.6 * noise
    return jnp.clip(sign_pattern * amplitude, -6.0, 6.0)


def draw_src_p_prev(key, part):
    return checker_field(key, 101)


def draw_src_p_now(key, part):
    return checker_field(key, 102)


def draw_src_q_prev(key, part):
    return checker_field(key, 103)


def draw_src_q_now(key, part):
    return checker_field(key, 104)


def draw_rec_p_next(key, part):
    return checker_field(key, 105)


def draw_rec_p_now(key, part):
    return checker_field(key, 106)


def draw_rec_q_next(key, part):
    return checker_field(key, 107)


def draw_rec_q_now(key, part):
    return checker_field(key, 108)


def place_ends(result, stream_key, least, largest):
    place = [jax.random.randint(jax.random.fold_in(stream_key, axis), (), 0, length) for axis, length in enumerate(result.shape)]
    longest = result.shape.index(max(result.shape))
    neighbour = place[:longest] + [(place[longest] + 1) % result.shape[longest]] + place[longest + 1:]
    return result.at[tuple(place)].set(least).at[tuple(neighbour)].set(largest)


def levels(key, dims, pieces, least, high):
    gain, own = 1.0, jax.random.fold_in(key, 6)
    for position, parts in pieces:
        steps = jnp.exp(jax.random.uniform(jax.random.fold_in(own, position), (parts,), jnp.float32, least / len(pieces), high / len(pieces)))
        gain = gain * jnp.repeat(steps, dims[position] // parts).reshape([-1 if axis == position else 1 for axis in range(len(dims))])
    return gain


def gaussian(stream_key, shape, spread, limit, shards=(), held_as=jnp.bfloat16):
    drawn = jax.random.normal(stream_key, shape, jnp.float32) * spread
    if len(shards) > 0:
        drawn = levels(stream_key, shape, shards, -0.22, 0.18) * drawn
    return jnp.clip(drawn, min=-limit, max=limit).astype(held_as)


def setup_inputs(seed: int = 0, part: int = 0) -> dict:
    keys = jax.random.split(jax.random.key(seed), 18)
    own_keys = jax.random.split(jax.random.fold_in(keys[17], part), 18)
    src_p_prev = draw_src_p_prev(jax.random.fold_in(jax.random.fold_in(keys[17], part), 71), part)
    src_p_now = draw_src_p_now(jax.random.fold_in(jax.random.fold_in(keys[17], part), 71), part)
    src_q_prev = draw_src_q_prev(jax.random.fold_in(jax.random.fold_in(keys[17], part), 71), part)
    src_q_now = draw_src_q_now(jax.random.fold_in(jax.random.fold_in(keys[17], part), 71), part)
    rec_p_next = draw_rec_p_next(jax.random.fold_in(jax.random.fold_in(keys[17], part), 71), part)
    rec_p_now = draw_rec_p_now(jax.random.fold_in(jax.random.fold_in(keys[17], part), 71), part)
    rec_q_next = draw_rec_q_next(jax.random.fold_in(jax.random.fold_in(keys[17], part), 71), part)
    rec_q_now = draw_rec_q_now(jax.random.fold_in(jax.random.fold_in(keys[17], part), 71), part)
    velocity_term = jnp.clip(0.12 + 0.04 * jax.random.uniform(keys[8], (NX, NY, NZ), jnp.float32) ** levels(keys[8], (NX, NY, NZ), ((0, 4), (1, 4)), -0.2, 0.2), 0.12, 0.16)
    epsilon = jnp.clip(0.2 + 0.2 * jax.random.uniform(keys[9], (NX, NY, NZ), jnp.float32) ** levels(keys[9], (NX, NY, NZ), ((0, 4), (1, 4)), -0.2, 0.2), 0.2, 0.4)
    delta = jnp.clip(0.2 * jax.random.uniform(keys[10], (NX, NY, NZ), jnp.float32) ** levels(keys[10], (NX, NY, NZ), ((0, 4), (1, 4)), -0.2, 0.2), 0.0, 0.2)
    tilt = jnp.clip(1.2 * jax.random.uniform(keys[11], (NX, NY, NZ), jnp.float32) ** levels(keys[11], (NX, NY, NZ), ((0, 4), (1, 4)), -0.2, 0.2), 0.0, 1.2)
    azimuth = jnp.clip(jax.random.uniform(keys[12], (NX, NY, NZ), jnp.float32, -3.140625, 3.140625), -3.140625, 3.140625)
    traces = gaussian(own_keys[13], (NT, NREC), 1.0, 6.0, ((1, 16),), jnp.float32)
    receiver_x = place_ends(jax.random.randint(keys[14], (NREC,), 0, NX), jax.random.fold_in(keys[14], 1), 0, NX - 1).astype(jnp.int32)
    receiver_y = place_ends(jax.random.randint(keys[15], (NREC,), 0, NY), jax.random.fold_in(keys[15], 1), 0, NY - 1).astype(jnp.int32)
    segment_start = jax.random.randint(keys[16], (1,), 0, NT - STEPS + 1).astype(jnp.int32)
    return dict(src_p_prev=src_p_prev, src_p_now=src_p_now, src_q_prev=src_q_prev, src_q_now=src_q_now, rec_p_next=rec_p_next, rec_p_now=rec_p_now, rec_q_next=rec_q_next, rec_q_now=rec_q_now, velocity_term=velocity_term, epsilon=epsilon, delta=delta, tilt=tilt, azimuth=azimuth, traces=traces, receiver_x=receiver_x, receiver_y=receiver_y, segment_start=segment_start)


def factors_of(velocity_term, epsilon, delta, tilt, azimuth):
    sin_tilt = jnp.sin(tilt)
    cos_tilt = jnp.cos(tilt)
    sin_azim = jnp.sin(azimuth)
    cos_azim = jnp.cos(azimuth)
    sin_square = sin_tilt * sin_tilt
    double_tilt = 2.0 * sin_tilt * cos_tilt
    return (velocity_term, 1.0 + 2.0 * epsilon, jnp.sqrt(1.0 + 2.0 * delta), sin_square * cos_azim * cos_azim, sin_square * sin_azim * sin_azim, cos_tilt * cos_tilt, 2.0 * sin_square * sin_azim * cos_azim, double_tilt * cos_azim, double_tilt * sin_azim)

def rotated(padded, factors):
    center = padded[1:-1, 1:-1, 1:-1]
    d_xx = padded[2:, 1:-1, 1:-1] - 2.0 * center + padded[:-2, 1:-1, 1:-1]
    d_yy = padded[1:-1, 2:, 1:-1] - 2.0 * center + padded[1:-1, :-2, 1:-1]
    d_zz = padded[1:-1, 1:-1, 2:] - 2.0 * center + padded[1:-1, 1:-1, :-2]
    d_xy = 0.25 * (padded[2:, 2:, 1:-1] - padded[2:, :-2, 1:-1] - padded[:-2, 2:, 1:-1] + padded[:-2, :-2, 1:-1])
    d_xz = 0.25 * (padded[2:, 1:-1, 2:] - padded[2:, 1:-1, :-2] - padded[:-2, 1:-1, 2:] + padded[:-2, 1:-1, :-2])
    d_yz = 0.25 * (padded[1:-1, 2:, 2:] - padded[1:-1, 2:, :-2] - padded[1:-1, :-2, 2:] + padded[1:-1, :-2, :-2])
    along_axis = factors[3] * d_xx + factors[4] * d_yy + factors[5] * d_zz + factors[6] * d_xy + factors[7] * d_xz + factors[8] * d_yz
    return (along_axis, d_xx + d_yy + d_zz)

def advance(wave_state, factors):
    p_prev, p_now, q_prev, q_now = wave_state
    p_axis, p_laplace = rotated(jnp.pad(p_now, 1), factors)
    q_axis = rotated(jnp.pad(q_now, 1), factors)[0]
    p_across = p_laplace - p_axis
    p_next = 2.0 * p_now - p_prev + factors[0] * (factors[1] * p_across + factors[2] * q_axis)
    q_next = 2.0 * q_now - q_prev + factors[0] * (factors[2] * p_across + q_axis)
    return (p_next, q_next)

def reference(src_p_prev, src_p_now, src_q_prev, src_q_now, rec_p_next, rec_p_now, rec_q_next, rec_q_now, velocity_term, epsilon, delta, tilt, azimuth, traces, receiver_x, receiver_y, segment_start):
    factors = factors_of(velocity_term, epsilon, delta, tilt, azimuth)
    source_snaps = [src_p_now]
    wave_state = (src_p_prev, src_p_now, src_q_prev, src_q_now)
    for turn_index in range(STEPS):
        p_next, q_next = advance(wave_state, factors)
        wave_state = (wave_state[1], p_next, wave_state[3], q_next)
        source_snaps.append(p_next)
    window = lax.dynamic_slice_in_dim(traces, segment_start[0], STEPS, 0)
    image_sum = source_snaps[STEPS] * rec_p_now
    wave_state = (rec_p_next, rec_p_now, rec_q_next, rec_q_now)
    for turn_index in range(STEPS):
        sample = STEPS - 1 - turn_index
        p_next, q_next = advance(wave_state, factors)
        planes = jnp.zeros((NX, NY), jnp.float32).at[receiver_x, receiver_y].add(window[sample])
        p_next = p_next.at[:, :, REC_DEPTH].add(planes)
        wave_state = (wave_state[1], p_next, wave_state[3], q_next)
        image_sum = image_sum + source_snaps[sample] * p_next
    return (image_sum, wave_state[1], wave_state[3])
```

```python
import functools

import jax
import jax.numpy as jnp
from jax import lax
from jax.experimental import pallas as pl
from jax.experimental.pallas import tpu as pltpu
from jax.sharding import PartitionSpec as P

STEPS = 4
REC_DEPTH = 4
RIM = STEPS
FIELDS = 8
VMEM_LIMIT = 48 * 1024 * 1024
HIGH = 1
LOW = -1


def whole_vmem(count):
    return [pl.BlockSpec(memory_space=pltpu.VMEM)] * count


DIRECTIONS = ((0, HIGH), (0, LOW), (HIGH, 0), (LOW, 0), (HIGH, HIGH), (HIGH, LOW), (LOW, HIGH), (LOW, LOW))


def rim_range(direction, length):
    if direction == 0:
        return slice(0, length)
    return slice(length - RIM, length) if direction == HIGH else slice(0, RIM)


def pack_kernel(count, *refs):
    blocks, packed = refs[:count], refs[count:]
    cells_x, cells_y = blocks[0].shape[:2]
    for out, (dir_x, dir_y) in zip(packed, DIRECTIONS):
        for number, block in enumerate(blocks):
            out[number] = block[rim_range(dir_x, cells_x), rim_range(dir_y, cells_y), :]


def pack(blocks):
    cells_x, cells_y, depth = blocks[0].shape
    count = len(blocks)
    shapes = [
        jax.ShapeDtypeStruct(
            (count, RIM if dir_x else cells_x, RIM if dir_y else cells_y, depth), jnp.float32
        )
        for dir_x, dir_y in DIRECTIONS
    ]
    return pl.pallas_call(
        functools.partial(pack_kernel, count),
        out_shape=shapes,
        in_specs=whole_vmem(count),
        out_specs=whole_vmem(len(shapes)),
        compiler_params=pltpu.CompilerParams(vmem_limit_bytes=VMEM_LIMIT),
        name="pack_rims",
    )(*blocks)


def send(value, direction):
    dir_x, dir_y = direction
    size_x, size_y = lax.axis_size("gx"), lax.axis_size("gy")
    pairs = [
        (x * size_y + y, (x + dir_x) * size_y + y + dir_y)
        for x in range(size_x)
        for y in range(size_y)
        if 0 <= x + dir_x < size_x and 0 <= y + dir_y < size_y
    ]
    return lax.ppermute(value, ("gx", "gy"), pairs)


def shifted_z(plane, lane):
    depth = plane.shape[-1]
    above = jnp.where(lane < depth - 1, pltpu.roll(plane, depth - 1, 1), 0.0)
    below = jnp.where(lane > 0, pltpu.roll(plane, 1, 1), 0.0)
    return above, below


def shifted_y(plane):
    rows = plane.shape[0]
    return pltpu.roll(plane, rows - 1, 0), pltpu.roll(plane, 1, 0)


def slopes(plane, lane):
    above, below = shifted_z(plane, lane)
    after, before = shifted_y(plane)
    return after - before, above - below, after + before, above + below


def main_kernel(count, cells_x, cells_y, *refs):
    blocks = refs[:count]
    rims = refs[count : count + len(DIRECTIONS)]
    planes = refs[count + len(DIRECTIONS)]
    image, p_last, q_last = refs[count + len(DIRECTIONS) + 1 : count + len(DIRECTIONS) + 4]
    scratch = refs[count + len(DIRECTIONS) + 4 :]
    waves, model, factors = scratch
    span_x = cells_x + 2 * RIM
    rows = cells_y + 2 * RIM
    depth = blocks[0].shape[-1]

    def place_x(direction):
        if direction == 0:
            return slice(RIM, RIM + cells_x)
        return slice(0, RIM) if direction == HIGH else slice(RIM + cells_x, span_x)

    def place_y(direction):
        if direction == 0:
            return slice(0, cells_y)
        return slice(cells_y + RIM, rows) if direction == HIGH else slice(cells_y, cells_y + RIM)

    targets = [waves.at[number, slot] for number in range(4) for slot in range(2)]
    targets += [model.at[number] for number in range(count - FIELDS)]
    for number, target in enumerate(targets):
        target[place_x(0), place_y(0), :] = blocks[number][...]
        for (dir_x, dir_y), rim in zip(DIRECTIONS, rims):
            target[place_x(dir_x), place_y(dir_y), :] = rim[number]

    lane = lax.broadcasted_iota(jnp.int32, (rows, depth), 1)

    def make_factors(x, carry):
        velocity = model[0, x]
        f_e = 1.0 + 2.0 * model[1, x]
        f_d = jnp.sqrt(1.0 + 2.0 * model[2, x])
        tilt = model[3, x]
        azimuth = model[4, x]
        sin_tilt, cos_tilt = jnp.sin(tilt), jnp.cos(tilt)
        sin_azim, cos_azim = jnp.sin(azimuth), jnp.cos(azimuth)
        sin_square = sin_tilt * sin_tilt
        double_tilt = 0.5 * sin_tilt * cos_tilt
        factors[0, x] = velocity
        factors[1, x] = velocity * f_e
        factors[2, x] = velocity * f_d
        factors[3, x] = sin_square * cos_azim * cos_azim
        factors[4, x] = sin_square * sin_azim * sin_azim
        factors[5, x] = cos_tilt * cos_tilt
        factors[6, x] = 0.5 * sin_square * sin_azim * cos_azim
        factors[7, x] = double_tilt * cos_azim
        factors[8, x] = double_tilt * sin_azim
        return carry

    lax.fori_loop(1, span_x - 1, make_factors, 0)

    def step(pair, turn, plane_ref):
        p_number, q_number = 2 * pair, 2 * pair + 1
        first, last = turn + 1, span_x - 1 - turn

        def stencil(number, x, before, now):
            u_now = waves[number, turn + 1, x]
            u_after = waves[number, turn + 1, x + 1]
            u_before = waves[number, turn + 1, x - 1]
            dy_after, dz_after, sy_after, sz_after = slopes(u_after, lane)
            dy_now, dz_now, sy_now, sz_now = now
            dy_before, dz_before = before
            double = 2.0 * u_now
            d_xx = (u_after + u_before) - double
            d_yy = sy_now - double
            d_zz = sz_now - double
            d_xy = dy_after - dy_before
            d_xz = dz_after - dz_before
            dz_up, dz_down = shifted_y(dz_now)
            d_yz = dz_up - dz_down
            along = (
                factors[3, x] * d_xx
                + factors[4, x] * d_yy
                + factors[5, x] * d_zz
                + factors[6, x] * d_xy
                + factors[7, x] * d_xz
                + factors[8, x] * d_yz
            )
            return (
                along,
                (d_xx + d_yy) + d_zz,
                double,
                (dy_now, dz_now),
                (dy_after, dz_after, sy_after, sz_after),
            )

        def body(x, carry):
            p_before, p_now, q_before, q_now = carry
            p_axis, p_laplace, p_double, p_before, p_now = stencil(p_number, x, p_before, p_now)
            q_axis, _, q_double, q_before, q_now = stencil(q_number, x, q_before, q_now)
            across = p_laplace - p_axis
            p_next = (p_double - waves[p_number, turn, x]) + (
                factors[1, x] * across + factors[2, x] * q_axis
            )
            q_next = (q_double - waves[q_number, turn, x]) + (
                factors[2, x] * across + factors[0, x] * q_axis
            )
            if plane_ref is not None:
                moved = pltpu.roll(plane_ref[...], lax.rem(REC_DEPTH - x + depth, depth), 1)
                p_next = p_next + jnp.where(lane == REC_DEPTH, moved, 0.0)
            waves[p_number, turn + 2, x] = p_next
            waves[q_number, turn + 2, x] = q_next
            return p_before, p_now, q_before, q_now

        def start(number):
            before = slopes(waves[number, turn + 1, first - 1], lane)
            now = slopes(waves[number, turn + 1, first], lane)
            return before[:2], now

        p_before, p_now = start(p_number)
        q_before, q_now = start(q_number)
        lax.fori_loop(first, last, body, (p_before, p_now, q_before, q_now))

    for turn in range(STEPS):
        step(0, turn, None)
    for turn in range(STEPS):
        step(1, turn, planes.at[STEPS - 1 - turn])

    def finish(x, carry):
        total = waves[0, 1 + STEPS, x, :cells_y] * waves[2, 1, x, :cells_y]
        for back in range(1, STEPS + 1):
            total = total + waves[0, 1 + STEPS - back, x, :cells_y] * waves[2, 1 + back, x, :cells_y]
        image[x - RIM] = total
        p_last[x - RIM] = waves[2, 1 + STEPS, x, :cells_y]
        q_last[x - RIM] = waves[3, 1 + STEPS, x, :cells_y]
        return carry

    lax.fori_loop(RIM, RIM + cells_x, finish, 0)


def migrate(blocks, rims, planes):
    cells_x, cells_y, depth = blocks[0].shape
    count = len(blocks)
    span_x, rows = cells_x + 2 * RIM, cells_y + 2 * RIM
    out = jax.ShapeDtypeStruct((cells_x, cells_y, depth), jnp.float32)
    return pl.pallas_call(
        functools.partial(main_kernel, count, cells_x, cells_y),
        out_shape=[out] * 3,
        in_specs=whole_vmem(count + len(rims) + 1),
        out_specs=whole_vmem(3),
        scratch_shapes=[
            pltpu.VMEM((4, STEPS + 2, span_x, rows, depth), jnp.float32),
            pltpu.VMEM((count - FIELDS, span_x, rows, depth), jnp.float32),
            pltpu.VMEM((9, span_x, rows, depth), jnp.float32),
        ],
        compiler_params=pltpu.CompilerParams(vmem_limit_bytes=VMEM_LIMIT),
        name="migrate",
    )(*blocks, *rims, planes)


def gathered(window):
    devices = lax.axis_size("gx") * lax.axis_size("gy")
    copies = jnp.broadcast_to(window[None], (devices,) + window.shape)
    everyone = lax.all_to_all(copies, ("gx", "gy"), 0, 0)
    return everyone.transpose(1, 0, 2).reshape(window.shape[0], -1)


def injected(everyone, receiver_x, receiver_y, cells_x, cells_y, depth):
    x_global = lax.axis_index("gx") * cells_x - RIM + jnp.arange(depth, dtype=jnp.int32)
    y_local = jnp.arange(cells_y + 2 * RIM, dtype=jnp.int32)
    y_local = jnp.where(y_local < cells_y + RIM, y_local, y_local - cells_y - 2 * RIM)
    y_global = lax.axis_index("gy") * cells_y + y_local
    pick_x = (receiver_x[None, :] == x_global[:, None]).astype(jnp.float32)
    pick_y = (receiver_y[None, :] == y_global[:, None]).astype(jnp.float32)
    weighted = everyone[:, None, :] * pick_y[None, :, :]
    return jnp.einsum("kyr,xr->kyx", weighted, pick_x, precision=lax.Precision.HIGHEST)


def per_device(
    src_p_prev,
    src_p_now,
    src_q_prev,
    src_q_now,
    rec_p_next,
    rec_p_now,
    rec_q_next,
    rec_q_now,
    velocity_term,
    epsilon,
    delta,
    tilt,
    azimuth,
    traces,
    receiver_x,
    receiver_y,
    segment_start,
):
    blocks = (
        src_p_prev,
        src_p_now,
        src_q_prev,
        src_q_now,
        rec_p_next,
        rec_p_now,
        rec_q_next,
        rec_q_now,
        velocity_term,
        epsilon,
        delta,
        tilt,
        azimuth,
    )
    cells_x, cells_y, depth = src_p_now.shape
    window = lax.dynamic_slice_in_dim(traces, segment_start[0], STEPS, 0)
    everyone = gathered(window)
    rims = [send(packed, direction) for packed, direction in zip(pack(blocks), DIRECTIONS)]
    planes = injected(everyone, receiver_x, receiver_y, cells_x, cells_y, depth)
    return tuple(migrate(blocks, rims, planes))


def solution(mesh):
    state = P(("shot", "gx"), "gy", None)
    earth = P("gx", "gy", None)
    return jax.shard_map(
        per_device,
        mesh=mesh,
        in_specs=(state,) * FIELDS + (earth,) * 5 + (P("shot", ("gx", "gy")), P(), P(), P()),
        out_specs=(state,) * 3,
        check_vma=False,
    )
```

```python
import functools

import jax
import jax.numpy as jnp
from jax import lax
from jax.experimental import pallas as pl
from jax.experimental.pallas import tpu as pltpu
from jax.sharding import PartitionSpec as P

STEPS = 4
REC_DEPTH = 4
RIM = STEPS
FIELDS = 8
SUBLANES = 8
LANES = 128
VMEM_LIMIT = 48 * 1024 * 1024
PARAMS = pltpu.CompilerParams(vmem_limit_bytes=VMEM_LIMIT)


def in_vmem(count):
    return [pl.BlockSpec(memory_space=pltpu.VMEM)] * count


def is_odd(axis):
    return lax.rem(lax.axis_index(axis), 2) == 1


def swap(value, axis, first):
    size = lax.axis_size(axis)
    lower = range(first, size - 1, 2)
    pairs = [(i, i + 1) for i in lower] + [(i + 1, i) for i in lower]
    return lax.ppermute(value, axis, pairs)


def pack_kernel(count, *refs):
    blocks, traces, start = refs[:count], refs[count], refs[count + 1]
    y_a, y_b, x_a, x_b, copies = refs[count + 2 : count + 7]
    held, sems = refs[count + 7 :]
    cells_x, cells_y = blocks[0].shape[:2]
    moves = [
        pltpu.make_async_copy(block, held.at[number], sems.at[number])
        for number, block in enumerate(blocks)
    ]
    for move in moves:
        move.start()
    odd_x, odd_y = is_odd("gx"), is_odd("gy")
    begin = start[0]
    samples = traces.shape[1]
    copies[...] = jnp.zeros_like(copies)
    for sample in range(STEPS):
        row = traces[pl.ds(begin + sample, 1), :]
        for device in range(copies.shape[0]):
            copies[device, sample : sample + 1, :samples] = row
    for move in moves:
        move.wait()

    def put_y(low, high):
        for number in range(count):
            low[number] = held[number, :, :RIM, :]
            high[number] = held[number, :, cells_y - RIM :, :]

    @pl.when(odd_y)
    def _():
        put_y(y_a, y_b)

    @pl.when(jnp.logical_not(odd_y))
    def _():
        put_y(y_b, y_a)

    from_a = jnp.where(odd_x, 0, cells_x - RIM)
    from_b = jnp.where(odd_x, cells_x - RIM, 0)
    for number in range(count):
        x_a[number] = held[number, pl.ds(from_a, RIM)]
        x_b[number] = held[number, pl.ds(from_b, RIM)]


def pack(blocks, traces, segment_start):
    cells_x, cells_y, depth = blocks[0].shape
    count = len(blocks)
    devices = lax.axis_size("gx") * lax.axis_size("gy")
    rim_y = jax.ShapeDtypeStruct((count, cells_x, RIM, depth), jnp.float32)
    rim_x = jax.ShapeDtypeStruct((count, RIM, cells_y, depth), jnp.float32)
    copies = jax.ShapeDtypeStruct((devices, SUBLANES, LANES), jnp.float32)
    return pl.pallas_call(
        functools.partial(pack_kernel, count),
        out_shape=[rim_y, rim_y, rim_x, rim_x, copies],
        in_specs=[pl.BlockSpec(memory_space=pltpu.HBM)] * count
        + in_vmem(1)
        + [pl.BlockSpec(memory_space=pltpu.SMEM)],
        out_specs=in_vmem(5),
        scratch_shapes=[
            pltpu.VMEM((count, cells_x, cells_y, depth), jnp.float32),
            pltpu.SemaphoreType.DMA((count,)),
        ],
        compiler_params=PARAMS,
        name="pack_rims",
    )(*blocks, traces, segment_start)


def corner_kernel(y_a, y_b, c_a, c_b):
    count, cells_x = y_a.shape[:2]
    odd_x, odd_y = is_odd("gx"), is_odd("gy")
    from_a = jnp.where(odd_x, 0, cells_x - RIM)
    from_b = jnp.where(odd_x, cells_x - RIM, 0)

    def put(low, high):
        for number in range(count):
            for begin, out in ((from_a, c_a), (from_b, c_b)):
                out[number, :, :RIM, :] = high[number, pl.ds(begin, RIM)]
                out[number, :, RIM:, :] = low[number, pl.ds(begin, RIM)]

    @pl.when(odd_y)
    def _():
        put(y_a, y_b)

    @pl.when(jnp.logical_not(odd_y))
    def _():
        put(y_b, y_a)


def corners(y_a, y_b):
    count, _, _, depth = y_a.shape
    corner = jax.ShapeDtypeStruct((count, RIM, 2 * RIM, depth), jnp.float32)
    return pl.pallas_call(
        corner_kernel,
        out_shape=[corner, corner],
        in_specs=in_vmem(2),
        out_specs=in_vmem(2),
        compiler_params=PARAMS,
        name="pack_corners",
    )(y_a, y_b)


def sine_cosine(angle):
    square = angle * angle
    sine = 1.0 / 6227020800.0
    for term in (-1.0 / 39916800.0, 1.0 / 362880.0, -1.0 / 5040.0, 1.0 / 120.0, -1.0 / 6.0, 1.0):
        sine = sine * square + term
    cosine = 1.0 / 479001600.0
    for term in (-1.0 / 3628800.0, 1.0 / 40320.0, -1.0 / 720.0, 1.0 / 24.0, -0.5, 1.0):
        cosine = cosine * square + term
    return sine * angle, cosine


def main_kernel(count, cells_x, cells_y, *refs):
    blocks = refs[:count]
    y_a, y_b, x_a, x_b, c_a, c_b, planes = refs[count : count + 7]
    image, p_last, q_last = refs[count + 7 : count + 10]
    wide, waves, factors, local = refs[count + 10 :]
    span_x = cells_x + 2 * RIM
    rows = cells_y + 2 * RIM
    tiles = rows // SUBLANES
    depth = wide.shape[-1]
    odd_x, odd_y = is_odd("gx"), is_odd("gy")

    def place_y(low, high):
        for number in range(count):
            wide[number, RIM : RIM + cells_x, cells_y : cells_y + RIM, :] = high[number]
            wide[number, RIM : RIM + cells_x, cells_y + RIM :, :] = low[number]

    for number in range(count):
        wide[number, RIM : RIM + cells_x, :cells_y, :] = blocks[number][...]

    @pl.when(odd_y)
    def _():
        place_y(y_a, y_b)

    @pl.when(jnp.logical_not(odd_y))
    def _():
        place_y(y_b, y_a)

    to_a = jnp.where(odd_x, 0, RIM + cells_x)
    to_b = jnp.where(odd_x, RIM + cells_x, 0)
    for number in range(count):
        for begin, side, corner in ((to_a, x_a, c_a), (to_b, x_b, c_b)):
            wide[number, pl.ds(begin, RIM), :cells_y, :] = side[number]
            wide[number, pl.ds(begin, RIM), cells_y:, :] = corner[number]

    def wide_tiles(number, x):
        return [wide[number, x, pl.ds(tile, SUBLANES, stride=tiles), :] for tile in range(tiles)]

    def wave_tiles(number, slot, x):
        if slot < 2:
            return wide_tiles(2 * number + slot, x)
        return [waves[number, slot - 2, x, tile] for tile in range(tiles)]

    lane = lax.broadcasted_iota(jnp.int32, (SUBLANES, depth), 1)
    not_last, not_first = lane < depth - 1, lane > 0
    at_depth = lane == REC_DEPTH

    def next_y(value):
        return value[1:] + [pltpu.roll(value[0], SUBLANES - 1, 0)]

    def previous_y(value):
        return [pltpu.roll(value[-1], 1, 0)] + value[:-1]

    def make_factors(i, carry):
        stores = []
        for x in (1 + 2 * i, 2 + 2 * i):
            raw = [wide_tiles(FIELDS + number, x) for number in range(count - FIELDS)]
            for tile in range(tiles):
                velocity, epsilon, delta, tilt, azimuth = [value[tile] for value in raw]
                f_e = 1.0 + 2.0 * epsilon
                f_d = jnp.sqrt(1.0 + 2.0 * delta)
                sin_tilt, cos_tilt = sine_cosine(tilt)
                sin_half, cos_half = sine_cosine(0.5 * azimuth)
                sin_azim = 2.0 * sin_half * cos_half
                cos_azim = 1.0 - 2.0 * sin_half * sin_half
                sin_square = sin_tilt * sin_tilt
                half_tilt = 0.5 * sin_tilt * cos_tilt
                along_x = sin_square * cos_azim
                values = (
                    velocity,
                    velocity * f_e,
                    velocity * f_d,
                    along_x * cos_azim,
                    sin_square * sin_azim * sin_azim,
                    cos_tilt * cos_tilt,
                    0.5 * along_x * sin_azim,
                    half_tilt * cos_azim,
                    half_tilt * sin_azim,
                )
                stores += [(number, x, tile, value) for number, value in enumerate(values)]
        for number, x, tile, value in stores:
            factors[number, x, tile] = value
        return carry

    lax.fori_loop(0, (span_x - 2) // 2, make_factors, 0)

    def plane_part(turn, x, stores):
        ayy = [factors[4, x, tile] for tile in range(tiles)]
        azz = [factors[5, x, tile] for tile in range(tiles)]
        ayz = [factors[8, x, tile] for tile in range(tiles)]
        for number in range(4):
            now = wave_tiles(number, turn + 1, x)
            above = [jnp.where(not_last, pltpu.roll(u, depth - 1, 1), 0.0) for u in now]
            below = [jnp.where(not_first, pltpu.roll(u, 1, 1), 0.0) for u in now]
            slope_z = [a - b for a, b in zip(above, below)]
            after, before = next_y(now), previous_y(now)
            slope_after, slope_before = next_y(slope_z), previous_y(slope_z)
            for tile in range(tiles):
                double = now[tile] + now[tile]
                sum_y = after[tile] + before[tile]
                sum_z = above[tile] + below[tile]
                part = (
                    (ayy[tile] * sum_y + azz[tile] * sum_z)
                    + ayz[tile] * (slope_after[tile] - slope_before[tile])
                ) - double
                stores.append((local, (number, 0, x, tile), part))
                stores.append((local, (number, 1, x, tile), after[tile] - before[tile]))
                stores.append((local, (number, 2, x, tile), slope_z[tile]))
                if number % 2 == 0:
                    rest = (sum_y + sum_z) - 3.0 * double
                    stores.append((local, (number, 3, x, tile), rest))

    def next_part(turn, x, stores):
        held = [wave_tiles(number, turn, x) for number in range(4)]
        now = [wave_tiles(number, turn + 1, x) for number in range(4)]
        after = [wave_tiles(number, turn + 1, x + 1) for number in range(4)]
        before = [wave_tiles(number, turn + 1, x - 1) for number in range(4)]
        for tile in range(tiles):
            velocity, with_e, with_d = [factors[number, x, tile] for number in range(3)]
            axx, axy, axz = [factors[number, x, tile] for number in (3, 6, 7)]
            for pair in range(2):
                sums, axis = [], []
                for number in (2 * pair, 2 * pair + 1):
                    sum_x = after[number][tile] + before[number][tile]
                    d_xy = local[number, 1, x + 1, tile] - local[number, 1, x - 1, tile]
                    d_xz = local[number, 2, x + 1, tile] - local[number, 2, x - 1, tile]
                    sums.append(sum_x)
                    axis.append((local[number, 0, x, tile] + axx * sum_x) + (axy * d_xy + axz * d_xz))
                p_number, q_number = 2 * pair, 2 * pair + 1
                across = (sums[0] + local[p_number, 3, x, tile]) - axis[0]
                p_now, q_now = now[p_number][tile], now[q_number][tile]
                p_next = ((p_now + p_now) - held[p_number][tile]) + (
                    with_e * across + with_d * axis[1]
                )
                q_next = ((q_now + q_now) - held[q_number][tile]) + (
                    with_d * across + velocity * axis[1]
                )
                if pair == 1:
                    shift = lax.rem(REC_DEPTH - x + depth, depth)
                    moved = pltpu.roll(planes[STEPS - 1 - turn, tile], shift, 1)
                    p_next = p_next + jnp.where(at_depth, moved, 0.0)
                stores.append((waves, (p_number, turn, x, tile), p_next))
                stores.append((waves, (q_number, turn, x, tile), q_next))

    def write(stores):
        for ref, index, value in stores:
            ref[index] = value

    for turn in range(STEPS):
        first, last = turn + 1, span_x - 1 - turn
        for x in range(first - 1, first + 3):
            stores = []
            plane_part(turn, x, stores)
            write(stores)

        def body(i, carry, turn=turn, first=first):
            x = first + 2 * i
            stores = []
            next_part(turn, x, stores)
            next_part(turn, x + 1, stores)
            plane_part(turn, x + 3, stores)
            plane_part(turn, x + 4, stores)
            write(stores)
            return carry

        lax.fori_loop(0, (last - first) // 2, body, 0)

    def finish(i, carry):
        x = RIM + i
        total = None
        for back in range(STEPS + 1):
            source = wave_tiles(0, 1 + STEPS - back, x)
            receiver = wave_tiles(2, 1 + back, x)
            product = [a * b for a, b in zip(source, receiver)]
            total = product if total is None else [a + b for a, b in zip(total, product)]
        for out, value in (
            (0, total),
            (1, wave_tiles(2, 1 + STEPS, x)),
            (2, wave_tiles(3, 1 + STEPS, x)),
        ):
            for tile in range(tiles):
                wide[out, x, pl.ds(tile, SUBLANES, stride=tiles), :] = value[tile]
        return carry

    lax.fori_loop(0, cells_x, finish, 0)
    for out, ref in enumerate((image, p_last, q_last)):
        ref[...] = wide[out, RIM : RIM + cells_x, :cells_y, :]


def migrate(blocks, rims, planes):
    cells_x, cells_y, depth = blocks[0].shape
    count = len(blocks)
    planes_x, rows = cells_x + 2 * RIM + 2, cells_y + 2 * RIM
    tile = (rows // SUBLANES, SUBLANES, depth)
    out = jax.ShapeDtypeStruct((cells_x, cells_y, depth), jnp.float32)
    return pl.pallas_call(
        functools.partial(main_kernel, count, cells_x, cells_y),
        out_shape=[out] * 3,
        in_specs=in_vmem(count + len(rims) + 1),
        out_specs=in_vmem(3),
        scratch_shapes=[
            pltpu.VMEM((count, planes_x, rows, depth), jnp.float32),
            pltpu.VMEM((4, STEPS, planes_x) + tile, jnp.float32),
            pltpu.VMEM((9, planes_x) + tile, jnp.float32),
            pltpu.VMEM((4, 4, planes_x) + tile, jnp.float32),
        ],
        compiler_params=PARAMS,
        name="migrate",
    )(*blocks, *rims, planes)


def injected(gathered, receiver_x, receiver_y, samples, cells_x, cells_y, depth):
    everyone = gathered[:, :STEPS, :samples].transpose(1, 0, 2).reshape(STEPS, -1)
    rows = cells_y + 2 * RIM
    tiles = rows // SUBLANES
    x_global = lax.axis_index("gx") * cells_x - RIM + jnp.arange(depth, dtype=jnp.int32)
    place = jnp.arange(rows, dtype=jnp.int32)
    row = tiles * (place % SUBLANES) + place // SUBLANES
    y_local = jnp.where(row < cells_y + RIM, row, row - rows)
    y_global = lax.axis_index("gy") * cells_y + y_local
    pick_x = (receiver_x[None, :] == x_global[:, None]).astype(jnp.float32)
    pick_y = (receiver_y[None, :] == y_global[:, None]).astype(jnp.float32)
    weighted = everyone[:, None, :] * pick_y[None, :, :]
    planes = jnp.einsum("kyr,xr->kyx", weighted, pick_x, precision=lax.Precision.HIGHEST)
    return planes.reshape(STEPS, tiles, SUBLANES, depth)


def per_device(
    src_p_prev,
    src_p_now,
    src_q_prev,
    src_q_now,
    rec_p_next,
    rec_p_now,
    rec_q_next,
    rec_q_now,
    velocity_term,
    epsilon,
    delta,
    tilt,
    azimuth,
    traces,
    receiver_x,
    receiver_y,
    segment_start,
):
    blocks = (
        src_p_prev,
        src_p_now,
        src_q_prev,
        src_q_now,
        rec_p_next,
        rec_p_now,
        rec_q_next,
        rec_q_now,
        velocity_term,
        epsilon,
        delta,
        tilt,
        azimuth,
    )
    cells_x, cells_y, depth = src_p_now.shape
    y_a, y_b, x_a, x_b, copies = pack(blocks, traces, segment_start)
    y_a, y_b = swap(y_a, "gy", 0), swap(y_b, "gy", 1)
    x_a, x_b = swap(x_a, "gx", 0), swap(x_b, "gx", 1)
    gathered = lax.all_to_all(copies, ("gx", "gy"), 0, 0, tiled=True)
    c_a, c_b = corners(y_a, y_b)
    c_a, c_b = swap(c_a, "gx", 0), swap(c_b, "gx", 1)
    planes = injected(
        gathered, receiver_x, receiver_y, traces.shape[1], cells_x, cells_y, depth
    )
    return tuple(migrate(blocks, (y_a, y_b, x_a, x_b, c_a, c_b), planes))


def solution(mesh):
    state = P(("shot", "gx"), "gy", None)
    earth = P("gx", "gy", None)
    return jax.shard_map(
        per_device,
        mesh=mesh,
        in_specs=(state,) * FIELDS + (earth,) * 5 + (P("shot", ("gx", "gy")), P(), P(), P()),
        out_specs=(state,) * 3,
        check_vma=False,
    )
```

```python
import functools

import jax
import jax.numpy as jnp
from jax import lax
from jax.experimental import pallas as pl
from jax.experimental.pallas import tpu as pltpu
from jax.sharding import PartitionSpec as P

STEPS = 4
REC_DEPTH = 4
RIM = STEPS
FIELDS = 8
SUBLANES = 8
LANES = 128
VMEM_LIMIT = 48 * 1024 * 1024
PARAMS = pltpu.CompilerParams(vmem_limit_bytes=VMEM_LIMIT)


def in_vmem(count):
    return [pl.BlockSpec(memory_space=pltpu.VMEM)] * count


def is_odd(axis):
    return lax.rem(lax.axis_index(axis), 2) == 1


def swap(value, axis, first):
    size = lax.axis_size(axis)
    lower = range(first, size - 1, 2)
    pairs = [(i, i + 1) for i in lower] + [(i + 1, i) for i in lower]
    return lax.ppermute(value, axis, pairs)


NOW = (1, 3, 5, 7)
REST = (0, 2, 4, 6, 8, 9, 10, 11, 12)
SLIM = RIM - 1


def y_slots():
    slots = [((number, 0, RIM, 0),) for number in NOW]
    whole = len(REST) - len(REST) // RIM
    for place in range(whole):
        parts = [(REST[place], 0, SLIM, 0)]
        guest = whole + place // SLIM
        if guest < len(REST):
            parts.append((REST[guest], place % SLIM, 1, SLIM))
        slots.append(tuple(parts))
    return slots


def each_y_part(slots, high):
    for slot, parts in enumerate(slots):
        for number, row, rows, place in parts:
            if not high:
                yield slot, number, row, place, rows
            else:
                width = RIM if number in NOW else SLIM
                yield slot, number, RIM - width + row, 0 if place else RIM - rows, rows


def x_parts():
    parts, place = [], 0
    for number in NOW:
        parts.append((number, RIM, place))
        place += RIM
    for number in REST:
        parts.append((number, SLIM, place))
        place += SLIM
    return parts, place


def pinned(value, space):
    return pltpu.with_memory_space_constraint(value, space)


def vmem_out(*shape):
    return pltpu.VMEM(shape, jnp.float32)


def pack_kernel(count, *refs):
    blocks, traces, start = refs[:count], refs[count], refs[count + 1]
    wide, y_a, y_b, x_a, x_b, copies, sems = refs[count + 2 :]
    cells_x, cells_y = blocks[0].shape[:2]
    core_x = pl.ds(RIM, cells_x)
    moves = [
        pltpu.make_async_copy(block, wide.at[number, core_x, pl.ds(0, cells_y)], sems.at[number])
        for number, block in enumerate(blocks)
    ]
    for move in moves:
        move.start()
    odd_x, odd_y = is_odd("gx"), is_odd("gy")
    begin = start[0]
    samples = traces.shape[1]
    rows = [traces[pl.ds(begin + sample, 1), :] for sample in range(STEPS)]
    for device in range(copies.shape[0]):
        for sample in range(STEPS):
            copies[device, sample : sample + 1, :samples] = rows[sample]
    for move in moves:
        move.wait()

    def put_y(low, high):
        for out, is_high, base in ((low, False, 0), (high, True, cells_y - RIM)):
            for slot, number, row, place, length in each_y_part(y_slots(), is_high):
                out[slot, :, place : place + length, :] = wide[
                    number, RIM : RIM + cells_x, base + row : base + row + length, :
                ]

    @pl.when(odd_y)
    def _():
        put_y(y_a, y_b)

    @pl.when(jnp.logical_not(odd_y))
    def _():
        put_y(y_b, y_a)

    for number, width, place in x_parts()[0]:
        first, last = RIM, RIM + cells_x - width
        for out, begin in ((x_a, jnp.where(odd_x, first, last)), (x_b, jnp.where(odd_x, last, first))):
            out[place : place + width] = wide[number, pl.ds(begin, width), :cells_y, :]


def pack(blocks, traces, segment_start):
    cells_x, cells_y, depth = blocks[0].shape
    count = len(blocks)
    devices = lax.axis_size("gx") * lax.axis_size("gy")
    rim_y = vmem_out(len(y_slots()), cells_x, RIM, depth)
    rim_x = vmem_out(x_parts()[1], cells_y, depth)
    wide = vmem_out(count, cells_x + 2 * RIM + 2, cells_y + 2 * RIM, depth)
    return pl.pallas_call(
        functools.partial(pack_kernel, count),
        out_shape=[wide, rim_y, rim_y, rim_x, rim_x, vmem_out(devices, SUBLANES, LANES)],
        in_specs=[pl.BlockSpec(memory_space=pltpu.HBM)] * count
        + in_vmem(1)
        + [pl.BlockSpec(memory_space=pltpu.SMEM)],
        out_specs=in_vmem(6),
        scratch_shapes=[pltpu.SemaphoreType.DMA((count,))],
        compiler_params=PARAMS,
        name="pack_rims",
    )(*(pinned(block, pltpu.HBM) for block in blocks), traces, segment_start)


def corner_kernel(_, y_a, y_b, wide, c_a, c_b):
    cells_x = y_a.shape[1]
    cells_y = wide.shape[2] - 2 * RIM
    odd_x, odd_y = is_odd("gx"), is_odd("gy")

    def place_y(low, high):
        for rim, is_high, base in ((high, False, cells_y), (low, True, cells_y + RIM)):
            for slot, number, row, place, length in each_y_part(y_slots(), is_high):
                wide[number, RIM : RIM + cells_x, base + row : base + row + length, :] = rim[
                    slot, :, place : place + length, :
                ]

    @pl.when(odd_y)
    def _():
        place_y(y_a, y_b)

    @pl.when(jnp.logical_not(odd_y))
    def _():
        place_y(y_b, y_a)

    for number, width, place in x_parts()[0]:
        first, last = RIM, RIM + cells_x - width
        for out, begin in ((c_a, jnp.where(odd_x, first, last)), (c_b, jnp.where(odd_x, last, first))):
            out[place : place + width] = wide[number, pl.ds(begin, width), cells_y:, :]


def corners(wide, y_a, y_b):
    corner = vmem_out(x_parts()[1], 2 * RIM, wide.shape[-1])
    return pl.pallas_call(
        corner_kernel,
        out_shape=[vmem_out(*wide.shape), corner, corner],
        in_specs=in_vmem(3),
        out_specs=in_vmem(3),
        input_output_aliases={0: 0},
        compiler_params=PARAMS,
        name="pack_corners",
    )(pinned(wide, pltpu.VMEM), y_a, y_b)


def sine_cosine(angle):
    square = angle * angle
    sine = 1.0 / 6227020800.0
    for term in (-1.0 / 39916800.0, 1.0 / 362880.0, -1.0 / 5040.0, 1.0 / 120.0, -1.0 / 6.0, 1.0):
        sine = sine * square + term
    cosine = 1.0 / 479001600.0
    for term in (-1.0 / 3628800.0, 1.0 / 40320.0, -1.0 / 720.0, 1.0 / 24.0, -0.5, 1.0):
        cosine = cosine * square + term
    return sine * angle, cosine


def main_kernel(_, x_a, x_b, c_a, c_b, planes, wide, image, p_last, q_last, waves, factors, local):
    count = wide.shape[0]
    cells_x, cells_y, depth = image.shape
    span_x = cells_x + 2 * RIM
    tiles = (cells_y + 2 * RIM) // SUBLANES
    odd_x = is_odd("gx")
    for number, width, place in x_parts()[0]:
        low, high = RIM - width, RIM + cells_x
        for begin, side, corner in (
            (jnp.where(odd_x, low, high), x_a, c_a),
            (jnp.where(odd_x, high, low), x_b, c_b),
        ):
            wide[number, pl.ds(begin, width), :cells_y, :] = side[place : place + width]
            wide[number, pl.ds(begin, width), cells_y:, :] = corner[place : place + width]

    def wide_tiles(number, x):
        return [wide[number, x, pl.ds(tile, SUBLANES, stride=tiles), :] for tile in range(tiles)]

    def wave_tiles(number, slot, x):
        if slot < 2:
            return wide_tiles(2 * number + slot, x)
        return [waves[number, slot - 2, x, tile] for tile in range(tiles)]

    lane = lax.broadcasted_iota(jnp.int32, (SUBLANES, depth), 1)
    not_last, not_first = lane < depth - 1, lane > 0
    at_depth = lane == REC_DEPTH

    def next_y(value):
        return value[1:] + [pltpu.roll(value[0], SUBLANES - 1, 0)]

    def previous_y(value):
        return [pltpu.roll(value[-1], 1, 0)] + value[:-1]

    def make_factors(i, carry):
        stores = []
        for x in (1 + 2 * i, 2 + 2 * i):
            raw = [wide_tiles(FIELDS + number, x) for number in range(count - FIELDS)]
            for tile in range(tiles):
                velocity, epsilon, delta, tilt, azimuth = [value[tile] for value in raw]
                f_e = 1.0 + 2.0 * epsilon
                f_d = jnp.sqrt(1.0 + 2.0 * delta)
                sin_tilt, cos_tilt = sine_cosine(tilt)
                sin_half, cos_half = sine_cosine(0.5 * azimuth)
                sin_azim = 2.0 * sin_half * cos_half
                cos_azim = 1.0 - 2.0 * sin_half * sin_half
                sin_square = sin_tilt * sin_tilt
                half_tilt = 0.5 * sin_tilt * cos_tilt
                along_x = sin_square * cos_azim
                values = (
                    velocity,
                    velocity * f_e,
                    velocity * f_d,
                    along_x * cos_azim,
                    sin_square * sin_azim * sin_azim,
                    cos_tilt * cos_tilt,
                    0.5 * along_x * sin_azim,
                    half_tilt * cos_azim,
                    half_tilt * sin_azim,
                )
                stores += [(number, x, tile, value) for number, value in enumerate(values)]
        for number, x, tile, value in stores:
            factors[number, x, tile] = value
        return carry

    lax.fori_loop(0, (span_x - 2) // 2, make_factors, 0)

    def plane_part(turn, x, stores):
        ayy = [factors[4, x, tile] for tile in range(tiles)]
        azz = [factors[5, x, tile] for tile in range(tiles)]
        ayz = [factors[8, x, tile] for tile in range(tiles)]
        for number in range(4):
            now = wave_tiles(number, turn + 1, x)
            above = [jnp.where(not_last, pltpu.roll(u, depth - 1, 1), 0.0) for u in now]
            below = [jnp.where(not_first, pltpu.roll(u, 1, 1), 0.0) for u in now]
            slope_z = [a - b for a, b in zip(above, below)]
            after, before = next_y(now), previous_y(now)
            slope_after, slope_before = next_y(slope_z), previous_y(slope_z)
            for tile in range(tiles):
                double = now[tile] + now[tile]
                sum_y = after[tile] + before[tile]
                sum_z = above[tile] + below[tile]
                part = (
                    (ayy[tile] * sum_y + azz[tile] * sum_z)
                    + ayz[tile] * (slope_after[tile] - slope_before[tile])
                ) - double
                stores.append((local, (number, 0, x, tile), part))
                stores.append((local, (number, 1, x, tile), after[tile] - before[tile]))
                stores.append((local, (number, 2, x, tile), slope_z[tile]))
                if number % 2 == 0:
                    rest = (sum_y + sum_z) - 3.0 * double
                    stores.append((local, (number, 3, x, tile), rest))

    def next_part(turn, x, stores):
        held = [wave_tiles(number, turn, x) for number in range(4)]
        now = [wave_tiles(number, turn + 1, x) for number in range(4)]
        after = [wave_tiles(number, turn + 1, x + 1) for number in range(4)]
        before = [wave_tiles(number, turn + 1, x - 1) for number in range(4)]
        for tile in range(tiles):
            velocity, with_e, with_d = [factors[number, x, tile] for number in range(3)]
            axx, axy, axz = [factors[number, x, tile] for number in (3, 6, 7)]
            for pair in range(2):
                sums, axis = [], []
                for number in (2 * pair, 2 * pair + 1):
                    sum_x = after[number][tile] + before[number][tile]
                    d_xy = local[number, 1, x + 1, tile] - local[number, 1, x - 1, tile]
                    d_xz = local[number, 2, x + 1, tile] - local[number, 2, x - 1, tile]
                    sums.append(sum_x)
                    axis.append((local[number, 0, x, tile] + axx * sum_x) + (axy * d_xy + axz * d_xz))
                p_number, q_number = 2 * pair, 2 * pair + 1
                across = (sums[0] + local[p_number, 3, x, tile]) - axis[0]
                p_now, q_now = now[p_number][tile], now[q_number][tile]
                p_next = ((p_now + p_now) - held[p_number][tile]) + (
                    with_e * across + with_d * axis[1]
                )
                q_next = ((q_now + q_now) - held[q_number][tile]) + (
                    with_d * across + velocity * axis[1]
                )
                if pair == 1:
                    shift = lax.rem(REC_DEPTH - x + depth, depth)
                    moved = pltpu.roll(planes[STEPS - 1 - turn, tile], shift, 1)
                    p_next = p_next + jnp.where(at_depth, moved, 0.0)
                stores.append((waves, (p_number, turn, x, tile), p_next))
                stores.append((waves, (q_number, turn, x, tile), q_next))

    def write(stores):
        for ref, index, value in stores:
            ref[index] = value

    for turn in range(STEPS):
        first, last = turn + 1, span_x - 1 - turn
        for x in range(first - 1, first + 3):
            stores = []
            plane_part(turn, x, stores)
            write(stores)

        def body(i, carry, turn=turn, first=first):
            x = first + 2 * i
            stores = []
            next_part(turn, x, stores)
            next_part(turn, x + 1, stores)
            plane_part(turn, x + 3, stores)
            plane_part(turn, x + 4, stores)
            write(stores)
            return carry

        lax.fori_loop(0, (last - first) // 2, body, 0)

    def finish(i, carry):
        x = RIM + i
        total = None
        for back in range(STEPS + 1):
            source = wave_tiles(0, 1 + STEPS - back, x)
            receiver = wave_tiles(2, 1 + back, x)
            product = [a * b for a, b in zip(source, receiver)]
            total = product if total is None else [a + b for a, b in zip(total, product)]
        for out, value in (
            (0, total),
            (1, wave_tiles(2, 1 + STEPS, x)),
            (2, wave_tiles(3, 1 + STEPS, x)),
        ):
            for tile in range(tiles):
                wide[out, x, pl.ds(tile, SUBLANES, stride=tiles), :] = value[tile]
        return carry

    lax.fori_loop(0, cells_x, finish, 0)
    for out, ref in enumerate((image, p_last, q_last)):
        ref[...] = wide[out, RIM : RIM + cells_x, :cells_y, :]


def migrate(wide, rims, planes, cells_x, cells_y):
    count, planes_x, rows, depth = wide.shape
    tile = (rows // SUBLANES, SUBLANES, depth)
    out = jax.ShapeDtypeStruct((cells_x, cells_y, depth), jnp.float32)
    return pl.pallas_call(
        main_kernel,
        out_shape=[vmem_out(*wide.shape)] + [out] * 3,
        in_specs=in_vmem(len(rims) + 2),
        out_specs=in_vmem(4),
        input_output_aliases={0: 0},
        scratch_shapes=[
            pltpu.VMEM((4, STEPS, planes_x) + tile, jnp.float32),
            pltpu.VMEM((9, planes_x) + tile, jnp.float32),
            pltpu.VMEM((4, 4, planes_x) + tile, jnp.float32),
        ],
        compiler_params=PARAMS,
        name="migrate",
    )(pinned(wide, pltpu.VMEM), *rims, planes)[1:]


def injected(gathered, receiver_x, receiver_y, samples, cells_x, cells_y, depth):
    everyone = gathered[:, :STEPS, :samples].transpose(1, 0, 2).reshape(STEPS, -1)
    rows = cells_y + 2 * RIM
    tiles = rows // SUBLANES
    x_global = lax.axis_index("gx") * cells_x - RIM + jnp.arange(depth, dtype=jnp.int32)
    place = jnp.arange(rows, dtype=jnp.int32)
    row = tiles * (place % SUBLANES) + place // SUBLANES
    y_local = jnp.where(row < cells_y + RIM, row, row - rows)
    y_global = lax.axis_index("gy") * cells_y + y_local
    pick_x = (receiver_x[None, :] == x_global[:, None]).astype(jnp.float32)
    pick_y = (receiver_y[None, :] == y_global[:, None]).astype(jnp.float32)
    weighted = everyone[:, None, :] * pick_y[None, :, :]
    planes = jnp.einsum("kyr,xr->kyx", weighted, pick_x, precision=lax.Precision.HIGHEST)
    return planes.reshape(STEPS, tiles, SUBLANES, depth)


def per_device(
    src_p_prev,
    src_p_now,
    src_q_prev,
    src_q_now,
    rec_p_next,
    rec_p_now,
    rec_q_next,
    rec_q_now,
    velocity_term,
    epsilon,
    delta,
    tilt,
    azimuth,
    traces,
    receiver_x,
    receiver_y,
    segment_start,
):
    blocks = (
        src_p_prev,
        src_p_now,
        src_q_prev,
        src_q_now,
        rec_p_next,
        rec_p_now,
        rec_q_next,
        rec_q_now,
        velocity_term,
        epsilon,
        delta,
        tilt,
        azimuth,
    )
    cells_x, cells_y, depth = src_p_now.shape
    wide, y_a, y_b, x_a, x_b, copies = pack(blocks, traces, segment_start)
    y_a, y_b = swap(y_a, "gy", 0), swap(y_b, "gy", 1)
    x_a, x_b = swap(x_a, "gx", 0), swap(x_b, "gx", 1)
    gathered = lax.all_to_all(copies, ("gx", "gy"), 0, 0, tiled=True)
    wide, c_a, c_b = corners(wide, y_a, y_b)
    c_a, c_b = swap(c_a, "gx", 0), swap(c_b, "gx", 1)
    planes = injected(
        gathered, receiver_x, receiver_y, traces.shape[1], cells_x, cells_y, depth
    )
    return tuple(migrate(wide, (x_a, x_b, c_a, c_b), planes, cells_x, cells_y))


def solution(mesh):
    state = P(("shot", "gx"), "gy", None)
    earth = P("gx", "gy", None)
    return jax.shard_map(
        per_device,
        mesh=mesh,
        in_specs=(state,) * FIELDS + (earth,) * 5 + (P("shot", ("gx", "gy")), P(), P(), P()),
        out_specs=(state,) * 3,
        check_vma=False,
    )
```

```python
import functools

import jax
import jax.numpy as jnp
from jax import lax
from jax.experimental import pallas as pl
from jax.experimental.pallas import tpu as pltpu
from jax.sharding import PartitionSpec as P

STEPS = 4
REC_DEPTH = 4
RIM = STEPS
FIELDS = 8
SUBLANES = 8
LANES = 128
VMEM_LIMIT = 48 * 1024 * 1024
PARAMS = pltpu.CompilerParams(vmem_limit_bytes=VMEM_LIMIT)


def in_vmem(count):
    return [pl.BlockSpec(memory_space=pltpu.VMEM)] * count


def is_odd(axis):
    return lax.rem(lax.axis_index(axis), 2) == 1


def swap(value, axis, first):
    size = lax.axis_size(axis)
    lower = range(first, size - 1, 2)
    pairs = [(i, i + 1) for i in lower] + [(i + 1, i) for i in lower]
    return lax.ppermute(value, axis, pairs)


NOW = (1, 3, 5, 7)
REST = (0, 2, 4, 6, 8, 9, 10, 11, 12)
SLIM = RIM - 1


def y_slots():
    slots = [((number, 0, RIM, 0),) for number in NOW]
    whole = len(REST) - len(REST) // RIM
    for place in range(whole):
        parts = [(REST[place], 0, SLIM, 0)]
        guest = whole + place // SLIM
        if guest < len(REST):
            parts.append((REST[guest], place % SLIM, 1, SLIM))
        slots.append(tuple(parts))
    return slots


def each_y_part(slots, high):
    for slot, parts in enumerate(slots):
        for number, row, rows, place in parts:
            if not high:
                yield slot, number, row, place, rows
            else:
                width = RIM if number in NOW else SLIM
                yield slot, number, RIM - width + row, 0 if place else RIM - rows, rows


def x_parts():
    parts, place = [], 0
    for number in NOW:
        parts.append((number, RIM, place))
        place += RIM
    for number in REST:
        parts.append((number, SLIM, place))
        place += SLIM
    return parts, place


def pinned(value, space):
    return pltpu.with_memory_space_constraint(value, space)


def vmem_out(*shape):
    return pltpu.VMEM(shape, jnp.float32)


def pack_kernel(count, *refs):
    blocks, traces, start = refs[:count], refs[count], refs[count + 1]
    wide, y_a, y_b, window, held, sems = refs[count + 2 :]
    cells_x, cells_y = blocks[0].shape[:2]
    core_x = pl.ds(RIM, cells_x)
    moves = [
        pltpu.make_async_copy(block, wide.at[number, core_x, pl.ds(0, cells_y)], sems.at[number])
        for number, block in enumerate(blocks)
    ]
    moves.append(pltpu.make_async_copy(traces, held, sems.at[count]))
    for move in moves:
        move.start()
    odd_y = is_odd("gy")
    begin = start[0]
    samples = traces.shape[1]
    window[...] = jnp.zeros_like(window)
    for move in moves:
        move.wait()
    for sample in range(STEPS):
        window[0, sample : sample + 1, :samples] = held[pl.ds(begin + sample, 1), :]

    def put_y(low, high):
        for out, is_high, base in ((low, False, 0), (high, True, cells_y - RIM)):
            for slot, number, row, place, length in each_y_part(y_slots(), is_high):
                out[slot, :, place : place + length, :] = wide[
                    number, RIM : RIM + cells_x, base + row : base + row + length, :
                ]

    @pl.when(odd_y)
    def _():
        put_y(y_a, y_b)

    @pl.when(jnp.logical_not(odd_y))
    def _():
        put_y(y_b, y_a)


def pack(blocks, traces, segment_start):
    cells_x, cells_y, depth = blocks[0].shape
    count = len(blocks)
    rim_y = vmem_out(len(y_slots()), cells_x, RIM, depth)
    wide = vmem_out(count, cells_x + 2 * RIM + 2, cells_y + 2 * RIM, depth)
    return pl.pallas_call(
        functools.partial(pack_kernel, count),
        out_shape=[wide, rim_y, rim_y, vmem_out(1, STEPS, LANES)],
        in_specs=[pl.BlockSpec(memory_space=pltpu.HBM)] * (count + 1)
        + [pl.BlockSpec(memory_space=pltpu.SMEM)],
        out_specs=in_vmem(4),
        scratch_shapes=[
            pltpu.VMEM(traces.shape, jnp.float32),
            pltpu.SemaphoreType.DMA((count + 1,)),
        ],
        compiler_params=PARAMS,
        name="pack_y_rims",
    )(*(pinned(value, pltpu.HBM) for value in (*blocks, traces)), segment_start)


def pack_x_kernel(_, window, wide, x_a, x_b):
    cells_x, cells_y = wide.shape[1] - 2 * RIM - 2, wide.shape[2] - 2 * RIM
    odd_x = is_odd("gx")
    parts, total = x_parts()
    for number, width, place in parts:
        first, last = RIM, RIM + cells_x - width
        for out, begin in ((x_a, jnp.where(odd_x, first, last)), (x_b, jnp.where(odd_x, last, first))):
            out[place : place + width] = wide[number, pl.ds(begin, width), :cells_y, :]
    x_a[total] = jnp.zeros_like(x_a[total])
    x_a[total, :STEPS, :] = window[0]


def pack_x(wide, window):
    _, _, rows, depth = wide.shape
    total = x_parts()[1]
    return pl.pallas_call(
        pack_x_kernel,
        out_shape=[
            vmem_out(*wide.shape),
            vmem_out(total + 1, rows - 2 * RIM, depth),
            vmem_out(total, rows - 2 * RIM, depth),
        ],
        in_specs=in_vmem(2),
        out_specs=in_vmem(3),
        input_output_aliases={0: 0},
        compiler_params=PARAMS,
        name="pack_x_rims",
    )(pinned(wide, pltpu.VMEM), window)


def corner_kernel(_, y_a, y_b, wide, c_a, c_b):
    cells_x = y_a.shape[1]
    cells_y = wide.shape[2] - 2 * RIM
    odd_x, odd_y = is_odd("gx"), is_odd("gy")

    def place_y(low, high):
        for rim, is_high, base in ((high, False, cells_y), (low, True, cells_y + RIM)):
            for slot, number, row, place, length in each_y_part(y_slots(), is_high):
                wide[number, RIM : RIM + cells_x, base + row : base + row + length, :] = rim[
                    slot, :, place : place + length, :
                ]

    @pl.when(odd_y)
    def _():
        place_y(y_a, y_b)

    @pl.when(jnp.logical_not(odd_y))
    def _():
        place_y(y_b, y_a)

    for number, width, place in x_parts()[0]:
        first, last = RIM, RIM + cells_x - width
        for out, begin in ((c_a, jnp.where(odd_x, first, last)), (c_b, jnp.where(odd_x, last, first))):
            out[place : place + width] = wide[number, pl.ds(begin, width), cells_y:, :]


def corners(wide, y_a, y_b):
    corner = vmem_out(x_parts()[1], 2 * RIM, wide.shape[-1])
    return pl.pallas_call(
        corner_kernel,
        out_shape=[vmem_out(*wide.shape), corner, corner],
        in_specs=in_vmem(3),
        out_specs=in_vmem(3),
        input_output_aliases={0: 0},
        compiler_params=PARAMS,
        name="pack_corners",
    )(pinned(wide, pltpu.VMEM), y_a, y_b)


def sine_cosine(angle):
    square = angle * angle
    sine = 1.0 / 6227020800.0
    for term in (-1.0 / 39916800.0, 1.0 / 362880.0, -1.0 / 5040.0, 1.0 / 120.0, -1.0 / 6.0, 1.0):
        sine = sine * square + term
    cosine = 1.0 / 479001600.0
    for term in (-1.0 / 3628800.0, 1.0 / 40320.0, -1.0 / 720.0, 1.0 / 24.0, -0.5, 1.0):
        cosine = cosine * square + term
    return sine * angle, cosine


def main_kernel(_, x_a, x_b, c_a, c_b, planes, wide, image, p_last, q_last, waves, factors, local):
    count = wide.shape[0]
    cells_x, cells_y, depth = image.shape
    span_x = cells_x + 2 * RIM
    tiles = (cells_y + 2 * RIM) // SUBLANES
    odd_x = is_odd("gx")
    for number, width, place in x_parts()[0]:
        low, high = RIM - width, RIM + cells_x
        for begin, side, corner in (
            (jnp.where(odd_x, low, high), x_a, c_a),
            (jnp.where(odd_x, high, low), x_b, c_b),
        ):
            wide[number, pl.ds(begin, width), :cells_y, :] = side[place : place + width]
            wide[number, pl.ds(begin, width), cells_y:, :] = corner[place : place + width]

    def wide_tiles(number, x):
        return [wide[number, x, pl.ds(tile, SUBLANES, stride=tiles), :] for tile in range(tiles)]

    def wave_tiles(number, slot, x):
        if slot < 2:
            return wide_tiles(2 * number + slot, x)
        return [waves[number, slot - 2, x, tile] for tile in range(tiles)]

    lane = lax.broadcasted_iota(jnp.int32, (SUBLANES, depth), 1)
    not_last, not_first = lane < depth - 1, lane > 0
    at_depth = lane == REC_DEPTH

    def next_y(value):
        return value[1:] + [pltpu.roll(value[0], SUBLANES - 1, 0)]

    def previous_y(value):
        return [pltpu.roll(value[-1], 1, 0)] + value[:-1]

    def make_factors(i, carry):
        stores = []
        for x in (1 + 2 * i, 2 + 2 * i):
            raw = [wide_tiles(FIELDS + number, x) for number in range(count - FIELDS)]
            for tile in range(tiles):
                velocity, epsilon, delta, tilt, azimuth = [value[tile] for value in raw]
                f_e = 1.0 + 2.0 * epsilon
                f_d = jnp.sqrt(1.0 + 2.0 * delta)
                sin_tilt, cos_tilt = sine_cosine(tilt)
                sin_half, cos_half = sine_cosine(0.5 * azimuth)
                sin_azim = 2.0 * sin_half * cos_half
                cos_azim = 1.0 - 2.0 * sin_half * sin_half
                sin_square = sin_tilt * sin_tilt
                half_tilt = 0.5 * sin_tilt * cos_tilt
                along_x = sin_square * cos_azim
                values = (
                    velocity,
                    velocity * f_e,
                    velocity * f_d,
                    along_x * cos_azim,
                    sin_square * sin_azim * sin_azim,
                    cos_tilt * cos_tilt,
                    0.5 * along_x * sin_azim,
                    half_tilt * cos_azim,
                    half_tilt * sin_azim,
                )
                stores += [(number, x, tile, value) for number, value in enumerate(values)]
        for number, x, tile, value in stores:
            factors[number, x, tile] = value
        return carry

    lax.fori_loop(0, (span_x - 2) // 2, make_factors, 0)

    def plane_part(turn, x, stores):
        ayy = [factors[4, x, tile] for tile in range(tiles)]
        azz = [factors[5, x, tile] for tile in range(tiles)]
        ayz = [factors[8, x, tile] for tile in range(tiles)]
        for number in range(4):
            now = wave_tiles(number, turn + 1, x)
            above = [jnp.where(not_last, pltpu.roll(u, depth - 1, 1), 0.0) for u in now]
            below = [jnp.where(not_first, pltpu.roll(u, 1, 1), 0.0) for u in now]
            slope_z = [a - b for a, b in zip(above, below)]
            after, before = next_y(now), previous_y(now)
            slope_after, slope_before = next_y(slope_z), previous_y(slope_z)
            for tile in range(tiles):
                double = now[tile] + now[tile]
                sum_y = after[tile] + before[tile]
                sum_z = above[tile] + below[tile]
                part = (
                    (ayy[tile] * sum_y + azz[tile] * sum_z)
                    + ayz[tile] * (slope_after[tile] - slope_before[tile])
                ) - double
                stores.append((local, (number, 0, x, tile), part))
                stores.append((local, (number, 1, x, tile), after[tile] - before[tile]))
                stores.append((local, (number, 2, x, tile), slope_z[tile]))
                if number % 2 == 0:
                    rest = (sum_y + sum_z) - 3.0 * double
                    stores.append((local, (number, 3, x, tile), rest))

    def next_part(turn, x, stores):
        held = [wave_tiles(number, turn, x) for number in range(4)]
        now = [wave_tiles(number, turn + 1, x) for number in range(4)]
        after = [wave_tiles(number, turn + 1, x + 1) for number in range(4)]
        before = [wave_tiles(number, turn + 1, x - 1) for number in range(4)]
        for tile in range(tiles):
            velocity, with_e, with_d = [factors[number, x, tile] for number in range(3)]
            axx, axy, axz = [factors[number, x, tile] for number in (3, 6, 7)]
            for pair in range(2):
                sums, axis = [], []
                for number in (2 * pair, 2 * pair + 1):
                    sum_x = after[number][tile] + before[number][tile]
                    d_xy = local[number, 1, x + 1, tile] - local[number, 1, x - 1, tile]
                    d_xz = local[number, 2, x + 1, tile] - local[number, 2, x - 1, tile]
                    sums.append(sum_x)
                    axis.append((local[number, 0, x, tile] + axx * sum_x) + (axy * d_xy + axz * d_xz))
                p_number, q_number = 2 * pair, 2 * pair + 1
                across = (sums[0] + local[p_number, 3, x, tile]) - axis[0]
                p_now, q_now = now[p_number][tile], now[q_number][tile]
                p_next = ((p_now + p_now) - held[p_number][tile]) + (
                    with_e * across + with_d * axis[1]
                )
                q_next = ((q_now + q_now) - held[q_number][tile]) + (
                    with_d * across + velocity * axis[1]
                )
                if pair == 1:
                    shift = lax.rem(REC_DEPTH - x + depth, depth)
                    moved = pltpu.roll(planes[STEPS - 1 - turn, tile], shift, 1)
                    p_next = p_next + jnp.where(at_depth, moved, 0.0)
                stores.append((waves, (p_number, turn, x, tile), p_next))
                stores.append((waves, (q_number, turn, x, tile), q_next))

    def write(stores):
        for ref, index, value in stores:
            ref[index] = value

    for turn in range(STEPS):
        first, last = turn + 1, span_x - 1 - turn
        for x in range(first - 1, first + 3):
            stores = []
            plane_part(turn, x, stores)
            write(stores)

        def body(i, carry, turn=turn, first=first):
            x = first + 2 * i
            stores = []
            next_part(turn, x, stores)
            next_part(turn, x + 1, stores)
            plane_part(turn, x + 3, stores)
            plane_part(turn, x + 4, stores)
            write(stores)
            return carry

        lax.fori_loop(0, (last - first) // 2, body, 0)

    def finish(i, carry):
        x = RIM + i
        total = None
        for back in range(STEPS + 1):
            source = wave_tiles(0, 1 + STEPS - back, x)
            receiver = wave_tiles(2, 1 + back, x)
            product = [a * b for a, b in zip(source, receiver)]
            total = product if total is None else [a + b for a, b in zip(total, product)]
        for out, value in (
            (0, total),
            (1, wave_tiles(2, 1 + STEPS, x)),
            (2, wave_tiles(3, 1 + STEPS, x)),
        ):
            for tile in range(tiles):
                wide[out, x, pl.ds(tile, SUBLANES, stride=tiles), :] = value[tile]
        return carry

    lax.fori_loop(0, cells_x, finish, 0)
    for out, ref in enumerate((image, p_last, q_last)):
        ref[...] = wide[out, RIM : RIM + cells_x, :cells_y, :]


def migrate(wide, rims, planes, cells_x, cells_y):
    count, planes_x, rows, depth = wide.shape
    tile = (rows // SUBLANES, SUBLANES, depth)
    out = jax.ShapeDtypeStruct((cells_x, cells_y, depth), jnp.float32)
    return pl.pallas_call(
        main_kernel,
        out_shape=[vmem_out(*wide.shape)] + [out] * 3,
        in_specs=in_vmem(len(rims) + 2),
        out_specs=in_vmem(4),
        input_output_aliases={0: 0},
        scratch_shapes=[
            pltpu.VMEM((4, STEPS, planes_x) + tile, jnp.float32),
            pltpu.VMEM((9, planes_x) + tile, jnp.float32),
            pltpu.VMEM((4, 4, planes_x) + tile, jnp.float32),
        ],
        compiler_params=PARAMS,
        name="migrate",
    )(pinned(wide, pltpu.VMEM), *rims, planes)[1:]


def bits_of(axis):
    size = lax.axis_size(axis)
    return [1 << bit for bit in range(size.bit_length() - 1)] if size & (size - 1) == 0 else None


def doubled(windows, axis, bit):
    pairs = [(i, i ^ bit) for i in range(lax.axis_size(axis))]
    return jnp.concatenate([windows, lax.ppermute(windows, axis, pairs)], axis=0)


def in_gathered_order(receivers, samples):
    size_x, size_y = lax.axis_size("gx"), lax.axis_size("gy")
    grid = receivers.reshape(size_x, size_y, samples).transpose(1, 0, 2)
    for dim, axis, size in ((0, "gy", size_y), (1, "gx", size_x)):
        for bit in bits_of(axis):
            shape = grid.shape[:dim] + (size // (2 * bit), 2, bit) + grid.shape[dim + 1 :]
            apart = grid.reshape(shape)
            swapped = jnp.flip(apart, dim + 1)
            is_set = (lax.axis_index(axis) // bit) % 2 == 1
            grid = jnp.where(is_set, swapped, apart).reshape(grid.shape)
    return grid.reshape(-1)


def injected(gathered, receiver_x, receiver_y, samples, cells_x, cells_y, depth):
    everyone = gathered[:, :, :samples].transpose(1, 0, 2).reshape(STEPS, -1)
    rows = cells_y + 2 * RIM
    tiles = rows // SUBLANES
    x_global = lax.axis_index("gx") * cells_x - RIM + jnp.arange(depth, dtype=jnp.int32)
    place = jnp.arange(rows, dtype=jnp.int32)
    row = tiles * (place % SUBLANES) + place // SUBLANES
    y_local = jnp.where(row < cells_y + RIM, row, row - rows)
    y_global = lax.axis_index("gy") * cells_y + y_local
    order_x = in_gathered_order(receiver_x, samples)
    order_y = in_gathered_order(receiver_y, samples)
    pick_x = (order_x[None, :] == x_global[:, None]).astype(jnp.float32)
    pick_y = (order_y[None, :] == y_global[:, None]).astype(jnp.float32)
    weighted = everyone[:, None, :] * pick_y[None, :, :]
    planes = jnp.einsum("kyr,xr->kyx", weighted, pick_x, precision=lax.Precision.HIGHEST)
    return planes.reshape(STEPS, tiles, SUBLANES, depth)


def per_device(
    src_p_prev,
    src_p_now,
    src_q_prev,
    src_q_now,
    rec_p_next,
    rec_p_now,
    rec_q_next,
    rec_q_now,
    velocity_term,
    epsilon,
    delta,
    tilt,
    azimuth,
    traces,
    receiver_x,
    receiver_y,
    segment_start,
):
    blocks = (
        src_p_prev,
        src_p_now,
        src_q_prev,
        src_q_now,
        rec_p_next,
        rec_p_now,
        rec_q_next,
        rec_q_now,
        velocity_term,
        epsilon,
        delta,
        tilt,
        azimuth,
    )
    cells_x, cells_y, depth = src_p_now.shape
    wide, y_a, y_b, window = pack(blocks, traces, segment_start)
    y_a, y_b = swap(y_a, "gy", 0), swap(y_b, "gy", 1)
    wide, x_a, x_b = pack_x(wide, window)
    x_a, x_b = swap(x_a, "gx", 0), swap(x_b, "gx", 1)
    windows = jnp.concatenate([window, x_a[x_parts()[1] :, :STEPS, :]], axis=0)
    for bit in bits_of("gx")[1:]:
        windows = doubled(windows, "gx", bit)
    for bit in bits_of("gy"):
        windows = doubled(windows, "gy", bit)
    wide, c_a, c_b = corners(wide, y_a, y_b)
    c_a, c_b = swap(c_a, "gx", 0), swap(c_b, "gx", 1)
    planes = injected(
        windows, receiver_x, receiver_y, traces.shape[1], cells_x, cells_y, depth
    )
    return tuple(migrate(wide, (x_a, x_b, c_a, c_b), planes, cells_x, cells_y))


def solution(mesh):
    state = P(("shot", "gx"), "gy", None)
    earth = P("gx", "gy", None)
    return jax.shard_map(
        per_device,
        mesh=mesh,
        in_specs=(state,) * FIELDS + (earth,) * 5 + (P("shot", ("gx", "gy")), P(), P(), P()),
        out_specs=(state,) * 3,
        check_vma=False,
    )
```

```python
import functools

import jax
import jax.numpy as jnp
from jax import lax
from jax.experimental import pallas as pl
from jax.experimental.pallas import tpu as pltpu
from jax.sharding import PartitionSpec as P

STEPS = 4
REC_DEPTH = 4
RIM = STEPS
FIELDS = 8
SUBLANES = 8
LANES = 128
VMEM_LIMIT = 48 * 1024 * 1024
PARAMS = pltpu.CompilerParams(vmem_limit_bytes=VMEM_LIMIT)


def in_vmem(count):
    return [pl.BlockSpec(memory_space=pltpu.VMEM)] * count


def is_odd(axis):
    return lax.rem(lax.axis_index(axis), 2) == 1


def swap(value, axis, first):
    size = lax.axis_size(axis)
    lower = range(first, size - 1, 2)
    pairs = [(i, i + 1) for i in lower] + [(i + 1, i) for i in lower]
    return lax.ppermute(value, axis, pairs)


NOW = (1, 3, 5, 7)
REST = (0, 2, 4, 6, 8, 9, 10, 11, 12)
SLIM = RIM - 1


def y_slots():
    slots = [((number, 0, RIM, 0),) for number in NOW]
    whole = len(REST) - len(REST) // RIM
    for place in range(whole):
        parts = [(REST[place], 0, SLIM, 0)]
        guest = whole + place // SLIM
        if guest < len(REST):
            parts.append((REST[guest], place % SLIM, 1, SLIM))
        slots.append(tuple(parts))
    return slots


def each_y_part(slots, high):
    for slot, parts in enumerate(slots):
        for number, row, rows, place in parts:
            if not high:
                yield slot, number, row, place, rows
            else:
                width = RIM if number in NOW else SLIM
                yield slot, number, RIM - width + row, 0 if place else RIM - rows, rows


def x_parts():
    parts, place = [], 0
    for number in NOW:
        parts.append((number, RIM, place))
        place += RIM
    for number in REST:
        parts.append((number, SLIM, place))
        place += SLIM
    return parts, place


def pinned(value, space):
    return pltpu.with_memory_space_constraint(value, space)


def vmem_out(*shape):
    return pltpu.VMEM(shape, jnp.float32)


def pack_kernel(count, *refs):
    blocks, traces, start = refs[:count], refs[count], refs[count + 1]
    wide, y_a, y_b, window, held, sems = refs[count + 2 :]
    cells_x, cells_y = blocks[0].shape[:2]
    core_x = pl.ds(RIM, cells_x)
    moves = [
        pltpu.make_async_copy(block, wide.at[number, core_x, pl.ds(0, cells_y)], sems.at[number])
        for number, block in enumerate(blocks)
    ]
    moves.append(pltpu.make_async_copy(traces, held, sems.at[count]))
    for move in moves:
        move.start()
    odd_y = is_odd("gy")
    begin = start[0]
    samples = traces.shape[1]
    window[...] = jnp.zeros_like(window)
    for move in moves:
        move.wait()
    for sample in range(STEPS):
        window[0, sample : sample + 1, :samples] = held[pl.ds(begin + sample, 1), :]

    def put_y(low, high):
        for out, is_high, base in ((low, False, 0), (high, True, cells_y - RIM)):
            for slot, number, row, place, length in each_y_part(y_slots(), is_high):
                out[slot, :, place : place + length, :] = wide[
                    number, RIM : RIM + cells_x, base + row : base + row + length, :
                ]

    @pl.when(odd_y)
    def _():
        put_y(y_a, y_b)

    @pl.when(jnp.logical_not(odd_y))
    def _():
        put_y(y_b, y_a)


def pack(blocks, traces, segment_start):
    cells_x, cells_y, depth = blocks[0].shape
    count = len(blocks)
    rim_y = vmem_out(len(y_slots()), cells_x, RIM, depth)
    wide = vmem_out(count, cells_x + 2 * RIM + 2, cells_y + 2 * RIM, depth)
    return pl.pallas_call(
        functools.partial(pack_kernel, count),
        out_shape=[wide, rim_y, rim_y, vmem_out(1, STEPS, LANES)],
        in_specs=[pl.BlockSpec(memory_space=pltpu.HBM)] * (count + 1)
        + [pl.BlockSpec(memory_space=pltpu.SMEM)],
        out_specs=in_vmem(4),
        scratch_shapes=[
            pltpu.VMEM(traces.shape, jnp.float32),
            pltpu.SemaphoreType.DMA((count + 1,)),
        ],
        compiler_params=PARAMS,
        name="pack_y_rims",
    )(*(pinned(value, pltpu.HBM) for value in (*blocks, traces)), segment_start)


def pack_x_kernel(_, window, wide, x_a, x_b):
    cells_x, cells_y = wide.shape[1] - 2 * RIM - 2, wide.shape[2] - 2 * RIM
    odd_x = is_odd("gx")
    parts, total = x_parts()
    for number, width, place in parts:
        first, last = RIM, RIM + cells_x - width
        for out, begin in ((x_a, jnp.where(odd_x, first, last)), (x_b, jnp.where(odd_x, last, first))):
            out[place : place + width] = wide[number, pl.ds(begin, width), :cells_y, :]
    x_a[total] = jnp.zeros_like(x_a[total])
    x_a[total, :STEPS, :] = window[0]


def pack_x(wide, window):
    _, _, rows, depth = wide.shape
    total = x_parts()[1]
    return pl.pallas_call(
        pack_x_kernel,
        out_shape=[
            vmem_out(*wide.shape),
            vmem_out(total + 1, rows - 2 * RIM, depth),
            vmem_out(total, rows - 2 * RIM, depth),
        ],
        in_specs=in_vmem(2),
        out_specs=in_vmem(3),
        input_output_aliases={0: 0},
        compiler_params=PARAMS,
        name="pack_x_rims",
    )(pinned(wide, pltpu.VMEM), window)


def corner_kernel(_, y_a, y_b, wide, c_a, c_b):
    cells_x = y_a.shape[1]
    cells_y = wide.shape[2] - 2 * RIM
    odd_x, odd_y = is_odd("gx"), is_odd("gy")

    def place_y(low, high):
        for rim, is_high, base in ((high, False, cells_y), (low, True, cells_y + RIM)):
            for slot, number, row, place, length in each_y_part(y_slots(), is_high):
                wide[number, RIM : RIM + cells_x, base + row : base + row + length, :] = rim[
                    slot, :, place : place + length, :
                ]

    @pl.when(odd_y)
    def _():
        place_y(y_a, y_b)

    @pl.when(jnp.logical_not(odd_y))
    def _():
        place_y(y_b, y_a)

    for number, width, place in x_parts()[0]:
        first, last = RIM, RIM + cells_x - width
        for out, begin in ((c_a, jnp.where(odd_x, first, last)), (c_b, jnp.where(odd_x, last, first))):
            out[place : place + width] = wide[number, pl.ds(begin, width), cells_y:, :]


def corners(wide, y_a, y_b):
    corner = vmem_out(x_parts()[1], 2 * RIM, wide.shape[-1])
    return pl.pallas_call(
        corner_kernel,
        out_shape=[vmem_out(*wide.shape), corner, corner],
        in_specs=in_vmem(3),
        out_specs=in_vmem(3),
        input_output_aliases={0: 0},
        compiler_params=PARAMS,
        name="pack_corners",
    )(pinned(wide, pltpu.VMEM), y_a, y_b)


def sine_cosine(angle):
    square = angle * angle
    sine = 1.0 / 6227020800.0
    for term in (-1.0 / 39916800.0, 1.0 / 362880.0, -1.0 / 5040.0, 1.0 / 120.0, -1.0 / 6.0, 1.0):
        sine = sine * square + term
    cosine = 1.0 / 479001600.0
    for term in (-1.0 / 3628800.0, 1.0 / 40320.0, -1.0 / 720.0, 1.0 / 24.0, -0.5, 1.0):
        cosine = cosine * square + term
    return sine * angle, cosine


def main_kernel(_, x_a, x_b, c_a, c_b, planes, wide, image, p_last, q_last, waves, factors, local):
    count = wide.shape[0]
    cells_x, cells_y, depth = image.shape
    span_x = cells_x + 2 * RIM
    tiles = (cells_y + 2 * RIM) // SUBLANES
    odd_x = is_odd("gx")
    for number, width, place in x_parts()[0]:
        low, high = RIM - width, RIM + cells_x
        for begin, side, corner in (
            (jnp.where(odd_x, low, high), x_a, c_a),
            (jnp.where(odd_x, high, low), x_b, c_b),
        ):
            wide[number, pl.ds(begin, width), :cells_y, :] = side[place : place + width]
            wide[number, pl.ds(begin, width), cells_y:, :] = corner[place : place + width]

    def wide_tiles(number, x):
        return [wide[number, x, pl.ds(tile, SUBLANES, stride=tiles), :] for tile in range(tiles)]

    def wave_tiles(number, slot, x):
        if slot < 2:
            return wide_tiles(2 * number + slot, x)
        return [waves[number, slot - 2, x, tile] for tile in range(tiles)]

    lane = lax.broadcasted_iota(jnp.int32, (SUBLANES, depth), 1)
    not_last, not_first = lane < depth - 1, lane > 0
    at_depth = lane == REC_DEPTH

    def next_y(value):
        return value[1:] + [pltpu.roll(value[0], SUBLANES - 1, 0)]

    def previous_y(value):
        return [pltpu.roll(value[-1], 1, 0)] + value[:-1]

    def make_factors(i, carry):
        stores = []
        for x in (1 + 2 * i, 2 + 2 * i):
            raw = [wide_tiles(FIELDS + number, x) for number in range(count - FIELDS)]
            for tile in range(tiles):
                velocity, epsilon, delta, tilt, azimuth = [value[tile] for value in raw]
                f_e = 1.0 + 2.0 * epsilon
                f_d = jnp.sqrt(1.0 + 2.0 * delta)
                sin_tilt, cos_tilt = sine_cosine(tilt)
                sin_half, cos_half = sine_cosine(0.5 * azimuth)
                sin_azim = 2.0 * sin_half * cos_half
                cos_azim = 1.0 - 2.0 * sin_half * sin_half
                sin_square = sin_tilt * sin_tilt
                half_tilt = 0.5 * sin_tilt * cos_tilt
                along_x = sin_square * cos_azim
                values = (
                    velocity,
                    velocity * f_e,
                    velocity * f_d,
                    along_x * cos_azim,
                    sin_square * sin_azim * sin_azim,
                    cos_tilt * cos_tilt,
                    0.5 * along_x * sin_azim,
                    half_tilt * cos_azim,
                    half_tilt * sin_azim,
                )
                stores += [(number, x, tile, value) for number, value in enumerate(values)]
        for number, x, tile, value in stores:
            factors[number, x, tile] = value
        return carry

    lax.fori_loop(0, (span_x - 2) // 2, make_factors, 0)

    def plane_part(turn, x, stores):
        ayy = [factors[4, x, tile] for tile in range(tiles)]
        azz = [factors[5, x, tile] for tile in range(tiles)]
        ayz = [factors[8, x, tile] for tile in range(tiles)]
        for number in range(4):
            now = wave_tiles(number, turn + 1, x)
            above = [jnp.where(not_last, pltpu.roll(u, depth - 1, 1), 0.0) for u in now]
            below = [jnp.where(not_first, pltpu.roll(u, 1, 1), 0.0) for u in now]
            slope_z = [a - b for a, b in zip(above, below)]
            after, before = next_y(now), previous_y(now)
            slope_after, slope_before = next_y(slope_z), previous_y(slope_z)
            for tile in range(tiles):
                double = now[tile] + now[tile]
                sum_y = after[tile] + before[tile]
                sum_z = above[tile] + below[tile]
                part = (
                    (ayy[tile] * sum_y + azz[tile] * sum_z)
                    + ayz[tile] * (slope_after[tile] - slope_before[tile])
                ) - double
                stores.append((local, (number, 0, x, tile), part))
                stores.append((local, (number, 1, x, tile), after[tile] - before[tile]))
                stores.append((local, (number, 2, x, tile), slope_z[tile]))
                if number % 2 == 0:
                    rest = (sum_y + sum_z) - 3.0 * double
                    stores.append((local, (number, 3, x, tile), rest))

    def next_part(turn, x, stores):
        held = [wave_tiles(number, turn, x) for number in range(4)]
        now = [wave_tiles(number, turn + 1, x) for number in range(4)]
        after = [wave_tiles(number, turn + 1, x + 1) for number in range(4)]
        before = [wave_tiles(number, turn + 1, x - 1) for number in range(4)]
        for tile in range(tiles):
            velocity, with_e, with_d = [factors[number, x, tile] for number in range(3)]
            axx, axy, axz = [factors[number, x, tile] for number in (3, 6, 7)]
            for pair in range(2):
                sums, axis = [], []
                for number in (2 * pair, 2 * pair + 1):
                    sum_x = after[number][tile] + before[number][tile]
                    d_xy = local[number, 1, x + 1, tile] - local[number, 1, x - 1, tile]
                    d_xz = local[number, 2, x + 1, tile] - local[number, 2, x - 1, tile]
                    sums.append(sum_x)
                    axis.append((local[number, 0, x, tile] + axx * sum_x) + (axy * d_xy + axz * d_xz))
                p_number, q_number = 2 * pair, 2 * pair + 1
                across = (sums[0] + local[p_number, 3, x, tile]) - axis[0]
                p_now, q_now = now[p_number][tile], now[q_number][tile]
                p_next = ((p_now + p_now) - held[p_number][tile]) + (
                    with_e * across + with_d * axis[1]
                )
                q_next = ((q_now + q_now) - held[q_number][tile]) + (
                    with_d * across + velocity * axis[1]
                )
                if pair == 1:
                    shift = lax.rem(REC_DEPTH - x + depth, depth)
                    moved = pltpu.roll(planes[STEPS - 1 - turn, tile], shift, 1)
                    p_next = p_next + jnp.where(at_depth, moved, 0.0)
                stores.append((waves, (p_number, turn, x, tile), p_next))
                stores.append((waves, (q_number, turn, x, tile), q_next))

    def write(stores):
        for ref, index, value in stores:
            ref[index] = value

    for turn in range(STEPS):
        first, last = turn + 1, span_x - 1 - turn
        for x in range(first - 1, first + 3):
            stores = []
            plane_part(turn, x, stores)
            write(stores)

        def body(i, carry, turn=turn, first=first):
            x = first + 2 * i
            stores = []
            next_part(turn, x, stores)
            next_part(turn, x + 1, stores)
            plane_part(turn, x + 3, stores)
            plane_part(turn, x + 4, stores)
            write(stores)
            return carry

        lax.fori_loop(0, (last - first) // 2, body, 0)

    def finish(i, carry):
        x = RIM + i
        total = None
        for back in range(STEPS + 1):
            source = wave_tiles(0, 1 + STEPS - back, x)
            receiver = wave_tiles(2, 1 + back, x)
            product = [a * b for a, b in zip(source, receiver)]
            total = product if total is None else [a + b for a, b in zip(total, product)]
        for out, value in (
            (0, total),
            (1, wave_tiles(2, 1 + STEPS, x)),
            (2, wave_tiles(3, 1 + STEPS, x)),
        ):
            for tile in range(tiles):
                wide[out, x, pl.ds(tile, SUBLANES, stride=tiles), :] = value[tile]
        return carry

    lax.fori_loop(0, cells_x, finish, 0)
    for out, ref in enumerate((image, p_last, q_last)):
        ref[...] = wide[out, RIM : RIM + cells_x, :cells_y, :]


def migrate(wide, rims, planes, cells_x, cells_y):
    count, planes_x, rows, depth = wide.shape
    tile = (rows // SUBLANES, SUBLANES, depth)
    out = jax.ShapeDtypeStruct((cells_x, cells_y, depth), jnp.float32)
    return pl.pallas_call(
        main_kernel,
        out_shape=[vmem_out(*wide.shape)] + [out] * 3,
        in_specs=in_vmem(len(rims) + 2),
        out_specs=in_vmem(4),
        input_output_aliases={0: 0},
        scratch_shapes=[
            pltpu.VMEM((4, STEPS, planes_x) + tile, jnp.float32),
            pltpu.VMEM((9, planes_x) + tile, jnp.float32),
            pltpu.VMEM((4, 4, planes_x) + tile, jnp.float32),
        ],
        compiler_params=PARAMS,
        name="migrate",
    )(pinned(wide, pltpu.VMEM), *rims, planes)[1:]


def bits_of(axis):
    size = lax.axis_size(axis)
    return [1 << bit for bit in range(size.bit_length() - 1)] if size & (size - 1) == 0 else None


def doubled(windows, axis, bit):
    pairs = [(i, i ^ bit) for i in range(lax.axis_size(axis))]
    return jnp.concatenate([windows, lax.ppermute(windows, axis, pairs)], axis=0)


def inject_kernel(samples, cells_x, cells_y, gathered, table_x, table_y, planes, weights, picks):
    size_y = lax.axis_size("gy")
    own_x, own_y = lax.axis_index("gx"), lax.axis_index("gy")
    rows = cells_y + 2 * RIM
    tiles = rows // SUBLANES
    wide_x = picks.shape[0]
    in_row = LANES // samples
    place = lax.broadcasted_iota(jnp.int32, (rows, LANES), 0)
    row = tiles * lax.rem(place, SUBLANES) + lax.div(place, SUBLANES)
    y_global = own_y * cells_y + jnp.where(row < cells_y + RIM, row, row - rows)
    x_global = own_x * cells_x - RIM + lax.broadcasted_iota(jnp.int32, (wide_x, LANES), 0)
    lane = lax.broadcasted_iota(jnp.int32, (1, LANES), 1)
    bits_x, bits_y = bits_of("gx"), bits_of("gy")

    def source(place):
        device_x, device_y = own_x, own_y
        for number, bit in enumerate(bits_x):
            if place >> number & 1:
                device_x = jnp.bitwise_xor(device_x, bit)
        for number, bit in enumerate(bits_y):
            if place >> (len(bits_x) + number) & 1:
                device_y = jnp.bitwise_xor(device_y, bit)
        return device_x * size_y + device_y

    for group in range(gathered.shape[0] // in_row):
        at_x = at_y = jnp.zeros((1, LANES), jnp.int32)
        window = jnp.zeros((STEPS, LANES), jnp.float32)
        for part in range(in_row):
            place = group * in_row + part
            device = source(place)
            here = (lane >= part * samples) & (lane < (part + 1) * samples)
            shift = lax.rem((part - lax.rem(device, in_row)) * samples + LANES, LANES)
            table_row = pl.ds(lax.div(device, in_row), 1)
            at_x = jnp.where(here, pltpu.roll(table_x[table_row, :], shift, 1), at_x)
            at_y = jnp.where(here, pltpu.roll(table_y[table_row, :], shift, 1), at_y)
            moved = gathered[place]
            if part:
                moved = pltpu.roll(moved, part * samples, 1)
            window = jnp.where(here, moved, window)
        span = slice(group * LANES, (group + 1) * LANES)
        picks[:, span] = (at_x == x_global).astype(jnp.float32)
        is_y = at_y == y_global
        for sample in range(STEPS):
            weights[sample * rows : (sample + 1) * rows, span] = jnp.where(
                is_y, window[sample : sample + 1], 0.0
            )
    rest = weights[...]
    pick = picks[...].astype(jnp.bfloat16)
    total = None
    for _ in range(3):
        part = rest.astype(jnp.bfloat16)
        rest = rest - part.astype(jnp.float32)
        product = lax.dot_general(
            part, pick, (((1,), (1,)), ((), ())), preferred_element_type=jnp.float32
        )
        total = product if total is None else total + product
    planes[...] = jnp.zeros_like(planes)
    for sample in range(STEPS):
        for tile in range(tiles):
            begin = sample * rows + tile * SUBLANES
            planes[sample, tile, :, :wide_x] = total[begin : begin + SUBLANES]


def injected(gathered, receiver_x, receiver_y, samples, cells_x, cells_y, depth):
    rows = cells_y + 2 * RIM
    receivers = receiver_x.shape[0]
    wide_x = -(-(cells_x + 2 * RIM) // 32) * 32
    return pl.pallas_call(
        functools.partial(inject_kernel, samples, cells_x, cells_y),
        out_shape=vmem_out(STEPS, rows // SUBLANES, SUBLANES, depth),
        in_specs=in_vmem(3),
        out_specs=in_vmem(1)[0],
        scratch_shapes=[
            pltpu.VMEM((STEPS * rows, receivers), jnp.float32),
            pltpu.VMEM((wide_x, receivers), jnp.float32),
        ],
        compiler_params=PARAMS,
        name="inject",
    )(gathered, receiver_x.reshape(-1, LANES), receiver_y.reshape(-1, LANES))


def per_device(
    src_p_prev,
    src_p_now,
    src_q_prev,
    src_q_now,
    rec_p_next,
    rec_p_now,
    rec_q_next,
    rec_q_now,
    velocity_term,
    epsilon,
    delta,
    tilt,
    azimuth,
    traces,
    receiver_x,
    receiver_y,
    segment_start,
):
    blocks = (
        src_p_prev,
        src_p_now,
        src_q_prev,
        src_q_now,
        rec_p_next,
        rec_p_now,
        rec_q_next,
        rec_q_now,
        velocity_term,
        epsilon,
        delta,
        tilt,
        azimuth,
    )
    cells_x, cells_y, depth = src_p_now.shape
    wide, y_a, y_b, window = pack(blocks, traces, segment_start)
    y_a, y_b = swap(y_a, "gy", 0), swap(y_b, "gy", 1)
    wide, x_a, x_b = pack_x(wide, window)
    x_a, x_b = swap(x_a, "gx", 0), swap(x_b, "gx", 1)
    windows = jnp.concatenate([window, x_a[x_parts()[1] :, :STEPS, :]], axis=0)
    for bit in bits_of("gx")[1:]:
        windows = doubled(windows, "gx", bit)
    for bit in bits_of("gy"):
        windows = doubled(windows, "gy", bit)
    wide, c_a, c_b = corners(wide, y_a, y_b)
    c_a, c_b = swap(c_a, "gx", 0), swap(c_b, "gx", 1)
    planes = injected(
        windows, receiver_x, receiver_y, traces.shape[1], cells_x, cells_y, depth
    )
    return tuple(migrate(wide, (x_a, x_b, c_a, c_b), planes, cells_x, cells_y))


def solution(mesh):
    state = P(("shot", "gx"), "gy", None)
    earth = P("gx", "gy", None)
    return jax.shard_map(
        per_device,
        mesh=mesh,
        in_specs=(state,) * FIELDS + (earth,) * 5 + (P("shot", ("gx", "gy")), P(), P(), P()),
        out_specs=(state,) * 3,
        check_vma=False,
    )
```

```python
import functools

import jax
import jax.numpy as jnp
from jax import lax
from jax.experimental import pallas as pl
from jax.experimental.pallas import tpu as pltpu
from jax.sharding import PartitionSpec as P

STEPS = 4
REC_DEPTH = 4
RIM = STEPS
FIELDS = 8
SUBLANES = 8
LANES = 128
VMEM_LIMIT = 48 * 1024 * 1024
PARAMS = pltpu.CompilerParams(vmem_limit_bytes=VMEM_LIMIT)


def in_vmem(count):
    return [pl.BlockSpec(memory_space=pltpu.VMEM)] * count


def is_odd(axis):
    return lax.rem(lax.axis_index(axis), 2) == 1


def swap(value, axis, first):
    size = lax.axis_size(axis)
    lower = range(first, size - 1, 2)
    pairs = [(i, i + 1) for i in lower] + [(i + 1, i) for i in lower]
    return lax.ppermute(value, axis, pairs)


NOW = (1, 3, 5, 7)
REST = (0, 2, 4, 6, 8, 9, 10, 11, 12)
SLIM = RIM - 1


def y_slots():
    slots = [((number, 0, RIM, 0),) for number in NOW]
    whole = len(REST) - len(REST) // RIM
    for place in range(whole):
        parts = [(REST[place], 0, SLIM, 0)]
        guest = whole + place // SLIM
        if guest < len(REST):
            parts.append((REST[guest], place % SLIM, 1, SLIM))
        slots.append(tuple(parts))
    return slots


def each_y_part(slots, high):
    for slot, parts in enumerate(slots):
        for number, row, rows, place in parts:
            if not high:
                yield slot, number, row, place, rows
            else:
                width = RIM if number in NOW else SLIM
                yield slot, number, RIM - width + row, 0 if place else RIM - rows, rows


def x_parts():
    parts, place = [], 0
    for number in NOW:
        parts.append((number, RIM, place))
        place += RIM
    for number in REST:
        parts.append((number, SLIM, place))
        place += SLIM
    return parts, place


def pinned(value, space):
    return pltpu.with_memory_space_constraint(value, space)


def vmem_out(*shape):
    return pltpu.VMEM(shape, jnp.float32)


def pack_kernel(count, *refs):
    blocks, traces, start = refs[:count], refs[count], refs[count + 1]
    wide, y_a, y_b, window, held, sems = refs[count + 2 :]
    cells_x, cells_y = blocks[0].shape[:2]
    core_x = pl.ds(RIM, cells_x)
    moves = [
        pltpu.make_async_copy(block, wide.at[number, core_x, pl.ds(0, cells_y)], sems.at[number])
        for number, block in enumerate(blocks)
    ]
    moves.append(pltpu.make_async_copy(traces, held, sems.at[count]))
    for move in moves:
        move.start()
    odd_y = is_odd("gy")
    begin = start[0]
    samples = traces.shape[1]
    window[...] = jnp.zeros_like(window)
    for move in moves:
        move.wait()
    for sample in range(STEPS):
        window[0, sample : sample + 1, :samples] = held[pl.ds(begin + sample, 1), :]

    def put_y(low, high):
        for out, is_high, base in ((low, False, 0), (high, True, cells_y - RIM)):
            for slot, number, row, place, length in each_y_part(y_slots(), is_high):
                out[slot, :, place : place + length, :] = wide[
                    number, RIM : RIM + cells_x, base + row : base + row + length, :
                ]

    @pl.when(odd_y)
    def _():
        put_y(y_a, y_b)

    @pl.when(jnp.logical_not(odd_y))
    def _():
        put_y(y_b, y_a)


def pack(blocks, traces, segment_start):
    cells_x, cells_y, depth = blocks[0].shape
    count = len(blocks)
    rim_y = vmem_out(len(y_slots()), cells_x, RIM, depth)
    wide = vmem_out(count, cells_x + 2 * RIM + 2, cells_y + 2 * RIM, depth)
    return pl.pallas_call(
        functools.partial(pack_kernel, count),
        out_shape=[wide, rim_y, rim_y, vmem_out(1, STEPS, LANES)],
        in_specs=[pl.BlockSpec(memory_space=pltpu.HBM)] * (count + 1)
        + [pl.BlockSpec(memory_space=pltpu.SMEM)],
        out_specs=in_vmem(4),
        scratch_shapes=[
            pltpu.VMEM(traces.shape, jnp.float32),
            pltpu.SemaphoreType.DMA((count + 1,)),
        ],
        compiler_params=PARAMS,
        name="pack_y_rims",
    )(*(pinned(value, pltpu.HBM) for value in (*blocks, traces)), segment_start)


def pack_x_kernel(_, window, wide, x_a, x_b):
    cells_x, cells_y = wide.shape[1] - 2 * RIM - 2, wide.shape[2] - 2 * RIM
    odd_x = is_odd("gx")
    parts, total = x_parts()
    for number, width, place in parts:
        first, last = RIM, RIM + cells_x - width
        for out, begin in ((x_a, jnp.where(odd_x, first, last)), (x_b, jnp.where(odd_x, last, first))):
            out[place : place + width] = wide[number, pl.ds(begin, width), :cells_y, :]
    x_a[total] = jnp.zeros_like(x_a[total])
    x_a[total, :STEPS, :] = window[0]


def pack_x(wide, window):
    _, _, rows, depth = wide.shape
    total = x_parts()[1]
    return pl.pallas_call(
        pack_x_kernel,
        out_shape=[
            vmem_out(*wide.shape),
            vmem_out(total + 1, rows - 2 * RIM, depth),
            vmem_out(total, rows - 2 * RIM, depth),
        ],
        in_specs=in_vmem(2),
        out_specs=in_vmem(3),
        input_output_aliases={0: 0},
        compiler_params=PARAMS,
        name="pack_x_rims",
    )(pinned(wide, pltpu.VMEM), window)


def corner_kernel(_, y_a, y_b, __, wide, c_a, c_b):
    cells_x = y_a.shape[1]
    cells_y = wide.shape[2] - 2 * RIM
    odd_x, odd_y = is_odd("gx"), is_odd("gy")

    def place_y(low, high):
        for rim, is_high, base in ((high, False, cells_y), (low, True, cells_y + RIM)):
            for slot, number, row, place, length in each_y_part(y_slots(), is_high):
                wide[number, RIM : RIM + cells_x, base + row : base + row + length, :] = rim[
                    slot, :, place : place + length, :
                ]

    @pl.when(odd_y)
    def _():
        place_y(y_a, y_b)

    @pl.when(jnp.logical_not(odd_y))
    def _():
        place_y(y_b, y_a)

    for number, width, place in x_parts()[0]:
        first, last = RIM, RIM + cells_x - width
        for out, begin in ((c_a, jnp.where(odd_x, first, last)), (c_b, jnp.where(odd_x, last, first))):
            out[place : place + width] = wide[number, pl.ds(begin, width), cells_y:, :]


def corners(wide, y_a, y_b, earlier):
    corner = vmem_out(x_parts()[1], 2 * RIM, wide.shape[-1])
    return pl.pallas_call(
        corner_kernel,
        out_shape=[vmem_out(*wide.shape), corner, corner],
        in_specs=in_vmem(4),
        out_specs=in_vmem(3),
        input_output_aliases={0: 0},
        compiler_params=PARAMS,
        name="pack_corners",
    )(pinned(wide, pltpu.VMEM), y_a, y_b, earlier)


def sine_cosine(angle):
    square = angle * angle
    sine = 1.0 / 6227020800.0
    for term in (-1.0 / 39916800.0, 1.0 / 362880.0, -1.0 / 5040.0, 1.0 / 120.0, -1.0 / 6.0, 1.0):
        sine = sine * square + term
    cosine = 1.0 / 479001600.0
    for term in (-1.0 / 3628800.0, 1.0 / 40320.0, -1.0 / 720.0, 1.0 / 24.0, -0.5, 1.0):
        cosine = cosine * square + term
    return sine * angle, cosine


def main_kernel(_, x_a, x_b, c_a, c_b, planes, wide, image, p_last, q_last, waves, factors, local):
    count = wide.shape[0]
    cells_x, cells_y, depth = image.shape
    span_x = cells_x + 2 * RIM
    tiles = (cells_y + 2 * RIM) // SUBLANES
    odd_x = is_odd("gx")
    for number, width, place in x_parts()[0]:
        low, high = RIM - width, RIM + cells_x
        for begin, side, corner in (
            (jnp.where(odd_x, low, high), x_a, c_a),
            (jnp.where(odd_x, high, low), x_b, c_b),
        ):
            wide[number, pl.ds(begin, width), :cells_y, :] = side[place : place + width]
            wide[number, pl.ds(begin, width), cells_y:, :] = corner[place : place + width]

    def wide_tiles(number, x):
        return [wide[number, x, pl.ds(tile, SUBLANES, stride=tiles), :] for tile in range(tiles)]

    def wave_tiles(number, slot, x):
        if slot < 2:
            return wide_tiles(2 * number + slot, x)
        return [waves[number, slot - 2, x, tile] for tile in range(tiles)]

    lane = lax.broadcasted_iota(jnp.int32, (SUBLANES, depth), 1)
    not_last, not_first = lane < depth - 1, lane > 0
    at_depth = lane == REC_DEPTH

    def next_y(value):
        return value[1:] + [pltpu.roll(value[0], SUBLANES - 1, 0)]

    def previous_y(value):
        return [pltpu.roll(value[-1], 1, 0)] + value[:-1]

    def make_factors(i, carry):
        stores = []
        for x in (1 + 2 * i, 2 + 2 * i):
            raw = [wide_tiles(FIELDS + number, x) for number in range(count - FIELDS)]
            for tile in range(tiles):
                velocity, epsilon, delta, tilt, azimuth = [value[tile] for value in raw]
                f_e = 1.0 + 2.0 * epsilon
                f_d = jnp.sqrt(1.0 + 2.0 * delta)
                sin_tilt, cos_tilt = sine_cosine(tilt)
                sin_half, cos_half = sine_cosine(0.5 * azimuth)
                sin_azim = 2.0 * sin_half * cos_half
                cos_azim = 1.0 - 2.0 * sin_half * sin_half
                sin_square = sin_tilt * sin_tilt
                half_tilt = 0.5 * sin_tilt * cos_tilt
                along_x = sin_square * cos_azim
                values = (
                    velocity,
                    velocity * f_e,
                    velocity * f_d,
                    along_x * cos_azim,
                    sin_square * sin_azim * sin_azim,
                    cos_tilt * cos_tilt,
                    0.5 * along_x * sin_azim,
                    half_tilt * cos_azim,
                    half_tilt * sin_azim,
                )
                stores += [(number, x, tile, value) for number, value in enumerate(values)]
        for number, x, tile, value in stores:
            factors[number, x, tile] = value
        return carry

    lax.fori_loop(0, (span_x - 2) // 2, make_factors, 0)

    def plane_part(turn, x, stores):
        ayy = [factors[4, x, tile] for tile in range(tiles)]
        azz = [factors[5, x, tile] for tile in range(tiles)]
        ayz = [factors[8, x, tile] for tile in range(tiles)]
        for number in range(4):
            now = wave_tiles(number, turn + 1, x)
            above = [jnp.where(not_last, pltpu.roll(u, depth - 1, 1), 0.0) for u in now]
            below = [jnp.where(not_first, pltpu.roll(u, 1, 1), 0.0) for u in now]
            slope_z = [a - b for a, b in zip(above, below)]
            after, before = next_y(now), previous_y(now)
            slope_after, slope_before = next_y(slope_z), previous_y(slope_z)
            for tile in range(tiles):
                double = now[tile] + now[tile]
                sum_y = after[tile] + before[tile]
                sum_z = above[tile] + below[tile]
                part = (
                    (ayy[tile] * sum_y + azz[tile] * sum_z)
                    + ayz[tile] * (slope_after[tile] - slope_before[tile])
                ) - double
                stores.append((local, (number, 0, x, tile), part))
                stores.append((local, (number, 1, x, tile), after[tile] - before[tile]))
                stores.append((local, (number, 2, x, tile), slope_z[tile]))
                if number % 2 == 0:
                    rest = (sum_y + sum_z) - 3.0 * double
                    stores.append((local, (number, 3, x, tile), rest))

    def next_part(turn, x, stores):
        held = [wave_tiles(number, turn, x) for number in range(4)]
        now = [wave_tiles(number, turn + 1, x) for number in range(4)]
        after = [wave_tiles(number, turn + 1, x + 1) for number in range(4)]
        before = [wave_tiles(number, turn + 1, x - 1) for number in range(4)]
        for tile in range(tiles):
            velocity, with_e, with_d = [factors[number, x, tile] for number in range(3)]
            axx, axy, axz = [factors[number, x, tile] for number in (3, 6, 7)]
            for pair in range(2):
                sums, axis = [], []
                for number in (2 * pair, 2 * pair + 1):
                    sum_x = after[number][tile] + before[number][tile]
                    d_xy = local[number, 1, x + 1, tile] - local[number, 1, x - 1, tile]
                    d_xz = local[number, 2, x + 1, tile] - local[number, 2, x - 1, tile]
                    sums.append(sum_x)
                    axis.append((local[number, 0, x, tile] + axx * sum_x) + (axy * d_xy + axz * d_xz))
                p_number, q_number = 2 * pair, 2 * pair + 1
                across = (sums[0] + local[p_number, 3, x, tile]) - axis[0]
                p_now, q_now = now[p_number][tile], now[q_number][tile]
                p_next = ((p_now + p_now) - held[p_number][tile]) + (
                    with_e * across + with_d * axis[1]
                )
                q_next = ((q_now + q_now) - held[q_number][tile]) + (
                    with_d * across + velocity * axis[1]
                )
                if pair == 1:
                    shift = lax.rem(REC_DEPTH - x + depth, depth)
                    moved = pltpu.roll(planes[STEPS - 1 - turn, tile], shift, 1)
                    p_next = p_next + jnp.where(at_depth, moved, 0.0)
                stores.append((waves, (p_number, turn, x, tile), p_next))
                stores.append((waves, (q_number, turn, x, tile), q_next))

    def write(stores):
        for ref, index, value in stores:
            ref[index] = value

    for turn in range(STEPS):
        first, last = turn + 1, span_x - 1 - turn
        for x in range(first - 1, first + 3):
            stores = []
            plane_part(turn, x, stores)
            write(stores)

        def body(i, carry, turn=turn, first=first):
            x = first + 2 * i
            stores = []
            next_part(turn, x, stores)
            next_part(turn, x + 1, stores)
            plane_part(turn, x + 3, stores)
            plane_part(turn, x + 4, stores)
            write(stores)
            return carry

        lax.fori_loop(0, (last - first) // 2, body, 0)

    def finish(i, carry):
        x = RIM + i
        total = None
        for back in range(STEPS + 1):
            source = wave_tiles(0, 1 + STEPS - back, x)
            receiver = wave_tiles(2, 1 + back, x)
            product = [a * b for a, b in zip(source, receiver)]
            total = product if total is None else [a + b for a, b in zip(total, product)]
        for out, value in (
            (0, total),
            (1, wave_tiles(2, 1 + STEPS, x)),
            (2, wave_tiles(3, 1 + STEPS, x)),
        ):
            for tile in range(tiles):
                wide[out, x, pl.ds(tile, SUBLANES, stride=tiles), :] = value[tile]
        return carry

    lax.fori_loop(0, cells_x, finish, 0)
    for out, ref in enumerate((image, p_last, q_last)):
        ref[...] = wide[out, RIM : RIM + cells_x, :cells_y, :]


def migrate(wide, rims, planes, cells_x, cells_y):
    count, planes_x, rows, depth = wide.shape
    tile = (rows // SUBLANES, SUBLANES, depth)
    out = jax.ShapeDtypeStruct((cells_x, cells_y, depth), jnp.float32)
    return pl.pallas_call(
        main_kernel,
        out_shape=[vmem_out(*wide.shape)] + [out] * 3,
        in_specs=in_vmem(len(rims) + 2),
        out_specs=in_vmem(4),
        input_output_aliases={0: 0},
        scratch_shapes=[
            pltpu.VMEM((4, STEPS, planes_x) + tile, jnp.float32),
            pltpu.VMEM((9, planes_x) + tile, jnp.float32),
            pltpu.VMEM((4, 4, planes_x) + tile, jnp.float32),
        ],
        compiler_params=PARAMS,
        name="migrate",
    )(pinned(wide, pltpu.VMEM), *rims, planes)[1:]


def bits_of(axis):
    size = lax.axis_size(axis)
    return [1 << bit for bit in range(size.bit_length() - 1)] if size & (size - 1) == 0 else None


def doubled(windows, axis, bit):
    pairs = [(i, i ^ bit) for i in range(lax.axis_size(axis))]
    return jnp.concatenate([windows, lax.ppermute(windows, axis, pairs)], axis=0)


def inject_kernel(samples, cells_x, cells_y, gathered, table_x, table_y, planes, weights, picks):
    size_y = lax.axis_size("gy")
    own_x, own_y = lax.axis_index("gx"), lax.axis_index("gy")
    rows = cells_y + 2 * RIM
    tiles = rows // SUBLANES
    wide_x = picks.shape[0]
    in_row = LANES // samples
    place = lax.broadcasted_iota(jnp.int32, (rows, LANES), 0)
    row = tiles * lax.rem(place, SUBLANES) + lax.div(place, SUBLANES)
    y_global = own_y * cells_y + jnp.where(row < cells_y + RIM, row, row - rows)
    x_global = own_x * cells_x - RIM + lax.broadcasted_iota(jnp.int32, (wide_x, LANES), 0)
    lane = lax.broadcasted_iota(jnp.int32, (1, LANES), 1)
    bits_x, bits_y = bits_of("gx"), bits_of("gy")

    def source(place):
        device_x, device_y = own_x, own_y
        for number, bit in enumerate(bits_x):
            if place >> number & 1:
                device_x = jnp.bitwise_xor(device_x, bit)
        for number, bit in enumerate(bits_y):
            if place >> (len(bits_x) + number) & 1:
                device_y = jnp.bitwise_xor(device_y, bit)
        return device_x * size_y + device_y

    for group in range(gathered.shape[0] // in_row):
        at_x = at_y = jnp.zeros((1, LANES), jnp.int32)
        window = jnp.zeros((STEPS, LANES), jnp.float32)
        for part in range(in_row):
            place = group * in_row + part
            device = source(place)
            here = (lane >= part * samples) & (lane < (part + 1) * samples)
            shift = lax.rem((part - lax.rem(device, in_row)) * samples + LANES, LANES)
            table_row = pl.ds(lax.div(device, in_row), 1)
            at_x = jnp.where(here, pltpu.roll(table_x[table_row, :], shift, 1), at_x)
            at_y = jnp.where(here, pltpu.roll(table_y[table_row, :], shift, 1), at_y)
            moved = gathered[place]
            if part:
                moved = pltpu.roll(moved, part * samples, 1)
            window = jnp.where(here, moved, window)
        span = slice(group * LANES, (group + 1) * LANES)
        picks[:, span] = (at_x == x_global).astype(jnp.float32)
        is_y = at_y == y_global
        for sample in range(STEPS):
            weights[sample * rows : (sample + 1) * rows, span] = jnp.where(
                is_y, window[sample : sample + 1], 0.0
            )
    rest = weights[...]
    pick = picks[...].astype(jnp.bfloat16)
    total = None
    for _ in range(3):
        part = rest.astype(jnp.bfloat16)
        rest = rest - part.astype(jnp.float32)
        product = lax.dot_general(
            part, pick, (((1,), (1,)), ((), ())), preferred_element_type=jnp.float32
        )
        total = product if total is None else total + product
    planes[...] = jnp.zeros_like(planes)
    for sample in range(STEPS):
        for tile in range(tiles):
            begin = sample * rows + tile * SUBLANES
            planes[sample, tile, :, :wide_x] = total[begin : begin + SUBLANES]


def injected(gathered, receiver_x, receiver_y, samples, cells_x, cells_y, depth):
    rows = cells_y + 2 * RIM
    receivers = receiver_x.shape[0]
    wide_x = -(-(cells_x + 2 * RIM) // 32) * 32
    return pl.pallas_call(
        functools.partial(inject_kernel, samples, cells_x, cells_y),
        out_shape=vmem_out(STEPS, rows // SUBLANES, SUBLANES, depth),
        in_specs=in_vmem(3),
        out_specs=in_vmem(1)[0],
        scratch_shapes=[
            pltpu.VMEM((STEPS * rows, receivers), jnp.float32),
            pltpu.VMEM((wide_x, receivers), jnp.float32),
        ],
        compiler_params=PARAMS,
        name="inject",
    )(gathered, receiver_x.reshape(-1, LANES), receiver_y.reshape(-1, LANES))


def per_device(
    src_p_prev,
    src_p_now,
    src_q_prev,
    src_q_now,
    rec_p_next,
    rec_p_now,
    rec_q_next,
    rec_q_now,
    velocity_term,
    epsilon,
    delta,
    tilt,
    azimuth,
    traces,
    receiver_x,
    receiver_y,
    segment_start,
):
    blocks = (
        src_p_prev,
        src_p_now,
        src_q_prev,
        src_q_now,
        rec_p_next,
        rec_p_now,
        rec_q_next,
        rec_q_now,
        velocity_term,
        epsilon,
        delta,
        tilt,
        azimuth,
    )
    cells_x, cells_y, depth = src_p_now.shape
    wide, y_a, y_b, window = pack(blocks, traces, segment_start)
    y_a, y_b = swap(y_a, "gy", 0), swap(y_b, "gy", 1)
    wide, x_a, x_b = pack_x(wide, window)
    x_a, x_b = swap(x_a, "gx", 0), swap(x_b, "gx", 1)
    windows = jnp.concatenate([window, x_a[x_parts()[1] :, :STEPS, :]], axis=0)
    for bit in bits_of("gx")[1:]:
        windows = doubled(windows, "gx", bit)
    for bit in bits_of("gy")[:-1]:
        windows = doubled(windows, "gy", bit)
    wide, c_a, c_b = corners(wide, y_a, y_b, windows)
    for bit in bits_of("gy")[-1:]:
        windows = doubled(windows, "gy", bit)
    c_a, c_b = swap(c_a, "gx", 0), swap(c_b, "gx", 1)
    planes = injected(
        windows, receiver_x, receiver_y, traces.shape[1], cells_x, cells_y, depth
    )
    return tuple(migrate(wide, (x_a, x_b, c_a, c_b), planes, cells_x, cells_y))


def solution(mesh):
    state = P(("shot", "gx"), "gy", None)
    earth = P("gx", "gy", None)
    return jax.shard_map(
        per_device,
        mesh=mesh,
        in_specs=(state,) * FIELDS + (earth,) * 5 + (P("shot", ("gx", "gy")), P(), P(), P()),
        out_specs=(state,) * 3,
        check_vma=False,
    )
```

```python
import functools

import jax
import jax.numpy as jnp
from jax import lax
from jax.experimental import pallas as pl
from jax.experimental.pallas import tpu as pltpu
from jax.sharding import PartitionSpec as P

STEPS = 4
REC_DEPTH = 4
RIM = STEPS
FIELDS = 8
SUBLANES = 8
LANES = 128
PARAMS = pltpu.CompilerParams(vmem_limit_bytes=16 * 1024 * 1024)
PACK_PARAMS = pltpu.CompilerParams(vmem_limit_bytes=48 * 1024 * 1024)


def in_vmem(count):
    return [pl.BlockSpec(memory_space=pltpu.VMEM)] * count


def is_odd(axis):
    return lax.rem(lax.axis_index(axis), 2) == 1


def swap(value, axis, first):
    size = lax.axis_size(axis)
    lower = range(first, size - 1, 2)
    pairs = [(i, i + 1) for i in lower] + [(i + 1, i) for i in lower]
    return lax.ppermute(value, axis, pairs)


NOW = (1, 3, 5, 7)
REST = (0, 2, 4, 6, 8, 9, 10, 11, 12)
SLIM = RIM - 1


def y_slots():
    slots = [((number, 0, RIM, 0),) for number in NOW]
    whole = len(REST) - len(REST) // RIM
    for place in range(whole):
        parts = [(REST[place], 0, SLIM, 0)]
        guest = whole + place // SLIM
        if guest < len(REST):
            parts.append((REST[guest], place % SLIM, 1, SLIM))
        slots.append(tuple(parts))
    return slots


def each_y_part(slots, high):
    for slot, parts in enumerate(slots):
        for number, row, rows, place in parts:
            if not high:
                yield slot, number, row, place, rows
            else:
                width = RIM if number in NOW else SLIM
                yield slot, number, RIM - width + row, 0 if place else RIM - rows, rows


def x_parts():
    parts, place = [], 0
    for number in NOW:
        parts.append((number, RIM, place))
        place += RIM
    for number in REST:
        parts.append((number, SLIM, place))
        place += SLIM
    return parts, place


def pinned(value, space):
    return pltpu.with_memory_space_constraint(value, space)


def vmem_out(*shape):
    return pltpu.VMEM(shape, jnp.float32)


def pack_kernel(count, *refs):
    blocks, traces, start = refs[:count], refs[count], refs[count + 1]
    wide, y_a, y_b, window, held, sems = refs[count + 2 :]
    cells_x, cells_y = blocks[0].shape[:2]
    core_x = pl.ds(RIM, cells_x)
    moves = [
        pltpu.make_async_copy(block, wide.at[number, core_x, pl.ds(0, cells_y)], sems.at[number])
        for number, block in enumerate(blocks)
    ]
    moves.append(pltpu.make_async_copy(traces, held, sems.at[count]))
    for move in moves:
        move.start()
    odd_y = is_odd("gy")
    begin = start[0]
    samples = traces.shape[1]
    window[...] = jnp.zeros_like(window)
    for move in moves:
        move.wait()
    for sample in range(STEPS):
        window[0, sample : sample + 1, :samples] = held[pl.ds(begin + sample, 1), :]

    def put_y(low, high):
        for out, is_high, base in ((low, False, 0), (high, True, cells_y - RIM)):
            for slot, number, row, place, length in each_y_part(y_slots(), is_high):
                out[slot, :, place : place + length, :] = wide[
                    number, RIM : RIM + cells_x, base + row : base + row + length, :
                ]

    @pl.when(odd_y)
    def _():
        put_y(y_a, y_b)

    @pl.when(jnp.logical_not(odd_y))
    def _():
        put_y(y_b, y_a)


def pack(blocks, traces, segment_start):
    cells_x, cells_y, depth = blocks[0].shape
    count = len(blocks)
    rim_y = vmem_out(len(y_slots()), cells_x, RIM, depth)
    wide = vmem_out(count, cells_x + 2 * RIM + 2, cells_y + 2 * RIM, depth)
    return pl.pallas_call(
        functools.partial(pack_kernel, count),
        out_shape=[wide, rim_y, rim_y, vmem_out(1, STEPS, LANES)],
        in_specs=[pl.BlockSpec(memory_space=pltpu.HBM)] * (count + 1)
        + [pl.BlockSpec(memory_space=pltpu.SMEM)],
        out_specs=in_vmem(4),
        scratch_shapes=[
            pltpu.VMEM(traces.shape, jnp.float32),
            pltpu.SemaphoreType.DMA((count + 1,)),
        ],
        compiler_params=PACK_PARAMS,
        name="pack_y_rims",
    )(*(pinned(value, pltpu.HBM) for value in (*blocks, traces)), segment_start)


def pack_x_kernel(_, window, wide, x_a, x_b):
    cells_x, cells_y = wide.shape[1] - 2 * RIM - 2, wide.shape[2] - 2 * RIM
    odd_x = is_odd("gx")
    parts, total = x_parts()
    for number, width, place in parts:
        first, last = RIM, RIM + cells_x - width
        for out, begin in ((x_a, jnp.where(odd_x, first, last)), (x_b, jnp.where(odd_x, last, first))):
            out[place : place + width] = wide[number, pl.ds(begin, width), :cells_y, :]
    x_a[total] = jnp.zeros_like(x_a[total])
    x_a[total, :STEPS, :] = window[0]


def pack_x(wide, window):
    _, _, rows, depth = wide.shape
    total = x_parts()[1]
    return pl.pallas_call(
        pack_x_kernel,
        out_shape=[
            vmem_out(*wide.shape),
            vmem_out(total + 1, rows - 2 * RIM, depth),
            vmem_out(total, rows - 2 * RIM, depth),
        ],
        in_specs=in_vmem(2),
        out_specs=in_vmem(3),
        input_output_aliases={0: 0},
        compiler_params=PARAMS,
        name="pack_x_rims",
    )(pinned(wide, pltpu.VMEM), window)


def corner_kernel(_, y_a, y_b, __, wide, c_a, c_b):
    cells_x = y_a.shape[1]
    cells_y = wide.shape[2] - 2 * RIM
    odd_x, odd_y = is_odd("gx"), is_odd("gy")

    def place_y(low, high):
        for rim, is_high, base in ((high, False, cells_y), (low, True, cells_y + RIM)):
            for slot, number, row, place, length in each_y_part(y_slots(), is_high):
                wide[number, RIM : RIM + cells_x, base + row : base + row + length, :] = rim[
                    slot, :, place : place + length, :
                ]

    @pl.when(odd_y)
    def _():
        place_y(y_a, y_b)

    @pl.when(jnp.logical_not(odd_y))
    def _():
        place_y(y_b, y_a)

    for number, width, place in x_parts()[0]:
        first, last = RIM, RIM + cells_x - width
        for out, begin in ((c_a, jnp.where(odd_x, first, last)), (c_b, jnp.where(odd_x, last, first))):
            out[place : place + width] = wide[number, pl.ds(begin, width), cells_y:, :]


def corners(wide, y_a, y_b, earlier):
    corner = vmem_out(x_parts()[1], 2 * RIM, wide.shape[-1])
    return pl.pallas_call(
        corner_kernel,
        out_shape=[vmem_out(*wide.shape), corner, corner],
        in_specs=in_vmem(4),
        out_specs=in_vmem(3),
        input_output_aliases={0: 0},
        compiler_params=PARAMS,
        name="pack_corners",
    )(pinned(wide, pltpu.VMEM), y_a, y_b, earlier)


def sine_cosine(angle):
    square = angle * angle
    sine = 1.0 / 6227020800.0
    for term in (-1.0 / 39916800.0, 1.0 / 362880.0, -1.0 / 5040.0, 1.0 / 120.0, -1.0 / 6.0, 1.0):
        sine = sine * square + term
    cosine = 1.0 / 479001600.0
    for term in (-1.0 / 3628800.0, 1.0 / 40320.0, -1.0 / 720.0, 1.0 / 24.0, -0.5, 1.0):
        cosine = cosine * square + term
    return sine * angle, cosine


class Steps:
    def __init__(self, wide, planes, waves, factors, local):
        self.wide, self.planes, self.waves, self.factors, self.local = wide, planes, waves, factors, local
        self.count, _, rows, self.depth = wide.shape
        self.tiles = rows // SUBLANES
        self.cells_x = wide.shape[1] - 2 * RIM - 2
        lane = lax.broadcasted_iota(jnp.int32, (SUBLANES, self.depth), 1)
        self.not_last, self.not_first = lane < self.depth - 1, lane > 0
        self.at_depth = lane == REC_DEPTH

    def wide_tiles(self, number, x):
        return [
            self.wide[number, x, pl.ds(tile, SUBLANES, stride=self.tiles), :]
            for tile in range(self.tiles)
        ]

    def wave_tiles(self, number, slot, x):
        if slot < 2:
            return self.wide_tiles(2 * number + slot, x)
        return [self.waves[slot - 2][number, x, tile] for tile in range(self.tiles)]

    def next_y(self, value):
        return value[1:] + [pltpu.roll(value[0], SUBLANES - 1, 0)]

    def previous_y(self, value):
        return [pltpu.roll(value[-1], 1, 0)] + value[:-1]

    def make_factors(self, x):
        raw = [self.wide_tiles(FIELDS + number, x) for number in range(self.count - FIELDS)]
        for tile in range(self.tiles):
            velocity, epsilon, delta, tilt, azimuth = [value[tile] for value in raw]
            f_e = 1.0 + 2.0 * epsilon
            f_d = jnp.sqrt(1.0 + 2.0 * delta)
            sin_tilt, cos_tilt = sine_cosine(tilt)
            sin_half, cos_half = sine_cosine(0.5 * azimuth)
            sin_azim = 2.0 * sin_half * cos_half
            cos_azim = 1.0 - 2.0 * sin_half * sin_half
            sin_square = sin_tilt * sin_tilt
            half_tilt = 0.5 * sin_tilt * cos_tilt
            along_x = sin_square * cos_azim
            values = (
                velocity,
                velocity * f_e,
                velocity * f_d,
                along_x * cos_azim,
                sin_square * sin_azim * sin_azim,
                cos_tilt * cos_tilt,
                0.5 * along_x * sin_azim,
                half_tilt * cos_azim,
                half_tilt * sin_azim,
            )
            for number, value in enumerate(values):
                self.factors[number, x, tile] = value

    def plane_part(self, turn, x):
        factors, local, tiles = self.factors, self.local[turn], self.tiles
        ayy = [factors[4, x, tile] for tile in range(tiles)]
        azz = [factors[5, x, tile] for tile in range(tiles)]
        ayz = [factors[8, x, tile] for tile in range(tiles)]
        for number in range(4):
            now = self.wave_tiles(number, turn + 1, x)
            above = [jnp.where(self.not_last, pltpu.roll(u, self.depth - 1, 1), 0.0) for u in now]
            below = [jnp.where(self.not_first, pltpu.roll(u, 1, 1), 0.0) for u in now]
            slope_z = [a - b for a, b in zip(above, below)]
            after, before = self.next_y(now), self.previous_y(now)
            slope_after, slope_before = self.next_y(slope_z), self.previous_y(slope_z)
            for tile in range(tiles):
                double = now[tile] + now[tile]
                sum_y = after[tile] + before[tile]
                sum_z = above[tile] + below[tile]
                local[number, 0, x, tile] = (
                    (ayy[tile] * sum_y + azz[tile] * sum_z)
                    + ayz[tile] * (slope_after[tile] - slope_before[tile])
                ) - double
                local[number, 1, x, tile] = after[tile] - before[tile]
                local[number, 2, x, tile] = slope_z[tile]
                if number % 2 == 0:
                    local[number, 3, x, tile] = (sum_y + sum_z) - 3.0 * double

    def next_part(self, turn, x):
        factors, local = self.factors, self.local[turn]
        held = [self.wave_tiles(number, turn, x) for number in range(4)]
        now = [self.wave_tiles(number, turn + 1, x) for number in range(4)]
        after = [self.wave_tiles(number, turn + 1, x + 1) for number in range(4)]
        before = [self.wave_tiles(number, turn + 1, x - 1) for number in range(4)]
        for tile in range(self.tiles):
            velocity, with_e, with_d = [factors[number, x, tile] for number in range(3)]
            axx, axy, axz = [factors[number, x, tile] for number in (3, 6, 7)]
            for pair in range(2):
                sums, axis = [], []
                for number in (2 * pair, 2 * pair + 1):
                    sum_x = after[number][tile] + before[number][tile]
                    d_xy = local[number, 1, x + 1, tile] - local[number, 1, x - 1, tile]
                    d_xz = local[number, 2, x + 1, tile] - local[number, 2, x - 1, tile]
                    sums.append(sum_x)
                    axis.append((local[number, 0, x, tile] + axx * sum_x) + (axy * d_xy + axz * d_xz))
                p_number, q_number = 2 * pair, 2 * pair + 1
                across = (sums[0] + local[p_number, 3, x, tile]) - axis[0]
                p_now, q_now = now[p_number][tile], now[q_number][tile]
                p_next = ((p_now + p_now) - held[p_number][tile]) + (
                    with_e * across + with_d * axis[1]
                )
                q_next = ((q_now + q_now) - held[q_number][tile]) + (
                    with_d * across + velocity * axis[1]
                )
                if pair == 1:
                    shift = lax.rem(REC_DEPTH - x + self.depth, self.depth)
                    moved = pltpu.roll(self.planes[STEPS - 1 - turn, tile], shift, 1)
                    p_next = p_next + jnp.where(self.at_depth, moved, 0.0)
                self.waves[turn][p_number, x, tile] = p_next
                self.waves[turn][q_number, x, tile] = q_next


def repeat(count, body):
    def run(i, carry):
        body(i)
        return carry

    lax.fori_loop(0, count, run, 0)


def inner_kernel(wide, planes, *refs):
    waves, factors, local = refs[:STEPS], refs[STEPS], refs[STEPS + 1 :]
    steps = Steps(wide, planes, waves, factors, local)
    cells_x = steps.cells_x

    def factor_pair(i):
        steps.make_factors(RIM + 2 * i)
        steps.make_factors(RIM + 2 * i + 1)

    repeat(cells_x // 2, factor_pair)
    for turn in range(STEPS):
        first, last = RIM + 1 + turn, RIM + cells_x - 1 - turn
        for x in range(first - 1, first + 3):
            steps.plane_part(turn, x)

        def pair(i, turn=turn, first=first):
            x = first + 2 * i
            steps.next_part(turn, x)
            steps.next_part(turn, x + 1)
            steps.plane_part(turn, x + 3)
            steps.plane_part(turn, x + 4)

        repeat((last - first) // 2, pair)


def outer_kernel(*refs):
    x_a, x_b, c_a, c_b, planes = refs[1:6]
    refs = refs[6 + 2 * STEPS + 1 :]
    wide, waves, factors, local = refs[0], refs[1 : 1 + STEPS], refs[1 + STEPS], refs[2 + STEPS : -3]
    image, p_last, q_last = refs[-3:]
    cells_x, cells_y, depth = image.shape
    odd_x = is_odd("gx")
    for number, width, place in x_parts()[0]:
        low, high = RIM - width, RIM + cells_x
        for begin, side, corner in (
            (jnp.where(odd_x, low, high), x_a, c_a),
            (jnp.where(odd_x, high, low), x_b, c_b),
        ):
            wide[number, pl.ds(begin, width), :cells_y, :] = side[place : place + width]
            wide[number, pl.ds(begin, width), cells_y:, :] = corner[place : place + width]

    steps = Steps(wide, planes, waves, factors, local)

    def factor_pair(i):
        steps.make_factors(RIM - SLIM + i)
        steps.make_factors(RIM + cells_x + i)

    repeat(SLIM, factor_pair)
    for turn in range(STEPS):

        def parts(i, turn=turn):
            steps.plane_part(turn, turn + i)
            steps.plane_part(turn, RIM + cells_x - turn + i)

        def nexts(i, turn=turn):
            steps.next_part(turn, turn + 1 + i)
            steps.next_part(turn, RIM + cells_x - 1 - turn + i)

        repeat(RIM, parts)
        repeat(RIM, nexts)

    tiles = steps.tiles

    def finish(i):
        x = RIM + i
        total = None
        for back in range(STEPS + 1):
            source = steps.wave_tiles(0, 1 + STEPS - back, x)
            receiver = steps.wave_tiles(2, 1 + back, x)
            product = [a * b for a, b in zip(source, receiver)]
            total = product if total is None else [a + b for a, b in zip(total, product)]
        for out, value in (
            (0, total),
            (1, steps.wave_tiles(2, 1 + STEPS, x)),
            (2, steps.wave_tiles(3, 1 + STEPS, x)),
        ):
            for tile in range(tiles):
                wide[out, x, pl.ds(tile, SUBLANES, stride=tiles), :] = value[tile]

    repeat(cells_x, finish)
    for out, ref in enumerate((image, p_last, q_last)):
        ref[...] = wide[out, RIM : RIM + cells_x, :cells_y, :]


def inner(wide, planes):
    _, planes_x, rows, depth = wide.shape
    tile = (planes_x, rows // SUBLANES, SUBLANES, depth)
    return pl.pallas_call(
        inner_kernel,
        out_shape=[vmem_out(4, *tile)] * STEPS
        + [vmem_out(9, *tile)]
        + [vmem_out(4, 4, *tile)] * STEPS,
        in_specs=in_vmem(2),
        out_specs=in_vmem(2 * STEPS + 1),
        compiler_params=PARAMS,
        name="inner_steps",
    )(pinned(wide, pltpu.VMEM), planes)


def outer(wide, rims, planes, state, cells_x, cells_y):
    out = jax.ShapeDtypeStruct((cells_x, cells_y, wide.shape[-1]), jnp.float32)
    kept = [vmem_out(*wide.shape)] + [vmem_out(*value.shape) for value in state]
    first = len(rims) + 2
    aliases = {0: 0} | {first + number: 1 + number for number in range(len(state))}
    return pl.pallas_call(
        outer_kernel,
        out_shape=kept + [out] * 3,
        in_specs=in_vmem(first + len(state)),
        out_specs=in_vmem(len(kept) + 3),
        input_output_aliases=aliases,
        compiler_params=PARAMS,
        name="outer_steps",
    )(
        pinned(wide, pltpu.VMEM),
        *rims,
        planes,
        *(pinned(value, pltpu.VMEM) for value in state),
    )[-3:]


def bits_of(axis):
    size = lax.axis_size(axis)
    return [1 << bit for bit in range(size.bit_length() - 1)] if size & (size - 1) == 0 else None


def doubled(windows, axis, bit):
    pairs = [(i, i ^ bit) for i in range(lax.axis_size(axis))]
    return jnp.concatenate([windows, lax.ppermute(windows, axis, pairs)], axis=0)


def inject_kernel(samples, cells_x, cells_y, gathered, table_x, table_y, planes, weights, picks):
    size_y = lax.axis_size("gy")
    own_x, own_y = lax.axis_index("gx"), lax.axis_index("gy")
    rows = cells_y + 2 * RIM
    tiles = rows // SUBLANES
    wide_x = picks.shape[0]
    in_row = LANES // samples
    place = lax.broadcasted_iota(jnp.int32, (rows, LANES), 0)
    row = tiles * lax.rem(place, SUBLANES) + lax.div(place, SUBLANES)
    y_global = own_y * cells_y + jnp.where(row < cells_y + RIM, row, row - rows)
    x_global = own_x * cells_x - RIM + lax.broadcasted_iota(jnp.int32, (wide_x, LANES), 0)
    lane = lax.broadcasted_iota(jnp.int32, (1, LANES), 1)
    bits_x, bits_y = bits_of("gx"), bits_of("gy")

    def source(place):
        device_x, device_y = own_x, own_y
        for number, bit in enumerate(bits_x):
            if place >> number & 1:
                device_x = jnp.bitwise_xor(device_x, bit)
        for number, bit in enumerate(bits_y):
            if place >> (len(bits_x) + number) & 1:
                device_y = jnp.bitwise_xor(device_y, bit)
        return device_x * size_y + device_y

    for group in range(gathered.shape[0] // in_row):
        at_x = at_y = jnp.zeros((1, LANES), jnp.int32)
        window = jnp.zeros((STEPS, LANES), jnp.float32)
        for part in range(in_row):
            place = group * in_row + part
            device = source(place)
            here = (lane >= part * samples) & (lane < (part + 1) * samples)
            shift = lax.rem((part - lax.rem(device, in_row)) * samples + LANES, LANES)
            table_row = pl.ds(lax.div(device, in_row), 1)
            at_x = jnp.where(here, pltpu.roll(table_x[table_row, :], shift, 1), at_x)
            at_y = jnp.where(here, pltpu.roll(table_y[table_row, :], shift, 1), at_y)
            moved = gathered[place]
            if part:
                moved = pltpu.roll(moved, part * samples, 1)
            window = jnp.where(here, moved, window)
        span = slice(group * LANES, (group + 1) * LANES)
        picks[:, span] = (at_x == x_global).astype(jnp.float32)
        is_y = at_y == y_global
        for sample in range(STEPS):
            weights[sample * rows : (sample + 1) * rows, span] = jnp.where(
                is_y, window[sample : sample + 1], 0.0
            )
    rest = weights[...]
    pick = picks[...].astype(jnp.bfloat16)
    total = None
    for _ in range(3):
        part = rest.astype(jnp.bfloat16)
        rest = rest - part.astype(jnp.float32)
        product = lax.dot_general(
            part, pick, (((1,), (1,)), ((), ())), preferred_element_type=jnp.float32
        )
        total = product if total is None else total + product
    planes[...] = jnp.zeros_like(planes)
    for sample in range(STEPS):
        for tile in range(tiles):
            begin = sample * rows + tile * SUBLANES
            planes[sample, tile, :, :wide_x] = total[begin : begin + SUBLANES]


def injected(gathered, receiver_x, receiver_y, samples, cells_x, cells_y, depth):
    rows = cells_y + 2 * RIM
    receivers = receiver_x.shape[0]
    wide_x = -(-(cells_x + 2 * RIM) // 32) * 32
    return pl.pallas_call(
        functools.partial(inject_kernel, samples, cells_x, cells_y),
        out_shape=vmem_out(STEPS, rows // SUBLANES, SUBLANES, depth),
        in_specs=in_vmem(3),
        out_specs=in_vmem(1)[0],
        scratch_shapes=[
            pltpu.VMEM((STEPS * rows, receivers), jnp.float32),
            pltpu.VMEM((wide_x, receivers), jnp.float32),
        ],
        compiler_params=PARAMS,
        name="inject",
    )(gathered, receiver_x.reshape(-1, LANES), receiver_y.reshape(-1, LANES))


def per_device(
    src_p_prev,
    src_p_now,
    src_q_prev,
    src_q_now,
    rec_p_next,
    rec_p_now,
    rec_q_next,
    rec_q_now,
    velocity_term,
    epsilon,
    delta,
    tilt,
    azimuth,
    traces,
    receiver_x,
    receiver_y,
    segment_start,
):
    blocks = (
        src_p_prev,
        src_p_now,
        src_q_prev,
        src_q_now,
        rec_p_next,
        rec_p_now,
        rec_q_next,
        rec_q_now,
        velocity_term,
        epsilon,
        delta,
        tilt,
        azimuth,
    )
    cells_x, cells_y, depth = src_p_now.shape
    wide, y_a, y_b, window = pack(blocks, traces, segment_start)
    y_a, y_b = swap(y_a, "gy", 0), swap(y_b, "gy", 1)
    wide, x_a, x_b = pack_x(wide, window)
    x_a, x_b = swap(x_a, "gx", 0), swap(x_b, "gx", 1)
    windows = jnp.concatenate([window, x_a[x_parts()[1] :, :STEPS, :]], axis=0)
    for bit in bits_of("gx")[1:]:
        windows = doubled(windows, "gx", bit)
    for bit in bits_of("gy")[:-1]:
        windows = doubled(windows, "gy", bit)
    wide, c_a, c_b = corners(wide, y_a, y_b, windows)
    for bit in bits_of("gy")[-1:]:
        windows = doubled(windows, "gy", bit)
    c_a, c_b = swap(c_a, "gx", 0), swap(c_b, "gx", 1)
    planes = injected(
        windows, receiver_x, receiver_y, traces.shape[1], cells_x, cells_y, depth
    )
    state = inner(wide, planes)
    return tuple(outer(wide, (x_a, x_b, c_a, c_b), planes, state, cells_x, cells_y))


def solution(mesh):
    state = P(("shot", "gx"), "gy", None)
    earth = P("gx", "gy", None)
    return jax.shard_map(
        per_device,
        mesh=mesh,
        in_specs=(state,) * FIELDS + (earth,) * 5 + (P("shot", ("gx", "gy")), P(), P(), P()),
        out_specs=(state,) * 3,
        check_vma=False,
    )
```

```python
import functools

import jax
import jax.numpy as jnp
from jax import lax
from jax.experimental import pallas as pl
from jax.experimental.pallas import tpu as pltpu
from jax.sharding import PartitionSpec as P

STEPS = 4
REC_DEPTH = 4
RIM = STEPS
FIELDS = 8
SUBLANES = 8
LANES = 128
PARAMS = pltpu.CompilerParams(vmem_limit_bytes=16 * 1024 * 1024)
PACK_PARAMS = pltpu.CompilerParams(vmem_limit_bytes=48 * 1024 * 1024)


def in_vmem(count):
    return [pl.BlockSpec(memory_space=pltpu.VMEM)] * count


def is_odd(axis):
    return lax.rem(lax.axis_index(axis), 2) == 1


def swap(value, axis, first):
    size = lax.axis_size(axis)
    lower = range(first, size - 1, 2)
    pairs = [(i, i + 1) for i in lower] + [(i + 1, i) for i in lower]
    return lax.ppermute(value, axis, pairs)


NOW = (1, 3, 5, 7)
REST = (0, 2, 4, 6, 8, 9, 10, 11, 12)
SLIM = RIM - 1


def y_slots():
    slots = [((number, 0, RIM, 0),) for number in NOW]
    whole = len(REST) - len(REST) // RIM
    for place in range(whole):
        parts = [(REST[place], 0, SLIM, 0)]
        guest = whole + place // SLIM
        if guest < len(REST):
            parts.append((REST[guest], place % SLIM, 1, SLIM))
        slots.append(tuple(parts))
    return slots


def each_y_part(slots, high):
    for slot, parts in enumerate(slots):
        for number, row, rows, place in parts:
            if not high:
                yield slot, number, row, place, rows
            else:
                width = RIM if number in NOW else SLIM
                yield slot, number, RIM - width + row, 0 if place else RIM - rows, rows


def x_parts():
    parts, place = [], 0
    for number in NOW:
        parts.append((number, RIM, place))
        place += RIM
    for number in REST:
        parts.append((number, SLIM, place))
        place += SLIM
    return parts, place


def pinned(value, space):
    return pltpu.with_memory_space_constraint(value, space)


def vmem_out(*shape):
    return pltpu.VMEM(shape, jnp.float32)


def pack_kernel(count, *refs):
    blocks, traces, start = refs[:count], refs[count], refs[count + 1]
    wide, y_a, y_b, window, held, sems = refs[count + 2 :]
    cells_x, cells_y = blocks[0].shape[:2]
    core_x = pl.ds(RIM, cells_x)
    moves = [
        pltpu.make_async_copy(block, wide.at[number, core_x, pl.ds(0, cells_y)], sems.at[number])
        for number, block in enumerate(blocks)
    ]
    moves.append(pltpu.make_async_copy(traces, held, sems.at[count]))
    for move in moves:
        move.start()
    odd_y = is_odd("gy")
    begin = start[0]
    samples = traces.shape[1]
    window[...] = jnp.zeros_like(window)
    for move in moves:
        move.wait()
    for sample in range(STEPS):
        window[0, sample : sample + 1, :samples] = held[pl.ds(begin + sample, 1), :]

    def put_y(low, high):
        for out, is_high, base in ((low, False, 0), (high, True, cells_y - RIM)):
            for slot, number, row, place, length in each_y_part(y_slots(), is_high):
                out[slot, :, place : place + length, :] = wide[
                    number, RIM : RIM + cells_x, base + row : base + row + length, :
                ]

    @pl.when(odd_y)
    def _():
        put_y(y_a, y_b)

    @pl.when(jnp.logical_not(odd_y))
    def _():
        put_y(y_b, y_a)


def pack(blocks, traces, segment_start):
    cells_x, cells_y, depth = blocks[0].shape
    count = len(blocks)
    rim_y = vmem_out(len(y_slots()), cells_x, RIM, depth)
    wide = vmem_out(count, cells_x + 2 * RIM + 2, cells_y + 2 * RIM, depth)
    return pl.pallas_call(
        functools.partial(pack_kernel, count),
        out_shape=[wide, rim_y, rim_y, vmem_out(1, STEPS, LANES)],
        in_specs=[pl.BlockSpec(memory_space=pltpu.HBM)] * (count + 1)
        + [pl.BlockSpec(memory_space=pltpu.SMEM)],
        out_specs=in_vmem(4),
        scratch_shapes=[
            pltpu.VMEM(traces.shape, jnp.float32),
            pltpu.SemaphoreType.DMA((count + 1,)),
        ],
        compiler_params=PACK_PARAMS,
        name="pack_y_rims",
    )(*(pinned(value, pltpu.HBM) for value in (*blocks, traces)), segment_start)


def pack_x_kernel(_, window, wide, x_a, x_b):
    cells_x, cells_y = wide.shape[1] - 2 * RIM - 2, wide.shape[2] - 2 * RIM
    odd_x = is_odd("gx")
    parts, total = x_parts()
    for number, width, place in parts:
        first, last = RIM, RIM + cells_x - width
        for out, begin in ((x_a, jnp.where(odd_x, first, last)), (x_b, jnp.where(odd_x, last, first))):
            out[place : place + width] = wide[number, pl.ds(begin, width), :cells_y, :]
    x_a[total] = jnp.zeros_like(x_a[total])
    x_a[total, :STEPS, :] = window[0]


def pack_x(wide, window):
    _, _, rows, depth = wide.shape
    total = x_parts()[1]
    return pl.pallas_call(
        pack_x_kernel,
        out_shape=[
            vmem_out(*wide.shape),
            vmem_out(total + 1, rows - 2 * RIM, depth),
            vmem_out(total, rows - 2 * RIM, depth),
        ],
        in_specs=in_vmem(2),
        out_specs=in_vmem(3),
        input_output_aliases={0: 0},
        compiler_params=PARAMS,
        name="pack_x_rims",
    )(pinned(wide, pltpu.VMEM), window)


def corner_kernel(_, y_a, y_b, __, wide, c_a, c_b):
    cells_x = y_a.shape[1]
    cells_y = wide.shape[2] - 2 * RIM
    odd_x, odd_y = is_odd("gx"), is_odd("gy")

    def place_y(low, high):
        for rim, is_high, base in ((high, False, cells_y), (low, True, cells_y + RIM)):
            for slot, number, row, place, length in each_y_part(y_slots(), is_high):
                wide[number, RIM : RIM + cells_x, base + row : base + row + length, :] = rim[
                    slot, :, place : place + length, :
                ]

    @pl.when(odd_y)
    def _():
        place_y(y_a, y_b)

    @pl.when(jnp.logical_not(odd_y))
    def _():
        place_y(y_b, y_a)

    for number, width, place in x_parts()[0]:
        first, last = RIM, RIM + cells_x - width
        for out, begin in ((c_a, jnp.where(odd_x, first, last)), (c_b, jnp.where(odd_x, last, first))):
            out[place : place + width] = wide[number, pl.ds(begin, width), cells_y:, :]


def corners(wide, y_a, y_b, earlier):
    corner = vmem_out(x_parts()[1], 2 * RIM, wide.shape[-1])
    return pl.pallas_call(
        corner_kernel,
        out_shape=[vmem_out(*wide.shape), corner, corner],
        in_specs=in_vmem(4),
        out_specs=in_vmem(3),
        input_output_aliases={0: 0},
        compiler_params=PARAMS,
        name="pack_corners",
    )(pinned(wide, pltpu.VMEM), y_a, y_b, earlier)


def sine_cosine(angle):
    square = angle * angle
    sine = 1.0 / 6227020800.0
    for term in (-1.0 / 39916800.0, 1.0 / 362880.0, -1.0 / 5040.0, 1.0 / 120.0, -1.0 / 6.0, 1.0):
        sine = sine * square + term
    cosine = 1.0 / 479001600.0
    for term in (-1.0 / 3628800.0, 1.0 / 40320.0, -1.0 / 720.0, 1.0 / 24.0, -0.5, 1.0):
        cosine = cosine * square + term
    return sine * angle, cosine


class Steps:
    def __init__(self, wide, planes, waves, factors):
        self.wide, self.planes, self.waves, self.factors = wide, planes, waves, factors
        self.count, _, rows, self.depth = wide.shape
        self.tiles = rows // SUBLANES
        self.cells_x = wide.shape[1] - 2 * RIM - 2
        lane = lax.broadcasted_iota(jnp.int32, (SUBLANES, self.depth), 1)
        self.not_last, self.not_first = lane < self.depth - 1, lane > 0
        self.at_depth = lane == REC_DEPTH

    def wide_tiles(self, number, x):
        return [
            self.wide[number, x, pl.ds(tile, SUBLANES, stride=self.tiles), :]
            for tile in range(self.tiles)
        ]

    def wave_tiles(self, number, slot, x):
        if slot < 2:
            return self.wide_tiles(2 * number + slot, x)
        return [self.waves[slot - 2][number, x, tile] for tile in range(self.tiles)]

    def next_y(self, value):
        return value[1:] + [pltpu.roll(value[0], SUBLANES - 1, 0)]

    def previous_y(self, value):
        return [pltpu.roll(value[-1], 1, 0)] + value[:-1]

    def make_factors(self, x):
        raw = [self.wide_tiles(FIELDS + number, x) for number in range(self.count - FIELDS)]
        for tile in range(self.tiles):
            velocity, epsilon, delta, tilt, azimuth = [value[tile] for value in raw]
            f_e = 1.0 + 2.0 * epsilon
            f_d = jnp.sqrt(1.0 + 2.0 * delta)
            sin_tilt, cos_tilt = sine_cosine(tilt)
            sin_half, cos_half = sine_cosine(0.5 * azimuth)
            sin_azim = 2.0 * sin_half * cos_half
            cos_azim = 1.0 - 2.0 * sin_half * sin_half
            sin_square = sin_tilt * sin_tilt
            half_tilt = 0.5 * sin_tilt * cos_tilt
            along_x = sin_square * cos_azim
            values = (
                velocity,
                velocity * f_e,
                velocity * f_d,
                along_x * cos_azim,
                sin_square * sin_azim * sin_azim,
                cos_tilt * cos_tilt,
                0.5 * along_x * sin_azim,
                half_tilt * cos_azim,
                half_tilt * sin_azim,
            )
            for number, value in enumerate(values):
                self.factors[number, x, tile] = value

    def sides_z(self, value):
        above = [jnp.where(self.not_last, pltpu.roll(u, self.depth - 1, 1), 0.0) for u in value]
        below = [jnp.where(self.not_first, pltpu.roll(u, 1, 1), 0.0) for u in value]
        return above, below

    def stencil(self, factors, before, now, after, full):
        slope_x = [a - b for a, b in zip(after, before)]
        above, below = self.sides_z(now)
        slope_z = [a - b for a, b in zip(above, below)]
        next_now, previous_now = self.next_y(now), self.previous_y(now)
        above_x, below_x = self.sides_z(slope_x)
        next_x, previous_x = self.next_y(slope_x), self.previous_y(slope_x)
        next_z, previous_z = self.next_y(slope_z), self.previous_y(slope_z)
        axis, laplace = [], []
        for tile in range(self.tiles):
            axx, ayy, azz, axy, axz, ayz = [value[tile] for value in factors]
            double = now[tile] + now[tile]
            sum_x = after[tile] + before[tile]
            sum_y = next_now[tile] + previous_now[tile]
            sum_z = above[tile] + below[tile]
            straight = ((axx * sum_x + ayy * sum_y) + azz * sum_z) - double
            mixed = (
                axy * (next_x[tile] - previous_x[tile]) + axz * (above_x[tile] - below_x[tile])
            ) + ayz * (next_z[tile] - previous_z[tile])
            axis.append(straight + mixed)
            if full:
                laplace.append(((sum_x + sum_y) + sum_z) - 3.0 * double)
        return axis, laplace

    def step(self, turn, x, count):
        tiles, factors = range(self.tiles), self.factors
        for pair in range(2):
            p_number, q_number = 2 * pair, 2 * pair + 1
            p = [self.wave_tiles(p_number, turn + 1, x - 1 + i) for i in range(count + 2)]
            q = [self.wave_tiles(q_number, turn + 1, x - 1 + i) for i in range(count + 2)]
            for i in range(count):
                now = x + i
                mixing = [[factors[number, now, tile] for tile in tiles] for number in range(3, 9)]
                p_axis, p_laplace = self.stencil(mixing, p[i], p[i + 1], p[i + 2], True)
                q_axis, _ = self.stencil(mixing, q[i], q[i + 1], q[i + 2], False)
                p_held = self.wave_tiles(p_number, turn, now)
                q_held = self.wave_tiles(q_number, turn, now)
                for tile in tiles:
                    velocity, with_e, with_d = [factors[number, now, tile] for number in range(3)]
                    across = p_laplace[tile] - p_axis[tile]
                    p_now, q_now = p[i + 1][tile], q[i + 1][tile]
                    p_next = ((p_now + p_now) - p_held[tile]) + (
                        with_e * across + with_d * q_axis[tile]
                    )
                    q_next = ((q_now + q_now) - q_held[tile]) + (
                        with_d * across + velocity * q_axis[tile]
                    )
                    if pair == 1:
                        shift = lax.rem(REC_DEPTH - now + self.depth, self.depth)
                        moved = pltpu.roll(self.planes[STEPS - 1 - turn, tile], shift, 1)
                        p_next = p_next + jnp.where(self.at_depth, moved, 0.0)
                    self.waves[turn][p_number, now, tile] = p_next
                    self.waves[turn][q_number, now, tile] = q_next


def repeat(count, body):
    def run(i, carry):
        body(i)
        return carry

    lax.fori_loop(0, count, run, 0)


def inner_kernel(wide, planes, *refs):
    steps = Steps(wide, planes, refs[:STEPS], refs[STEPS])
    cells_x = steps.cells_x

    def factor_pair(i):
        steps.make_factors(RIM + 2 * i)
        steps.make_factors(RIM + 2 * i + 1)

    repeat(cells_x // 2, factor_pair)
    for turn in range(STEPS):
        first, last = RIM + 1 + turn, RIM + cells_x - 1 - turn
        repeat((last - first) // 2, lambda i, turn=turn, first=first: steps.step(turn, first + 2 * i, 2))


def outer_kernel(*refs):
    x_a, x_b, c_a, c_b, planes = refs[1:6]
    refs = refs[6 + STEPS + 1 :]
    wide, waves, factors = refs[0], refs[1 : 1 + STEPS], refs[1 + STEPS]
    image, p_last, q_last = refs[-3:]
    cells_x, cells_y, depth = image.shape
    odd_x = is_odd("gx")
    for number, width, place in x_parts()[0]:
        low, high = RIM - width, RIM + cells_x
        for begin, side, corner in (
            (jnp.where(odd_x, low, high), x_a, c_a),
            (jnp.where(odd_x, high, low), x_b, c_b),
        ):
            wide[number, pl.ds(begin, width), :cells_y, :] = side[place : place + width]
            wide[number, pl.ds(begin, width), cells_y:, :] = corner[place : place + width]

    steps = Steps(wide, planes, waves, factors)

    def factor_pair(i):
        steps.make_factors(RIM - SLIM + i)
        steps.make_factors(RIM + cells_x + i)

    repeat(SLIM, factor_pair)
    for turn in range(STEPS):

        def both(i, turn=turn):
            steps.step(turn, turn + 1 + 2 * i, 2)
            steps.step(turn, RIM + cells_x - 1 - turn + 2 * i, 2)

        repeat(RIM // 2, both)

    tiles = steps.tiles

    def finish(i):
        x = RIM + i
        total = None
        for back in range(STEPS + 1):
            source = steps.wave_tiles(0, 1 + STEPS - back, x)
            receiver = steps.wave_tiles(2, 1 + back, x)
            product = [a * b for a, b in zip(source, receiver)]
            total = product if total is None else [a + b for a, b in zip(total, product)]
        for out, value in (
            (0, total),
            (1, steps.wave_tiles(2, 1 + STEPS, x)),
            (2, steps.wave_tiles(3, 1 + STEPS, x)),
        ):
            for tile in range(tiles):
                wide[out, x, pl.ds(tile, SUBLANES, stride=tiles), :] = value[tile]

    repeat(cells_x, finish)
    for out, ref in enumerate((image, p_last, q_last)):
        ref[...] = wide[out, RIM : RIM + cells_x, :cells_y, :]


def inner(wide, planes):
    _, planes_x, rows, depth = wide.shape
    tile = (planes_x, rows // SUBLANES, SUBLANES, depth)
    return pl.pallas_call(
        inner_kernel,
        out_shape=[vmem_out(4, *tile)] * STEPS + [vmem_out(9, *tile)],
        in_specs=in_vmem(2),
        out_specs=in_vmem(STEPS + 1),
        compiler_params=PARAMS,
        name="inner_steps",
    )(pinned(wide, pltpu.VMEM), planes)


def outer(wide, rims, planes, state, cells_x, cells_y):
    out = jax.ShapeDtypeStruct((cells_x, cells_y, wide.shape[-1]), jnp.float32)
    kept = [vmem_out(*wide.shape)] + [vmem_out(*value.shape) for value in state]
    first = len(rims) + 2
    aliases = {0: 0} | {first + number: 1 + number for number in range(len(state))}
    return pl.pallas_call(
        outer_kernel,
        out_shape=kept + [out] * 3,
        in_specs=in_vmem(first + len(state)),
        out_specs=in_vmem(len(kept) + 3),
        input_output_aliases=aliases,
        compiler_params=PARAMS,
        name="outer_steps",
    )(
        pinned(wide, pltpu.VMEM),
        *rims,
        planes,
        *(pinned(value, pltpu.VMEM) for value in state),
    )[-3:]


def bits_of(axis):
    size = lax.axis_size(axis)
    return [1 << bit for bit in range(size.bit_length() - 1)] if size & (size - 1) == 0 else None


def doubled(windows, axis, bit):
    pairs = [(i, i ^ bit) for i in range(lax.axis_size(axis))]
    return jnp.concatenate([windows, lax.ppermute(windows, axis, pairs)], axis=0)


def inject_kernel(samples, cells_x, cells_y, gathered, table_x, table_y, planes, weights, picks):
    size_y = lax.axis_size("gy")
    own_x, own_y = lax.axis_index("gx"), lax.axis_index("gy")
    rows = cells_y + 2 * RIM
    tiles = rows // SUBLANES
    wide_x = picks.shape[0]
    in_row = LANES // samples
    place = lax.broadcasted_iota(jnp.int32, (rows, LANES), 0)
    row = tiles * lax.rem(place, SUBLANES) + lax.div(place, SUBLANES)
    y_global = own_y * cells_y + jnp.where(row < cells_y + RIM, row, row - rows)
    x_global = own_x * cells_x - RIM + lax.broadcasted_iota(jnp.int32, (wide_x, LANES), 0)
    lane = lax.broadcasted_iota(jnp.int32, (1, LANES), 1)
    bits_x, bits_y = bits_of("gx"), bits_of("gy")

    def source(place):
        device_x, device_y = own_x, own_y
        for number, bit in enumerate(bits_x):
            if place >> number & 1:
                device_x = jnp.bitwise_xor(device_x, bit)
        for number, bit in enumerate(bits_y):
            if place >> (len(bits_x) + number) & 1:
                device_y = jnp.bitwise_xor(device_y, bit)
        return device_x * size_y + device_y

    for group in range(gathered.shape[0] // in_row):
        at_x = at_y = jnp.zeros((1, LANES), jnp.int32)
        window = jnp.zeros((STEPS, LANES), jnp.float32)
        for part in range(in_row):
            place = group * in_row + part
            device = source(place)
            here = (lane >= part * samples) & (lane < (part + 1) * samples)
            shift = lax.rem((part - lax.rem(device, in_row)) * samples + LANES, LANES)
            table_row = pl.ds(lax.div(device, in_row), 1)
            at_x = jnp.where(here, pltpu.roll(table_x[table_row, :], shift, 1), at_x)
            at_y = jnp.where(here, pltpu.roll(table_y[table_row, :], shift, 1), at_y)
            moved = gathered[place]
            if part:
                moved = pltpu.roll(moved, part * samples, 1)
            window = jnp.where(here, moved, window)
        span = slice(group * LANES, (group + 1) * LANES)
        picks[:, span] = (at_x == x_global).astype(jnp.float32)
        is_y = at_y == y_global
        for sample in range(STEPS):
            weights[sample * rows : (sample + 1) * rows, span] = jnp.where(
                is_y, window[sample : sample + 1], 0.0
            )
    rest = weights[...]
    pick = picks[...].astype(jnp.bfloat16)
    total = None
    for _ in range(3):
        part = rest.astype(jnp.bfloat16)
        rest = rest - part.astype(jnp.float32)
        product = lax.dot_general(
            part, pick, (((1,), (1,)), ((), ())), preferred_element_type=jnp.float32
        )
        total = product if total is None else total + product
    planes[...] = jnp.zeros_like(planes)
    for sample in range(STEPS):
        for tile in range(tiles):
            begin = sample * rows + tile * SUBLANES
            planes[sample, tile, :, :wide_x] = total[begin : begin + SUBLANES]


def injected(gathered, receiver_x, receiver_y, samples, cells_x, cells_y, depth):
    rows = cells_y + 2 * RIM
    receivers = receiver_x.shape[0]
    wide_x = -(-(cells_x + 2 * RIM) // 32) * 32
    return pl.pallas_call(
        functools.partial(inject_kernel, samples, cells_x, cells_y),
        out_shape=vmem_out(STEPS, rows // SUBLANES, SUBLANES, depth),
        in_specs=in_vmem(3),
        out_specs=in_vmem(1)[0],
        scratch_shapes=[
            pltpu.VMEM((STEPS * rows, receivers), jnp.float32),
            pltpu.VMEM((wide_x, receivers), jnp.float32),
        ],
        compiler_params=PARAMS,
        name="inject",
    )(gathered, receiver_x.reshape(-1, LANES), receiver_y.reshape(-1, LANES))


def per_device(
    src_p_prev,
    src_p_now,
    src_q_prev,
    src_q_now,
    rec_p_next,
    rec_p_now,
    rec_q_next,
    rec_q_now,
    velocity_term,
    epsilon,
    delta,
    tilt,
    azimuth,
    traces,
    receiver_x,
    receiver_y,
    segment_start,
):
    blocks = (
        src_p_prev,
        src_p_now,
        src_q_prev,
        src_q_now,
        rec_p_next,
        rec_p_now,
        rec_q_next,
        rec_q_now,
        velocity_term,
        epsilon,
        delta,
        tilt,
        azimuth,
    )
    cells_x, cells_y, depth = src_p_now.shape
    wide, y_a, y_b, window = pack(blocks, traces, segment_start)
    y_a, y_b = swap(y_a, "gy", 0), swap(y_b, "gy", 1)
    wide, x_a, x_b = pack_x(wide, window)
    x_a, x_b = swap(x_a, "gx", 0), swap(x_b, "gx", 1)
    windows = jnp.concatenate([window, x_a[x_parts()[1] :, :STEPS, :]], axis=0)
    for bit in bits_of("gx")[1:]:
        windows = doubled(windows, "gx", bit)
    for bit in bits_of("gy")[:-1]:
        windows = doubled(windows, "gy", bit)
    wide, c_a, c_b = corners(wide, y_a, y_b, windows)
    for bit in bits_of("gy")[-1:]:
        windows = doubled(windows, "gy", bit)
    c_a, c_b = swap(c_a, "gx", 0), swap(c_b, "gx", 1)
    planes = injected(
        windows, receiver_x, receiver_y, traces.shape[1], cells_x, cells_y, depth
    )
    state = inner(wide, planes)
    return tuple(outer(wide, (x_a, x_b, c_a, c_b), planes, state, cells_x, cells_y))


def solution(mesh):
    state = P(("shot", "gx"), "gy", None)
    earth = P("gx", "gy", None)
    return jax.shard_map(
        per_device,
        mesh=mesh,
        in_specs=(state,) * FIELDS + (earth,) * 5 + (P("shot", ("gx", "gy")), P(), P(), P()),
        out_specs=(state,) * 3,
        check_vma=False,
    )
```

```python
import functools

import jax
import jax.numpy as jnp
from jax import lax
from jax.experimental import pallas as pl
from jax.experimental.pallas import tpu as pltpu
from jax.sharding import PartitionSpec as P

STEPS = 4
REC_DEPTH = 4
RIM = STEPS
FIELDS = 8
SUBLANES = 8
LANES = 128
PARAMS = pltpu.CompilerParams(vmem_limit_bytes=16 * 1024 * 1024)
PACK_PARAMS = pltpu.CompilerParams(vmem_limit_bytes=48 * 1024 * 1024)


def in_vmem(count):
    return [pl.BlockSpec(memory_space=pltpu.VMEM)] * count


def is_odd(axis):
    return lax.rem(lax.axis_index(axis), 2) == 1


def swap(value, axis, first):
    size = lax.axis_size(axis)
    lower = range(first, size - 1, 2)
    pairs = [(i, i + 1) for i in lower] + [(i + 1, i) for i in lower]
    return lax.ppermute(value, axis, pairs)


NOW = (1, 3, 5, 7)
REST = (0, 2, 4, 6, 8, 9, 10, 11, 12)
SLIM = RIM - 1


def y_slots():
    slots = [((number, 0, RIM, 0),) for number in NOW]
    whole = len(REST) - len(REST) // RIM
    for place in range(whole):
        parts = [(REST[place], 0, SLIM, 0)]
        guest = whole + place // SLIM
        if guest < len(REST):
            parts.append((REST[guest], place % SLIM, 1, SLIM))
        slots.append(tuple(parts))
    return slots


def each_y_part(slots, high):
    for slot, parts in enumerate(slots):
        for number, row, rows, place in parts:
            if not high:
                yield slot, number, row, place, rows
            else:
                width = RIM if number in NOW else SLIM
                yield slot, number, RIM - width + row, 0 if place else RIM - rows, rows


def x_parts():
    parts, place = [], 0
    for number in NOW:
        parts.append((number, RIM, place))
        place += RIM
    for number in REST:
        parts.append((number, SLIM, place))
        place += SLIM
    return parts, place


def pinned(value, space):
    return pltpu.with_memory_space_constraint(value, space)


def vmem_out(*shape):
    return pltpu.VMEM(shape, jnp.float32)


def pack_kernel(count, *refs):
    blocks, traces, start = refs[:count], refs[count], refs[count + 1]
    wide, y_a, y_b, window, held, sems = refs[count + 2 :]
    cells_x, cells_y = blocks[0].shape[:2]
    core_x = pl.ds(RIM, cells_x)
    moves = [
        pltpu.make_async_copy(block, wide.at[number, core_x, pl.ds(0, cells_y)], sems.at[number])
        for number, block in enumerate(blocks)
    ]
    moves.append(pltpu.make_async_copy(traces, held, sems.at[count]))
    for move in moves:
        move.start()
    odd_y = is_odd("gy")
    begin = start[0]
    samples = traces.shape[1]
    window[...] = jnp.zeros_like(window)
    for move in moves:
        move.wait()
    for sample in range(STEPS):
        window[0, sample : sample + 1, :samples] = held[pl.ds(begin + sample, 1), :]

    def put_y(low, high):
        for out, is_high, base in ((low, False, 0), (high, True, cells_y - RIM)):
            for slot, number, row, place, length in each_y_part(y_slots(), is_high):
                out[slot, :, place : place + length, :] = wide[
                    number, RIM : RIM + cells_x, base + row : base + row + length, :
                ]

    @pl.when(odd_y)
    def _():
        put_y(y_a, y_b)

    @pl.when(jnp.logical_not(odd_y))
    def _():
        put_y(y_b, y_a)


def pack(blocks, traces, segment_start):
    cells_x, cells_y, depth = blocks[0].shape
    count = len(blocks)
    rim_y = vmem_out(len(y_slots()), cells_x, RIM, depth)
    wide = vmem_out(count, cells_x + 2 * RIM + 2, cells_y + 2 * RIM, depth)
    return pl.pallas_call(
        functools.partial(pack_kernel, count),
        out_shape=[wide, rim_y, rim_y, vmem_out(1, STEPS, LANES)],
        in_specs=[pl.BlockSpec(memory_space=pltpu.HBM)] * (count + 1)
        + [pl.BlockSpec(memory_space=pltpu.SMEM)],
        out_specs=in_vmem(4),
        scratch_shapes=[
            pltpu.VMEM(traces.shape, jnp.float32),
            pltpu.SemaphoreType.DMA((count + 1,)),
        ],
        compiler_params=PACK_PARAMS,
        name="pack_y_rims",
    )(*(pinned(value, pltpu.HBM) for value in (*blocks, traces)), segment_start)


def pack_x_kernel(_, window, wide, x_a, x_b):
    cells_x, cells_y = wide.shape[1] - 2 * RIM - 2, wide.shape[2] - 2 * RIM
    odd_x = is_odd("gx")
    parts, total = x_parts()
    for number, width, place in parts:
        first, last = RIM, RIM + cells_x - width
        for out, begin in ((x_a, jnp.where(odd_x, first, last)), (x_b, jnp.where(odd_x, last, first))):
            out[place : place + width] = wide[number, pl.ds(begin, width), :cells_y, :]
    x_a[total] = jnp.zeros_like(x_a[total])
    x_a[total, :STEPS, :] = window[0]


def pack_x(wide, window):
    _, _, rows, depth = wide.shape
    total = x_parts()[1]
    return pl.pallas_call(
        pack_x_kernel,
        out_shape=[
            vmem_out(*wide.shape),
            vmem_out(total + 1, rows - 2 * RIM, depth),
            vmem_out(total, rows - 2 * RIM, depth),
        ],
        in_specs=in_vmem(2),
        out_specs=in_vmem(3),
        input_output_aliases={0: 0},
        compiler_params=PARAMS,
        name="pack_x_rims",
    )(pinned(wide, pltpu.VMEM), window)


def corner_kernel(_, y_a, y_b, __, ___, wide, c_a, c_b):
    cells_x = y_a.shape[1]
    cells_y = wide.shape[2] - 2 * RIM
    odd_x, odd_y = is_odd("gx"), is_odd("gy")

    def place_y(low, high):
        for rim, is_high, base in ((high, False, cells_y), (low, True, cells_y + RIM)):
            for slot, number, row, place, length in each_y_part(y_slots(), is_high):
                wide[number, RIM : RIM + cells_x, base + row : base + row + length, :] = rim[
                    slot, :, place : place + length, :
                ]

    @pl.when(odd_y)
    def _():
        place_y(y_a, y_b)

    @pl.when(jnp.logical_not(odd_y))
    def _():
        place_y(y_b, y_a)

    for number, width, place in x_parts()[0]:
        first, last = RIM, RIM + cells_x - width
        for out, begin in ((c_a, jnp.where(odd_x, first, last)), (c_b, jnp.where(odd_x, last, first))):
            out[place : place + width] = wide[number, pl.ds(begin, width), cells_y:, :]


def corners(wide, y_a, y_b, *earlier):
    corner = vmem_out(x_parts()[1], 2 * RIM, wide.shape[-1])
    return pl.pallas_call(
        corner_kernel,
        out_shape=[vmem_out(*wide.shape), corner, corner],
        in_specs=in_vmem(5),
        out_specs=in_vmem(3),
        input_output_aliases={0: 0},
        compiler_params=PARAMS,
        name="pack_corners",
    )(pinned(wide, pltpu.VMEM), y_a, y_b, *earlier)


def sine_cosine(angle):
    square = angle * angle
    sine = 1.0 / 6227020800.0
    for term in (-1.0 / 39916800.0, 1.0 / 362880.0, -1.0 / 5040.0, 1.0 / 120.0, -1.0 / 6.0, 1.0):
        sine = sine * square + term
    cosine = 1.0 / 479001600.0
    for term in (-1.0 / 3628800.0, 1.0 / 40320.0, -1.0 / 720.0, 1.0 / 24.0, -0.5, 1.0):
        cosine = cosine * square + term
    return sine * angle, cosine


def factors_of(velocity, epsilon, delta, tilt, azimuth):
    f_e = 1.0 + 2.0 * epsilon
    f_d = jnp.sqrt(1.0 + 2.0 * delta)
    sin_tilt, cos_tilt = sine_cosine(tilt)
    sin_half, cos_half = sine_cosine(0.5 * azimuth)
    sin_azim = 2.0 * sin_half * cos_half
    cos_azim = 1.0 - 2.0 * sin_half * sin_half
    sin_square = sin_tilt * sin_tilt
    half_tilt = 0.5 * sin_tilt * cos_tilt
    along_x = sin_square * cos_azim
    return (
        velocity,
        velocity * f_e,
        velocity * f_d,
        along_x * cos_azim,
        sin_square * sin_azim * sin_azim,
        cos_tilt * cos_tilt,
        0.5 * along_x * sin_azim,
        half_tilt * cos_azim,
        half_tilt * sin_azim,
    )


FACTORS = 9


def own_kernel(wide, _, own):
    _, cells_x, cells_y, _ = own.shape

    def body(i):
        for x in [4 * i + k for k in range(4)]:
            raw = [wide[FIELDS + number, RIM + x, :cells_y, :] for number in range(5)]
            for number, value in enumerate(factors_of(*raw)):
                own[number, x] = value

    repeat(cells_x // 4, body)


def own_factors(wide, earlier):
    _, planes_x, rows, depth = wide.shape
    cells_x, cells_y = planes_x - 2 * RIM - 2, rows - 2 * RIM
    return pl.pallas_call(
        own_kernel,
        out_shape=vmem_out(FACTORS, cells_x, cells_y, depth),
        in_specs=in_vmem(2),
        out_specs=in_vmem(1)[0],
        compiler_params=PARAMS,
        name="own_factors",
    )(pinned(wide, pltpu.VMEM), earlier)


class Steps:
    def __init__(self, wide, planes, waves, factors):
        self.wide, self.planes, self.waves, self.factors = wide, planes, waves, factors
        self.count, _, rows, self.depth = wide.shape
        self.tiles = rows // SUBLANES
        self.cells_x = wide.shape[1] - 2 * RIM - 2
        lane = lax.broadcasted_iota(jnp.int32, (SUBLANES, self.depth), 1)
        self.not_last, self.not_first = lane < self.depth - 1, lane > 0
        self.at_depth = lane == REC_DEPTH

    def wide_tiles(self, number, x):
        return [
            self.wide[number, x, pl.ds(tile, SUBLANES, stride=self.tiles), :]
            for tile in range(self.tiles)
        ]

    def wave_tiles(self, number, slot, x):
        if slot < 2:
            return self.wide_tiles(2 * number + slot, x)
        return [self.waves[slot - 2][number, x, tile] for tile in range(self.tiles)]

    def next_y(self, value):
        return value[1:] + [pltpu.roll(value[0], SUBLANES - 1, 0)]

    def previous_y(self, value):
        return [pltpu.roll(value[-1], 1, 0)] + value[:-1]

    def make_factors(self, x):
        raw = [self.wide_tiles(FIELDS + number, x) for number in range(self.count - FIELDS)]
        for tile in range(self.tiles):
            for number, value in enumerate(factors_of(*[value[tile] for value in raw])):
                self.factors[number, x, tile] = value

    def sides_z(self, value):
        above = [jnp.where(self.not_last, pltpu.roll(u, self.depth - 1, 1), 0.0) for u in value]
        below = [jnp.where(self.not_first, pltpu.roll(u, 1, 1), 0.0) for u in value]
        return above, below

    def stencil(self, factors, before, now, after, full):
        slope_x = [a - b for a, b in zip(after, before)]
        above, below = self.sides_z(now)
        slope_z = [a - b for a, b in zip(above, below)]
        next_now, previous_now = self.next_y(now), self.previous_y(now)
        above_x, below_x = self.sides_z(slope_x)
        next_x, previous_x = self.next_y(slope_x), self.previous_y(slope_x)
        next_z, previous_z = self.next_y(slope_z), self.previous_y(slope_z)
        axis, laplace = [], []
        for tile in range(self.tiles):
            axx, ayy, azz, axy, axz, ayz = [value[tile] for value in factors]
            double = now[tile] + now[tile]
            sum_x = after[tile] + before[tile]
            sum_y = next_now[tile] + previous_now[tile]
            sum_z = above[tile] + below[tile]
            straight = ((axx * sum_x + ayy * sum_y) + azz * sum_z) - double
            mixed = (
                axy * (next_x[tile] - previous_x[tile]) + axz * (above_x[tile] - below_x[tile])
            ) + ayz * (next_z[tile] - previous_z[tile])
            axis.append(straight + mixed)
            if full:
                laplace.append(((sum_x + sum_y) + sum_z) - 3.0 * double)
        return axis, laplace

    def step(self, turn, x, count):
        tiles, factors = range(self.tiles), self.factors
        for pair in range(2):
            p_number, q_number = 2 * pair, 2 * pair + 1
            p = [self.wave_tiles(p_number, turn + 1, x - 1 + i) for i in range(count + 2)]
            q = [self.wave_tiles(q_number, turn + 1, x - 1 + i) for i in range(count + 2)]
            for i in range(count):
                now = x + i
                mixing = [[factors[number, now, tile] for tile in tiles] for number in range(3, 9)]
                p_axis, p_laplace = self.stencil(mixing, p[i], p[i + 1], p[i + 2], True)
                q_axis, _ = self.stencil(mixing, q[i], q[i + 1], q[i + 2], False)
                p_held = self.wave_tiles(p_number, turn, now)
                q_held = self.wave_tiles(q_number, turn, now)
                for tile in tiles:
                    velocity, with_e, with_d = [factors[number, now, tile] for number in range(3)]
                    across = p_laplace[tile] - p_axis[tile]
                    p_now, q_now = p[i + 1][tile], q[i + 1][tile]
                    p_next = ((p_now + p_now) - p_held[tile]) + (
                        with_e * across + with_d * q_axis[tile]
                    )
                    q_next = ((q_now + q_now) - q_held[tile]) + (
                        with_d * across + velocity * q_axis[tile]
                    )
                    if pair == 1:
                        shift = lax.rem(REC_DEPTH - now + self.depth, self.depth)
                        moved = pltpu.roll(self.planes[STEPS - 1 - turn, tile], shift, 1)
                        p_next = p_next + jnp.where(self.at_depth, moved, 0.0)
                    self.waves[turn][p_number, now, tile] = p_next
                    self.waves[turn][q_number, now, tile] = q_next


def repeat(count, body):
    def run(i, carry):
        body(i)
        return carry

    lax.fori_loop(0, count, run, 0)


def inner_kernel(wide, planes, own, *refs):
    steps = Steps(wide, planes, refs[:STEPS], refs[STEPS])
    natural = refs[STEPS + 1]
    cells_x, cells_y, tiles = steps.cells_x, own.shape[2], steps.tiles

    def rim_rows(i):
        for x in [4 * i + k for k in range(4)]:
            raw = [wide[FIELDS + number, RIM + x, cells_y:, :] for number in range(5)]
            for number, value in enumerate(factors_of(*raw)):
                natural[number, x, cells_y:, :] = value
                natural[number, x, :cells_y, :] = own[number, x]

    def in_step_order(i):
        for x in [2 * i + k for k in range(2)]:
            for number in range(FACTORS):
                for tile in range(tiles):
                    steps.factors[number, RIM + x, tile] = natural[
                        number, x, pl.ds(tile, SUBLANES, stride=tiles), :
                    ]

    repeat(cells_x // 4, rim_rows)
    repeat(cells_x // 2, in_step_order)
    for turn in range(STEPS):
        first, last = RIM + 1 + turn, RIM + cells_x - 1 - turn
        repeat((last - first) // 2, lambda i, turn=turn, first=first: steps.step(turn, first + 2 * i, 2))


def outer_kernel(*refs):
    x_a, x_b, c_a, c_b, planes = refs[1:6]
    refs = refs[6 + STEPS + 1 :]
    wide, waves, factors = refs[0], refs[1 : 1 + STEPS], refs[1 + STEPS]
    image, p_last, q_last = refs[-3:]
    cells_x, cells_y, depth = image.shape
    odd_x = is_odd("gx")
    for number, width, place in x_parts()[0]:
        low, high = RIM - width, RIM + cells_x
        for begin, side, corner in (
            (jnp.where(odd_x, low, high), x_a, c_a),
            (jnp.where(odd_x, high, low), x_b, c_b),
        ):
            wide[number, pl.ds(begin, width), :cells_y, :] = side[place : place + width]
            wide[number, pl.ds(begin, width), cells_y:, :] = corner[place : place + width]

    steps = Steps(wide, planes, waves, factors)

    for x in range(SLIM):
        steps.make_factors(RIM - SLIM + x)
        steps.make_factors(RIM + cells_x + x)
    for turn in range(STEPS):

        def both(i, turn=turn):
            steps.step(turn, turn + 1 + 2 * i, 2)
            steps.step(turn, RIM + cells_x - 1 - turn + 2 * i, 2)

        repeat(RIM // 2, both)

    tiles = steps.tiles

    def finish(i):
        x = RIM + i
        total = None
        for back in range(STEPS + 1):
            source = steps.wave_tiles(0, 1 + STEPS - back, x)
            receiver = steps.wave_tiles(2, 1 + back, x)
            product = [a * b for a, b in zip(source, receiver)]
            total = product if total is None else [a + b for a, b in zip(total, product)]
        for out, value in (
            (0, total),
            (1, steps.wave_tiles(2, 1 + STEPS, x)),
            (2, steps.wave_tiles(3, 1 + STEPS, x)),
        ):
            for tile in range(tiles):
                wide[out, x, pl.ds(tile, SUBLANES, stride=tiles), :] = value[tile]

    repeat(cells_x, finish)
    for out, ref in enumerate((image, p_last, q_last)):
        ref[...] = wide[out, RIM : RIM + cells_x, :cells_y, :]


def inner(wide, planes, own):
    _, planes_x, rows, depth = wide.shape
    tile = (planes_x, rows // SUBLANES, SUBLANES, depth)
    return pl.pallas_call(
        inner_kernel,
        out_shape=[vmem_out(4, *tile)] * STEPS + [vmem_out(FACTORS, *tile)],
        in_specs=in_vmem(3),
        out_specs=in_vmem(STEPS + 1),
        scratch_shapes=[pltpu.VMEM((FACTORS, own.shape[1], rows, depth), jnp.float32)],
        compiler_params=PARAMS,
        name="inner_steps",
    )(pinned(wide, pltpu.VMEM), planes, pinned(own, pltpu.VMEM))


def outer(wide, rims, planes, state, cells_x, cells_y):
    out = jax.ShapeDtypeStruct((cells_x, cells_y, wide.shape[-1]), jnp.float32)
    kept = [vmem_out(*wide.shape)] + [vmem_out(*value.shape) for value in state]
    first = len(rims) + 2
    aliases = {0: 0} | {first + number: 1 + number for number in range(len(state))}
    return pl.pallas_call(
        outer_kernel,
        out_shape=kept + [out] * 3,
        in_specs=in_vmem(first + len(state)),
        out_specs=in_vmem(len(kept) + 3),
        input_output_aliases=aliases,
        compiler_params=PARAMS,
        name="outer_steps",
    )(
        pinned(wide, pltpu.VMEM),
        *rims,
        planes,
        *(pinned(value, pltpu.VMEM) for value in state),
    )[-3:]


def bits_of(axis):
    size = lax.axis_size(axis)
    return [1 << bit for bit in range(size.bit_length() - 1)] if size & (size - 1) == 0 else None


def doubled(windows, axis, bit):
    pairs = [(i, i ^ bit) for i in range(lax.axis_size(axis))]
    return jnp.concatenate([windows, lax.ppermute(windows, axis, pairs)], axis=0)


def inject_kernel(samples, cells_x, cells_y, gathered, table_x, table_y, planes, weights, picks):
    size_y = lax.axis_size("gy")
    own_x, own_y = lax.axis_index("gx"), lax.axis_index("gy")
    rows = cells_y + 2 * RIM
    tiles = rows // SUBLANES
    wide_x = picks.shape[0]
    in_row = LANES // samples
    place = lax.broadcasted_iota(jnp.int32, (rows, LANES), 0)
    row = tiles * lax.rem(place, SUBLANES) + lax.div(place, SUBLANES)
    y_global = own_y * cells_y + jnp.where(row < cells_y + RIM, row, row - rows)
    x_global = own_x * cells_x - RIM + lax.broadcasted_iota(jnp.int32, (wide_x, LANES), 0)
    lane = lax.broadcasted_iota(jnp.int32, (1, LANES), 1)
    bits_x, bits_y = bits_of("gx"), bits_of("gy")

    def source(place):
        device_x, device_y = own_x, own_y
        for number, bit in enumerate(bits_x):
            if place >> number & 1:
                device_x = jnp.bitwise_xor(device_x, bit)
        for number, bit in enumerate(bits_y):
            if place >> (len(bits_x) + number) & 1:
                device_y = jnp.bitwise_xor(device_y, bit)
        return device_x * size_y + device_y

    for group in range(gathered.shape[0] // in_row):
        at_x = at_y = jnp.zeros((1, LANES), jnp.int32)
        window = jnp.zeros((STEPS, LANES), jnp.float32)
        for part in range(in_row):
            place = group * in_row + part
            device = source(place)
            here = (lane >= part * samples) & (lane < (part + 1) * samples)
            shift = lax.rem((part - lax.rem(device, in_row)) * samples + LANES, LANES)
            table_row = pl.ds(lax.div(device, in_row), 1)
            at_x = jnp.where(here, pltpu.roll(table_x[table_row, :], shift, 1), at_x)
            at_y = jnp.where(here, pltpu.roll(table_y[table_row, :], shift, 1), at_y)
            moved = gathered[place]
            if part:
                moved = pltpu.roll(moved, part * samples, 1)
            window = jnp.where(here, moved, window)
        span = slice(group * LANES, (group + 1) * LANES)
        picks[:, span] = (at_x == x_global).astype(jnp.float32)
        is_y = at_y == y_global
        for sample in range(STEPS):
            weights[sample * rows : (sample + 1) * rows, span] = jnp.where(
                is_y, window[sample : sample + 1], 0.0
            )
    rest = weights[...]
    pick = picks[...].astype(jnp.bfloat16)
    total = None
    for _ in range(3):
        part = rest.astype(jnp.bfloat16)
        rest = rest - part.astype(jnp.float32)
        product = lax.dot_general(
            part, pick, (((1,), (1,)), ((), ())), preferred_element_type=jnp.float32
        )
        total = product if total is None else total + product
    planes[...] = jnp.zeros_like(planes)
    for sample in range(STEPS):
        for tile in range(tiles):
            begin = sample * rows + tile * SUBLANES
            planes[sample, tile, :, :wide_x] = total[begin : begin + SUBLANES]


def injected(gathered, receiver_x, receiver_y, samples, cells_x, cells_y, depth):
    rows = cells_y + 2 * RIM
    receivers = receiver_x.shape[0]
    wide_x = -(-(cells_x + 2 * RIM) // 32) * 32
    return pl.pallas_call(
        functools.partial(inject_kernel, samples, cells_x, cells_y),
        out_shape=vmem_out(STEPS, rows // SUBLANES, SUBLANES, depth),
        in_specs=in_vmem(3),
        out_specs=in_vmem(1)[0],
        scratch_shapes=[
            pltpu.VMEM((STEPS * rows, receivers), jnp.float32),
            pltpu.VMEM((wide_x, receivers), jnp.float32),
        ],
        compiler_params=PARAMS,
        name="inject",
    )(gathered, receiver_x.reshape(-1, LANES), receiver_y.reshape(-1, LANES))


def per_device(
    src_p_prev,
    src_p_now,
    src_q_prev,
    src_q_now,
    rec_p_next,
    rec_p_now,
    rec_q_next,
    rec_q_now,
    velocity_term,
    epsilon,
    delta,
    tilt,
    azimuth,
    traces,
    receiver_x,
    receiver_y,
    segment_start,
):
    blocks = (
        src_p_prev,
        src_p_now,
        src_q_prev,
        src_q_now,
        rec_p_next,
        rec_p_now,
        rec_q_next,
        rec_q_now,
        velocity_term,
        epsilon,
        delta,
        tilt,
        azimuth,
    )
    cells_x, cells_y, depth = src_p_now.shape
    wide, y_a, y_b, window = pack(blocks, traces, segment_start)
    y_a, y_b = swap(y_a, "gy", 0), swap(y_b, "gy", 1)
    wide, x_a, x_b = pack_x(wide, window)
    x_a, x_b = swap(x_a, "gx", 0), swap(x_b, "gx", 1)
    windows = jnp.concatenate([window, x_a[x_parts()[1] :, :STEPS, :]], axis=0)
    for bit in bits_of("gx")[1:]:
        windows = doubled(windows, "gx", bit)
    own = own_factors(wide, windows)
    for bit in bits_of("gy")[:-1]:
        windows = doubled(windows, "gy", bit)
    wide, c_a, c_b = corners(wide, y_a, y_b, windows, pinned(own, pltpu.VMEM))
    for bit in bits_of("gy")[-1:]:
        windows = doubled(windows, "gy", bit)
    c_a, c_b = swap(c_a, "gx", 0), swap(c_b, "gx", 1)
    planes = injected(
        windows, receiver_x, receiver_y, traces.shape[1], cells_x, cells_y, depth
    )
    state = inner(wide, planes, own)
    return tuple(outer(wide, (x_a, x_b, c_a, c_b), planes, state, cells_x, cells_y))


def solution(mesh):
    state = P(("shot", "gx"), "gy", None)
    earth = P("gx", "gy", None)
    return jax.shard_map(
        per_device,
        mesh=mesh,
        in_specs=(state,) * FIELDS + (earth,) * 5 + (P("shot", ("gx", "gy")), P(), P(), P()),
        out_specs=(state,) * 3,
        check_vma=False,
    )
```

```python
import functools

import jax
import jax.numpy as jnp
from jax import lax
from jax.experimental import pallas as pl
from jax.experimental.pallas import tpu as pltpu
from jax.sharding import PartitionSpec as P

STEPS = 4
REC_DEPTH = 4
RIM = STEPS
FIELDS = 8
SUBLANES = 8
LANES = 128
PARAMS = pltpu.CompilerParams(vmem_limit_bytes=16 * 1024 * 1024)
PACK_PARAMS = pltpu.CompilerParams(vmem_limit_bytes=48 * 1024 * 1024)


def in_vmem(count):
    return [pl.BlockSpec(memory_space=pltpu.VMEM)] * count


def is_odd(axis):
    return lax.rem(lax.axis_index(axis), 2) == 1


def swap(value, axis, first):
    size = lax.axis_size(axis)
    lower = range(first, size - 1, 2)
    pairs = [(i, i + 1) for i in lower] + [(i + 1, i) for i in lower]
    return lax.ppermute(value, axis, pairs)


NOW = (1, 3, 5, 7)
REST = (0, 2, 4, 6, 8, 9, 10, 11, 12)
SLIM = RIM - 1


def y_slots():
    slots = [((number, 0, RIM, 0),) for number in NOW]
    whole = len(REST) - len(REST) // RIM
    for place in range(whole):
        parts = [(REST[place], 0, SLIM, 0)]
        guest = whole + place // SLIM
        if guest < len(REST):
            parts.append((REST[guest], place % SLIM, 1, SLIM))
        slots.append(tuple(parts))
    return slots


def each_y_part(slots, high):
    for slot, parts in enumerate(slots):
        for number, row, rows, place in parts:
            if not high:
                yield slot, number, row, place, rows
            else:
                width = RIM if number in NOW else SLIM
                yield slot, number, RIM - width + row, 0 if place else RIM - rows, rows


def x_parts():
    parts, place = [], 0
    for number in NOW:
        parts.append((number, RIM, place))
        place += RIM
    for number in REST:
        parts.append((number, SLIM, place))
        place += SLIM
    return parts, place


def pinned(value, space):
    return pltpu.with_memory_space_constraint(value, space)


def vmem_out(*shape):
    return pltpu.VMEM(shape, jnp.float32)


def pack_kernel(count, *refs):
    blocks, traces, start = refs[:count], refs[count], refs[count + 1]
    wide, y_a, y_b, window, held, sems = refs[count + 2 :]
    cells_x, cells_y = blocks[0].shape[:2]
    core_x = pl.ds(RIM, cells_x)
    moves = [
        pltpu.make_async_copy(block, wide.at[number, core_x, pl.ds(0, cells_y)], sems.at[number])
        for number, block in enumerate(blocks)
    ]
    moves.append(pltpu.make_async_copy(traces, held, sems.at[count]))
    for move in moves:
        move.start()
    odd_y = is_odd("gy")
    begin = start[0]
    samples = traces.shape[1]
    window[...] = jnp.zeros_like(window)
    for move in moves:
        move.wait()
    for sample in range(STEPS):
        window[0, sample : sample + 1, :samples] = held[pl.ds(begin + sample, 1), :]

    def put_y(low, high):
        for out, is_high, base in ((low, False, 0), (high, True, cells_y - RIM)):
            for slot, number, row, place, length in each_y_part(y_slots(), is_high):
                out[slot, :, place : place + length, :] = wide[
                    number, RIM : RIM + cells_x, base + row : base + row + length, :
                ]

    @pl.when(odd_y)
    def _():
        put_y(y_a, y_b)

    @pl.when(jnp.logical_not(odd_y))
    def _():
        put_y(y_b, y_a)


def pack(blocks, traces, segment_start):
    cells_x, cells_y, depth = blocks[0].shape
    count = len(blocks)
    rim_y = vmem_out(len(y_slots()), cells_x, RIM, depth)
    wide = vmem_out(count, cells_x + 2 * RIM + 2, cells_y + 2 * RIM, depth)
    return pl.pallas_call(
        functools.partial(pack_kernel, count),
        out_shape=[wide, rim_y, rim_y, vmem_out(1, STEPS, LANES)],
        in_specs=[pl.BlockSpec(memory_space=pltpu.HBM)] * (count + 1)
        + [pl.BlockSpec(memory_space=pltpu.SMEM)],
        out_specs=in_vmem(4),
        scratch_shapes=[
            pltpu.VMEM(traces.shape, jnp.float32),
            pltpu.SemaphoreType.DMA((count + 1,)),
        ],
        compiler_params=PACK_PARAMS,
        name="pack_y_rims",
    )(*(pinned(value, pltpu.HBM) for value in (*blocks, traces)), segment_start)


def pack_x_kernel(_, window, wide, x_a, x_b):
    cells_x, cells_y = wide.shape[1] - 2 * RIM - 2, wide.shape[2] - 2 * RIM
    odd_x = is_odd("gx")
    parts, total = x_parts()
    for number, width, place in parts:
        first, last = RIM, RIM + cells_x - width
        for out, begin in ((x_a, jnp.where(odd_x, first, last)), (x_b, jnp.where(odd_x, last, first))):
            out[place : place + width] = wide[number, pl.ds(begin, width), :cells_y, :]
    x_a[total] = jnp.zeros_like(x_a[total])
    x_a[total, :STEPS, :] = window[0]


def pack_x(wide, window):
    _, _, rows, depth = wide.shape
    total = x_parts()[1]
    return pl.pallas_call(
        pack_x_kernel,
        out_shape=[
            vmem_out(*wide.shape),
            vmem_out(total + 1, rows - 2 * RIM, depth),
            vmem_out(total, rows - 2 * RIM, depth),
        ],
        in_specs=in_vmem(2),
        out_specs=in_vmem(3),
        input_output_aliases={0: 0},
        compiler_params=PARAMS,
        name="pack_x_rims",
    )(pinned(wide, pltpu.VMEM), window)


def corner_kernel(_, y_a, y_b, __, ___, wide, c_a, c_b):
    cells_x = y_a.shape[1]
    cells_y = wide.shape[2] - 2 * RIM
    odd_x, odd_y = is_odd("gx"), is_odd("gy")

    def place_y(low, high):
        for rim, is_high, base in ((high, False, cells_y), (low, True, cells_y + RIM)):
            for slot, number, row, place, length in each_y_part(y_slots(), is_high):
                wide[number, RIM : RIM + cells_x, base + row : base + row + length, :] = rim[
                    slot, :, place : place + length, :
                ]

    @pl.when(odd_y)
    def _():
        place_y(y_a, y_b)

    @pl.when(jnp.logical_not(odd_y))
    def _():
        place_y(y_b, y_a)

    for number, width, place in x_parts()[0]:
        first, last = RIM, RIM + cells_x - width
        for out, begin in ((c_a, jnp.where(odd_x, first, last)), (c_b, jnp.where(odd_x, last, first))):
            out[place : place + width] = wide[number, pl.ds(begin, width), cells_y:, :]


def corners(wide, y_a, y_b, *earlier):
    corner = vmem_out(x_parts()[1], 2 * RIM, wide.shape[-1])
    return pl.pallas_call(
        corner_kernel,
        out_shape=[vmem_out(*wide.shape), corner, corner],
        in_specs=in_vmem(5),
        out_specs=in_vmem(3),
        input_output_aliases={0: 0},
        compiler_params=PARAMS,
        name="pack_corners",
    )(pinned(wide, pltpu.VMEM), y_a, y_b, *earlier)


def sine_cosine(angle):
    square = angle * angle
    sine = 1.0 / 6227020800.0
    for term in (-1.0 / 39916800.0, 1.0 / 362880.0, -1.0 / 5040.0, 1.0 / 120.0, -1.0 / 6.0, 1.0):
        sine = sine * square + term
    cosine = 1.0 / 479001600.0
    for term in (-1.0 / 3628800.0, 1.0 / 40320.0, -1.0 / 720.0, 1.0 / 24.0, -0.5, 1.0):
        cosine = cosine * square + term
    return sine * angle, cosine


def factors_of(velocity, epsilon, delta, tilt, azimuth):
    f_e = 1.0 + 2.0 * epsilon
    f_d = jnp.sqrt(1.0 + 2.0 * delta)
    sin_tilt, cos_tilt = sine_cosine(tilt)
    sin_half, cos_half = sine_cosine(0.5 * azimuth)
    sin_azim = 2.0 * sin_half * cos_half
    cos_azim = 1.0 - 2.0 * sin_half * sin_half
    sin_square = sin_tilt * sin_tilt
    half_tilt = 0.5 * sin_tilt * cos_tilt
    along_x = sin_square * cos_azim
    return (
        velocity,
        velocity * f_e,
        velocity * f_d,
        along_x * cos_azim,
        sin_square * sin_azim * sin_azim,
        cos_tilt * cos_tilt,
        0.5 * along_x * sin_azim,
        half_tilt * cos_azim,
        half_tilt * sin_azim,
    )


FACTORS = 9


def own_kernel(wide, _, own):
    _, cells_x, cells_y, _ = own.shape

    def body(i):
        for x in [4 * i + k for k in range(4)]:
            raw = [wide[FIELDS + number, RIM + x, :cells_y, :] for number in range(5)]
            for number, value in enumerate(factors_of(*raw)):
                own[number, x] = value

    repeat(cells_x // 4, body)


def own_factors(wide, earlier):
    _, planes_x, rows, depth = wide.shape
    cells_x, cells_y = planes_x - 2 * RIM - 2, rows - 2 * RIM
    return pl.pallas_call(
        own_kernel,
        out_shape=vmem_out(FACTORS, cells_x, cells_y, depth),
        in_specs=in_vmem(2),
        out_specs=in_vmem(1)[0],
        compiler_params=PARAMS,
        name="own_factors",
    )(pinned(wide, pltpu.VMEM), earlier)


class Steps:
    def __init__(self, wide, planes, waves, factors):
        self.wide, self.planes, self.waves, self.factors = wide, planes, waves, factors
        self.count, _, rows, self.depth = wide.shape
        self.tiles = rows // SUBLANES
        self.cells_x = wide.shape[1] - 2 * RIM - 2
        lane = lax.broadcasted_iota(jnp.int32, (SUBLANES, self.depth), 1)
        self.not_last, self.not_first = lane < self.depth - 1, lane > 0
        self.at_depth = lane == REC_DEPTH

    def wide_tiles(self, number, x):
        return [
            self.wide[number, x, pl.ds(tile, SUBLANES, stride=self.tiles), :]
            for tile in range(self.tiles)
        ]

    def wave_tiles(self, number, slot, x):
        if slot < 2:
            return self.wide_tiles(2 * number + slot, x)
        return [self.waves[slot - 2][number, x, tile] for tile in range(self.tiles)]

    def next_y(self, value):
        return value[1:] + [pltpu.roll(value[0], SUBLANES - 1, 0)]

    def previous_y(self, value):
        return [pltpu.roll(value[-1], 1, 0)] + value[:-1]

    def make_factors(self, x):
        raw = [self.wide_tiles(FIELDS + number, x) for number in range(self.count - FIELDS)]
        for tile in range(self.tiles):
            for number, value in enumerate(factors_of(*[value[tile] for value in raw])):
                self.factors[number, x, tile] = value

    def sides_z(self, value):
        above = [jnp.where(self.not_last, pltpu.roll(u, self.depth - 1, 1), 0.0) for u in value]
        below = [jnp.where(self.not_first, pltpu.roll(u, 1, 1), 0.0) for u in value]
        return above, below

    def stencil(self, factors, before, now, after, full):
        slope_x = [a - b for a, b in zip(after, before)]
        above, below = self.sides_z(now)
        slope_z = [a - b for a, b in zip(above, below)]
        next_now, previous_now = self.next_y(now), self.previous_y(now)
        above_x, below_x = self.sides_z(slope_x)
        next_x, previous_x = self.next_y(slope_x), self.previous_y(slope_x)
        next_z, previous_z = self.next_y(slope_z), self.previous_y(slope_z)
        axis, laplace = [], []
        for tile in range(self.tiles):
            axx, ayy, azz, axy, axz, ayz = [value[tile] for value in factors]
            double = now[tile] + now[tile]
            sum_x = after[tile] + before[tile]
            sum_y = next_now[tile] + previous_now[tile]
            sum_z = above[tile] + below[tile]
            straight = ((axx * sum_x + ayy * sum_y) + azz * sum_z) - double
            mixed = (
                axy * (next_x[tile] - previous_x[tile]) + axz * (above_x[tile] - below_x[tile])
            ) + ayz * (next_z[tile] - previous_z[tile])
            axis.append(straight + mixed)
            if full:
                laplace.append(((sum_x + sum_y) + sum_z) - 3.0 * double)
        return axis, laplace

    def step(self, turn, x, count):
        tiles, factors = range(self.tiles), self.factors
        for pair in range(2):
            p_number, q_number = 2 * pair, 2 * pair + 1
            p = [self.wave_tiles(p_number, turn + 1, x - 1 + i) for i in range(count + 2)]
            q = [self.wave_tiles(q_number, turn + 1, x - 1 + i) for i in range(count + 2)]
            for i in range(count):
                now = x + i
                mixing = [[factors[number, now, tile] for tile in tiles] for number in range(3, 9)]
                p_axis, p_laplace = self.stencil(mixing, p[i], p[i + 1], p[i + 2], True)
                q_axis, _ = self.stencil(mixing, q[i], q[i + 1], q[i + 2], False)
                p_held = self.wave_tiles(p_number, turn, now)
                q_held = self.wave_tiles(q_number, turn, now)
                for tile in tiles:
                    velocity, with_e, with_d = [factors[number, now, tile] for number in range(3)]
                    across = p_laplace[tile] - p_axis[tile]
                    p_now, q_now = p[i + 1][tile], q[i + 1][tile]
                    p_next = ((p_now + p_now) - p_held[tile]) + (
                        with_e * across + with_d * q_axis[tile]
                    )
                    q_next = ((q_now + q_now) - q_held[tile]) + (
                        with_d * across + velocity * q_axis[tile]
                    )
                    if pair == 1:
                        shift = lax.rem(REC_DEPTH - now + self.depth, self.depth)
                        moved = pltpu.roll(self.planes[STEPS - 1 - turn, tile], shift, 1)
                        p_next = p_next + jnp.where(self.at_depth, moved, 0.0)
                    self.waves[turn][p_number, now, tile] = p_next
                    self.waves[turn][q_number, now, tile] = q_next


def repeat(count, body):
    def run(i, carry):
        body(i)
        return carry

    lax.fori_loop(0, count, run, 0)


def inner_kernel(wide, planes, own, *refs):
    steps = Steps(wide, planes, refs[:STEPS], refs[STEPS])
    natural = refs[STEPS + 1]
    cells_x, cells_y, tiles = steps.cells_x, own.shape[2], steps.tiles

    def rim_rows(i):
        for x in [4 * i + k for k in range(4)]:
            raw = [wide[FIELDS + number, RIM + x, cells_y:, :] for number in range(5)]
            for number, value in enumerate(factors_of(*raw)):
                natural[number, x, cells_y:, :] = value
                natural[number, x, :cells_y, :] = own[number, x]

    def in_step_order(i):
        for x in [2 * i + k for k in range(2)]:
            for number in range(FACTORS):
                for tile in range(tiles):
                    steps.factors[number, RIM + x, tile] = natural[
                        number, x, pl.ds(tile, SUBLANES, stride=tiles), :
                    ]

    repeat(cells_x // 4, rim_rows)
    repeat(cells_x // 2, in_step_order)
    for turn in range(STEPS):
        first, last = RIM + 1 + turn, RIM + cells_x - 1 - turn
        half = (last - first) // 2
        repeat(2, lambda i, turn=turn, first=first, half=half: steps.step(turn, first + half * i, half))


def outer_kernel(*refs):
    x_a, x_b, c_a, c_b, planes = refs[1:6]
    refs = refs[6 + STEPS + 1 :]
    wide, waves, factors = refs[0], refs[1 : 1 + STEPS], refs[1 + STEPS]
    image, p_last, q_last = refs[-3:]
    cells_x, cells_y, depth = image.shape
    odd_x = is_odd("gx")
    for number, width, place in x_parts()[0]:
        low, high = RIM - width, RIM + cells_x
        for begin, side, corner in (
            (jnp.where(odd_x, low, high), x_a, c_a),
            (jnp.where(odd_x, high, low), x_b, c_b),
        ):
            wide[number, pl.ds(begin, width), :cells_y, :] = side[place : place + width]
            wide[number, pl.ds(begin, width), cells_y:, :] = corner[place : place + width]

    steps = Steps(wide, planes, waves, factors)

    for x in range(SLIM):
        steps.make_factors(RIM - SLIM + x)
        steps.make_factors(RIM + cells_x + x)
    for turn in range(STEPS):
        steps.step(turn, turn + 1, RIM)
        steps.step(turn, RIM + cells_x - 1 - turn, RIM)

    tiles = steps.tiles

    def finish(i):
        x = RIM + i
        total = None
        for back in range(STEPS + 1):
            source = steps.wave_tiles(0, 1 + STEPS - back, x)
            receiver = steps.wave_tiles(2, 1 + back, x)
            product = [a * b for a, b in zip(source, receiver)]
            total = product if total is None else [a + b for a, b in zip(total, product)]
        for out, value in (
            (0, total),
            (1, steps.wave_tiles(2, 1 + STEPS, x)),
            (2, steps.wave_tiles(3, 1 + STEPS, x)),
        ):
            for tile in range(tiles):
                wide[out, x, pl.ds(tile, SUBLANES, stride=tiles), :] = value[tile]

    repeat(cells_x, finish)
    for out, ref in enumerate((image, p_last, q_last)):
        ref[...] = wide[out, RIM : RIM + cells_x, :cells_y, :]


def inner(wide, planes, own):
    _, planes_x, rows, depth = wide.shape
    tile = (planes_x, rows // SUBLANES, SUBLANES, depth)
    return pl.pallas_call(
        inner_kernel,
        out_shape=[vmem_out(4, *tile)] * STEPS + [vmem_out(FACTORS, *tile)],
        in_specs=in_vmem(3),
        out_specs=in_vmem(STEPS + 1),
        scratch_shapes=[pltpu.VMEM((FACTORS, own.shape[1], rows, depth), jnp.float32)],
        compiler_params=PARAMS,
        name="inner_steps",
    )(pinned(wide, pltpu.VMEM), planes, pinned(own, pltpu.VMEM))


def outer(wide, rims, planes, state, cells_x, cells_y):
    out = jax.ShapeDtypeStruct((cells_x, cells_y, wide.shape[-1]), jnp.float32)
    kept = [vmem_out(*wide.shape)] + [vmem_out(*value.shape) for value in state]
    first = len(rims) + 2
    aliases = {0: 0} | {first + number: 1 + number for number in range(len(state))}
    return pl.pallas_call(
        outer_kernel,
        out_shape=kept + [out] * 3,
        in_specs=in_vmem(first + len(state)),
        out_specs=in_vmem(len(kept) + 3),
        input_output_aliases=aliases,
        compiler_params=PARAMS,
        name="outer_steps",
    )(
        pinned(wide, pltpu.VMEM),
        *rims,
        planes,
        *(pinned(value, pltpu.VMEM) for value in state),
    )[-3:]


def bits_of(axis):
    size = lax.axis_size(axis)
    return [1 << bit for bit in range(size.bit_length() - 1)] if size & (size - 1) == 0 else None


def doubled(windows, axis, bit):
    pairs = [(i, i ^ bit) for i in range(lax.axis_size(axis))]
    return jnp.concatenate([windows, lax.ppermute(windows, axis, pairs)], axis=0)


def inject_kernel(samples, cells_x, cells_y, gathered, table_x, table_y, planes, weights, picks):
    size_y = lax.axis_size("gy")
    own_x, own_y = lax.axis_index("gx"), lax.axis_index("gy")
    rows = cells_y + 2 * RIM
    tiles = rows // SUBLANES
    wide_x = picks.shape[0]
    in_row = LANES // samples
    place = lax.broadcasted_iota(jnp.int32, (rows, LANES), 0)
    row = tiles * lax.rem(place, SUBLANES) + lax.div(place, SUBLANES)
    y_global = own_y * cells_y + jnp.where(row < cells_y + RIM, row, row - rows)
    x_global = own_x * cells_x - RIM + lax.broadcasted_iota(jnp.int32, (wide_x, LANES), 0)
    lane = lax.broadcasted_iota(jnp.int32, (1, LANES), 1)
    bits_x, bits_y = bits_of("gx"), bits_of("gy")

    def source(place):
        device_x, device_y = own_x, own_y
        for number, bit in enumerate(bits_x):
            if place >> number & 1:
                device_x = jnp.bitwise_xor(device_x, bit)
        for number, bit in enumerate(bits_y):
            if place >> (len(bits_x) + number) & 1:
                device_y = jnp.bitwise_xor(device_y, bit)
        return device_x * size_y + device_y

    for group in range(gathered.shape[0] // in_row):
        at_x = at_y = jnp.zeros((1, LANES), jnp.int32)
        window = jnp.zeros((STEPS, LANES), jnp.float32)
        for part in range(in_row):
            place = group * in_row + part
            device = source(place)
            here = (lane >= part * samples) & (lane < (part + 1) * samples)
            shift = lax.rem((part - lax.rem(device, in_row)) * samples + LANES, LANES)
            table_row = pl.ds(lax.div(device, in_row), 1)
            at_x = jnp.where(here, pltpu.roll(table_x[table_row, :], shift, 1), at_x)
            at_y = jnp.where(here, pltpu.roll(table_y[table_row, :], shift, 1), at_y)
            moved = gathered[place]
            if part:
                moved = pltpu.roll(moved, part * samples, 1)
            window = jnp.where(here, moved, window)
        span = slice(group * LANES, (group + 1) * LANES)
        picks[:, span] = (at_x == x_global).astype(jnp.float32)
        is_y = at_y == y_global
        for sample in range(STEPS):
            weights[sample * rows : (sample + 1) * rows, span] = jnp.where(
                is_y, window[sample : sample + 1], 0.0
            )
    rest = weights[...]
    pick = picks[...].astype(jnp.bfloat16)
    total = None
    for _ in range(3):
        part = rest.astype(jnp.bfloat16)
        rest = rest - part.astype(jnp.float32)
        product = lax.dot_general(
            part, pick, (((1,), (1,)), ((), ())), preferred_element_type=jnp.float32
        )
        total = product if total is None else total + product
    planes[...] = jnp.zeros_like(planes)
    for sample in range(STEPS):
        for tile in range(tiles):
            begin = sample * rows + tile * SUBLANES
            planes[sample, tile, :, :wide_x] = total[begin : begin + SUBLANES]


def injected(gathered, receiver_x, receiver_y, samples, cells_x, cells_y, depth):
    rows = cells_y + 2 * RIM
    receivers = receiver_x.shape[0]
    wide_x = -(-(cells_x + 2 * RIM) // 32) * 32
    return pl.pallas_call(
        functools.partial(inject_kernel, samples, cells_x, cells_y),
        out_shape=vmem_out(STEPS, rows // SUBLANES, SUBLANES, depth),
        in_specs=in_vmem(3),
        out_specs=in_vmem(1)[0],
        scratch_shapes=[
            pltpu.VMEM((STEPS * rows, receivers), jnp.float32),
            pltpu.VMEM((wide_x, receivers), jnp.float32),
        ],
        compiler_params=PARAMS,
        name="inject",
    )(gathered, receiver_x.reshape(-1, LANES), receiver_y.reshape(-1, LANES))


def per_device(
    src_p_prev,
    src_p_now,
    src_q_prev,
    src_q_now,
    rec_p_next,
    rec_p_now,
    rec_q_next,
    rec_q_now,
    velocity_term,
    epsilon,
    delta,
    tilt,
    azimuth,
    traces,
    receiver_x,
    receiver_y,
    segment_start,
):
    blocks = (
        src_p_prev,
        src_p_now,
        src_q_prev,
        src_q_now,
        rec_p_next,
        rec_p_now,
        rec_q_next,
        rec_q_now,
        velocity_term,
        epsilon,
        delta,
        tilt,
        azimuth,
    )
    cells_x, cells_y, depth = src_p_now.shape
    wide, y_a, y_b, window = pack(blocks, traces, segment_start)
    y_a, y_b = swap(y_a, "gy", 0), swap(y_b, "gy", 1)
    wide, x_a, x_b = pack_x(wide, window)
    x_a, x_b = swap(x_a, "gx", 0), swap(x_b, "gx", 1)
    windows = jnp.concatenate([window, x_a[x_parts()[1] :, :STEPS, :]], axis=0)
    for bit in bits_of("gx")[1:]:
        windows = doubled(windows, "gx", bit)
    own = own_factors(wide, windows)
    for bit in bits_of("gy")[:-1]:
        windows = doubled(windows, "gy", bit)
    wide, c_a, c_b = corners(wide, y_a, y_b, windows, pinned(own, pltpu.VMEM))
    for bit in bits_of("gy")[-1:]:
        windows = doubled(windows, "gy", bit)
    c_a, c_b = swap(c_a, "gx", 0), swap(c_b, "gx", 1)
    planes = injected(
        windows, receiver_x, receiver_y, traces.shape[1], cells_x, cells_y, depth
    )
    state = inner(wide, planes, own)
    return tuple(outer(wide, (x_a, x_b, c_a, c_b), planes, state, cells_x, cells_y))


def solution(mesh):
    state = P(("shot", "gx"), "gy", None)
    earth = P("gx", "gy", None)
    return jax.shard_map(
        per_device,
        mesh=mesh,
        in_specs=(state,) * FIELDS + (earth,) * 5 + (P("shot", ("gx", "gy")), P(), P(), P()),
        out_specs=(state,) * 3,
        check_vma=False,
    )
```

```python
import functools

import jax
import jax.numpy as jnp
from jax import lax
from jax.experimental import pallas as pl
from jax.experimental.pallas import tpu as pltpu
from jax.sharding import PartitionSpec as P

STEPS = 4
REC_DEPTH = 4
RIM = STEPS
FIELDS = 8
SUBLANES = 8
LANES = 128
PARAMS = pltpu.CompilerParams(vmem_limit_bytes=16 * 1024 * 1024)
PACK_PARAMS = pltpu.CompilerParams(vmem_limit_bytes=48 * 1024 * 1024)


def in_vmem(count):
    return [pl.BlockSpec(memory_space=pltpu.VMEM)] * count


def is_odd(axis):
    return lax.rem(lax.axis_index(axis), 2) == 1


def swap(value, axis, first):
    size = lax.axis_size(axis)
    lower = range(first, size - 1, 2)
    pairs = [(i, i + 1) for i in lower] + [(i + 1, i) for i in lower]
    return lax.ppermute(value, axis, pairs)


NOW = (1, 3, 5, 7)
REST = (0, 2, 4, 6, 8, 9, 10, 11, 12)
SLIM = RIM - 1


def y_slots():
    slots = [((number, 0, RIM, 0),) for number in NOW]
    whole = len(REST) - len(REST) // RIM
    for place in range(whole):
        parts = [(REST[place], 0, SLIM, 0)]
        guest = whole + place // SLIM
        if guest < len(REST):
            parts.append((REST[guest], place % SLIM, 1, SLIM))
        slots.append(tuple(parts))
    return slots


def each_y_part(slots, high):
    for slot, parts in enumerate(slots):
        for number, row, rows, place in parts:
            if not high:
                yield slot, number, row, place, rows
            else:
                width = RIM if number in NOW else SLIM
                yield slot, number, RIM - width + row, 0 if place else RIM - rows, rows


def x_parts():
    parts, place = [], 0
    for number in NOW:
        parts.append((number, RIM, place))
        place += RIM
    for number in REST:
        parts.append((number, SLIM, place))
        place += SLIM
    return parts, place


def pinned(value, space):
    return pltpu.with_memory_space_constraint(value, space)


def vmem_out(*shape):
    return pltpu.VMEM(shape, jnp.float32)


def swap_far(value, axis):
    size = lax.axis_size(axis)
    pairs = [(i, i + 2) for i in range(0, size - 2, 2)] + [(i, i - 2) for i in range(3, size, 2)]
    return lax.ppermute(swap(value, axis, 0), axis, pairs)


def pack_kernel(count, *refs):
    blocks, traces, start = refs[:count], refs[count], refs[count + 1]
    wide, y_a, y_b, window, held, sems = refs[count + 2 :]
    cells_x, cells_y = blocks[0].shape[:2]
    core_x = pl.ds(RIM, cells_x)
    moves = [
        pltpu.make_async_copy(block, wide.at[number, core_x, pl.ds(0, cells_y)], sems.at[number])
        for number, block in enumerate(blocks)
    ]
    moves.append(pltpu.make_async_copy(traces, held, sems.at[count]))
    for move in moves:
        move.start()
    odd_y = is_odd("gy")
    begin = start[0]
    samples = traces.shape[1]
    window[...] = jnp.zeros_like(window)
    for move in moves:
        move.wait()
    for sample in range(STEPS):
        window[0, sample : sample + 1, :samples] = held[pl.ds(begin + sample, 1), :]

    def put_y(low, high):
        for out, is_high, base in ((low, False, 0), (high, True, cells_y - RIM)):
            for slot, number, row, place, length in each_y_part(y_slots(), is_high):
                out[slot, :, place : place + length, :] = wide[
                    number, RIM : RIM + cells_x, base + row : base + row + length, :
                ]

    @pl.when(odd_y)
    def _():
        put_y(y_a, y_b)

    @pl.when(jnp.logical_not(odd_y))
    def _():
        put_y(y_b, y_a)


def pack(blocks, traces, segment_start):
    cells_x, cells_y, depth = blocks[0].shape
    count = len(blocks)
    rim_y = vmem_out(len(y_slots()), cells_x, RIM, depth)
    wide = vmem_out(count, cells_x + 2 * RIM + 2, cells_y + 2 * RIM, depth)
    return pl.pallas_call(
        functools.partial(pack_kernel, count),
        out_shape=[wide, rim_y, rim_y, vmem_out(1, STEPS, LANES)],
        in_specs=[pl.BlockSpec(memory_space=pltpu.HBM)] * (count + 1)
        + [pl.BlockSpec(memory_space=pltpu.SMEM)],
        out_specs=in_vmem(4),
        scratch_shapes=[
            pltpu.VMEM(traces.shape, jnp.float32),
            pltpu.SemaphoreType.DMA((count + 1,)),
        ],
        compiler_params=PACK_PARAMS,
        name="pack_y_rims",
    )(*(pinned(value, pltpu.HBM) for value in (*blocks, traces)), segment_start)


def pack_x_kernel(_, window, wide, x_a, x_b):
    cells_x, cells_y = wide.shape[1] - 2 * RIM - 2, wide.shape[2] - 2 * RIM
    odd_x = is_odd("gx")
    parts, total = x_parts()
    for number, width, place in parts:
        first, last = RIM, RIM + cells_x - width
        for out, begin in ((x_a, jnp.where(odd_x, first, last)), (x_b, jnp.where(odd_x, last, first))):
            out[place : place + width] = wide[number, pl.ds(begin, width), :cells_y, :]
    x_a[total] = jnp.zeros_like(x_a[total])
    x_a[total, :STEPS, :] = window[0]


def pack_x(wide, window):
    _, _, rows, depth = wide.shape
    total = x_parts()[1]
    return pl.pallas_call(
        pack_x_kernel,
        out_shape=[
            vmem_out(*wide.shape),
            vmem_out(total + 1, rows - 2 * RIM, depth),
            vmem_out(total, rows - 2 * RIM, depth),
        ],
        in_specs=in_vmem(2),
        out_specs=in_vmem(3),
        input_output_aliases={0: 0},
        compiler_params=PARAMS,
        name="pack_x_rims",
    )(pinned(wide, pltpu.VMEM), window)


def corner_kernel(_, y_a, y_b, __, ___, wide, c_a, c_b):
    cells_x = y_a.shape[1]
    cells_y = wide.shape[2] - 2 * RIM
    odd_x, odd_y = is_odd("gx"), is_odd("gy")

    def place_y(low, high):
        for rim, is_high, base in ((high, False, cells_y), (low, True, cells_y + RIM)):
            for slot, number, row, place, length in each_y_part(y_slots(), is_high):
                wide[number, RIM : RIM + cells_x, base + row : base + row + length, :] = rim[
                    slot, :, place : place + length, :
                ]

    @pl.when(odd_y)
    def _():
        place_y(y_a, y_b)

    @pl.when(jnp.logical_not(odd_y))
    def _():
        place_y(y_b, y_a)

    for number, width, place in x_parts()[0]:
        first, last = RIM, RIM + cells_x - width
        for out, begin in ((c_a, jnp.where(odd_x, first, last)), (c_b, jnp.where(odd_x, last, first))):
            out[place : place + width] = wide[number, pl.ds(begin, width), cells_y:, :]


def corners(wide, y_a, y_b, *earlier):
    corner = vmem_out(x_parts()[1], 2 * RIM, wide.shape[-1])
    return pl.pallas_call(
        corner_kernel,
        out_shape=[vmem_out(*wide.shape), corner, corner],
        in_specs=in_vmem(5),
        out_specs=in_vmem(3),
        input_output_aliases={0: 0},
        compiler_params=PARAMS,
        name="pack_corners",
    )(pinned(wide, pltpu.VMEM), y_a, y_b, *earlier)


def sine_cosine(angle):
    square = angle * angle
    sine = 1.0 / 6227020800.0
    for term in (-1.0 / 39916800.0, 1.0 / 362880.0, -1.0 / 5040.0, 1.0 / 120.0, -1.0 / 6.0, 1.0):
        sine = sine * square + term
    cosine = 1.0 / 479001600.0
    for term in (-1.0 / 3628800.0, 1.0 / 40320.0, -1.0 / 720.0, 1.0 / 24.0, -0.5, 1.0):
        cosine = cosine * square + term
    return sine * angle, cosine


def factors_of(velocity, epsilon, delta, tilt, azimuth):
    f_e = 1.0 + 2.0 * epsilon
    f_d = jnp.sqrt(1.0 + 2.0 * delta)
    sin_tilt, cos_tilt = sine_cosine(tilt)
    sin_half, cos_half = sine_cosine(0.5 * azimuth)
    sin_azim = 2.0 * sin_half * cos_half
    cos_azim = 1.0 - 2.0 * sin_half * sin_half
    sin_square = sin_tilt * sin_tilt
    half_tilt = 0.5 * sin_tilt * cos_tilt
    along_x = sin_square * cos_azim
    return (
        velocity,
        velocity * f_e,
        velocity * f_d,
        along_x * cos_azim,
        sin_square * sin_azim * sin_azim,
        cos_tilt * cos_tilt,
        0.5 * along_x * sin_azim,
        half_tilt * cos_azim,
        half_tilt * sin_azim,
    )


FACTORS = 9


def own_kernel(wide, _, own):
    _, cells_x, cells_y, _ = own.shape

    def body(i):
        for x in [4 * i + k for k in range(4)]:
            raw = [wide[FIELDS + number, RIM + x, :cells_y, :] for number in range(5)]
            for number, value in enumerate(factors_of(*raw)):
                own[number, x] = value

    repeat(cells_x // 4, body)


def own_factors(wide, earlier):
    _, planes_x, rows, depth = wide.shape
    cells_x, cells_y = planes_x - 2 * RIM - 2, rows - 2 * RIM
    return pl.pallas_call(
        own_kernel,
        out_shape=vmem_out(FACTORS, cells_x, cells_y, depth),
        in_specs=in_vmem(2),
        out_specs=in_vmem(1)[0],
        compiler_params=PARAMS,
        name="own_factors",
    )(pinned(wide, pltpu.VMEM), earlier)


class Steps:
    def __init__(self, wide, planes, waves, factors):
        self.wide, self.planes, self.waves, self.factors = wide, planes, waves, factors
        self.count, _, rows, self.depth = wide.shape
        self.tiles = rows // SUBLANES
        self.cells_x = wide.shape[1] - 2 * RIM - 2
        lane = lax.broadcasted_iota(jnp.int32, (SUBLANES, self.depth), 1)
        self.not_last, self.not_first = lane < self.depth - 1, lane > 0
        self.at_depth = lane == REC_DEPTH

    def wide_tiles(self, number, x):
        return [
            self.wide[number, x, pl.ds(tile, SUBLANES, stride=self.tiles), :]
            for tile in range(self.tiles)
        ]

    def wave_tiles(self, number, slot, x):
        if slot < 2:
            return self.wide_tiles(2 * number + slot, x)
        return [self.waves[slot - 2][number, x, tile] for tile in range(self.tiles)]

    def next_y(self, value):
        return value[1:] + [pltpu.roll(value[0], SUBLANES - 1, 0)]

    def previous_y(self, value):
        return [pltpu.roll(value[-1], 1, 0)] + value[:-1]

    def make_factors(self, x):
        raw = [self.wide_tiles(FIELDS + number, x) for number in range(self.count - FIELDS)]
        for tile in range(self.tiles):
            for number, value in enumerate(factors_of(*[value[tile] for value in raw])):
                self.factors[number, x, tile] = value

    def sides_z(self, value):
        above = [jnp.where(self.not_last, pltpu.roll(u, self.depth - 1, 1), 0.0) for u in value]
        below = [jnp.where(self.not_first, pltpu.roll(u, 1, 1), 0.0) for u in value]
        return above, below

    def stencil(self, factors, before, now, after, full):
        slope_x = [a - b for a, b in zip(after, before)]
        above, below = self.sides_z(now)
        slope_z = [a - b for a, b in zip(above, below)]
        next_now, previous_now = self.next_y(now), self.previous_y(now)
        above_x, below_x = self.sides_z(slope_x)
        next_x, previous_x = self.next_y(slope_x), self.previous_y(slope_x)
        next_z, previous_z = self.next_y(slope_z), self.previous_y(slope_z)
        axis, laplace = [], []
        for tile in range(self.tiles):
            axx, ayy, azz, axy, axz, ayz = [value[tile] for value in factors]
            double = now[tile] + now[tile]
            sum_x = after[tile] + before[tile]
            sum_y = next_now[tile] + previous_now[tile]
            sum_z = above[tile] + below[tile]
            straight = ((axx * sum_x + ayy * sum_y) + azz * sum_z) - double
            mixed = (
                axy * (next_x[tile] - previous_x[tile]) + axz * (above_x[tile] - below_x[tile])
            ) + ayz * (next_z[tile] - previous_z[tile])
            axis.append(straight + mixed)
            if full:
                laplace.append(((sum_x + sum_y) + sum_z) - 3.0 * double)
        return axis, laplace

    def step(self, turn, x, count):
        tiles, factors = range(self.tiles), self.factors
        for pair in range(2):
            p_number, q_number = 2 * pair, 2 * pair + 1
            p = [self.wave_tiles(p_number, turn + 1, x - 1 + i) for i in range(count + 2)]
            q = [self.wave_tiles(q_number, turn + 1, x - 1 + i) for i in range(count + 2)]
            for i in range(count):
                now = x + i
                mixing = [[factors[number, now, tile] for tile in tiles] for number in range(3, 9)]
                p_axis, p_laplace = self.stencil(mixing, p[i], p[i + 1], p[i + 2], True)
                q_axis, _ = self.stencil(mixing, q[i], q[i + 1], q[i + 2], False)
                p_held = self.wave_tiles(p_number, turn, now)
                q_held = self.wave_tiles(q_number, turn, now)
                for tile in tiles:
                    velocity, with_e, with_d = [factors[number, now, tile] for number in range(3)]
                    across = p_laplace[tile] - p_axis[tile]
                    p_now, q_now = p[i + 1][tile], q[i + 1][tile]
                    p_next = ((p_now + p_now) - p_held[tile]) + (
                        with_e * across + with_d * q_axis[tile]
                    )
                    q_next = ((q_now + q_now) - q_held[tile]) + (
                        with_d * across + velocity * q_axis[tile]
                    )
                    if pair == 1:
                        shift = lax.rem(REC_DEPTH - now + self.depth, self.depth)
                        moved = pltpu.roll(self.planes[STEPS - 1 - turn, tile], shift, 1)
                        p_next = p_next + jnp.where(self.at_depth, moved, 0.0)
                    self.waves[turn][p_number, now, tile] = p_next
                    self.waves[turn][q_number, now, tile] = q_next


def repeat(count, body):
    def run(i, carry):
        body(i)
        return carry

    lax.fori_loop(0, count, run, 0)


def inner_kernel(wide, planes, own, *refs):
    steps = Steps(wide, planes, refs[:STEPS], refs[STEPS])
    natural = refs[STEPS + 1]
    cells_x, cells_y, tiles = steps.cells_x, own.shape[2], steps.tiles

    def rim_rows(i):
        for x in [4 * i + k for k in range(4)]:
            raw = [wide[FIELDS + number, RIM + x, cells_y:, :] for number in range(5)]
            for number, value in enumerate(factors_of(*raw)):
                natural[number, x, cells_y:, :] = value
                natural[number, x, :cells_y, :] = own[number, x]

    def in_step_order(i):
        for x in [2 * i + k for k in range(2)]:
            for number in range(FACTORS):
                for tile in range(tiles):
                    steps.factors[number, RIM + x, tile] = natural[
                        number, x, pl.ds(tile, SUBLANES, stride=tiles), :
                    ]

    repeat(cells_x // 4, rim_rows)
    repeat(cells_x // 2, in_step_order)
    for turn in range(STEPS):
        first, last = RIM + 1 + turn, RIM + cells_x - 1 - turn
        half = (last - first) // 2
        repeat(2, lambda i, turn=turn, first=first, half=half: steps.step(turn, first + half * i, half))


def outer_kernel(*refs):
    x_a, x_b, c_a, c_b, planes = refs[1:6]
    refs = refs[6 + STEPS + 1 :]
    wide, waves, factors = refs[0], refs[1 : 1 + STEPS], refs[1 + STEPS]
    image, p_last, q_last = refs[-3:]
    cells_x, cells_y, depth = image.shape
    odd_x = is_odd("gx")
    for number, width, place in x_parts()[0]:
        low, high = RIM - width, RIM + cells_x
        for begin, side, corner in (
            (jnp.where(odd_x, low, high), x_a, c_a),
            (jnp.where(odd_x, high, low), x_b, c_b),
        ):
            wide[number, pl.ds(begin, width), :cells_y, :] = side[place : place + width]
            wide[number, pl.ds(begin, width), cells_y:, :] = corner[place : place + width]

    steps = Steps(wide, planes, waves, factors)

    for x in range(SLIM):
        steps.make_factors(RIM - SLIM + x)
        steps.make_factors(RIM + cells_x + x)
    for turn in range(STEPS):
        steps.step(turn, turn + 1, RIM)
        steps.step(turn, RIM + cells_x - 1 - turn, RIM)

    tiles = steps.tiles

    def finish(i):
        x = RIM + i
        total = None
        for back in range(STEPS + 1):
            source = steps.wave_tiles(0, 1 + STEPS - back, x)
            receiver = steps.wave_tiles(2, 1 + back, x)
            product = [a * b for a, b in zip(source, receiver)]
            total = product if total is None else [a + b for a, b in zip(total, product)]
        for out, value in (
            (0, total),
            (1, steps.wave_tiles(2, 1 + STEPS, x)),
            (2, steps.wave_tiles(3, 1 + STEPS, x)),
        ):
            for tile in range(tiles):
                wide[out, x, pl.ds(tile, SUBLANES, stride=tiles), :] = value[tile]

    repeat(cells_x, finish)
    for out, ref in enumerate((image, p_last, q_last)):
        ref[...] = wide[out, RIM : RIM + cells_x, :cells_y, :]


def inner(wide, planes, own):
    _, planes_x, rows, depth = wide.shape
    tile = (planes_x, rows // SUBLANES, SUBLANES, depth)
    return pl.pallas_call(
        inner_kernel,
        out_shape=[vmem_out(4, *tile)] * STEPS + [vmem_out(FACTORS, *tile)],
        in_specs=in_vmem(3),
        out_specs=in_vmem(STEPS + 1),
        scratch_shapes=[pltpu.VMEM((FACTORS, own.shape[1], rows, depth), jnp.float32)],
        compiler_params=PARAMS,
        name="inner_steps",
    )(pinned(wide, pltpu.VMEM), planes, pinned(own, pltpu.VMEM))


def outer(wide, rims, planes, state, cells_x, cells_y):
    out = jax.ShapeDtypeStruct((cells_x, cells_y, wide.shape[-1]), jnp.float32)
    kept = [vmem_out(*wide.shape)] + [vmem_out(*value.shape) for value in state]
    first = len(rims) + 2
    aliases = {0: 0} | {first + number: 1 + number for number in range(len(state))}
    return pl.pallas_call(
        outer_kernel,
        out_shape=kept + [out] * 3,
        in_specs=in_vmem(first + len(state)),
        out_specs=in_vmem(len(kept) + 3),
        input_output_aliases=aliases,
        compiler_params=PARAMS,
        name="outer_steps",
    )(
        pinned(wide, pltpu.VMEM),
        *rims,
        planes,
        *(pinned(value, pltpu.VMEM) for value in state),
    )[-3:]


def bits_of(axis):
    size = lax.axis_size(axis)
    return [1 << bit for bit in range(size.bit_length() - 1)] if size & (size - 1) == 0 else None


def doubled(windows, axis, bit):
    pairs = [(i, i ^ bit) for i in range(lax.axis_size(axis))]
    return jnp.concatenate([windows, lax.ppermute(windows, axis, pairs)], axis=0)


def inject_kernel(samples, cells_x, cells_y, gathered, table_x, table_y, planes, weights, picks):
    size_y = lax.axis_size("gy")
    own_x, own_y = lax.axis_index("gx"), lax.axis_index("gy")
    rows = cells_y + 2 * RIM
    tiles = rows // SUBLANES
    wide_x = picks.shape[0]
    in_row = LANES // samples
    place = lax.broadcasted_iota(jnp.int32, (rows, LANES), 0)
    row = tiles * lax.rem(place, SUBLANES) + lax.div(place, SUBLANES)
    y_global = own_y * cells_y + jnp.where(row < cells_y + RIM, row, row - rows)
    x_global = own_x * cells_x - RIM + lax.broadcasted_iota(jnp.int32, (wide_x, LANES), 0)
    lane = lax.broadcasted_iota(jnp.int32, (1, LANES), 1)
    bits_x, bits_y = bits_of("gx"), bits_of("gy")

    def source(place):
        device_x, device_y = own_x, own_y
        for number, bit in enumerate(bits_x):
            if place >> number & 1:
                device_x = jnp.bitwise_xor(device_x, bit)
        for number, bit in enumerate(bits_y):
            if place >> (len(bits_x) + number) & 1:
                device_y = jnp.bitwise_xor(device_y, bit)
        return device_x * size_y + device_y

    for group in range(gathered.shape[0] // in_row):
        at_x = at_y = jnp.zeros((1, LANES), jnp.int32)
        window = jnp.zeros((STEPS, LANES), jnp.float32)
        for part in range(in_row):
            place = group * in_row + part
            device = source(place)
            here = (lane >= part * samples) & (lane < (part + 1) * samples)
            shift = lax.rem((part - lax.rem(device, in_row)) * samples + LANES, LANES)
            table_row = pl.ds(lax.div(device, in_row), 1)
            at_x = jnp.where(here, pltpu.roll(table_x[table_row, :], shift, 1), at_x)
            at_y = jnp.where(here, pltpu.roll(table_y[table_row, :], shift, 1), at_y)
            moved = gathered[place]
            if part:
                moved = pltpu.roll(moved, part * samples, 1)
            window = jnp.where(here, moved, window)
        span = slice(group * LANES, (group + 1) * LANES)
        picks[:, span] = (at_x == x_global).astype(jnp.float32)
        is_y = at_y == y_global
        for sample in range(STEPS):
            weights[sample * rows : (sample + 1) * rows, span] = jnp.where(
                is_y, window[sample : sample + 1], 0.0
            )
    rest = weights[...]
    pick = picks[...].astype(jnp.bfloat16)
    total = None
    for _ in range(3):
        part = rest.astype(jnp.bfloat16)
        rest = rest - part.astype(jnp.float32)
        product = lax.dot_general(
            part, pick, (((1,), (1,)), ((), ())), preferred_element_type=jnp.float32
        )
        total = product if total is None else total + product
    planes[...] = jnp.zeros_like(planes)
    for sample in range(STEPS):
        for tile in range(tiles):
            begin = sample * rows + tile * SUBLANES
            planes[sample, tile, :, :wide_x] = total[begin : begin + SUBLANES]


def injected(gathered, receiver_x, receiver_y, samples, cells_x, cells_y, depth):
    rows = cells_y + 2 * RIM
    receivers = receiver_x.shape[0]
    wide_x = -(-(cells_x + 2 * RIM) // 32) * 32
    return pl.pallas_call(
        functools.partial(inject_kernel, samples, cells_x, cells_y),
        out_shape=vmem_out(STEPS, rows // SUBLANES, SUBLANES, depth),
        in_specs=in_vmem(3),
        out_specs=in_vmem(1)[0],
        scratch_shapes=[
            pltpu.VMEM((STEPS * rows, receivers), jnp.float32),
            pltpu.VMEM((wide_x, receivers), jnp.float32),
        ],
        compiler_params=PARAMS,
        name="inject",
    )(gathered, receiver_x.reshape(-1, LANES), receiver_y.reshape(-1, LANES))


def per_device(
    src_p_prev,
    src_p_now,
    src_q_prev,
    src_q_now,
    rec_p_next,
    rec_p_now,
    rec_q_next,
    rec_q_now,
    velocity_term,
    epsilon,
    delta,
    tilt,
    azimuth,
    traces,
    receiver_x,
    receiver_y,
    segment_start,
):
    blocks = (
        src_p_prev,
        src_p_now,
        src_q_prev,
        src_q_now,
        rec_p_next,
        rec_p_now,
        rec_q_next,
        rec_q_now,
        velocity_term,
        epsilon,
        delta,
        tilt,
        azimuth,
    )
    cells_x, cells_y, depth = src_p_now.shape
    wide, y_a, y_b, window = pack(blocks, traces, segment_start)
    y_b = swap(y_b, "gy", 1)
    y_a = swap(y_a, "gy", 0)
    wide, x_a, x_b = pack_x(wide, window)
    x_a, x_b = swap(x_a, "gx", 0), swap_far(x_b, "gx")
    windows = jnp.concatenate([window, x_a[x_parts()[1] :, :STEPS, :]], axis=0)
    for bit in bits_of("gx")[1:]:
        windows = doubled(windows, "gx", bit)
    own = own_factors(wide, windows)
    for bit in bits_of("gy")[:-1]:
        windows = doubled(windows, "gy", bit)
    wide, c_a, c_b = corners(wide, y_a, y_b, windows, pinned(own, pltpu.VMEM))
    for bit in bits_of("gy")[-1:]:
        windows = doubled(windows, "gy", bit)
    c_a, c_b = swap(c_a, "gx", 0), swap_far(c_b, "gx")
    planes = injected(
        windows, receiver_x, receiver_y, traces.shape[1], cells_x, cells_y, depth
    )
    state = inner(wide, planes, own)
    return tuple(outer(wide, (x_a, x_b, c_a, c_b), planes, state, cells_x, cells_y))


def solution(mesh):
    state = P(("shot", "gx"), "gy", None)
    earth = P("gx", "gy", None)
    return jax.shard_map(
        per_device,
        mesh=mesh,
        in_specs=(state,) * FIELDS + (earth,) * 5 + (P("shot", ("gx", "gy")), P(), P(), P()),
        out_specs=(state,) * 3,
        check_vma=False,
    )
```

```python
import functools

import jax
import jax.numpy as jnp
from jax import lax
from jax.experimental import pallas as pl
from jax.experimental.pallas import tpu as pltpu
from jax.sharding import PartitionSpec as P

STEPS = 4
REC_DEPTH = 4
RIM = STEPS
FIELDS = 8
SUBLANES = 8
LANES = 128
PARAMS = pltpu.CompilerParams(vmem_limit_bytes=16 * 1024 * 1024)
PACK_PARAMS = pltpu.CompilerParams(vmem_limit_bytes=48 * 1024 * 1024)


def in_vmem(count):
    return [pl.BlockSpec(memory_space=pltpu.VMEM)] * count


def is_odd(axis):
    return lax.rem(lax.axis_index(axis), 2) == 1


def swap(value, axis, first):
    size = lax.axis_size(axis)
    lower = range(first, size - 1, 2)
    pairs = [(i, i + 1) for i in lower] + [(i + 1, i) for i in lower]
    return lax.ppermute(value, axis, pairs)


NOW = (1, 3, 5, 7)
REST = (0, 2, 4, 6, 8, 9, 10, 11, 12)
SLIM = RIM - 1


def y_slots():
    slots = [((number, 0, RIM, 0),) for number in NOW]
    whole = len(REST) - len(REST) // RIM
    for place in range(whole):
        parts = [(REST[place], 0, SLIM, 0)]
        guest = whole + place // SLIM
        if guest < len(REST):
            parts.append((REST[guest], place % SLIM, 1, SLIM))
        slots.append(tuple(parts))
    return slots


def each_y_part(slots, high):
    for slot, parts in enumerate(slots):
        for number, row, rows, place in parts:
            if not high:
                yield slot, number, row, place, rows
            else:
                width = RIM if number in NOW else SLIM
                yield slot, number, RIM - width + row, 0 if place else RIM - rows, rows


def x_parts():
    parts, place = [], 0
    for number in NOW:
        parts.append((number, RIM, place))
        place += RIM
    for number in REST:
        parts.append((number, SLIM, place))
        place += SLIM
    return parts, place


def pinned(value, space):
    return pltpu.with_memory_space_constraint(value, space)


def vmem_out(*shape):
    return pltpu.VMEM(shape, jnp.float32)


def swap_far(value, axis):
    size = lax.axis_size(axis)
    pairs = [(i, i + 2) for i in range(0, size - 2, 2)] + [(i, i - 2) for i in range(3, size, 2)]
    return lax.ppermute(swap(value, axis, 0), axis, pairs)


def pack_kernel(count, *refs):
    blocks, traces, start = refs[:count], refs[count], refs[count + 1]
    wide, y_a, y_b, window, held, sems = refs[count + 2 :]
    cells_x, cells_y = blocks[0].shape[:2]
    core_x = pl.ds(RIM, cells_x)
    moves = [
        pltpu.make_async_copy(block, wide.at[number, core_x, pl.ds(0, cells_y)], sems.at[number])
        for number, block in enumerate(blocks)
    ]
    moves.append(pltpu.make_async_copy(traces, held, sems.at[count]))
    for move in moves:
        move.start()
    odd_y = is_odd("gy")
    begin = start[0]
    samples = traces.shape[1]
    window[...] = jnp.zeros_like(window)
    for move in moves:
        move.wait()
    for sample in range(STEPS):
        window[0, sample : sample + 1, :samples] = held[pl.ds(begin + sample, 1), :]

    def put_y(low, high):
        for out, is_high, base in ((low, False, 0), (high, True, cells_y - RIM)):
            for slot, number, row, place, length in each_y_part(y_slots(), is_high):
                out[slot, :, place : place + length, :] = wide[
                    number, RIM : RIM + cells_x, base + row : base + row + length, :
                ]

    @pl.when(odd_y)
    def _():
        put_y(y_a, y_b)

    @pl.when(jnp.logical_not(odd_y))
    def _():
        put_y(y_b, y_a)


def pack(blocks, traces, segment_start):
    cells_x, cells_y, depth = blocks[0].shape
    count = len(blocks)
    rim_y = vmem_out(len(y_slots()), cells_x, RIM, depth)
    wide = vmem_out(count, cells_x + 2 * RIM + 2, cells_y + 2 * RIM, depth)
    return pl.pallas_call(
        functools.partial(pack_kernel, count),
        out_shape=[wide, rim_y, rim_y, vmem_out(1, STEPS, LANES)],
        in_specs=[pl.BlockSpec(memory_space=pltpu.HBM)] * (count + 1)
        + [pl.BlockSpec(memory_space=pltpu.SMEM)],
        out_specs=in_vmem(4),
        scratch_shapes=[
            pltpu.VMEM(traces.shape, jnp.float32),
            pltpu.SemaphoreType.DMA((count + 1,)),
        ],
        compiler_params=PACK_PARAMS,
        name="pack_y_rims",
    )(*(pinned(value, pltpu.HBM) for value in (*blocks, traces)), segment_start)


def pack_x_kernel(_, window, wide, x_a, x_b):
    cells_x, cells_y = wide.shape[1] - 2 * RIM - 2, wide.shape[2] - 2 * RIM
    odd_x = is_odd("gx")
    parts, total = x_parts()
    for number, width, place in parts:
        first, last = RIM, RIM + cells_x - width
        for out, begin in ((x_a, jnp.where(odd_x, first, last)), (x_b, jnp.where(odd_x, last, first))):
            out[place : place + width] = wide[number, pl.ds(begin, width), :cells_y, :]
    x_a[total] = jnp.zeros_like(x_a[total])
    x_a[total, :STEPS, :] = window[0]


def pack_x(wide, window):
    _, _, rows, depth = wide.shape
    total = x_parts()[1]
    return pl.pallas_call(
        pack_x_kernel,
        out_shape=[
            vmem_out(*wide.shape),
            vmem_out(total + 1, rows - 2 * RIM, depth),
            vmem_out(total, rows - 2 * RIM, depth),
        ],
        in_specs=in_vmem(2),
        out_specs=in_vmem(3),
        input_output_aliases={0: 0},
        compiler_params=PARAMS,
        name="pack_x_rims",
    )(pinned(wide, pltpu.VMEM), window)


def corner_kernel(_, y_a, y_b, __, ___, wide, c_a, c_b):
    cells_x = y_a.shape[1]
    cells_y = wide.shape[2] - 2 * RIM
    odd_x, odd_y = is_odd("gx"), is_odd("gy")

    def place_y(low, high):
        for rim, is_high, base in ((high, False, cells_y), (low, True, cells_y + RIM)):
            for slot, number, row, place, length in each_y_part(y_slots(), is_high):
                wide[number, RIM : RIM + cells_x, base + row : base + row + length, :] = rim[
                    slot, :, place : place + length, :
                ]

    @pl.when(odd_y)
    def _():
        place_y(y_a, y_b)

    @pl.when(jnp.logical_not(odd_y))
    def _():
        place_y(y_b, y_a)

    for number, width, place in x_parts()[0]:
        first, last = RIM, RIM + cells_x - width
        for out, begin in ((c_a, jnp.where(odd_x, first, last)), (c_b, jnp.where(odd_x, last, first))):
            out[place : place + width] = wide[number, pl.ds(begin, width), cells_y:, :]


def corners(wide, y_a, y_b, *earlier):
    corner = vmem_out(x_parts()[1], 2 * RIM, wide.shape[-1])
    return pl.pallas_call(
        corner_kernel,
        out_shape=[vmem_out(*wide.shape), corner, corner],
        in_specs=in_vmem(5),
        out_specs=in_vmem(3),
        input_output_aliases={0: 0},
        compiler_params=PARAMS,
        name="pack_corners",
    )(pinned(wide, pltpu.VMEM), y_a, y_b, *earlier)


def sine_cosine(angle):
    square = angle * angle
    sine = 1.0 / 6227020800.0
    for term in (-1.0 / 39916800.0, 1.0 / 362880.0, -1.0 / 5040.0, 1.0 / 120.0, -1.0 / 6.0, 1.0):
        sine = sine * square + term
    cosine = 1.0 / 479001600.0
    for term in (-1.0 / 3628800.0, 1.0 / 40320.0, -1.0 / 720.0, 1.0 / 24.0, -0.5, 1.0):
        cosine = cosine * square + term
    return sine * angle, cosine


def factors_of(velocity, epsilon, delta, tilt, azimuth):
    f_e = 1.0 + 2.0 * epsilon
    f_d = jnp.sqrt(1.0 + 2.0 * delta)
    sin_tilt, cos_tilt = sine_cosine(tilt)
    sin_half, cos_half = sine_cosine(0.5 * azimuth)
    sin_azim = 2.0 * sin_half * cos_half
    cos_azim = 1.0 - 2.0 * sin_half * sin_half
    sin_square = sin_tilt * sin_tilt
    half_tilt = 0.5 * sin_tilt * cos_tilt
    along_x = sin_square * cos_azim
    return (
        velocity,
        velocity * f_e,
        velocity * f_d,
        along_x * cos_azim,
        sin_square * sin_azim * sin_azim,
        cos_tilt * cos_tilt,
        0.5 * along_x * sin_azim,
        half_tilt * cos_azim,
        half_tilt * sin_azim,
    )


FACTORS = 9


def own_kernel(wide, _, own):
    _, cells_x, cells_y, _ = own.shape

    def body(i):
        for x in [4 * i + k for k in range(4)]:
            raw = [wide[FIELDS + number, RIM + x, :cells_y, :] for number in range(5)]
            for number, value in enumerate(factors_of(*raw)):
                own[number, x] = value

    repeat(cells_x // 4, body)


def own_factors(wide, earlier):
    _, planes_x, rows, depth = wide.shape
    cells_x, cells_y = planes_x - 2 * RIM - 2, rows - 2 * RIM
    return pl.pallas_call(
        own_kernel,
        out_shape=vmem_out(FACTORS, cells_x, cells_y, depth),
        in_specs=in_vmem(2),
        out_specs=in_vmem(1)[0],
        compiler_params=PARAMS,
        name="own_factors",
    )(pinned(wide, pltpu.VMEM), earlier)


class Steps:
    def __init__(self, wide, planes, waves, factors):
        self.wide, self.planes, self.waves, self.factors = wide, planes, waves, factors
        self.count, _, rows, self.depth = wide.shape
        self.tiles = rows // SUBLANES
        self.cells_x = wide.shape[1] - 2 * RIM - 2
        lane = lax.broadcasted_iota(jnp.int32, (SUBLANES, self.depth), 1)
        self.not_last, self.not_first = lane < self.depth - 1, lane > 0
        self.at_depth = lane == REC_DEPTH

    def wide_tiles(self, number, x):
        return [
            self.wide[number, x, pl.ds(tile, SUBLANES, stride=self.tiles), :]
            for tile in range(self.tiles)
        ]

    def wave_tiles(self, number, slot, x):
        if slot < 2:
            return self.wide_tiles(2 * number + slot, x)
        return [self.waves[slot - 2][number, x, tile] for tile in range(self.tiles)]

    def next_y(self, value):
        return value[1:] + [pltpu.roll(value[0], SUBLANES - 1, 0)]

    def previous_y(self, value):
        return [pltpu.roll(value[-1], 1, 0)] + value[:-1]

    def make_factors(self, x):
        raw = [self.wide_tiles(FIELDS + number, x) for number in range(self.count - FIELDS)]
        for tile in range(self.tiles):
            for number, value in enumerate(factors_of(*[value[tile] for value in raw])):
                self.factors[number, x, tile] = value

    def sides_z(self, value):
        above = [jnp.where(self.not_last, pltpu.roll(u, self.depth - 1, 1), 0.0) for u in value]
        below = [jnp.where(self.not_first, pltpu.roll(u, 1, 1), 0.0) for u in value]
        return above, below

    def stencil(self, factors, before, now, after, full):
        slope_x = [a - b for a, b in zip(after, before)]
        above, below = self.sides_z(now)
        slope_z = [a - b for a, b in zip(above, below)]
        next_now, previous_now = self.next_y(now), self.previous_y(now)
        above_x, below_x = self.sides_z(slope_x)
        next_x, previous_x = self.next_y(slope_x), self.previous_y(slope_x)
        next_z, previous_z = self.next_y(slope_z), self.previous_y(slope_z)
        axis, laplace = [], []
        for tile in range(self.tiles):
            axx, ayy, azz, axy, axz, ayz = [value[tile] for value in factors]
            double = now[tile] + now[tile]
            sum_x = after[tile] + before[tile]
            sum_y = next_now[tile] + previous_now[tile]
            sum_z = above[tile] + below[tile]
            straight = ((axx * sum_x + ayy * sum_y) + azz * sum_z) - double
            mixed = (
                axy * (next_x[tile] - previous_x[tile]) + axz * (above_x[tile] - below_x[tile])
            ) + ayz * (next_z[tile] - previous_z[tile])
            axis.append(straight + mixed)
            if full:
                laplace.append(((sum_x + sum_y) + sum_z) - 3.0 * double)
        return axis, laplace

    def step(self, turn, x, count):
        tiles, factors = range(self.tiles), self.factors
        for pair in range(2):
            p_number, q_number = 2 * pair, 2 * pair + 1
            p = [self.wave_tiles(p_number, turn + 1, x - 1 + i) for i in range(count + 2)]
            q = [self.wave_tiles(q_number, turn + 1, x - 1 + i) for i in range(count + 2)]
            for i in range(count):
                now = x + i
                mixing = [[factors[number, now, tile] for tile in tiles] for number in range(3, 9)]
                p_axis, p_laplace = self.stencil(mixing, p[i], p[i + 1], p[i + 2], True)
                q_axis, _ = self.stencil(mixing, q[i], q[i + 1], q[i + 2], False)
                p_held = self.wave_tiles(p_number, turn, now)
                q_held = self.wave_tiles(q_number, turn, now)
                for tile in tiles:
                    velocity, with_e, with_d = [factors[number, now, tile] for number in range(3)]
                    across = p_laplace[tile] - p_axis[tile]
                    p_now, q_now = p[i + 1][tile], q[i + 1][tile]
                    p_next = ((p_now + p_now) - p_held[tile]) + (
                        with_e * across + with_d * q_axis[tile]
                    )
                    q_next = ((q_now + q_now) - q_held[tile]) + (
                        with_d * across + velocity * q_axis[tile]
                    )
                    if pair == 1:
                        shift = lax.rem(REC_DEPTH - now + self.depth, self.depth)
                        moved = pltpu.roll(self.planes[STEPS - 1 - turn, tile], shift, 1)
                        p_next = p_next + jnp.where(self.at_depth, moved, 0.0)
                    self.waves[turn][p_number, now, tile] = p_next
                    self.waves[turn][q_number, now, tile] = q_next


def repeat(count, body):
    def run(i, carry):
        body(i)
        return carry

    lax.fori_loop(0, count, run, 0)


def inner_kernel(wide, planes, own, *refs):
    steps = Steps(wide, planes, refs[:STEPS], refs[STEPS])
    natural = refs[STEPS + 1]
    cells_x, cells_y, tiles = steps.cells_x, own.shape[2], steps.tiles

    def rim_rows(i):
        for x in [4 * i + k for k in range(4)]:
            raw = [wide[FIELDS + number, RIM + x, cells_y:, :] for number in range(5)]
            for number, value in enumerate(factors_of(*raw)):
                natural[number, x, cells_y:, :] = value
                natural[number, x, :cells_y, :] = own[number, x]

    def in_step_order(i):
        for x in [2 * i + k for k in range(2)]:
            for number in range(FACTORS):
                for tile in range(tiles):
                    steps.factors[number, RIM + x, tile] = natural[
                        number, x, pl.ds(tile, SUBLANES, stride=tiles), :
                    ]

    repeat(cells_x // 4, rim_rows)
    repeat(cells_x // 2, in_step_order)
    for turn in range(STEPS):
        first, last = RIM + 1 + turn, RIM + cells_x - 1 - turn
        half = (last - first) // 2
        repeat(2, lambda i, turn=turn, first=first, half=half: steps.step(turn, first + half * i, half))


def outer_kernel(*refs):
    x_a, x_b, c_a, c_b, planes = refs[1:6]
    refs = refs[6 + STEPS + 1 :]
    wide, waves, factors = refs[0], refs[1 : 1 + STEPS], refs[1 + STEPS]
    image, p_last, q_last = refs[-3:]
    cells_x, cells_y, depth = image.shape
    odd_x = is_odd("gx")
    for number, width, place in x_parts()[0]:
        low, high = RIM - width, RIM + cells_x
        for begin, side, corner in (
            (jnp.where(odd_x, low, high), x_a, c_a),
            (jnp.where(odd_x, high, low), x_b, c_b),
        ):
            wide[number, pl.ds(begin, width), :cells_y, :] = side[place : place + width]
            wide[number, pl.ds(begin, width), cells_y:, :] = corner[place : place + width]

    steps = Steps(wide, planes, waves, factors)

    for x in range(SLIM):
        steps.make_factors(RIM - SLIM + x)
        steps.make_factors(RIM + cells_x + x)
    for turn in range(STEPS):
        steps.step(turn, turn + 1, RIM)
        steps.step(turn, RIM + cells_x - 1 - turn, RIM)

    tiles = steps.tiles

    def finish(i):
        x = RIM + i
        total = None
        for back in range(STEPS + 1):
            source = steps.wave_tiles(0, 1 + STEPS - back, x)
            receiver = steps.wave_tiles(2, 1 + back, x)
            product = [a * b for a, b in zip(source, receiver)]
            total = product if total is None else [a + b for a, b in zip(total, product)]
        for out, value in (
            (0, total),
            (1, steps.wave_tiles(2, 1 + STEPS, x)),
            (2, steps.wave_tiles(3, 1 + STEPS, x)),
        ):
            for tile in range(tiles):
                wide[out, x, pl.ds(tile, SUBLANES, stride=tiles), :] = value[tile]

    repeat(cells_x, finish)
    for out, ref in enumerate((image, p_last, q_last)):
        ref[...] = wide[out, RIM : RIM + cells_x, :cells_y, :]


def inner(wide, planes, own):
    _, planes_x, rows, depth = wide.shape
    tile = (planes_x, rows // SUBLANES, SUBLANES, depth)
    return pl.pallas_call(
        inner_kernel,
        out_shape=[vmem_out(4, *tile)] * STEPS + [vmem_out(FACTORS, *tile)],
        in_specs=in_vmem(3),
        out_specs=in_vmem(STEPS + 1),
        scratch_shapes=[pltpu.VMEM((FACTORS, own.shape[1], rows, depth), jnp.float32)],
        compiler_params=PARAMS,
        name="inner_steps",
    )(pinned(wide, pltpu.VMEM), planes, pinned(own, pltpu.VMEM))


def outer(wide, rims, planes, state, cells_x, cells_y):
    out = jax.ShapeDtypeStruct((cells_x, cells_y, wide.shape[-1]), jnp.float32)
    kept = [vmem_out(*wide.shape)] + [vmem_out(*value.shape) for value in state]
    first = len(rims) + 2
    aliases = {0: 0} | {first + number: 1 + number for number in range(len(state))}
    return pl.pallas_call(
        outer_kernel,
        out_shape=kept + [out] * 3,
        in_specs=in_vmem(first + len(state)),
        out_specs=in_vmem(len(kept) + 3),
        input_output_aliases=aliases,
        compiler_params=PARAMS,
        name="outer_steps",
    )(
        pinned(wide, pltpu.VMEM),
        *rims,
        planes,
        *(pinned(value, pltpu.VMEM) for value in state),
    )[-3:]


def bits_of(axis):
    size = lax.axis_size(axis)
    return [1 << bit for bit in range(size.bit_length() - 1)] if size & (size - 1) == 0 else None


def doubled(windows, axis, bit):
    pairs = [(i, i ^ bit) for i in range(lax.axis_size(axis))]
    return jnp.concatenate([windows, lax.ppermute(windows, axis, pairs)], axis=0)


def inject_kernel(samples, cells_x, cells_y, gathered, table_x, table_y, planes, weights, picks):
    size_y = lax.axis_size("gy")
    own_x, own_y = lax.axis_index("gx"), lax.axis_index("gy")
    rows = cells_y + 2 * RIM
    tiles = rows // SUBLANES
    wide_x = picks.shape[0]
    in_row = LANES // samples
    place = lax.broadcasted_iota(jnp.int32, (rows, LANES), 0)
    row = tiles * lax.rem(place, SUBLANES) + lax.div(place, SUBLANES)
    y_global = own_y * cells_y + jnp.where(row < cells_y + RIM, row, row - rows)
    x_global = own_x * cells_x - RIM + lax.broadcasted_iota(jnp.int32, (wide_x, LANES), 0)
    lane = lax.broadcasted_iota(jnp.int32, (1, LANES), 1)
    bits_x, bits_y = bits_of("gx"), bits_of("gy")

    def source(place):
        device_x, device_y = own_x, own_y
        for number, bit in enumerate(bits_x):
            if place >> number & 1:
                device_x = jnp.bitwise_xor(device_x, bit)
        for number, bit in enumerate(bits_y):
            if place >> (len(bits_x) + number) & 1:
                device_y = jnp.bitwise_xor(device_y, bit)
        return device_x * size_y + device_y

    for group in range(gathered.shape[0] // in_row):
        at_x = at_y = jnp.zeros((1, LANES), jnp.int32)
        window = jnp.zeros((STEPS, LANES), jnp.float32)
        for part in range(in_row):
            place = group * in_row + part
            device = source(place)
            here = (lane >= part * samples) & (lane < (part + 1) * samples)
            shift = lax.rem((part - lax.rem(device, in_row)) * samples + LANES, LANES)
            table_row = pl.ds(lax.div(device, in_row), 1)
            at_x = jnp.where(here, pltpu.roll(table_x[table_row, :], shift, 1), at_x)
            at_y = jnp.where(here, pltpu.roll(table_y[table_row, :], shift, 1), at_y)
            moved = gathered[place]
            if part:
                moved = pltpu.roll(moved, part * samples, 1)
            window = jnp.where(here, moved, window)
        span = slice(group * LANES, (group + 1) * LANES)
        picks[:, span] = (at_x == x_global).astype(jnp.float32)
        is_y = at_y == y_global
        for sample in range(STEPS):
            weights[sample * rows : (sample + 1) * rows, span] = jnp.where(
                is_y, window[sample : sample + 1], 0.0
            )
    rest = weights[...]
    pick = picks[...].astype(jnp.bfloat16)
    total = None
    for _ in range(3):
        part = rest.astype(jnp.bfloat16)
        rest = rest - part.astype(jnp.float32)
        product = lax.dot_general(
            part, pick, (((1,), (1,)), ((), ())), preferred_element_type=jnp.float32
        )
        total = product if total is None else total + product
    planes[...] = jnp.zeros_like(planes)
    for sample in range(STEPS):
        for tile in range(tiles):
            begin = sample * rows + tile * SUBLANES
            planes[sample, tile, :, :wide_x] = total[begin : begin + SUBLANES]


def injected(gathered, receiver_x, receiver_y, samples, cells_x, cells_y, depth):
    rows = cells_y + 2 * RIM
    receivers = receiver_x.shape[0]
    wide_x = -(-(cells_x + 2 * RIM) // 32) * 32
    return pl.pallas_call(
        functools.partial(inject_kernel, samples, cells_x, cells_y),
        out_shape=vmem_out(STEPS, rows // SUBLANES, SUBLANES, depth),
        in_specs=in_vmem(3),
        out_specs=in_vmem(1)[0],
        scratch_shapes=[
            pltpu.VMEM((STEPS * rows, receivers), jnp.float32),
            pltpu.VMEM((wide_x, receivers), jnp.float32),
        ],
        compiler_params=PARAMS,
        name="inject",
    )(gathered, receiver_x.reshape(-1, LANES), receiver_y.reshape(-1, LANES))


def per_device(
    src_p_prev,
    src_p_now,
    src_q_prev,
    src_q_now,
    rec_p_next,
    rec_p_now,
    rec_q_next,
    rec_q_now,
    velocity_term,
    epsilon,
    delta,
    tilt,
    azimuth,
    traces,
    receiver_x,
    receiver_y,
    segment_start,
):
    blocks = (
        src_p_prev,
        src_p_now,
        src_q_prev,
        src_q_now,
        rec_p_next,
        rec_p_now,
        rec_q_next,
        rec_q_now,
        velocity_term,
        epsilon,
        delta,
        tilt,
        azimuth,
    )
    cells_x, cells_y, depth = src_p_now.shape
    wide, y_a, y_b, window = pack(blocks, traces, segment_start)
    y_a, y_b = swap(y_a, "gy", 0), swap(y_b, "gy", 1)
    wide, x_a, x_b = pack_x(wide, window)
    x_a, x_b = swap(x_a, "gx", 0), swap(x_b, "gx", 1)
    windows = jnp.concatenate([window, x_a[x_parts()[1] :, :STEPS, :]], axis=0)
    for bit in bits_of("gx")[1:]:
        windows = doubled(windows, "gx", bit)
    own = own_factors(wide, windows)
    for bit in bits_of("gy")[:-1]:
        windows = doubled(windows, "gy", bit)
    wide, c_a, c_b = corners(wide, y_a, y_b, windows, pinned(own, pltpu.VMEM))
    for bit in bits_of("gy")[-1:]:
        windows = doubled(windows, "gy", bit)
    c_a, c_b = swap(c_a, "gx", 0), swap_far(c_b, "gx")
    planes = injected(
        windows, receiver_x, receiver_y, traces.shape[1], cells_x, cells_y, depth
    )
    state = inner(wide, planes, own)
    return tuple(outer(wide, (x_a, x_b, c_a, c_b), planes, state, cells_x, cells_y))


def solution(mesh):
    state = P(("shot", "gx"), "gy", None)
    earth = P("gx", "gy", None)
    return jax.shard_map(
        per_device,
        mesh=mesh,
        in_specs=(state,) * FIELDS + (earth,) * 5 + (P("shot", ("gx", "gy")), P(), P(), P()),
        out_specs=(state,) * 3,
        check_vma=False,
    )
```

```python
import functools

import jax
import jax.numpy as jnp
from jax import lax
from jax.experimental import pallas as pl
from jax.experimental.pallas import tpu as pltpu
from jax.sharding import PartitionSpec as P

STEPS = 4
REC_DEPTH = 4
RIM = STEPS
FIELDS = 8
SUBLANES = 8
LANES = 128
PARAMS = pltpu.CompilerParams(vmem_limit_bytes=16 * 1024 * 1024)
PACK_PARAMS = pltpu.CompilerParams(vmem_limit_bytes=48 * 1024 * 1024)


def in_vmem(count):
    return [pl.BlockSpec(memory_space=pltpu.VMEM)] * count


def is_odd(axis):
    return lax.rem(lax.axis_index(axis), 2) == 1


def swap(value, axis, first):
    size = lax.axis_size(axis)
    lower = range(first, size - 1, 2)
    pairs = [(i, i + 1) for i in lower] + [(i + 1, i) for i in lower]
    return lax.ppermute(value, axis, pairs)


NOW = (1, 3, 5, 7)
REST = (0, 2, 4, 6, 8, 9, 10, 11, 12)
SLIM = RIM - 1


def y_slots():
    slots = [((number, 0, RIM, 0),) for number in NOW]
    whole = len(REST) - len(REST) // RIM
    for place in range(whole):
        parts = [(REST[place], 0, SLIM, 0)]
        guest = whole + place // SLIM
        if guest < len(REST):
            parts.append((REST[guest], place % SLIM, 1, SLIM))
        slots.append(tuple(parts))
    return slots


def each_y_part(slots, high):
    for slot, parts in enumerate(slots):
        for number, row, rows, place in parts:
            if not high:
                yield slot, number, row, place, rows
            else:
                width = RIM if number in NOW else SLIM
                yield slot, number, RIM - width + row, 0 if place else RIM - rows, rows


def x_parts():
    parts, place = [], 0
    for number in NOW:
        parts.append((number, RIM, place))
        place += RIM
    for number in REST:
        parts.append((number, SLIM, place))
        place += SLIM
    return parts, place


def pinned(value, space):
    return pltpu.with_memory_space_constraint(value, space)


def vmem_out(*shape):
    return pltpu.VMEM(shape, jnp.float32)


def hand_on(value, axis):
    size = lax.axis_size(axis)
    pairs = [(i, i + 2) for i in range(0, size - 2, 2)] + [(i, i - 2) for i in range(3, size, 2)]
    return lax.ppermute(value, axis, pairs)


def pack_kernel(count, *refs):
    blocks, traces, start = refs[:count], refs[count], refs[count + 1]
    wide, y_a, y_b, window, held, sems = refs[count + 2 :]
    cells_x, cells_y = blocks[0].shape[:2]
    core_x = pl.ds(RIM, cells_x)
    moves = [
        pltpu.make_async_copy(block, wide.at[number, core_x, pl.ds(0, cells_y)], sems.at[number])
        for number, block in enumerate(blocks)
    ]
    moves.append(pltpu.make_async_copy(traces, held, sems.at[count]))
    for move in moves:
        move.start()
    odd_y = is_odd("gy")
    begin = start[0]
    samples = traces.shape[1]
    window[...] = jnp.zeros_like(window)
    for move in moves:
        move.wait()
    for sample in range(STEPS):
        window[0, sample : sample + 1, :samples] = held[pl.ds(begin + sample, 1), :]

    def put_y(low, high):
        for out, is_high, base in ((low, False, 0), (high, True, cells_y - RIM)):
            for slot, number, row, place, length in each_y_part(y_slots(), is_high):
                out[slot, :, place : place + length, :] = wide[
                    number, RIM : RIM + cells_x, base + row : base + row + length, :
                ]

    @pl.when(odd_y)
    def _():
        put_y(y_a, y_b)

    @pl.when(jnp.logical_not(odd_y))
    def _():
        put_y(y_b, y_a)


def pack(blocks, traces, segment_start):
    cells_x, cells_y, depth = blocks[0].shape
    count = len(blocks)
    rim_y = vmem_out(len(y_slots()), cells_x, RIM, depth)
    wide = vmem_out(count, cells_x + 2 * RIM + 2, cells_y + 2 * RIM, depth)
    return pl.pallas_call(
        functools.partial(pack_kernel, count),
        out_shape=[wide, rim_y, rim_y, vmem_out(1, STEPS, LANES)],
        in_specs=[pl.BlockSpec(memory_space=pltpu.HBM)] * (count + 1)
        + [pl.BlockSpec(memory_space=pltpu.SMEM)],
        out_specs=in_vmem(4),
        scratch_shapes=[
            pltpu.VMEM(traces.shape, jnp.float32),
            pltpu.SemaphoreType.DMA((count + 1,)),
        ],
        compiler_params=PACK_PARAMS,
        name="pack_y_rims",
    )(*(pinned(value, pltpu.HBM) for value in (*blocks, traces)), segment_start)


def pack_x_kernel(_, window, wide, x_a, x_b):
    cells_x, cells_y = wide.shape[1] - 2 * RIM - 2, wide.shape[2] - 2 * RIM
    odd_x = is_odd("gx")
    parts, total = x_parts()
    for number, width, place in parts:
        first, last = RIM, RIM + cells_x - width
        for out, begin in ((x_a, jnp.where(odd_x, first, last)), (x_b, jnp.where(odd_x, last, first))):
            out[place : place + width] = wide[number, pl.ds(begin, width), :cells_y, :]
    x_a[total] = jnp.zeros_like(x_a[total])
    x_a[total, :STEPS, :] = window[0]


def pack_x(wide, window):
    _, _, rows, depth = wide.shape
    total = x_parts()[1]
    return pl.pallas_call(
        pack_x_kernel,
        out_shape=[
            vmem_out(*wide.shape),
            vmem_out(total + 1, rows - 2 * RIM, depth),
            vmem_out(total, rows - 2 * RIM, depth),
        ],
        in_specs=in_vmem(2),
        out_specs=in_vmem(3),
        input_output_aliases={0: 0},
        compiler_params=PARAMS,
        name="pack_x_rims",
    )(pinned(wide, pltpu.VMEM), window)


def corner_kernel(_, y_a, y_b, __, ___, ____, wide, c_a, c_b):
    cells_x = y_a.shape[1]
    cells_y = wide.shape[2] - 2 * RIM
    odd_x, odd_y = is_odd("gx"), is_odd("gy")

    def place_y(low, high):
        for rim, is_high, base in ((high, False, cells_y), (low, True, cells_y + RIM)):
            for slot, number, row, place, length in each_y_part(y_slots(), is_high):
                wide[number, RIM : RIM + cells_x, base + row : base + row + length, :] = rim[
                    slot, :, place : place + length, :
                ]

    @pl.when(odd_y)
    def _():
        place_y(y_a, y_b)

    @pl.when(jnp.logical_not(odd_y))
    def _():
        place_y(y_b, y_a)

    for number, width, place in x_parts()[0]:
        first, last = RIM, RIM + cells_x - width
        for out, begin in ((c_a, jnp.where(odd_x, first, last)), (c_b, jnp.where(odd_x, last, first))):
            out[place : place + width] = wide[number, pl.ds(begin, width), cells_y:, :]


def corners(wide, y_a, y_b, *earlier):
    corner = vmem_out(x_parts()[1], 2 * RIM, wide.shape[-1])
    return pl.pallas_call(
        corner_kernel,
        out_shape=[vmem_out(*wide.shape), corner, corner],
        in_specs=in_vmem(6),
        out_specs=in_vmem(3),
        input_output_aliases={0: 0},
        compiler_params=PARAMS,
        name="pack_corners",
    )(pinned(wide, pltpu.VMEM), y_a, y_b, *earlier)


def sine_cosine(angle):
    square = angle * angle
    sine = 1.0 / 6227020800.0
    for term in (-1.0 / 39916800.0, 1.0 / 362880.0, -1.0 / 5040.0, 1.0 / 120.0, -1.0 / 6.0, 1.0):
        sine = sine * square + term
    cosine = 1.0 / 479001600.0
    for term in (-1.0 / 3628800.0, 1.0 / 40320.0, -1.0 / 720.0, 1.0 / 24.0, -0.5, 1.0):
        cosine = cosine * square + term
    return sine * angle, cosine


def factors_of(velocity, epsilon, delta, tilt, azimuth):
    f_e = 1.0 + 2.0 * epsilon
    f_d = jnp.sqrt(1.0 + 2.0 * delta)
    sin_tilt, cos_tilt = sine_cosine(tilt)
    sin_half, cos_half = sine_cosine(0.5 * azimuth)
    sin_azim = 2.0 * sin_half * cos_half
    cos_azim = 1.0 - 2.0 * sin_half * sin_half
    sin_square = sin_tilt * sin_tilt
    half_tilt = 0.5 * sin_tilt * cos_tilt
    along_x = sin_square * cos_azim
    return (
        velocity,
        velocity * f_e,
        velocity * f_d,
        along_x * cos_azim,
        sin_square * sin_azim * sin_azim,
        cos_tilt * cos_tilt,
        0.5 * along_x * sin_azim,
        half_tilt * cos_azim,
        half_tilt * sin_azim,
    )


FACTORS = 9


def own_kernel(wide, _, own):
    _, cells_x, cells_y, _ = own.shape

    def body(i):
        for x in [4 * i + k for k in range(4)]:
            raw = [wide[FIELDS + number, RIM + x, :cells_y, :] for number in range(5)]
            for number, value in enumerate(factors_of(*raw)):
                own[number, x] = value

    repeat(cells_x // 4, body)


def own_factors(wide, earlier):
    _, planes_x, rows, depth = wide.shape
    cells_x, cells_y = planes_x - 2 * RIM - 2, rows - 2 * RIM
    return pl.pallas_call(
        own_kernel,
        out_shape=vmem_out(FACTORS, cells_x, cells_y, depth),
        in_specs=in_vmem(2),
        out_specs=in_vmem(1)[0],
        compiler_params=PARAMS,
        name="own_factors",
    )(pinned(wide, pltpu.VMEM), earlier)


class Steps:
    def __init__(self, wide, planes, waves, factors):
        self.wide, self.planes, self.waves, self.factors = wide, planes, waves, factors
        self.count, _, rows, self.depth = wide.shape
        self.tiles = rows // SUBLANES
        self.cells_x = wide.shape[1] - 2 * RIM - 2
        lane = lax.broadcasted_iota(jnp.int32, (SUBLANES, self.depth), 1)
        self.not_last, self.not_first = lane < self.depth - 1, lane > 0
        self.at_depth = lane == REC_DEPTH

    def wide_tiles(self, number, x):
        return [
            self.wide[number, x, pl.ds(tile, SUBLANES, stride=self.tiles), :]
            for tile in range(self.tiles)
        ]

    def wave_tiles(self, number, slot, x):
        if slot < 2:
            return self.wide_tiles(2 * number + slot, x)
        return [self.waves[slot - 2][number, x, tile] for tile in range(self.tiles)]

    def next_y(self, value):
        return value[1:] + [pltpu.roll(value[0], SUBLANES - 1, 0)]

    def previous_y(self, value):
        return [pltpu.roll(value[-1], 1, 0)] + value[:-1]

    def make_factors(self, x):
        raw = [self.wide_tiles(FIELDS + number, x) for number in range(self.count - FIELDS)]
        for tile in range(self.tiles):
            for number, value in enumerate(factors_of(*[value[tile] for value in raw])):
                self.factors[number, x, tile] = value

    def sides_z(self, value):
        above = [jnp.where(self.not_last, pltpu.roll(u, self.depth - 1, 1), 0.0) for u in value]
        below = [jnp.where(self.not_first, pltpu.roll(u, 1, 1), 0.0) for u in value]
        return above, below

    def stencil(self, factors, before, now, after, full):
        slope_x = [a - b for a, b in zip(after, before)]
        above, below = self.sides_z(now)
        slope_z = [a - b for a, b in zip(above, below)]
        next_now, previous_now = self.next_y(now), self.previous_y(now)
        above_x, below_x = self.sides_z(slope_x)
        next_x, previous_x = self.next_y(slope_x), self.previous_y(slope_x)
        next_z, previous_z = self.next_y(slope_z), self.previous_y(slope_z)
        axis, laplace = [], []
        for tile in range(self.tiles):
            axx, ayy, azz, axy, axz, ayz = [value[tile] for value in factors]
            double = now[tile] + now[tile]
            sum_x = after[tile] + before[tile]
            sum_y = next_now[tile] + previous_now[tile]
            sum_z = above[tile] + below[tile]
            straight = ((axx * sum_x + ayy * sum_y) + azz * sum_z) - double
            mixed = (
                axy * (next_x[tile] - previous_x[tile]) + axz * (above_x[tile] - below_x[tile])
            ) + ayz * (next_z[tile] - previous_z[tile])
            axis.append(straight + mixed)
            if full:
                laplace.append(((sum_x + sum_y) + sum_z) - 3.0 * double)
        return axis, laplace

    def step(self, turn, x, count):
        tiles, factors = range(self.tiles), self.factors
        for pair in range(2):
            p_number, q_number = 2 * pair, 2 * pair + 1
            p = [self.wave_tiles(p_number, turn + 1, x - 1 + i) for i in range(count + 2)]
            q = [self.wave_tiles(q_number, turn + 1, x - 1 + i) for i in range(count + 2)]
            for i in range(count):
                now = x + i
                mixing = [[factors[number, now, tile] for tile in tiles] for number in range(3, 9)]
                p_axis, p_laplace = self.stencil(mixing, p[i], p[i + 1], p[i + 2], True)
                q_axis, _ = self.stencil(mixing, q[i], q[i + 1], q[i + 2], False)
                p_held = self.wave_tiles(p_number, turn, now)
                q_held = self.wave_tiles(q_number, turn, now)
                for tile in tiles:
                    velocity, with_e, with_d = [factors[number, now, tile] for number in range(3)]
                    across = p_laplace[tile] - p_axis[tile]
                    p_now, q_now = p[i + 1][tile], q[i + 1][tile]
                    p_next = ((p_now + p_now) - p_held[tile]) + (
                        with_e * across + with_d * q_axis[tile]
                    )
                    q_next = ((q_now + q_now) - q_held[tile]) + (
                        with_d * across + velocity * q_axis[tile]
                    )
                    if pair == 1:
                        shift = lax.rem(REC_DEPTH - now + self.depth, self.depth)
                        moved = pltpu.roll(self.planes[STEPS - 1 - turn, tile], shift, 1)
                        p_next = p_next + jnp.where(self.at_depth, moved, 0.0)
                    self.waves[turn][p_number, now, tile] = p_next
                    self.waves[turn][q_number, now, tile] = q_next


def repeat(count, body):
    def run(i, carry):
        body(i)
        return carry

    lax.fori_loop(0, count, run, 0)


def order_kernel(wide, own, factors, natural):
    _, cells_x, cells_y, _ = own.shape
    tiles = factors.shape[2]

    def rim_rows(i):
        for x in [4 * i + k for k in range(4)]:
            raw = [wide[FIELDS + number, RIM + x, cells_y:, :] for number in range(5)]
            for number, value in enumerate(factors_of(*raw)):
                natural[number, x, cells_y:, :] = value
                natural[number, x, :cells_y, :] = own[number, x]

    def in_step_order(i):
        for x in [2 * i + k for k in range(2)]:
            for number in range(FACTORS):
                for tile in range(tiles):
                    factors[number, RIM + x, tile] = natural[
                        number, x, pl.ds(tile, SUBLANES, stride=tiles), :
                    ]

    repeat(cells_x // 4, rim_rows)
    repeat(cells_x // 2, in_step_order)


def ordered_factors(wide, own):
    _, planes_x, rows, depth = wide.shape
    return pl.pallas_call(
        order_kernel,
        out_shape=vmem_out(FACTORS, planes_x, rows // SUBLANES, SUBLANES, depth),
        in_specs=in_vmem(2),
        out_specs=in_vmem(1)[0],
        scratch_shapes=[pltpu.VMEM((FACTORS, own.shape[1], rows, depth), jnp.float32)],
        compiler_params=PARAMS,
        name="order_factors",
    )(pinned(wide, pltpu.VMEM), pinned(own, pltpu.VMEM))


def inner_kernel(wide, planes, factors, *waves):
    steps = Steps(wide, planes, waves, factors)
    cells_x = steps.cells_x
    for turn in range(STEPS):
        first, last = RIM + 1 + turn, RIM + cells_x - 1 - turn
        half = (last - first) // 2
        repeat(2, lambda i, turn=turn, first=first, half=half: steps.step(turn, first + half * i, half))


def outer_kernel(*refs):
    x_a, x_b, c_a, c_b, planes = refs[1:6]
    refs = refs[6 + STEPS + 1 :]
    wide, waves, factors = refs[0], refs[1 : 1 + STEPS], refs[1 + STEPS]
    image, p_last, q_last = refs[-3:]
    cells_x, cells_y, depth = image.shape
    odd_x = is_odd("gx")
    for number, width, place in x_parts()[0]:
        low, high = RIM - width, RIM + cells_x
        for begin, side, corner in (
            (jnp.where(odd_x, low, high), x_a, c_a),
            (jnp.where(odd_x, high, low), x_b, c_b),
        ):
            wide[number, pl.ds(begin, width), :cells_y, :] = side[place : place + width]
            wide[number, pl.ds(begin, width), cells_y:, :] = corner[place : place + width]

    steps = Steps(wide, planes, waves, factors)

    for x in range(SLIM):
        steps.make_factors(RIM - SLIM + x)
        steps.make_factors(RIM + cells_x + x)
    for turn in range(STEPS):
        steps.step(turn, turn + 1, RIM)
        steps.step(turn, RIM + cells_x - 1 - turn, RIM)

    tiles = steps.tiles

    def finish(i):
        x = RIM + i
        total = None
        for back in range(STEPS + 1):
            source = steps.wave_tiles(0, 1 + STEPS - back, x)
            receiver = steps.wave_tiles(2, 1 + back, x)
            product = [a * b for a, b in zip(source, receiver)]
            total = product if total is None else [a + b for a, b in zip(total, product)]
        for out, value in (
            (0, total),
            (1, steps.wave_tiles(2, 1 + STEPS, x)),
            (2, steps.wave_tiles(3, 1 + STEPS, x)),
        ):
            for tile in range(tiles):
                wide[out, x, pl.ds(tile, SUBLANES, stride=tiles), :] = value[tile]

    repeat(cells_x, finish)
    for out, ref in enumerate((image, p_last, q_last)):
        ref[...] = wide[out, RIM : RIM + cells_x, :cells_y, :]


def inner(wide, planes, factors):
    _, planes_x, rows, depth = wide.shape
    return pl.pallas_call(
        inner_kernel,
        out_shape=[vmem_out(4, planes_x, rows // SUBLANES, SUBLANES, depth)] * STEPS,
        in_specs=in_vmem(3),
        out_specs=in_vmem(STEPS),
        compiler_params=PARAMS,
        name="inner_steps",
    )(pinned(wide, pltpu.VMEM), planes, pinned(factors, pltpu.VMEM))


def outer(wide, rims, planes, state, cells_x, cells_y):
    out = jax.ShapeDtypeStruct((cells_x, cells_y, wide.shape[-1]), jnp.float32)
    kept = [vmem_out(*wide.shape)] + [vmem_out(*value.shape) for value in state]
    first = len(rims) + 2
    aliases = {0: 0} | {first + number: 1 + number for number in range(len(state))}
    return pl.pallas_call(
        outer_kernel,
        out_shape=kept + [out] * 3,
        in_specs=in_vmem(first + len(state)),
        out_specs=in_vmem(len(kept) + 3),
        input_output_aliases=aliases,
        compiler_params=PARAMS,
        name="outer_steps",
    )(
        pinned(wide, pltpu.VMEM),
        *rims,
        planes,
        *(pinned(value, pltpu.VMEM) for value in state),
    )[-3:]


def bits_of(axis):
    size = lax.axis_size(axis)
    return [1 << bit for bit in range(size.bit_length() - 1)] if size & (size - 1) == 0 else None


def doubled(windows, axis, bit):
    pairs = [(i, i ^ bit) for i in range(lax.axis_size(axis))]
    return jnp.concatenate([windows, lax.ppermute(windows, axis, pairs)], axis=0)


def inject_kernel(samples, cells_x, cells_y, gathered, table_x, table_y, _, planes, weights, picks):
    size_y = lax.axis_size("gy")
    own_x, own_y = lax.axis_index("gx"), lax.axis_index("gy")
    rows = cells_y + 2 * RIM
    tiles = rows // SUBLANES
    wide_x = picks.shape[0]
    in_row = LANES // samples
    place = lax.broadcasted_iota(jnp.int32, (rows, LANES), 0)
    row = tiles * lax.rem(place, SUBLANES) + lax.div(place, SUBLANES)
    y_global = own_y * cells_y + jnp.where(row < cells_y + RIM, row, row - rows)
    x_global = own_x * cells_x - RIM + lax.broadcasted_iota(jnp.int32, (wide_x, LANES), 0)
    lane = lax.broadcasted_iota(jnp.int32, (1, LANES), 1)
    bits_x, bits_y = bits_of("gx"), bits_of("gy")

    def source(place):
        device_x, device_y = own_x, own_y
        for number, bit in enumerate(bits_x):
            if place >> number & 1:
                device_x = jnp.bitwise_xor(device_x, bit)
        for number, bit in enumerate(bits_y):
            if place >> (len(bits_x) + number) & 1:
                device_y = jnp.bitwise_xor(device_y, bit)
        return device_x * size_y + device_y

    for group in range(gathered.shape[0] // in_row):
        at_x = at_y = jnp.zeros((1, LANES), jnp.int32)
        window = jnp.zeros((STEPS, LANES), jnp.float32)
        for part in range(in_row):
            place = group * in_row + part
            device = source(place)
            here = (lane >= part * samples) & (lane < (part + 1) * samples)
            shift = lax.rem((part - lax.rem(device, in_row)) * samples + LANES, LANES)
            table_row = pl.ds(lax.div(device, in_row), 1)
            at_x = jnp.where(here, pltpu.roll(table_x[table_row, :], shift, 1), at_x)
            at_y = jnp.where(here, pltpu.roll(table_y[table_row, :], shift, 1), at_y)
            moved = gathered[place]
            if part:
                moved = pltpu.roll(moved, part * samples, 1)
            window = jnp.where(here, moved, window)
        span = slice(group * LANES, (group + 1) * LANES)
        picks[:, span] = (at_x == x_global).astype(jnp.float32)
        is_y = at_y == y_global
        for sample in range(STEPS):
            weights[sample * rows : (sample + 1) * rows, span] = jnp.where(
                is_y, window[sample : sample + 1], 0.0
            )
    rest = weights[...]
    pick = picks[...].astype(jnp.bfloat16)
    total = None
    for _ in range(3):
        part = rest.astype(jnp.bfloat16)
        rest = rest - part.astype(jnp.float32)
        product = lax.dot_general(
            part, pick, (((1,), (1,)), ((), ())), preferred_element_type=jnp.float32
        )
        total = product if total is None else total + product
    planes[...] = jnp.zeros_like(planes)
    for sample in range(STEPS):
        for tile in range(tiles):
            begin = sample * rows + tile * SUBLANES
            planes[sample, tile, :, :wide_x] = total[begin : begin + SUBLANES]


def injected(gathered, receiver_x, receiver_y, earlier, samples, cells_x, cells_y, depth):
    rows = cells_y + 2 * RIM
    receivers = receiver_x.shape[0]
    wide_x = -(-(cells_x + 2 * RIM) // 32) * 32
    return pl.pallas_call(
        functools.partial(inject_kernel, samples, cells_x, cells_y),
        out_shape=vmem_out(STEPS, rows // SUBLANES, SUBLANES, depth),
        in_specs=in_vmem(4),
        out_specs=in_vmem(1)[0],
        scratch_shapes=[
            pltpu.VMEM((STEPS * rows, receivers), jnp.float32),
            pltpu.VMEM((wide_x, receivers), jnp.float32),
        ],
        compiler_params=PARAMS,
        name="inject",
    )(
        gathered,
        receiver_x.reshape(-1, LANES),
        receiver_y.reshape(-1, LANES),
        pinned(earlier, pltpu.VMEM),
    )


def per_device(
    src_p_prev,
    src_p_now,
    src_q_prev,
    src_q_now,
    rec_p_next,
    rec_p_now,
    rec_q_next,
    rec_q_now,
    velocity_term,
    epsilon,
    delta,
    tilt,
    azimuth,
    traces,
    receiver_x,
    receiver_y,
    segment_start,
):
    blocks = (
        src_p_prev,
        src_p_now,
        src_q_prev,
        src_q_now,
        rec_p_next,
        rec_p_now,
        rec_q_next,
        rec_q_now,
        velocity_term,
        epsilon,
        delta,
        tilt,
        azimuth,
    )
    cells_x, cells_y, depth = src_p_now.shape
    wide, y_a, y_b, window = pack(blocks, traces, segment_start)
    y_a, y_b = swap(y_a, "gy", 0), swap(y_b, "gy", 1)
    wide, x_a, x_b = pack_x(wide, window)
    x_a, x_b = swap(x_a, "gx", 0), swap(x_b, "gx", 1)
    windows = jnp.concatenate([window, x_a[x_parts()[1] :, :STEPS, :]], axis=0)
    for bit in bits_of("gx")[1:]:
        windows = doubled(windows, "gx", bit)
    own = own_factors(wide, windows)
    for bit in bits_of("gy")[:-1]:
        windows = doubled(windows, "gy", bit)
    wide, c_a, c_b = corners(wide, y_a, y_b, windows, pinned(own, pltpu.VMEM), x_b)
    for bit in bits_of("gy")[-1:]:
        windows = doubled(windows, "gy", bit)
    c_a, c_b = swap(c_a, "gx", 0), swap(c_b, "gx", 0)
    factors = ordered_factors(wide, own)
    planes = injected(
        windows, receiver_x, receiver_y, factors, traces.shape[1], cells_x, cells_y, depth
    )
    c_b, planes = lax.optimization_barrier((c_b, planes))
    c_b = hand_on(c_b, "gx")
    state = [*inner(wide, planes, factors), factors]
    return tuple(outer(wide, (x_a, x_b, c_a, c_b), planes, state, cells_x, cells_y))


def solution(mesh):
    state = P(("shot", "gx"), "gy", None)
    earth = P("gx", "gy", None)
    return jax.shard_map(
        per_device,
        mesh=mesh,
        in_specs=(state,) * FIELDS + (earth,) * 5 + (P("shot", ("gx", "gy")), P(), P(), P()),
        out_specs=(state,) * 3,
        check_vma=False,
    )
```

```python
import functools

import jax
import jax.numpy as jnp
from jax import lax
from jax.experimental import pallas as pl
from jax.experimental.pallas import tpu as pltpu
from jax.sharding import PartitionSpec as P

STEPS = 4
REC_DEPTH = 4
RIM = STEPS
FIELDS = 8
SUBLANES = 8
LANES = 128
PARAMS = pltpu.CompilerParams(vmem_limit_bytes=16 * 1024 * 1024)
PACK_PARAMS = pltpu.CompilerParams(vmem_limit_bytes=48 * 1024 * 1024)


def in_vmem(count):
    return [pl.BlockSpec(memory_space=pltpu.VMEM)] * count


def is_odd(axis):
    return lax.rem(lax.axis_index(axis), 2) == 1


def swap(value, axis, first):
    size = lax.axis_size(axis)
    lower = range(first, size - 1, 2)
    pairs = [(i, i + 1) for i in lower] + [(i + 1, i) for i in lower]
    return lax.ppermute(value, axis, pairs)


NOW = (1, 3, 5, 7)
REST = (0, 2, 4, 6, 8, 9, 10, 11, 12)
SLIM = RIM - 1


def y_slots():
    slots = [((number, 0, RIM, 0),) for number in NOW]
    whole = len(REST) - len(REST) // RIM
    for place in range(whole):
        parts = [(REST[place], 0, SLIM, 0)]
        guest = whole + place // SLIM
        if guest < len(REST):
            parts.append((REST[guest], place % SLIM, 1, SLIM))
        slots.append(tuple(parts))
    return slots


def each_y_part(slots, high):
    for slot, parts in enumerate(slots):
        for number, row, rows, place in parts:
            if not high:
                yield slot, number, row, place, rows
            else:
                width = RIM if number in NOW else SLIM
                yield slot, number, RIM - width + row, 0 if place else RIM - rows, rows


def x_parts():
    parts, place = [], 0
    for number in NOW:
        parts.append((number, RIM, place))
        place += RIM
    for number in REST:
        parts.append((number, SLIM, place))
        place += SLIM
    return parts, place


def pinned(value, space):
    return pltpu.with_memory_space_constraint(value, space)


def vmem_out(*shape):
    return pltpu.VMEM(shape, jnp.float32)


def pack_kernel(count, *refs):
    blocks, traces, start = refs[:count], refs[count], refs[count + 1]
    wide, y_a, y_b, window, held, sems = refs[count + 2 :]
    cells_x, cells_y = blocks[0].shape[:2]
    core_x = pl.ds(RIM, cells_x)
    moves = [
        pltpu.make_async_copy(block, wide.at[number, core_x, pl.ds(0, cells_y)], sems.at[number])
        for number, block in enumerate(blocks)
    ]
    moves.append(pltpu.make_async_copy(traces, held, sems.at[count]))
    for move in moves:
        move.start()
    odd_y = is_odd("gy")
    begin = start[0]
    samples = traces.shape[1]
    window[...] = jnp.zeros_like(window)
    for number in range(count):
        moves[number].wait()

        def put_y(low, high, number=number):
            for out, is_high, base in ((low, False, 0), (high, True, cells_y - RIM)):
                for slot, part, row, place, length in each_y_part(y_slots(), is_high):
                    if part == number:
                        out[slot, :, place : place + length, :] = wide[
                            number, RIM : RIM + cells_x, base + row : base + row + length, :
                        ]

        @pl.when(odd_y)
        def _(put_y=put_y):
            put_y(y_a, y_b)

        @pl.when(jnp.logical_not(odd_y))
        def _(put_y=put_y):
            put_y(y_b, y_a)

    moves[count].wait()
    for sample in range(STEPS):
        window[0, sample : sample + 1, :samples] = held[pl.ds(begin + sample, 1), :]


def pack(blocks, traces, segment_start):
    cells_x, cells_y, depth = blocks[0].shape
    count = len(blocks)
    rim_y = vmem_out(len(y_slots()), cells_x, RIM, depth)
    wide = vmem_out(count, cells_x + 2 * RIM + 2, cells_y + 2 * RIM, depth)
    return pl.pallas_call(
        functools.partial(pack_kernel, count),
        out_shape=[wide, rim_y, rim_y, vmem_out(1, STEPS, LANES)],
        in_specs=[pl.BlockSpec(memory_space=pltpu.HBM)] * (count + 1)
        + [pl.BlockSpec(memory_space=pltpu.SMEM)],
        out_specs=in_vmem(4),
        scratch_shapes=[
            pltpu.VMEM(traces.shape, jnp.float32),
            pltpu.SemaphoreType.DMA((count + 1,)),
        ],
        compiler_params=PACK_PARAMS,
        name="pack_y_rims",
    )(*(pinned(value, pltpu.HBM) for value in (*blocks, traces)), segment_start)


def pack_x_kernel(_, window, wide, x_a, x_b):
    cells_x, cells_y = wide.shape[1] - 2 * RIM - 2, wide.shape[2] - 2 * RIM
    odd_x = is_odd("gx")
    parts, total = x_parts()
    for number, width, place in parts:
        first, last = RIM, RIM + cells_x - width
        for out, begin in ((x_a, jnp.where(odd_x, first, last)), (x_b, jnp.where(odd_x, last, first))):
            out[place : place + width] = wide[number, pl.ds(begin, width), :cells_y, :]
    x_a[total] = jnp.zeros_like(x_a[total])
    x_a[total, :STEPS, :] = window[0]


def pack_x(wide, window):
    _, _, rows, depth = wide.shape
    total = x_parts()[1]
    return pl.pallas_call(
        pack_x_kernel,
        out_shape=[
            vmem_out(*wide.shape),
            vmem_out(total + 1, rows - 2 * RIM, depth),
            vmem_out(total, rows - 2 * RIM, depth),
        ],
        in_specs=in_vmem(2),
        out_specs=in_vmem(3),
        input_output_aliases={0: 0},
        compiler_params=PARAMS,
        name="pack_x_rims",
    )(pinned(wide, pltpu.VMEM), window)


def corner_kernel(_, y_a, y_b, __, ___, wide, c_a, c_b):
    cells_x = y_a.shape[1]
    cells_y = wide.shape[2] - 2 * RIM
    odd_x, odd_y = is_odd("gx"), is_odd("gy")

    def place_y(low, high):
        for rim, is_high, base in ((high, False, cells_y), (low, True, cells_y + RIM)):
            for slot, number, row, place, length in each_y_part(y_slots(), is_high):
                wide[number, RIM : RIM + cells_x, base + row : base + row + length, :] = rim[
                    slot, :, place : place + length, :
                ]

    @pl.when(odd_y)
    def _():
        place_y(y_a, y_b)

    @pl.when(jnp.logical_not(odd_y))
    def _():
        place_y(y_b, y_a)

    for number, width, place in x_parts()[0]:
        first, last = RIM, RIM + cells_x - width
        for out, begin in ((c_a, jnp.where(odd_x, first, last)), (c_b, jnp.where(odd_x, last, first))):
            out[place : place + width] = wide[number, pl.ds(begin, width), cells_y:, :]


def corners(wide, y_a, y_b, *earlier):
    corner = vmem_out(x_parts()[1], 2 * RIM, wide.shape[-1])
    return pl.pallas_call(
        corner_kernel,
        out_shape=[vmem_out(*wide.shape), corner, corner],
        in_specs=in_vmem(5),
        out_specs=in_vmem(3),
        input_output_aliases={0: 0},
        compiler_params=PARAMS,
        name="pack_corners",
    )(pinned(wide, pltpu.VMEM), y_a, y_b, *earlier)


def sine_cosine(angle):
    square = angle * angle
    sine = 1.0 / 6227020800.0
    for term in (-1.0 / 39916800.0, 1.0 / 362880.0, -1.0 / 5040.0, 1.0 / 120.0, -1.0 / 6.0, 1.0):
        sine = sine * square + term
    cosine = 1.0 / 479001600.0
    for term in (-1.0 / 3628800.0, 1.0 / 40320.0, -1.0 / 720.0, 1.0 / 24.0, -0.5, 1.0):
        cosine = cosine * square + term
    return sine * angle, cosine


def factors_of(velocity, epsilon, delta, tilt, azimuth):
    f_e = 1.0 + 2.0 * epsilon
    f_d = jnp.sqrt(1.0 + 2.0 * delta)
    sin_tilt, cos_tilt = sine_cosine(tilt)
    sin_half, cos_half = sine_cosine(0.5 * azimuth)
    sin_azim = 2.0 * sin_half * cos_half
    cos_azim = 1.0 - 2.0 * sin_half * sin_half
    sin_square = sin_tilt * sin_tilt
    half_tilt = 0.5 * sin_tilt * cos_tilt
    along_x = sin_square * cos_azim
    return (
        velocity,
        velocity * f_e,
        velocity * f_d,
        along_x * cos_azim,
        sin_square * sin_azim * sin_azim,
        cos_tilt * cos_tilt,
        0.5 * along_x * sin_azim,
        half_tilt * cos_azim,
        half_tilt * sin_azim,
    )


FACTORS = 9


def own_kernel(wide, _, own):
    _, cells_x, cells_y, _ = own.shape

    def body(i):
        for x in [4 * i + k for k in range(4)]:
            raw = [wide[FIELDS + number, RIM + x, :cells_y, :] for number in range(5)]
            for number, value in enumerate(factors_of(*raw)):
                own[number, x] = value

    repeat(cells_x // 4, body)


def own_factors(wide, earlier):
    _, planes_x, rows, depth = wide.shape
    cells_x, cells_y = planes_x - 2 * RIM - 2, rows - 2 * RIM
    return pl.pallas_call(
        own_kernel,
        out_shape=vmem_out(FACTORS, cells_x, cells_y, depth),
        in_specs=in_vmem(2),
        out_specs=in_vmem(1)[0],
        compiler_params=PARAMS,
        name="own_factors",
    )(pinned(wide, pltpu.VMEM), earlier)


class Steps:
    def __init__(self, wide, planes, waves, factors):
        self.wide, self.planes, self.waves, self.factors = wide, planes, waves, factors
        self.count, _, rows, self.depth = wide.shape
        self.tiles = rows // SUBLANES
        self.cells_x = wide.shape[1] - 2 * RIM - 2
        lane = lax.broadcasted_iota(jnp.int32, (SUBLANES, self.depth), 1)
        self.not_last, self.not_first = lane < self.depth - 1, lane > 0
        self.at_depth = lane == REC_DEPTH

    def wide_tiles(self, number, x):
        return [
            self.wide[number, x, pl.ds(tile, SUBLANES, stride=self.tiles), :]
            for tile in range(self.tiles)
        ]

    def wave_tiles(self, number, slot, x):
        if slot < 2:
            return self.wide_tiles(2 * number + slot, x)
        return [self.waves[slot - 2][number, x, tile] for tile in range(self.tiles)]

    def next_y(self, value):
        return value[1:] + [pltpu.roll(value[0], SUBLANES - 1, 0)]

    def previous_y(self, value):
        return [pltpu.roll(value[-1], 1, 0)] + value[:-1]

    def make_factors(self, x):
        raw = [self.wide_tiles(FIELDS + number, x) for number in range(self.count - FIELDS)]
        for tile in range(self.tiles):
            for number, value in enumerate(factors_of(*[value[tile] for value in raw])):
                self.factors[number, x, tile] = value

    def sides_z(self, value):
        above = [jnp.where(self.not_last, pltpu.roll(u, self.depth - 1, 1), 0.0) for u in value]
        below = [jnp.where(self.not_first, pltpu.roll(u, 1, 1), 0.0) for u in value]
        return above, below

    def plane_part(self, now):
        above, below = self.sides_z(now)
        after, before = self.next_y(now), self.previous_y(now)
        pairs_z, pairs_y = list(zip(above, below)), list(zip(after, before))
        return (
            [a - b for a, b in pairs_y],
            [a - b for a, b in pairs_z],
            [a + b for a, b in pairs_y],
            [a + b for a, b in pairs_z],
        )

    def stencil(self, number, turn, x, count, full):
        planes = [self.wave_tiles(number, turn + 1, x - 1 + i) for i in range(count + 2)]
        parts = [self.plane_part(planes[0]), self.plane_part(planes[1])]
        result = []
        for i in range(1, count + 1):
            parts.append(self.plane_part(planes[i + 1]))
            slope_y, slope_z, sums_y, sums_z = parts[i]
            next_z, previous_z = self.next_y(slope_z), self.previous_y(slope_z)
            axis, laplace = [], []
            for tile in range(self.tiles):
                axx, ayy, azz, axy, axz, ayz = [
                    self.factors[factor, x - 1 + i, tile] for factor in range(3, 9)
                ]
                now = planes[i][tile]
                double = now + now
                sum_x = planes[i + 1][tile] + planes[i - 1][tile]
                sum_y, sum_z = sums_y[tile], sums_z[tile]
                straight = ((axx * sum_x + ayy * sum_y) + azz * sum_z) - double
                mixed = (
                    axy * (parts[i + 1][0][tile] - parts[i - 1][0][tile])
                    + axz * (parts[i + 1][1][tile] - parts[i - 1][1][tile])
                ) + ayz * (next_z[tile] - previous_z[tile])
                axis.append(straight + mixed)
                if full:
                    laplace.append(((sum_x + sum_y) + sum_z) - 3.0 * double)
            result.append((planes[i], axis, laplace))
        return result

    def step(self, turn, x, count):
        tiles, factors = range(self.tiles), self.factors
        for pair in range(2):
            p_number, q_number = 2 * pair, 2 * pair + 1
            of_q = self.stencil(q_number, turn, x, count, False)
            of_p = self.stencil(p_number, turn, x, count, True)
            for i in range(count):
                now = x + i
                q, q_axis, _ = of_q[i]
                p, p_axis, p_laplace = of_p[i]
                p_held = self.wave_tiles(p_number, turn, now)
                q_held = self.wave_tiles(q_number, turn, now)
                for tile in tiles:
                    velocity, with_e, with_d = [factors[number, now, tile] for number in range(3)]
                    across = p_laplace[tile] - p_axis[tile]
                    p_next = ((p[tile] + p[tile]) - p_held[tile]) + (
                        with_e * across + with_d * q_axis[tile]
                    )
                    q_next = ((q[tile] + q[tile]) - q_held[tile]) + (
                        with_d * across + velocity * q_axis[tile]
                    )
                    if pair == 1:
                        shift = lax.rem(REC_DEPTH - now + self.depth, self.depth)
                        moved = pltpu.roll(self.planes[STEPS - 1 - turn, tile], shift, 1)
                        p_next = p_next + jnp.where(self.at_depth, moved, 0.0)
                    self.waves[turn][p_number, now, tile] = p_next
                    self.waves[turn][q_number, now, tile] = q_next


def repeat(count, body):
    def run(i, carry):
        body(i)
        return carry

    lax.fori_loop(0, count, run, 0)


def inner_kernel(wide, planes, own, *refs):
    steps = Steps(wide, planes, refs[:STEPS], refs[STEPS])
    natural = refs[STEPS + 1]
    cells_x, cells_y, tiles = steps.cells_x, own.shape[2], steps.tiles

    def rim_rows(i):
        for x in [4 * i + k for k in range(4)]:
            raw = [wide[FIELDS + number, RIM + x, cells_y:, :] for number in range(5)]
            for number, value in enumerate(factors_of(*raw)):
                natural[number, x, cells_y:, :] = value
                natural[number, x, :cells_y, :] = own[number, x]

    def in_step_order(i):
        for x in [2 * i + k for k in range(2)]:
            for number in range(FACTORS):
                for tile in range(tiles):
                    steps.factors[number, RIM + x, tile] = natural[
                        number, x, pl.ds(tile, SUBLANES, stride=tiles), :
                    ]

    repeat(cells_x // 4, rim_rows)
    repeat(cells_x // 2, in_step_order)
    for turn in range(STEPS):
        first, last = RIM + 1 + turn, RIM + cells_x - 1 - turn
        half = (last - first) // 2
        repeat(2, lambda i, turn=turn, first=first, half=half: steps.step(turn, first + half * i, half))


def outer_kernel(*refs):
    x_a, x_b, c_a, c_b, planes = refs[1:6]
    refs = refs[6 + STEPS + 1 :]
    wide, waves, factors = refs[0], refs[1 : 1 + STEPS], refs[1 + STEPS]
    image, p_last, q_last = refs[-3:]
    cells_x, cells_y, depth = image.shape
    odd_x = is_odd("gx")
    for number, width, place in x_parts()[0]:
        low, high = RIM - width, RIM + cells_x
        for begin, side, corner in (
            (jnp.where(odd_x, low, high), x_a, c_a),
            (jnp.where(odd_x, high, low), x_b, c_b),
        ):
            wide[number, pl.ds(begin, width), :cells_y, :] = side[place : place + width]
            wide[number, pl.ds(begin, width), cells_y:, :] = corner[place : place + width]

    steps = Steps(wide, planes, waves, factors)

    for x in range(SLIM):
        steps.make_factors(RIM - SLIM + x)
        steps.make_factors(RIM + cells_x + x)
    for turn in range(STEPS):
        steps.step(turn, turn + 1, RIM)
        steps.step(turn, RIM + cells_x - 1 - turn, RIM)

    tiles = steps.tiles

    def finish(i):
        x = RIM + i
        total = None
        for back in range(STEPS + 1):
            source = steps.wave_tiles(0, 1 + STEPS - back, x)
            receiver = steps.wave_tiles(2, 1 + back, x)
            product = [a * b for a, b in zip(source, receiver)]
            total = product if total is None else [a + b for a, b in zip(total, product)]
        for out, value in (
            (0, total),
            (1, steps.wave_tiles(2, 1 + STEPS, x)),
            (2, steps.wave_tiles(3, 1 + STEPS, x)),
        ):
            for tile in range(tiles):
                wide[out, x, pl.ds(tile, SUBLANES, stride=tiles), :] = value[tile]

    repeat(cells_x, finish)
    for out, ref in enumerate((image, p_last, q_last)):
        ref[...] = wide[out, RIM : RIM + cells_x, :cells_y, :]


def inner(wide, planes, own):
    _, planes_x, rows, depth = wide.shape
    tile = (planes_x, rows // SUBLANES, SUBLANES, depth)
    return pl.pallas_call(
        inner_kernel,
        out_shape=[vmem_out(4, *tile)] * STEPS + [vmem_out(FACTORS, *tile)],
        in_specs=in_vmem(3),
        out_specs=in_vmem(STEPS + 1),
        scratch_shapes=[pltpu.VMEM((FACTORS, own.shape[1], rows, depth), jnp.float32)],
        compiler_params=PARAMS,
        name="inner_steps",
    )(pinned(wide, pltpu.VMEM), planes, pinned(own, pltpu.VMEM))


def outer(wide, rims, planes, state, cells_x, cells_y):
    out = jax.ShapeDtypeStruct((cells_x, cells_y, wide.shape[-1]), jnp.float32)
    kept = [vmem_out(*wide.shape)] + [vmem_out(*value.shape) for value in state]
    first = len(rims) + 2
    aliases = {0: 0} | {first + number: 1 + number for number in range(len(state))}
    return pl.pallas_call(
        outer_kernel,
        out_shape=kept + [out] * 3,
        in_specs=in_vmem(first + len(state)),
        out_specs=in_vmem(len(kept) + 3),
        input_output_aliases=aliases,
        compiler_params=PARAMS,
        name="outer_steps",
    )(
        pinned(wide, pltpu.VMEM),
        *rims,
        planes,
        *(pinned(value, pltpu.VMEM) for value in state),
    )[-3:]


def bits_of(axis):
    size = lax.axis_size(axis)
    return [1 << bit for bit in range(size.bit_length() - 1)] if size & (size - 1) == 0 else None


def doubled(windows, axis, bit):
    pairs = [(i, i ^ bit) for i in range(lax.axis_size(axis))]
    return jnp.concatenate([windows, lax.ppermute(windows, axis, pairs)], axis=0)


def inject_kernel(samples, cells_x, cells_y, gathered, table_x, table_y, planes, weights, picks):
    size_y = lax.axis_size("gy")
    own_x, own_y = lax.axis_index("gx"), lax.axis_index("gy")
    rows = cells_y + 2 * RIM
    tiles = rows // SUBLANES
    wide_x = picks.shape[0]
    in_row = LANES // samples
    place = lax.broadcasted_iota(jnp.int32, (rows, LANES), 0)
    row = tiles * lax.rem(place, SUBLANES) + lax.div(place, SUBLANES)
    y_global = own_y * cells_y + jnp.where(row < cells_y + RIM, row, row - rows)
    x_global = own_x * cells_x - RIM + lax.broadcasted_iota(jnp.int32, (wide_x, LANES), 0)
    lane = lax.broadcasted_iota(jnp.int32, (1, LANES), 1)
    bits_x, bits_y = bits_of("gx"), bits_of("gy")

    def source(place):
        device_x, device_y = own_x, own_y
        for number, bit in enumerate(bits_x):
            if place >> number & 1:
                device_x = jnp.bitwise_xor(device_x, bit)
        for number, bit in enumerate(bits_y):
            if place >> (len(bits_x) + number) & 1:
                device_y = jnp.bitwise_xor(device_y, bit)
        return device_x * size_y + device_y

    for group in range(gathered.shape[0] // in_row):
        at_x = at_y = jnp.zeros((1, LANES), jnp.int32)
        window = jnp.zeros((STEPS, LANES), jnp.float32)
        for part in range(in_row):
            place = group * in_row + part
            device = source(place)
            here = (lane >= part * samples) & (lane < (part + 1) * samples)
            shift = lax.rem((part - lax.rem(device, in_row)) * samples + LANES, LANES)
            table_row = pl.ds(lax.div(device, in_row), 1)
            at_x = jnp.where(here, pltpu.roll(table_x[table_row, :], shift, 1), at_x)
            at_y = jnp.where(here, pltpu.roll(table_y[table_row, :], shift, 1), at_y)
            moved = gathered[place]
            if part:
                moved = pltpu.roll(moved, part * samples, 1)
            window = jnp.where(here, moved, window)
        span = slice(group * LANES, (group + 1) * LANES)
        picks[:, span] = (at_x == x_global).astype(jnp.float32)
        is_y = at_y == y_global
        for sample in range(STEPS):
            weights[sample * rows : (sample + 1) * rows, span] = jnp.where(
                is_y, window[sample : sample + 1], 0.0
            )
    rest = weights[...]
    pick = picks[...].astype(jnp.bfloat16)
    total = None
    for _ in range(3):
        part = rest.astype(jnp.bfloat16)
        rest = rest - part.astype(jnp.float32)
        product = lax.dot_general(
            part, pick, (((1,), (1,)), ((), ())), preferred_element_type=jnp.float32
        )
        total = product if total is None else total + product
    planes[...] = jnp.zeros_like(planes)
    for sample in range(STEPS):
        for tile in range(tiles):
            begin = sample * rows + tile * SUBLANES
            planes[sample, tile, :, :wide_x] = total[begin : begin + SUBLANES]


def injected(gathered, receiver_x, receiver_y, samples, cells_x, cells_y, depth):
    rows = cells_y + 2 * RIM
    receivers = receiver_x.shape[0]
    wide_x = -(-(cells_x + 2 * RIM) // 32) * 32
    return pl.pallas_call(
        functools.partial(inject_kernel, samples, cells_x, cells_y),
        out_shape=vmem_out(STEPS, rows // SUBLANES, SUBLANES, depth),
        in_specs=in_vmem(3),
        out_specs=in_vmem(1)[0],
        scratch_shapes=[
            pltpu.VMEM((STEPS * rows, receivers), jnp.float32),
            pltpu.VMEM((wide_x, receivers), jnp.float32),
        ],
        compiler_params=PARAMS,
        name="inject",
    )(gathered, receiver_x.reshape(-1, LANES), receiver_y.reshape(-1, LANES))


def per_device(
    src_p_prev,
    src_p_now,
    src_q_prev,
    src_q_now,
    rec_p_next,
    rec_p_now,
    rec_q_next,
    rec_q_now,
    velocity_term,
    epsilon,
    delta,
    tilt,
    azimuth,
    traces,
    receiver_x,
    receiver_y,
    segment_start,
):
    blocks = (
        src_p_prev,
        src_p_now,
        src_q_prev,
        src_q_now,
        rec_p_next,
        rec_p_now,
        rec_q_next,
        rec_q_now,
        velocity_term,
        epsilon,
        delta,
        tilt,
        azimuth,
    )
    cells_x, cells_y, depth = src_p_now.shape
    wide, y_a, y_b, window = pack(blocks, traces, segment_start)
    y_a, y_b = swap(y_a, "gy", 0), swap(y_b, "gy", 1)
    wide, x_a, x_b = pack_x(wide, window)
    x_a, x_b = swap(x_a, "gx", 0), swap(x_b, "gx", 1)
    windows = jnp.concatenate([window, x_a[x_parts()[1] :, :STEPS, :]], axis=0)
    for bit in bits_of("gx")[1:]:
        windows = doubled(windows, "gx", bit)
    own = own_factors(wide, windows)
    for bit in bits_of("gy")[:-1]:
        windows = doubled(windows, "gy", bit)
    wide, c_a, c_b = corners(wide, y_a, y_b, windows, pinned(own, pltpu.VMEM))
    for bit in bits_of("gy")[-1:]:
        windows = doubled(windows, "gy", bit)
    c_a, c_b = swap(c_a, "gx", 0), swap(c_b, "gx", 1)
    planes = injected(
        windows, receiver_x, receiver_y, traces.shape[1], cells_x, cells_y, depth
    )
    state = inner(wide, planes, own)
    return tuple(outer(wide, (x_a, x_b, c_a, c_b), planes, state, cells_x, cells_y))


def solution(mesh):
    state = P(("shot", "gx"), "gy", None)
    earth = P("gx", "gy", None)
    return jax.shard_map(
        per_device,
        mesh=mesh,
        in_specs=(state,) * FIELDS + (earth,) * 5 + (P("shot", ("gx", "gy")), P(), P(), P()),
        out_specs=(state,) * 3,
        check_vma=False,
    )
```

```python
import functools

import jax
import jax.numpy as jnp
from jax import lax
from jax.experimental import pallas as pl
from jax.experimental.pallas import tpu as pltpu
from jax.sharding import PartitionSpec as P

STEPS = 4
REC_DEPTH = 4
RIM = STEPS
QUARTERS = 4
FIELDS = 8
SUBLANES = 8
LANES = 128
PARAMS = pltpu.CompilerParams(vmem_limit_bytes=16 * 1024 * 1024)
PACK_PARAMS = pltpu.CompilerParams(vmem_limit_bytes=48 * 1024 * 1024)


def in_vmem(count):
    return [pl.BlockSpec(memory_space=pltpu.VMEM)] * count


def is_odd(axis):
    return lax.rem(lax.axis_index(axis), 2) == 1


def swap(value, axis, first):
    size = lax.axis_size(axis)
    lower = range(first, size - 1, 2)
    pairs = [(i, i + 1) for i in lower] + [(i + 1, i) for i in lower]
    return lax.ppermute(value, axis, pairs)


NOW = (1, 3, 5, 7)
REST = (0, 2, 4, 6, 8, 9, 10, 11, 12)
SLIM = RIM - 1


def y_slots():
    slots = [((number, 0, RIM, 0),) for number in NOW]
    whole = len(REST) - len(REST) // RIM
    for place in range(whole):
        parts = [(REST[place], 0, SLIM, 0)]
        guest = whole + place // SLIM
        if guest < len(REST):
            parts.append((REST[guest], place % SLIM, 1, SLIM))
        slots.append(tuple(parts))
    return slots


def each_y_part(slots, high):
    for slot, parts in enumerate(slots):
        for number, row, rows, place in parts:
            if not high:
                yield slot, number, row, place, rows
            else:
                width = RIM if number in NOW else SLIM
                yield slot, number, RIM - width + row, 0 if place else RIM - rows, rows


def x_parts():
    parts, place = [], 0
    for number in NOW:
        parts.append((number, RIM, place))
        place += RIM
    for number in REST:
        parts.append((number, SLIM, place))
        place += SLIM
    return parts, place


def pinned(value, space):
    return pltpu.with_memory_space_constraint(value, space)


def vmem_out(*shape):
    return pltpu.VMEM(shape, jnp.float32)


def pack_kernel(count, *refs):
    blocks, traces, start = refs[:count], refs[count], refs[count + 1]
    wide, y_a, y_b, window, held, sems = refs[count + 2 :]
    cells_x, cells_y = blocks[0].shape[:2]
    core_x = pl.ds(RIM, cells_x)
    moves = [
        pltpu.make_async_copy(block, wide.at[number, core_x, pl.ds(0, cells_y)], sems.at[number])
        for number, block in enumerate(blocks)
    ]
    moves.append(pltpu.make_async_copy(traces, held, sems.at[count]))
    for move in moves:
        move.start()
    odd_y = is_odd("gy")
    begin = start[0]
    samples = traces.shape[1]
    window[...] = jnp.zeros_like(window)
    for number in range(count):
        moves[number].wait()

        def put_y(low, high, number=number):
            for out, is_high, base in ((low, False, 0), (high, True, cells_y - RIM)):
                for slot, part, row, place, length in each_y_part(y_slots(), is_high):
                    if part == number:
                        out[slot, :, place : place + length, :] = wide[
                            number, RIM : RIM + cells_x, base + row : base + row + length, :
                        ]

        @pl.when(odd_y)
        def _(put_y=put_y):
            put_y(y_a, y_b)

        @pl.when(jnp.logical_not(odd_y))
        def _(put_y=put_y):
            put_y(y_b, y_a)

    moves[count].wait()
    for sample in range(STEPS):
        window[0, sample : sample + 1, :samples] = held[pl.ds(begin + sample, 1), :]


def pack(blocks, traces, segment_start):
    cells_x, cells_y, depth = blocks[0].shape
    count = len(blocks)
    rim_y = vmem_out(len(y_slots()), cells_x, RIM, depth)
    wide = vmem_out(count, cells_x + 2 * RIM + 2, cells_y + 2 * RIM, depth)
    return pl.pallas_call(
        functools.partial(pack_kernel, count),
        out_shape=[wide, rim_y, rim_y, vmem_out(1, STEPS, LANES)],
        in_specs=[pl.BlockSpec(memory_space=pltpu.HBM)] * (count + 1)
        + [pl.BlockSpec(memory_space=pltpu.SMEM)],
        out_specs=in_vmem(4),
        scratch_shapes=[
            pltpu.VMEM(traces.shape, jnp.float32),
            pltpu.SemaphoreType.DMA((count + 1,)),
        ],
        compiler_params=PACK_PARAMS,
        name="pack_y_rims",
    )(*(pinned(value, pltpu.HBM) for value in (*blocks, traces)), segment_start)


def pack_x_kernel(_, window, wide, x_a, x_b):
    cells_x, cells_y = wide.shape[1] - 2 * RIM - 2, wide.shape[2] - 2 * RIM
    odd_x = is_odd("gx")
    parts, total = x_parts()
    for number, width, place in parts:
        first, last = RIM, RIM + cells_x - width
        for out, begin in ((x_a, jnp.where(odd_x, first, last)), (x_b, jnp.where(odd_x, last, first))):
            out[place : place + width] = wide[number, pl.ds(begin, width), :cells_y, :]
    x_a[total] = jnp.zeros_like(x_a[total])
    x_a[total, :STEPS, :] = window[0]


def pack_x(wide, window):
    _, _, rows, depth = wide.shape
    total = x_parts()[1]
    return pl.pallas_call(
        pack_x_kernel,
        out_shape=[
            vmem_out(*wide.shape),
            vmem_out(total + 1, rows - 2 * RIM, depth),
            vmem_out(total, rows - 2 * RIM, depth),
        ],
        in_specs=in_vmem(2),
        out_specs=in_vmem(3),
        input_output_aliases={0: 0},
        compiler_params=PARAMS,
        name="pack_x_rims",
    )(pinned(wide, pltpu.VMEM), window)


def corner_kernel(_, y_a, y_b, __, ___, wide, c_a, c_b):
    cells_x = y_a.shape[1]
    cells_y = wide.shape[2] - 2 * RIM
    odd_x, odd_y = is_odd("gx"), is_odd("gy")

    def place_y(low, high):
        for rim, is_high, base in ((high, False, cells_y), (low, True, cells_y + RIM)):
            for slot, number, row, place, length in each_y_part(y_slots(), is_high):
                wide[number, RIM : RIM + cells_x, base + row : base + row + length, :] = rim[
                    slot, :, place : place + length, :
                ]

    @pl.when(odd_y)
    def _():
        place_y(y_a, y_b)

    @pl.when(jnp.logical_not(odd_y))
    def _():
        place_y(y_b, y_a)

    for number, width, place in x_parts()[0]:
        first, last = RIM, RIM + cells_x - width
        for out, begin in ((c_a, jnp.where(odd_x, first, last)), (c_b, jnp.where(odd_x, last, first))):
            out[place : place + width] = wide[number, pl.ds(begin, width), cells_y:, :]


def corners(wide, y_a, y_b, *earlier):
    corner = vmem_out(x_parts()[1], 2 * RIM, wide.shape[-1])
    return pl.pallas_call(
        corner_kernel,
        out_shape=[vmem_out(*wide.shape), corner, corner],
        in_specs=in_vmem(5),
        out_specs=in_vmem(3),
        input_output_aliases={0: 0},
        compiler_params=PARAMS,
        name="pack_corners",
    )(pinned(wide, pltpu.VMEM), y_a, y_b, *earlier)


def sine_cosine(angle):
    square = angle * angle
    sine = 1.0 / 6227020800.0
    for term in (-1.0 / 39916800.0, 1.0 / 362880.0, -1.0 / 5040.0, 1.0 / 120.0, -1.0 / 6.0, 1.0):
        sine = sine * square + term
    cosine = 1.0 / 479001600.0
    for term in (-1.0 / 3628800.0, 1.0 / 40320.0, -1.0 / 720.0, 1.0 / 24.0, -0.5, 1.0):
        cosine = cosine * square + term
    return sine * angle, cosine


def factors_of(velocity, epsilon, delta, tilt, azimuth):
    f_e = 1.0 + 2.0 * epsilon
    f_d = jnp.sqrt(1.0 + 2.0 * delta)
    sin_tilt, cos_tilt = sine_cosine(tilt)
    sin_half, cos_half = sine_cosine(0.5 * azimuth)
    sin_azim = 2.0 * sin_half * cos_half
    cos_azim = 1.0 - 2.0 * sin_half * sin_half
    sin_square = sin_tilt * sin_tilt
    half_tilt = 0.5 * sin_tilt * cos_tilt
    along_x = sin_square * cos_azim
    return (
        velocity,
        velocity * f_e,
        velocity * f_d,
        along_x * cos_azim,
        sin_square * sin_azim * sin_azim,
        cos_tilt * cos_tilt,
        0.5 * along_x * sin_azim,
        half_tilt * cos_azim,
        half_tilt * sin_azim,
    )


FACTORS = 9


def own_kernel(wide, _, own):
    _, cells_x, cells_y, _ = own.shape

    def body(i):
        for x in [4 * i + k for k in range(4)]:
            raw = [wide[FIELDS + number, RIM + x, :cells_y, :] for number in range(5)]
            for number, value in enumerate(factors_of(*raw)):
                own[number, x] = value

    repeat(cells_x // 4, body)


def own_factors(wide, earlier):
    _, planes_x, rows, depth = wide.shape
    cells_x, cells_y = planes_x - 2 * RIM - 2, rows - 2 * RIM
    return pl.pallas_call(
        own_kernel,
        out_shape=vmem_out(FACTORS, cells_x, cells_y, depth),
        in_specs=in_vmem(2),
        out_specs=in_vmem(1)[0],
        compiler_params=PARAMS,
        name="own_factors",
    )(pinned(wide, pltpu.VMEM), earlier)


class Steps:
    def __init__(self, wide, planes, waves, factors):
        self.wide, self.planes, self.waves, self.factors = wide, planes, waves, factors
        self.count, _, rows, self.depth = wide.shape
        self.tiles = rows // SUBLANES
        self.cells_x = wide.shape[1] - 2 * RIM - 2
        lane = lax.broadcasted_iota(jnp.int32, (SUBLANES, self.depth), 1)
        self.not_last, self.not_first = lane < self.depth - 1, lane > 0
        self.at_depth = lane == REC_DEPTH

    def wide_tiles(self, number, x):
        return [
            self.wide[number, x, pl.ds(tile, SUBLANES, stride=self.tiles), :]
            for tile in range(self.tiles)
        ]

    def wave_tiles(self, number, slot, x):
        if slot < 2:
            return self.wide_tiles(2 * number + slot, x)
        return [self.waves[slot - 2][number, x, tile] for tile in range(self.tiles)]

    def next_y(self, value):
        return value[1:] + [pltpu.roll(value[0], SUBLANES - 1, 0)]

    def previous_y(self, value):
        return [pltpu.roll(value[-1], 1, 0)] + value[:-1]

    def make_factors(self, x):
        raw = [self.wide_tiles(FIELDS + number, x) for number in range(self.count - FIELDS)]
        for tile in range(self.tiles):
            for number, value in enumerate(factors_of(*[value[tile] for value in raw])):
                self.factors[number, x, tile] = value

    def sides_z(self, value):
        above = [jnp.where(self.not_last, pltpu.roll(u, self.depth - 1, 1), 0.0) for u in value]
        below = [jnp.where(self.not_first, pltpu.roll(u, 1, 1), 0.0) for u in value]
        return above, below

    def plane_part(self, now):
        above, below = self.sides_z(now)
        after, before = self.next_y(now), self.previous_y(now)
        pairs_z, pairs_y = list(zip(above, below)), list(zip(after, before))
        return (
            [a - b for a, b in pairs_y],
            [a - b for a, b in pairs_z],
            [a + b for a, b in pairs_y],
            [a + b for a, b in pairs_z],
        )

    def stencil(self, number, turn, x, count, full):
        planes = [self.wave_tiles(number, turn + 1, x - 1 + i) for i in range(count + 2)]
        parts = [self.plane_part(planes[0]), self.plane_part(planes[1])]
        result = []
        for i in range(1, count + 1):
            parts.append(self.plane_part(planes[i + 1]))
            slope_y, slope_z, sums_y, sums_z = parts[i]
            next_z, previous_z = self.next_y(slope_z), self.previous_y(slope_z)
            axis, laplace = [], []
            for tile in range(self.tiles):
                axx, ayy, azz, axy, axz, ayz = [
                    self.factors[factor, x - 1 + i, tile] for factor in range(3, 9)
                ]
                now = planes[i][tile]
                double = now + now
                sum_x = planes[i + 1][tile] + planes[i - 1][tile]
                sum_y, sum_z = sums_y[tile], sums_z[tile]
                straight = ((axx * sum_x + ayy * sum_y) + azz * sum_z) - double
                mixed = (
                    axy * (parts[i + 1][0][tile] - parts[i - 1][0][tile])
                    + axz * (parts[i + 1][1][tile] - parts[i - 1][1][tile])
                ) + ayz * (next_z[tile] - previous_z[tile])
                axis.append(straight + mixed)
                if full:
                    laplace.append(((sum_x + sum_y) + sum_z) - 3.0 * double)
            result.append((planes[i], axis, laplace))
        return result

    def short_stencil(self, number, turn, x, count, full):
        planes = [self.wave_tiles(number, turn + 1, x - 1 + i) for i in range(count + 2)]
        result = []
        for i in range(1, count + 1):
            before, now, after = planes[i - 1 : i + 2]
            slope_x = [a - b for a, b in zip(after, before)]
            _, slope_z, sums_y, sums_z = self.plane_part(now)
            slope_xy, slope_xz, _, _ = self.plane_part(slope_x)
            next_z, previous_z = self.next_y(slope_z), self.previous_y(slope_z)
            axis, laplace = [], []
            for tile in range(self.tiles):
                axx, ayy, azz, axy, axz, ayz = [
                    self.factors[factor, x - 1 + i, tile] for factor in range(3, 9)
                ]
                double = now[tile] + now[tile]
                sum_x = after[tile] + before[tile]
                sum_y, sum_z = sums_y[tile], sums_z[tile]
                straight = ((axx * sum_x + ayy * sum_y) + azz * sum_z) - double
                mixed = (axy * slope_xy[tile] + axz * slope_xz[tile]) + ayz * (
                    next_z[tile] - previous_z[tile]
                )
                axis.append(straight + mixed)
                if full:
                    laplace.append(((sum_x + sum_y) + sum_z) - 3.0 * double)
            result.append((now, axis, laplace))
        return result

    def step(self, turn, x, count):
        tiles, factors = range(self.tiles), self.factors
        for pair in range(2):
            p_number, q_number = 2 * pair, 2 * pair + 1
            stencil = self.stencil if count > RIM else self.short_stencil
            of_q = stencil(q_number, turn, x, count, False)
            of_p = stencil(p_number, turn, x, count, True)
            for i in range(count):
                now = x + i
                q, q_axis, _ = of_q[i]
                p, p_axis, p_laplace = of_p[i]
                p_held = self.wave_tiles(p_number, turn, now)
                q_held = self.wave_tiles(q_number, turn, now)
                for tile in tiles:
                    velocity, with_e, with_d = [factors[number, now, tile] for number in range(3)]
                    across = p_laplace[tile] - p_axis[tile]
                    p_next = ((p[tile] + p[tile]) - p_held[tile]) + (
                        with_e * across + with_d * q_axis[tile]
                    )
                    q_next = ((q[tile] + q[tile]) - q_held[tile]) + (
                        with_d * across + velocity * q_axis[tile]
                    )
                    if pair == 1:
                        shift = lax.rem(REC_DEPTH - now + self.depth, self.depth)
                        moved = pltpu.roll(self.planes[STEPS - 1 - turn, tile], shift, 1)
                        p_next = p_next + jnp.where(self.at_depth, moved, 0.0)
                    self.waves[turn][p_number, now, tile] = p_next
                    if pair == 1 or turn < STEPS - 1:
                        self.waves[turn][q_number, now, tile] = q_next


def repeat(count, body):
    def run(i, carry):
        body(i)
        return carry

    lax.fori_loop(0, count, run, 0)


def inner_kernel(wide, planes, own, *refs):
    steps = Steps(wide, planes, refs[:STEPS], refs[STEPS])
    natural = refs[STEPS + 1]
    cells_x, cells_y, tiles = steps.cells_x, own.shape[2], steps.tiles

    def rim_rows(i):
        for x in [4 * i + k for k in range(4)]:
            raw = [wide[FIELDS + number, RIM + x, cells_y:, :] for number in range(5)]
            for number, value in enumerate(factors_of(*raw)):
                natural[number, x, cells_y:, :] = value
                natural[number, x, :cells_y, :] = own[number, x]

    def in_step_order(i):
        for x in [2 * i + k for k in range(2)]:
            for number in range(FACTORS):
                for tile in range(tiles):
                    steps.factors[number, RIM + x, tile] = natural[
                        number, x, pl.ds(tile, SUBLANES, stride=tiles), :
                    ]

    repeat(cells_x // 4, rim_rows)
    repeat(cells_x // 2, in_step_order)
    for turn in range(STEPS):
        first, last = RIM + 1 + turn, RIM + cells_x - 1 - turn
        half = (last - first) // 2
        repeat(2, lambda i, turn=turn, first=first, half=half: steps.step(turn, first + half * i, half))


def outer_kernel(*refs):
    x_a, x_b, c_a, c_b, planes = refs[1:6]
    refs = refs[6 + STEPS + 1 :]
    wide, waves, factors = refs[0], refs[1 : 1 + STEPS], refs[1 + STEPS]
    outputs, sems = refs[-4:-1], refs[-1]
    cells_x, cells_y, depth = outputs[0].shape
    odd_x = is_odd("gx")
    for number, width, place in x_parts()[0]:
        low, high = RIM - width, RIM + cells_x
        for begin, side, corner in (
            (jnp.where(odd_x, low, high), x_a, c_a),
            (jnp.where(odd_x, high, low), x_b, c_b),
        ):
            wide[number, pl.ds(begin, width), :cells_y, :] = side[place : place + width]
            wide[number, pl.ds(begin, width), cells_y:, :] = corner[place : place + width]

    steps = Steps(wide, planes, waves, factors)

    for x in range(SLIM):
        steps.make_factors(RIM - SLIM + x)
        steps.make_factors(RIM + cells_x + x)
    for turn in range(STEPS):
        steps.step(turn, turn + 1, RIM)
        steps.step(turn, RIM + cells_x - 1 - turn, RIM)

    tiles = steps.tiles

    def finish(i):
        x = RIM + i
        total = None
        for back in range(STEPS + 1):
            source = steps.wave_tiles(0, 1 + STEPS - back, x)
            receiver = steps.wave_tiles(2, 1 + back, x)
            product = [a * b for a, b in zip(source, receiver)]
            total = product if total is None else [a + b for a, b in zip(total, product)]
        for out, value in (
            (0, total),
            (1, steps.wave_tiles(2, 1 + STEPS, x)),
            (2, steps.wave_tiles(3, 1 + STEPS, x)),
        ):
            for tile in range(tiles):
                wide[out, x, pl.ds(tile, SUBLANES, stride=tiles), :] = value[tile]

    moves = []
    quarter = cells_x // QUARTERS
    for part in range(QUARTERS):
        begin = part * quarter
        repeat(quarter, lambda i, begin=begin: finish(begin + i))
        for out, ref in enumerate(outputs):
            source = wide.at[out, pl.ds(RIM + begin, quarter), pl.ds(0, cells_y)]
            move = pltpu.make_async_copy(source, ref.at[pl.ds(begin, quarter)], sems.at[out, part])
            move.start()
            moves.append(move)
    for move in moves:
        move.wait()


def inner(wide, planes, own):
    _, planes_x, rows, depth = wide.shape
    tile = (planes_x, rows // SUBLANES, SUBLANES, depth)
    return pl.pallas_call(
        inner_kernel,
        out_shape=[vmem_out(4, *tile)] * STEPS + [vmem_out(FACTORS, *tile)],
        in_specs=in_vmem(3),
        out_specs=in_vmem(STEPS + 1),
        scratch_shapes=[pltpu.VMEM((FACTORS, own.shape[1], rows, depth), jnp.float32)],
        compiler_params=PARAMS,
        name="inner_steps",
    )(pinned(wide, pltpu.VMEM), planes, pinned(own, pltpu.VMEM))


def outer(wide, rims, planes, state, cells_x, cells_y):
    out = pltpu.HBM((cells_x, cells_y, wide.shape[-1]), jnp.float32)
    kept = [vmem_out(*wide.shape)] + [vmem_out(*value.shape) for value in state]
    first = len(rims) + 2
    aliases = {0: 0} | {first + number: 1 + number for number in range(len(state))}
    return pl.pallas_call(
        outer_kernel,
        out_shape=kept + [out] * 3,
        in_specs=in_vmem(first + len(state)),
        out_specs=in_vmem(len(kept)) + [pl.BlockSpec(memory_space=pltpu.HBM)] * 3,
        input_output_aliases=aliases,
        scratch_shapes=[pltpu.SemaphoreType.DMA((3, QUARTERS))],
        compiler_params=PARAMS,
        name="outer_steps",
    )(
        pinned(wide, pltpu.VMEM),
        *rims,
        planes,
        *(pinned(value, pltpu.VMEM) for value in state),
    )[-3:]


def bits_of(axis):
    size = lax.axis_size(axis)
    return [1 << bit for bit in range(size.bit_length() - 1)] if size & (size - 1) == 0 else None


def doubled(windows, axis, bit):
    pairs = [(i, i ^ bit) for i in range(lax.axis_size(axis))]
    return jnp.concatenate([windows, lax.ppermute(windows, axis, pairs)], axis=0)


def inject_kernel(samples, cells_x, cells_y, gathered, table_x, table_y, planes, weights, picks):
    size_y = lax.axis_size("gy")
    own_x, own_y = lax.axis_index("gx"), lax.axis_index("gy")
    rows = cells_y + 2 * RIM
    tiles = rows // SUBLANES
    wide_x = picks.shape[0]
    in_row = LANES // samples
    place = lax.broadcasted_iota(jnp.int32, (rows, LANES), 0)
    row = tiles * lax.rem(place, SUBLANES) + lax.div(place, SUBLANES)
    y_global = own_y * cells_y + jnp.where(row < cells_y + RIM, row, row - rows)
    x_global = own_x * cells_x - RIM + lax.broadcasted_iota(jnp.int32, (wide_x, LANES), 0)
    lane = lax.broadcasted_iota(jnp.int32, (1, LANES), 1)
    bits_x, bits_y = bits_of("gx"), bits_of("gy")

    def source(place):
        device_x, device_y = own_x, own_y
        for number, bit in enumerate(bits_x):
            if place >> number & 1:
                device_x = jnp.bitwise_xor(device_x, bit)
        for number, bit in enumerate(bits_y):
            if place >> (len(bits_x) + number) & 1:
                device_y = jnp.bitwise_xor(device_y, bit)
        return device_x * size_y + device_y

    for group in range(gathered.shape[0] // in_row):
        at_x = at_y = jnp.zeros((1, LANES), jnp.int32)
        window = jnp.zeros((STEPS, LANES), jnp.float32)
        for part in range(in_row):
            place = group * in_row + part
            device = source(place)
            here = (lane >= part * samples) & (lane < (part + 1) * samples)
            shift = lax.rem((part - lax.rem(device, in_row)) * samples + LANES, LANES)
            table_row = pl.ds(lax.div(device, in_row), 1)
            at_x = jnp.where(here, pltpu.roll(table_x[table_row, :], shift, 1), at_x)
            at_y = jnp.where(here, pltpu.roll(table_y[table_row, :], shift, 1), at_y)
            moved = gathered[place]
            if part:
                moved = pltpu.roll(moved, part * samples, 1)
            window = jnp.where(here, moved, window)
        span = slice(group * LANES, (group + 1) * LANES)
        picks[:, span] = (at_x == x_global).astype(jnp.float32)
        is_y = at_y == y_global
        for sample in range(STEPS):
            weights[sample * rows : (sample + 1) * rows, span] = jnp.where(
                is_y, window[sample : sample + 1], 0.0
            )
    rest = weights[...]
    pick = picks[...].astype(jnp.bfloat16)
    total = None
    for _ in range(3):
        part = rest.astype(jnp.bfloat16)
        rest = rest - part.astype(jnp.float32)
        product = lax.dot_general(
            part, pick, (((1,), (1,)), ((), ())), preferred_element_type=jnp.float32
        )
        total = product if total is None else total + product
    planes[...] = jnp.zeros_like(planes)
    for sample in range(STEPS):
        for tile in range(tiles):
            begin = sample * rows + tile * SUBLANES
            planes[sample, tile, :, :wide_x] = total[begin : begin + SUBLANES]


def injected(gathered, receiver_x, receiver_y, samples, cells_x, cells_y, depth):
    rows = cells_y + 2 * RIM
    receivers = receiver_x.shape[0]
    wide_x = -(-(cells_x + 2 * RIM) // 32) * 32
    return pl.pallas_call(
        functools.partial(inject_kernel, samples, cells_x, cells_y),
        out_shape=vmem_out(STEPS, rows // SUBLANES, SUBLANES, depth),
        in_specs=in_vmem(3),
        out_specs=in_vmem(1)[0],
        scratch_shapes=[
            pltpu.VMEM((STEPS * rows, receivers), jnp.float32),
            pltpu.VMEM((wide_x, receivers), jnp.float32),
        ],
        compiler_params=PARAMS,
        name="inject",
    )(gathered, receiver_x.reshape(-1, LANES), receiver_y.reshape(-1, LANES))


def per_device(
    src_p_prev,
    src_p_now,
    src_q_prev,
    src_q_now,
    rec_p_next,
    rec_p_now,
    rec_q_next,
    rec_q_now,
    velocity_term,
    epsilon,
    delta,
    tilt,
    azimuth,
    traces,
    receiver_x,
    receiver_y,
    segment_start,
):
    blocks = (
        src_p_prev,
        src_p_now,
        src_q_prev,
        src_q_now,
        rec_p_next,
        rec_p_now,
        rec_q_next,
        rec_q_now,
        velocity_term,
        epsilon,
        delta,
        tilt,
        azimuth,
    )
    cells_x, cells_y, depth = src_p_now.shape
    wide, y_a, y_b, window = pack(blocks, traces, segment_start)
    y_a, y_b = swap(y_a, "gy", 0), swap(y_b, "gy", 1)
    wide, x_a, x_b = pack_x(wide, window)
    x_a, x_b = swap(x_a, "gx", 0), swap(x_b, "gx", 1)
    windows = jnp.concatenate([window, x_a[x_parts()[1] :, :STEPS, :]], axis=0)
    for bit in bits_of("gx")[1:]:
        windows = doubled(windows, "gx", bit)
    own = own_factors(wide, windows)
    for bit in bits_of("gy")[:-1]:
        windows = doubled(windows, "gy", bit)
    wide, c_a, c_b = corners(wide, y_a, y_b, windows, pinned(own, pltpu.VMEM))
    for bit in bits_of("gy")[-1:]:
        windows = doubled(windows, "gy", bit)
    c_a, c_b = swap(c_a, "gx", 0), swap(c_b, "gx", 1)
    planes = injected(
        windows, receiver_x, receiver_y, traces.shape[1], cells_x, cells_y, depth
    )
    state = inner(wide, planes, own)
    return tuple(outer(wide, (x_a, x_b, c_a, c_b), planes, state, cells_x, cells_y))


def solution(mesh):
    state = P(("shot", "gx"), "gy", None)
    earth = P("gx", "gy", None)
    return jax.shard_map(
        per_device,
        mesh=mesh,
        in_specs=(state,) * FIELDS + (earth,) * 5 + (P("shot", ("gx", "gy")), P(), P(), P()),
        out_specs=(state,) * 3,
        check_vma=False,
    )
```

```python
import functools

import jax
import jax.numpy as jnp
from jax import lax
from jax.experimental import pallas as pl
from jax.experimental.pallas import tpu as pltpu
from jax.sharding import PartitionSpec as P

STEPS = 4
REC_DEPTH = 4
RIM = STEPS
QUARTERS = 4
FIELDS = 8
SUBLANES = 8
LANES = 128
PARAMS = pltpu.CompilerParams(vmem_limit_bytes=16 * 1024 * 1024)
PACK_PARAMS = pltpu.CompilerParams(vmem_limit_bytes=48 * 1024 * 1024)


def in_vmem(count):
    return [pl.BlockSpec(memory_space=pltpu.VMEM)] * count


def is_odd(axis):
    return lax.rem(lax.axis_index(axis), 2) == 1


def swap(value, axis, first):
    size = lax.axis_size(axis)
    lower = range(first, size - 1, 2)
    pairs = [(i, i + 1) for i in lower] + [(i + 1, i) for i in lower]
    return lax.ppermute(value, axis, pairs)


NOW = (1, 3, 5, 7)
REST = (0, 2, 4, 6, 8, 9, 10, 11, 12)
SLIM = RIM - 1


def y_slots():
    slots = [((number, 0, RIM, 0),) for number in NOW]
    whole = len(REST) - len(REST) // RIM
    for place in range(whole):
        parts = [(REST[place], 0, SLIM, 0)]
        guest = whole + place // SLIM
        if guest < len(REST):
            parts.append((REST[guest], place % SLIM, 1, SLIM))
        slots.append(tuple(parts))
    return slots


def each_y_part(slots, high):
    for slot, parts in enumerate(slots):
        for number, row, rows, place in parts:
            if not high:
                yield slot, number, row, place, rows
            else:
                width = RIM if number in NOW else SLIM
                yield slot, number, RIM - width + row, 0 if place else RIM - rows, rows


def x_parts():
    parts, place = [], 0
    for number in NOW:
        parts.append((number, RIM, place))
        place += RIM
    for number in REST:
        parts.append((number, SLIM, place))
        place += SLIM
    return parts, place


def pinned(value, space):
    return pltpu.with_memory_space_constraint(value, space)


def vmem_out(*shape):
    return pltpu.VMEM(shape, jnp.float32)


def pack_kernel(count, *refs):
    blocks, traces, start = refs[:count], refs[count], refs[count + 1]
    wide, y_a, y_b, window, held, sems = refs[count + 2 :]
    cells_x, cells_y = blocks[0].shape[:2]
    core_x = pl.ds(RIM, cells_x)
    moves = [
        pltpu.make_async_copy(block, wide.at[number, core_x, pl.ds(0, cells_y)], sems.at[number])
        for number, block in enumerate(blocks)
    ]
    moves.append(pltpu.make_async_copy(traces, held, sems.at[count]))
    for move in moves:
        move.start()
    odd_y = is_odd("gy")
    begin = start[0]
    samples = traces.shape[1]
    window[...] = jnp.zeros_like(window)
    for number in range(count):
        moves[number].wait()

        def put_y(low, high, number=number):
            for out, is_high, base in ((low, False, 0), (high, True, cells_y - RIM)):
                for slot, part, row, place, length in each_y_part(y_slots(), is_high):
                    if part == number:
                        out[slot, :, place : place + length, :] = wide[
                            number, RIM : RIM + cells_x, base + row : base + row + length, :
                        ]

        @pl.when(odd_y)
        def _(put_y=put_y):
            put_y(y_a, y_b)

        @pl.when(jnp.logical_not(odd_y))
        def _(put_y=put_y):
            put_y(y_b, y_a)

    moves[count].wait()
    for sample in range(STEPS):
        window[0, sample : sample + 1, :samples] = held[pl.ds(begin + sample, 1), :]


def pack(blocks, traces, segment_start):
    cells_x, cells_y, depth = blocks[0].shape
    count = len(blocks)
    rim_y = vmem_out(len(y_slots()), cells_x, RIM, depth)
    wide = vmem_out(count, cells_x + 2 * RIM + 2, cells_y + 2 * RIM, depth)
    return pl.pallas_call(
        functools.partial(pack_kernel, count),
        out_shape=[wide, rim_y, rim_y, vmem_out(1, STEPS, LANES)],
        in_specs=[pl.BlockSpec(memory_space=pltpu.HBM)] * (count + 1)
        + [pl.BlockSpec(memory_space=pltpu.SMEM)],
        out_specs=in_vmem(4),
        scratch_shapes=[
            pltpu.VMEM(traces.shape, jnp.float32),
            pltpu.SemaphoreType.DMA((count + 1,)),
        ],
        compiler_params=PACK_PARAMS,
        name="pack_y_rims",
    )(*(pinned(value, pltpu.HBM) for value in (*blocks, traces)), segment_start)


def pack_x_kernel(_, window, wide, x_a, x_b):
    cells_x, cells_y = wide.shape[1] - 2 * RIM - 2, wide.shape[2] - 2 * RIM
    odd_x = is_odd("gx")
    parts, total = x_parts()
    for number, width, place in parts:
        first, last = RIM, RIM + cells_x - width
        for out, begin in ((x_a, jnp.where(odd_x, first, last)), (x_b, jnp.where(odd_x, last, first))):
            out[place : place + width] = wide[number, pl.ds(begin, width), :cells_y, :]
    x_a[total] = jnp.zeros_like(x_a[total])
    x_a[total, :STEPS, :] = window[0]


def pack_x(wide, window):
    _, _, rows, depth = wide.shape
    total = x_parts()[1]
    return pl.pallas_call(
        pack_x_kernel,
        out_shape=[
            vmem_out(*wide.shape),
            vmem_out(total + 1, rows - 2 * RIM, depth),
            vmem_out(total, rows - 2 * RIM, depth),
        ],
        in_specs=in_vmem(2),
        out_specs=in_vmem(3),
        input_output_aliases={0: 0},
        compiler_params=PARAMS,
        name="pack_x_rims",
    )(pinned(wide, pltpu.VMEM), window)


def corner_kernel(_, y_a, y_b, __, ___, ____, wide, c_a, c_b):
    cells_x = y_a.shape[1]
    cells_y = wide.shape[2] - 2 * RIM
    odd_x, odd_y = is_odd("gx"), is_odd("gy")

    def place_y(low, high):
        for rim, is_high, base in ((high, False, cells_y), (low, True, cells_y + RIM)):
            for slot, number, row, place, length in each_y_part(y_slots(), is_high):
                wide[number, RIM : RIM + cells_x, base + row : base + row + length, :] = rim[
                    slot, :, place : place + length, :
                ]

    @pl.when(odd_y)
    def _():
        place_y(y_a, y_b)

    @pl.when(jnp.logical_not(odd_y))
    def _():
        place_y(y_b, y_a)

    for number, width, place in x_parts()[0]:
        first, last = RIM, RIM + cells_x - width
        for out, begin in ((c_a, jnp.where(odd_x, first, last)), (c_b, jnp.where(odd_x, last, first))):
            out[place : place + width] = wide[number, pl.ds(begin, width), cells_y:, :]


def corners(wide, y_a, y_b, *earlier):
    corner = vmem_out(x_parts()[1], 2 * RIM, wide.shape[-1])
    return pl.pallas_call(
        corner_kernel,
        out_shape=[vmem_out(*wide.shape), corner, corner],
        in_specs=in_vmem(6),
        out_specs=in_vmem(3),
        input_output_aliases={0: 0},
        compiler_params=PARAMS,
        name="pack_corners",
    )(pinned(wide, pltpu.VMEM), y_a, y_b, *earlier)


def sine_cosine(angle):
    square = angle * angle
    sine = 1.0 / 6227020800.0
    for term in (-1.0 / 39916800.0, 1.0 / 362880.0, -1.0 / 5040.0, 1.0 / 120.0, -1.0 / 6.0, 1.0):
        sine = sine * square + term
    cosine = 1.0 / 479001600.0
    for term in (-1.0 / 3628800.0, 1.0 / 40320.0, -1.0 / 720.0, 1.0 / 24.0, -0.5, 1.0):
        cosine = cosine * square + term
    return sine * angle, cosine


def factors_of(velocity, epsilon, delta, tilt, azimuth):
    f_e = 1.0 + 2.0 * epsilon
    f_d = jnp.sqrt(1.0 + 2.0 * delta)
    sin_tilt, cos_tilt = sine_cosine(tilt)
    sin_half, cos_half = sine_cosine(0.5 * azimuth)
    sin_azim = 2.0 * sin_half * cos_half
    cos_azim = 1.0 - 2.0 * sin_half * sin_half
    sin_square = sin_tilt * sin_tilt
    half_tilt = 0.5 * sin_tilt * cos_tilt
    along_x = sin_square * cos_azim
    return (
        velocity,
        velocity * f_e,
        velocity * f_d,
        along_x * cos_azim,
        sin_square * sin_azim * sin_azim,
        cos_tilt * cos_tilt,
        0.5 * along_x * sin_azim,
        half_tilt * cos_azim,
        half_tilt * sin_azim,
    )


FACTORS = 9


def own_kernel(wide, _, own):
    _, cells_x, rows, _ = own.shape
    cells_y = rows - 2 * RIM

    def body(i):
        for x in [4 * i + k for k in range(4)]:
            raw = [wide[FIELDS + number, RIM + x, :cells_y, :] for number in range(5)]
            for number, value in enumerate(factors_of(*raw)):
                own[number, x, :cells_y, :] = value

    repeat(cells_x // 4, body)


def own_factors(wide, earlier):
    _, planes_x, rows, depth = wide.shape
    return pl.pallas_call(
        own_kernel,
        out_shape=vmem_out(FACTORS, planes_x - 2 * RIM - 2, rows, depth),
        in_specs=in_vmem(2),
        out_specs=in_vmem(1)[0],
        compiler_params=PARAMS,
        name="own_factors",
    )(pinned(wide, pltpu.VMEM), earlier)


class Steps:
    def __init__(self, wide, planes, waves, factors):
        self.wide, self.planes, self.waves, self.factors = wide, planes, waves, factors
        self.count, _, rows, self.depth = wide.shape
        self.tiles = rows // SUBLANES
        self.cells_x = wide.shape[1] - 2 * RIM - 2
        lane = lax.broadcasted_iota(jnp.int32, (SUBLANES, self.depth), 1)
        self.not_last, self.not_first = lane < self.depth - 1, lane > 0
        self.at_depth = lane == REC_DEPTH

    def wide_tiles(self, number, x):
        return [
            self.wide[number, x, pl.ds(tile, SUBLANES, stride=self.tiles), :]
            for tile in range(self.tiles)
        ]

    def wave_tiles(self, number, slot, x):
        if slot < 2:
            return self.wide_tiles(2 * number + slot, x)
        return [self.waves[slot - 2][number, x, tile] for tile in range(self.tiles)]

    def next_y(self, value):
        return value[1:] + [pltpu.roll(value[0], SUBLANES - 1, 0)]

    def previous_y(self, value):
        return [pltpu.roll(value[-1], 1, 0)] + value[:-1]

    def make_factors(self, x):
        raw = [self.wide_tiles(FIELDS + number, x) for number in range(self.count - FIELDS)]
        for tile in range(self.tiles):
            for number, value in enumerate(factors_of(*[value[tile] for value in raw])):
                self.factors[number, x, tile] = value

    def sides_z(self, value):
        above = [jnp.where(self.not_last, pltpu.roll(u, self.depth - 1, 1), 0.0) for u in value]
        below = [jnp.where(self.not_first, pltpu.roll(u, 1, 1), 0.0) for u in value]
        return above, below

    def plane_part(self, now):
        above, below = self.sides_z(now)
        after, before = self.next_y(now), self.previous_y(now)
        pairs_z, pairs_y = list(zip(above, below)), list(zip(after, before))
        return (
            [a - b for a, b in pairs_y],
            [a - b for a, b in pairs_z],
            [a + b for a, b in pairs_y],
            [a + b for a, b in pairs_z],
        )

    def stencil(self, number, turn, x, count, full):
        planes = [self.wave_tiles(number, turn + 1, x - 1 + i) for i in range(count + 2)]
        parts = [self.plane_part(planes[0]), self.plane_part(planes[1])]
        result = []
        for i in range(1, count + 1):
            parts.append(self.plane_part(planes[i + 1]))
            slope_y, slope_z, sums_y, sums_z = parts[i]
            next_z, previous_z = self.next_y(slope_z), self.previous_y(slope_z)
            axis, laplace = [], []
            for tile in range(self.tiles):
                axx, ayy, azz, axy, axz, ayz = [
                    self.factors[factor, x - 1 + i, tile] for factor in range(3, 9)
                ]
                now = planes[i][tile]
                double = now + now
                sum_x = planes[i + 1][tile] + planes[i - 1][tile]
                sum_y, sum_z = sums_y[tile], sums_z[tile]
                straight = ((axx * sum_x + ayy * sum_y) + azz * sum_z) - double
                mixed = (
                    axy * (parts[i + 1][0][tile] - parts[i - 1][0][tile])
                    + axz * (parts[i + 1][1][tile] - parts[i - 1][1][tile])
                ) + ayz * (next_z[tile] - previous_z[tile])
                axis.append(straight + mixed)
                if full:
                    laplace.append(((sum_x + sum_y) + sum_z) - 3.0 * double)
            result.append((planes[i], axis, laplace))
        return result

    def short_stencil(self, number, turn, x, count, full):
        planes = [self.wave_tiles(number, turn + 1, x - 1 + i) for i in range(count + 2)]
        result = []
        for i in range(1, count + 1):
            before, now, after = planes[i - 1 : i + 2]
            slope_x = [a - b for a, b in zip(after, before)]
            _, slope_z, sums_y, sums_z = self.plane_part(now)
            slope_xy, slope_xz, _, _ = self.plane_part(slope_x)
            next_z, previous_z = self.next_y(slope_z), self.previous_y(slope_z)
            axis, laplace = [], []
            for tile in range(self.tiles):
                axx, ayy, azz, axy, axz, ayz = [
                    self.factors[factor, x - 1 + i, tile] for factor in range(3, 9)
                ]
                double = now[tile] + now[tile]
                sum_x = after[tile] + before[tile]
                sum_y, sum_z = sums_y[tile], sums_z[tile]
                straight = ((axx * sum_x + ayy * sum_y) + azz * sum_z) - double
                mixed = (axy * slope_xy[tile] + axz * slope_xz[tile]) + ayz * (
                    next_z[tile] - previous_z[tile]
                )
                axis.append(straight + mixed)
                if full:
                    laplace.append(((sum_x + sum_y) + sum_z) - 3.0 * double)
            result.append((now, axis, laplace))
        return result

    def step(self, turn, x, count):
        tiles, factors = range(self.tiles), self.factors
        for pair in range(2):
            p_number, q_number = 2 * pair, 2 * pair + 1
            stencil = self.stencil if count > RIM else self.short_stencil
            of_q = stencil(q_number, turn, x, count, False)
            of_p = stencil(p_number, turn, x, count, True)
            for i in range(count):
                now = x + i
                q, q_axis, _ = of_q[i]
                p, p_axis, p_laplace = of_p[i]
                p_held = self.wave_tiles(p_number, turn, now)
                q_held = self.wave_tiles(q_number, turn, now)
                for tile in tiles:
                    velocity, with_e, with_d = [factors[number, now, tile] for number in range(3)]
                    across = p_laplace[tile] - p_axis[tile]
                    p_next = ((p[tile] + p[tile]) - p_held[tile]) + (
                        with_e * across + with_d * q_axis[tile]
                    )
                    q_next = ((q[tile] + q[tile]) - q_held[tile]) + (
                        with_d * across + velocity * q_axis[tile]
                    )
                    if pair == 1:
                        shift = lax.rem(REC_DEPTH - now + self.depth, self.depth)
                        moved = pltpu.roll(self.planes[STEPS - 1 - turn, tile], shift, 1)
                        p_next = p_next + jnp.where(self.at_depth, moved, 0.0)
                    self.waves[turn][p_number, now, tile] = p_next
                    if pair == 1 or turn < STEPS - 1:
                        self.waves[turn][q_number, now, tile] = q_next


def repeat(count, body):
    def run(i, carry):
        body(i)
        return carry

    lax.fori_loop(0, count, run, 0)


def inner_kernel(wide, planes, _, *refs):
    steps = Steps(wide, planes, refs[:STEPS], refs[STEPS])
    natural = refs[STEPS + 1]
    cells_x, cells_y, tiles = steps.cells_x, natural.shape[2] - 2 * RIM, steps.tiles

    def rim_rows(i):
        for x in [4 * i + k for k in range(4)]:
            raw = [wide[FIELDS + number, RIM + x, cells_y:, :] for number in range(5)]
            for number, value in enumerate(factors_of(*raw)):
                natural[number, x, cells_y:, :] = value

    def in_step_order(i):
        for x in [2 * i + k for k in range(2)]:
            for number in range(FACTORS):
                for tile in range(tiles):
                    steps.factors[number, RIM + x, tile] = natural[
                        number, x, pl.ds(tile, SUBLANES, stride=tiles), :
                    ]

    repeat(cells_x // 4, rim_rows)
    repeat(cells_x // 2, in_step_order)
    for turn in range(STEPS):
        first, last = RIM + 1 + turn, RIM + cells_x - 1 - turn
        half = (last - first) // 2
        repeat(2, lambda i, turn=turn, first=first, half=half: steps.step(turn, first + half * i, half))


def outer_kernel(*refs):
    x_a, x_b, c_a, c_b, planes = refs[1:6]
    refs = refs[6 + STEPS + 1 :]
    wide, waves, factors = refs[0], refs[1 : 1 + STEPS], refs[1 + STEPS]
    outputs, sems = refs[-4:-1], refs[-1]
    cells_x, cells_y, depth = outputs[0].shape
    odd_x = is_odd("gx")
    for number, width, place in x_parts()[0]:
        low, high = RIM - width, RIM + cells_x
        for begin, side, corner in (
            (jnp.where(odd_x, low, high), x_a, c_a),
            (jnp.where(odd_x, high, low), x_b, c_b),
        ):
            wide[number, pl.ds(begin, width), :cells_y, :] = side[place : place + width]
            wide[number, pl.ds(begin, width), cells_y:, :] = corner[place : place + width]

    steps = Steps(wide, planes, waves, factors)

    for x in range(SLIM):
        steps.make_factors(RIM - SLIM + x)
        steps.make_factors(RIM + cells_x + x)
    for turn in range(STEPS):
        steps.step(turn, turn + 1, RIM)
        steps.step(turn, RIM + cells_x - 1 - turn, RIM)

    tiles = steps.tiles

    def finish(i):
        x = RIM + i
        total = None
        for back in range(STEPS + 1):
            source = steps.wave_tiles(0, 1 + STEPS - back, x)
            receiver = steps.wave_tiles(2, 1 + back, x)
            product = [a * b for a, b in zip(source, receiver)]
            total = product if total is None else [a + b for a, b in zip(total, product)]
        for out, value in (
            (0, total),
            (1, steps.wave_tiles(2, 1 + STEPS, x)),
            (2, steps.wave_tiles(3, 1 + STEPS, x)),
        ):
            for tile in range(tiles):
                wide[out, x, pl.ds(tile, SUBLANES, stride=tiles), :] = value[tile]

    moves = []
    quarter = cells_x // QUARTERS
    for part in range(QUARTERS):
        begin = part * quarter
        repeat(quarter, lambda i, begin=begin: finish(begin + i))
        for out, ref in enumerate(outputs):
            source = wide.at[out, pl.ds(RIM + begin, quarter), pl.ds(0, cells_y)]
            move = pltpu.make_async_copy(source, ref.at[pl.ds(begin, quarter)], sems.at[out, part])
            move.start()
            moves.append(move)
    for move in moves:
        move.wait()


def inner(wide, planes, own):
    _, planes_x, rows, depth = wide.shape
    tile = (planes_x, rows // SUBLANES, SUBLANES, depth)
    return pl.pallas_call(
        inner_kernel,
        out_shape=[vmem_out(4, *tile)] * STEPS
        + [vmem_out(FACTORS, *tile), vmem_out(*own.shape)],
        in_specs=in_vmem(3),
        out_specs=in_vmem(STEPS + 2),
        input_output_aliases={2: STEPS + 1},
        compiler_params=PARAMS,
        name="inner_steps",
    )(pinned(wide, pltpu.VMEM), planes, pinned(own, pltpu.VMEM))[:-1]


def outer(wide, rims, planes, state, cells_x, cells_y):
    out = pltpu.HBM((cells_x, cells_y, wide.shape[-1]), jnp.float32)
    kept = [vmem_out(*wide.shape)] + [vmem_out(*value.shape) for value in state]
    first = len(rims) + 2
    aliases = {0: 0} | {first + number: 1 + number for number in range(len(state))}
    return pl.pallas_call(
        outer_kernel,
        out_shape=kept + [out] * 3,
        in_specs=in_vmem(first + len(state)),
        out_specs=in_vmem(len(kept)) + [pl.BlockSpec(memory_space=pltpu.HBM)] * 3,
        input_output_aliases=aliases,
        scratch_shapes=[pltpu.SemaphoreType.DMA((3, QUARTERS))],
        compiler_params=PARAMS,
        name="outer_steps",
    )(
        pinned(wide, pltpu.VMEM),
        *rims,
        planes,
        *(pinned(value, pltpu.VMEM) for value in state),
    )[-3:]


def bits_of(axis):
    size = lax.axis_size(axis)
    return [1 << bit for bit in range(size.bit_length() - 1)] if size & (size - 1) == 0 else None


def doubled(windows, axis, bit):
    pairs = [(i, i ^ bit) for i in range(lax.axis_size(axis))]
    return jnp.concatenate([windows, lax.ppermute(windows, axis, pairs)], axis=0)


def table_kernel(samples, cells_x, table_x, table_y, picks, rows_y):
    size_y = lax.axis_size("gy")
    own_x, own_y = lax.axis_index("gx"), lax.axis_index("gy")
    wide_x = picks.shape[0]
    in_row = LANES // samples
    x_global = own_x * cells_x - RIM + lax.broadcasted_iota(jnp.int32, (wide_x, LANES), 0)
    lane = lax.broadcasted_iota(jnp.int32, (1, LANES), 1)
    bits_x, bits_y = bits_of("gx"), bits_of("gy")

    def source(place):
        device_x, device_y = own_x, own_y
        for number, bit in enumerate(bits_x):
            if place >> number & 1:
                device_x = jnp.bitwise_xor(device_x, bit)
        for number, bit in enumerate(bits_y):
            if place >> (len(bits_x) + number) & 1:
                device_y = jnp.bitwise_xor(device_y, bit)
        return device_x * size_y + device_y

    for group in range(rows_y.shape[0]):
        at_x = at_y = jnp.zeros((1, LANES), jnp.int32)
        for part in range(in_row):
            device = source(group * in_row + part)
            here = (lane >= part * samples) & (lane < (part + 1) * samples)
            shift = lax.rem((part - lax.rem(device, in_row)) * samples + LANES, LANES)
            table_row = pl.ds(lax.div(device, in_row), 1)
            at_x = jnp.where(here, pltpu.roll(table_x[table_row, :], shift, 1), at_x)
            at_y = jnp.where(here, pltpu.roll(table_y[table_row, :], shift, 1), at_y)
        span = slice(group * LANES, (group + 1) * LANES)
        picks[:, span] = (at_x == x_global).astype(jnp.float32)
        rows_y[group : group + 1, :] = at_y


def receiver_tables(receiver_x, receiver_y, samples, cells_x):
    receivers = receiver_x.shape[0]
    wide_x = -(-(cells_x + 2 * RIM) // 32) * 32
    return pl.pallas_call(
        functools.partial(table_kernel, samples, cells_x),
        out_shape=[
            vmem_out(wide_x, receivers),
            pltpu.VMEM((receivers // LANES, LANES), jnp.int32),
        ],
        in_specs=in_vmem(2),
        out_specs=in_vmem(2),
        compiler_params=PARAMS,
        name="receiver_tables",
    )(receiver_x.reshape(-1, LANES), receiver_y.reshape(-1, LANES))


def inject_kernel(samples, cells_y, gathered, picks, rows_y, planes, weights):
    own_y = lax.axis_index("gy")
    rows = cells_y + 2 * RIM
    tiles = rows // SUBLANES
    wide_x = picks.shape[0]
    in_row = LANES // samples
    place = lax.broadcasted_iota(jnp.int32, (rows, LANES), 0)
    row = tiles * lax.rem(place, SUBLANES) + lax.div(place, SUBLANES)
    y_global = own_y * cells_y + jnp.where(row < cells_y + RIM, row, row - rows)
    lane = lax.broadcasted_iota(jnp.int32, (1, LANES), 1)
    for group in range(rows_y.shape[0]):
        window = gathered[group * in_row]
        for part in range(1, in_row):
            here = (lane >= part * samples) & (lane < (part + 1) * samples)
            moved = pltpu.roll(gathered[group * in_row + part], part * samples, 1)
            window = jnp.where(here, moved, window)
        span = slice(group * LANES, (group + 1) * LANES)
        is_y = rows_y[group : group + 1, :] == y_global
        for sample in range(STEPS):
            weights[sample * rows : (sample + 1) * rows, span] = jnp.where(
                is_y, window[sample : sample + 1], 0.0
            )
    rest = weights[...]
    pick = picks[...].astype(jnp.bfloat16)
    total = None
    for _ in range(3):
        part = rest.astype(jnp.bfloat16)
        rest = rest - part.astype(jnp.float32)
        product = lax.dot_general(
            part, pick, (((1,), (1,)), ((), ())), preferred_element_type=jnp.float32
        )
        total = product if total is None else total + product
    planes[...] = jnp.zeros_like(planes)
    for sample in range(STEPS):
        for tile in range(tiles):
            begin = sample * rows + tile * SUBLANES
            planes[sample, tile, :, :wide_x] = total[begin : begin + SUBLANES]


def injected(gathered, picks, rows_y, samples, cells_y, depth):
    rows = cells_y + 2 * RIM
    return pl.pallas_call(
        functools.partial(inject_kernel, samples, cells_y),
        out_shape=vmem_out(STEPS, rows // SUBLANES, SUBLANES, depth),
        in_specs=in_vmem(3),
        out_specs=in_vmem(1)[0],
        scratch_shapes=[pltpu.VMEM((STEPS * rows, picks.shape[1]), jnp.float32)],
        compiler_params=PARAMS,
        name="inject",
    )(gathered, pinned(picks, pltpu.VMEM), pinned(rows_y, pltpu.VMEM))


def per_device(
    src_p_prev,
    src_p_now,
    src_q_prev,
    src_q_now,
    rec_p_next,
    rec_p_now,
    rec_q_next,
    rec_q_now,
    velocity_term,
    epsilon,
    delta,
    tilt,
    azimuth,
    traces,
    receiver_x,
    receiver_y,
    segment_start,
):
    blocks = (
        src_p_prev,
        src_p_now,
        src_q_prev,
        src_q_now,
        rec_p_next,
        rec_p_now,
        rec_q_next,
        rec_q_now,
        velocity_term,
        epsilon,
        delta,
        tilt,
        azimuth,
    )
    cells_x, cells_y, depth = src_p_now.shape
    wide, y_a, y_b, window = pack(blocks, traces, segment_start)
    y_a, y_b = swap(y_a, "gy", 0), swap(y_b, "gy", 1)
    wide, x_a, x_b = pack_x(wide, window)
    x_a, x_b = swap(x_a, "gx", 0), swap(x_b, "gx", 1)
    windows = jnp.concatenate([window, x_a[x_parts()[1] :, :STEPS, :]], axis=0)
    for bit in bits_of("gx")[1:]:
        windows = doubled(windows, "gx", bit)
    own = own_factors(wide, windows)
    for bit in bits_of("gy")[:-1]:
        windows = doubled(windows, "gy", bit)
    picks, rows_y = receiver_tables(receiver_x, receiver_y, traces.shape[1], cells_x)
    wide, c_a, c_b = corners(
        wide, y_a, y_b, windows, pinned(own, pltpu.VMEM), pinned(rows_y, pltpu.VMEM)
    )
    for bit in bits_of("gy")[-1:]:
        windows = doubled(windows, "gy", bit)
    c_a, c_b = swap(c_a, "gx", 0), swap(c_b, "gx", 1)
    planes = injected(windows, picks, rows_y, traces.shape[1], cells_y, depth)
    state = inner(wide, planes, own)
    return tuple(outer(wide, (x_a, x_b, c_a, c_b), planes, state, cells_x, cells_y))


def solution(mesh):
    state = P(("shot", "gx"), "gy", None)
    earth = P("gx", "gy", None)
    return jax.shard_map(
        per_device,
        mesh=mesh,
        in_specs=(state,) * FIELDS + (earth,) * 5 + (P("shot", ("gx", "gy")), P(), P(), P()),
        out_specs=(state,) * 3,
        check_vma=False,
    )
```

```python
import functools

import jax
import jax.numpy as jnp
from jax import lax
from jax.experimental import pallas as pl
from jax.experimental.pallas import tpu as pltpu
from jax.sharding import PartitionSpec as P

STEPS = 4
REC_DEPTH = 4
RIM = STEPS
QUARTERS = 4
FIELDS = 8
SUBLANES = 8
LANES = 128
PARAMS = pltpu.CompilerParams(vmem_limit_bytes=16 * 1024 * 1024)
PACK_PARAMS = pltpu.CompilerParams(vmem_limit_bytes=48 * 1024 * 1024)


def in_vmem(count):
    return [pl.BlockSpec(memory_space=pltpu.VMEM)] * count


def is_odd(axis):
    return lax.rem(lax.axis_index(axis), 2) == 1


def swap(value, axis, first):
    size = lax.axis_size(axis)
    lower = range(first, size - 1, 2)
    pairs = [(i, i + 1) for i in lower] + [(i + 1, i) for i in lower]
    return lax.ppermute(value, axis, pairs)


NOW = (1, 3, 5, 7)
REST = (0, 2, 4, 6, 8, 9, 10, 11, 12)
SLIM = RIM - 1


def y_slots():
    slots = [((number, 0, RIM, 0),) for number in NOW]
    whole = len(REST) - len(REST) // RIM
    for place in range(whole):
        parts = [(REST[place], 0, SLIM, 0)]
        guest = whole + place // SLIM
        if guest < len(REST):
            parts.append((REST[guest], place % SLIM, 1, SLIM))
        slots.append(tuple(parts))
    return slots


def each_y_part(slots, high):
    for slot, parts in enumerate(slots):
        for number, row, rows, place in parts:
            if not high:
                yield slot, number, row, place, rows
            else:
                width = RIM if number in NOW else SLIM
                yield slot, number, RIM - width + row, 0 if place else RIM - rows, rows


def x_parts():
    parts, place = [], 0
    for number in NOW:
        parts.append((number, RIM, place))
        place += RIM
    for number in REST:
        parts.append((number, SLIM, place))
        place += SLIM
    return parts, place


def pinned(value, space):
    return pltpu.with_memory_space_constraint(value, space)


def vmem_out(*shape):
    return pltpu.VMEM(shape, jnp.float32)


def pack_kernel(count, *refs):
    blocks, traces, start = refs[:count], refs[count], refs[count + 1]
    wide, y_a, y_b, window, held, sems = refs[count + 2 :]
    cells_x, cells_y = blocks[0].shape[:2]
    core_x = pl.ds(RIM, cells_x)
    moves = [
        pltpu.make_async_copy(block, wide.at[number, core_x, pl.ds(0, cells_y)], sems.at[number])
        for number, block in enumerate(blocks)
    ]
    moves.append(pltpu.make_async_copy(traces, held, sems.at[count]))
    for move in moves:
        move.start()
    odd_y = is_odd("gy")
    begin = start[0]
    samples = traces.shape[1]
    window[...] = jnp.zeros_like(window)
    for number in range(count):
        moves[number].wait()

        def put_y(low, high, number=number):
            for out, is_high, base in ((low, False, 0), (high, True, cells_y - RIM)):
                for slot, part, row, place, length in each_y_part(y_slots(), is_high):
                    if part == number:
                        out[slot, :, place : place + length, :] = wide[
                            number, RIM : RIM + cells_x, base + row : base + row + length, :
                        ]

        @pl.when(odd_y)
        def _(put_y=put_y):
            put_y(y_a, y_b)

        @pl.when(jnp.logical_not(odd_y))
        def _(put_y=put_y):
            put_y(y_b, y_a)

    moves[count].wait()
    for sample in range(STEPS):
        window[0, sample : sample + 1, :samples] = held[pl.ds(begin + sample, 1), :]


def pack(blocks, traces, segment_start):
    cells_x, cells_y, depth = blocks[0].shape
    count = len(blocks)
    rim_y = vmem_out(len(y_slots()), cells_x, RIM, depth)
    wide = vmem_out(count, cells_x + 2 * RIM + 2, cells_y + 2 * RIM, depth)
    return pl.pallas_call(
        functools.partial(pack_kernel, count),
        out_shape=[wide, rim_y, rim_y, vmem_out(1, STEPS, LANES)],
        in_specs=[pl.BlockSpec(memory_space=pltpu.HBM)] * (count + 1)
        + [pl.BlockSpec(memory_space=pltpu.SMEM)],
        out_specs=in_vmem(4),
        scratch_shapes=[
            pltpu.VMEM(traces.shape, jnp.float32),
            pltpu.SemaphoreType.DMA((count + 1,)),
        ],
        compiler_params=PACK_PARAMS,
        name="pack_y_rims",
    )(*(pinned(value, pltpu.HBM) for value in (*blocks, traces)), segment_start)


def pack_x_kernel(_, window, wide, x_a, x_b):
    cells_x, cells_y = wide.shape[1] - 2 * RIM - 2, wide.shape[2] - 2 * RIM
    odd_x = is_odd("gx")
    parts, total = x_parts()
    for number, width, place in parts:
        first, last = RIM, RIM + cells_x - width
        for out, begin in ((x_a, jnp.where(odd_x, first, last)), (x_b, jnp.where(odd_x, last, first))):
            out[place : place + width] = wide[number, pl.ds(begin, width), :cells_y, :]
    x_a[total] = jnp.zeros_like(x_a[total])
    x_a[total, :STEPS, :] = window[0]


def pack_x(wide, window):
    _, _, rows, depth = wide.shape
    total = x_parts()[1]
    return pl.pallas_call(
        pack_x_kernel,
        out_shape=[
            vmem_out(*wide.shape),
            vmem_out(total + 1, rows - 2 * RIM, depth),
            vmem_out(total, rows - 2 * RIM, depth),
        ],
        in_specs=in_vmem(2),
        out_specs=in_vmem(3),
        input_output_aliases={0: 0},
        compiler_params=PARAMS,
        name="pack_x_rims",
    )(pinned(wide, pltpu.VMEM), window)


def corner_kernel(_, y_a, y_b, __, ___, ____, wide, c_a, c_b):
    cells_x = y_a.shape[1]
    cells_y = wide.shape[2] - 2 * RIM
    odd_x, odd_y = is_odd("gx"), is_odd("gy")

    def place_y(low, high):
        for rim, is_high, base in ((high, False, cells_y), (low, True, cells_y + RIM)):
            for slot, number, row, place, length in each_y_part(y_slots(), is_high):
                wide[number, RIM : RIM + cells_x, base + row : base + row + length, :] = rim[
                    slot, :, place : place + length, :
                ]

    @pl.when(odd_y)
    def _():
        place_y(y_a, y_b)

    @pl.when(jnp.logical_not(odd_y))
    def _():
        place_y(y_b, y_a)

    for number, width, place in x_parts()[0]:
        first, last = RIM, RIM + cells_x - width
        for out, begin in ((c_a, jnp.where(odd_x, first, last)), (c_b, jnp.where(odd_x, last, first))):
            out[place : place + width] = wide[number, pl.ds(begin, width), cells_y:, :]


def corners(wide, y_a, y_b, *earlier):
    corner = vmem_out(x_parts()[1], 2 * RIM, wide.shape[-1])
    return pl.pallas_call(
        corner_kernel,
        out_shape=[vmem_out(*wide.shape), corner, corner],
        in_specs=in_vmem(6),
        out_specs=in_vmem(3),
        input_output_aliases={0: 0},
        compiler_params=PARAMS,
        name="pack_corners",
    )(pinned(wide, pltpu.VMEM), y_a, y_b, *earlier)


def sine_cosine(angle):
    square = angle * angle
    sine = 1.0 / 6227020800.0
    for term in (-1.0 / 39916800.0, 1.0 / 362880.0, -1.0 / 5040.0, 1.0 / 120.0, -1.0 / 6.0, 1.0):
        sine = sine * square + term
    cosine = 1.0 / 479001600.0
    for term in (-1.0 / 3628800.0, 1.0 / 40320.0, -1.0 / 720.0, 1.0 / 24.0, -0.5, 1.0):
        cosine = cosine * square + term
    return sine * angle, cosine


def factors_of(velocity, epsilon, delta, tilt, azimuth):
    f_e = 1.0 + 2.0 * epsilon
    f_d = jnp.sqrt(1.0 + 2.0 * delta)
    sin_tilt, cos_tilt = sine_cosine(tilt)
    sin_half, cos_half = sine_cosine(0.5 * azimuth)
    sin_azim = 2.0 * sin_half * cos_half
    cos_azim = 1.0 - 2.0 * sin_half * sin_half
    sin_square = sin_tilt * sin_tilt
    half_tilt = 0.5 * sin_tilt * cos_tilt
    along_x = sin_square * cos_azim
    return (
        velocity,
        velocity * f_e,
        velocity * f_d,
        along_x * cos_azim,
        sin_square * sin_azim * sin_azim,
        cos_tilt * cos_tilt,
        0.5 * along_x * sin_azim,
        half_tilt * cos_azim,
        half_tilt * sin_azim,
    )


FACTORS = 9


def own_kernel(wide, _, own):
    _, cells_x, rows, _ = own.shape
    cells_y = rows - 2 * RIM

    def body(i):
        for x in [4 * i + k for k in range(4)]:
            raw = [wide[FIELDS + number, RIM + x, :cells_y, :] for number in range(5)]
            for number, value in enumerate(factors_of(*raw)):
                own[number, x, :cells_y, :] = value

    repeat(cells_x // 4, body)


def own_factors(wide, earlier):
    _, planes_x, rows, depth = wide.shape
    return pl.pallas_call(
        own_kernel,
        out_shape=vmem_out(FACTORS, planes_x - 2 * RIM - 2, rows, depth),
        in_specs=in_vmem(2),
        out_specs=in_vmem(1)[0],
        compiler_params=PARAMS,
        name="own_factors",
    )(pinned(wide, pltpu.VMEM), earlier)


class Steps:
    def __init__(self, wide, planes, waves, factors):
        self.wide, self.planes, self.waves, self.factors = wide, planes, waves, factors
        self.count, _, rows, self.depth = wide.shape
        self.tiles = rows // SUBLANES
        self.cells_x = wide.shape[1] - 2 * RIM - 2
        lane = lax.broadcasted_iota(jnp.int32, (SUBLANES, self.depth), 1)
        self.not_last, self.not_first = lane < self.depth - 1, lane > 0
        self.at_depth = lane == REC_DEPTH

    def wide_tiles(self, number, x):
        return [
            self.wide[number, x, pl.ds(tile, SUBLANES, stride=self.tiles), :]
            for tile in range(self.tiles)
        ]

    def wave_tiles(self, number, slot, x):
        if slot < 2:
            return self.wide_tiles(2 * number + slot, x)
        return [self.waves[slot - 2][number, x, tile] for tile in range(self.tiles)]

    def next_y(self, value):
        return value[1:] + [pltpu.roll(value[0], SUBLANES - 1, 0)]

    def previous_y(self, value):
        return [pltpu.roll(value[-1], 1, 0)] + value[:-1]

    def make_factors(self, x):
        raw = [self.wide_tiles(FIELDS + number, x) for number in range(self.count - FIELDS)]
        for tile in range(self.tiles):
            for number, value in enumerate(factors_of(*[value[tile] for value in raw])):
                self.factors[number, x, tile] = value

    def sides_z(self, value):
        above = [jnp.where(self.not_last, pltpu.roll(u, self.depth - 1, 1), 0.0) for u in value]
        below = [jnp.where(self.not_first, pltpu.roll(u, 1, 1), 0.0) for u in value]
        return above, below

    def plane_part(self, now):
        above, below = self.sides_z(now)
        after, before = self.next_y(now), self.previous_y(now)
        pairs_z, pairs_y = list(zip(above, below)), list(zip(after, before))
        return (
            [a - b for a, b in pairs_y],
            [a - b for a, b in pairs_z],
            [a + b for a, b in pairs_y],
            [a + b for a, b in pairs_z],
        )

    def stencil(self, number, turn, x, count, full):
        planes = [self.wave_tiles(number, turn + 1, x - 1 + i) for i in range(count + 2)]
        parts = [self.plane_part(planes[0]), self.plane_part(planes[1])]
        result = []
        for i in range(1, count + 1):
            parts.append(self.plane_part(planes[i + 1]))
            slope_y, slope_z, sums_y, sums_z = parts[i]
            next_z, previous_z = self.next_y(slope_z), self.previous_y(slope_z)
            axis, laplace = [], []
            for tile in range(self.tiles):
                axx, ayy, azz, axy, axz, ayz = [
                    self.factors[factor, x - 1 + i, tile] for factor in range(3, 9)
                ]
                now = planes[i][tile]
                double = now + now
                sum_x = planes[i + 1][tile] + planes[i - 1][tile]
                sum_y, sum_z = sums_y[tile], sums_z[tile]
                straight = ((axx * sum_x + ayy * sum_y) + azz * sum_z) - double
                mixed = (
                    axy * (parts[i + 1][0][tile] - parts[i - 1][0][tile])
                    + axz * (parts[i + 1][1][tile] - parts[i - 1][1][tile])
                ) + ayz * (next_z[tile] - previous_z[tile])
                axis.append(straight + mixed)
                if full:
                    laplace.append(((sum_x + sum_y) + sum_z) - 3.0 * double)
            result.append((planes[i], axis, laplace))
        return result

    def short_stencil(self, number, turn, x, count, full):
        planes = [self.wave_tiles(number, turn + 1, x - 1 + i) for i in range(count + 2)]
        result = []
        for i in range(1, count + 1):
            before, now, after = planes[i - 1 : i + 2]
            slope_x = [a - b for a, b in zip(after, before)]
            _, slope_z, sums_y, sums_z = self.plane_part(now)
            slope_xy, slope_xz, _, _ = self.plane_part(slope_x)
            next_z, previous_z = self.next_y(slope_z), self.previous_y(slope_z)
            axis, laplace = [], []
            for tile in range(self.tiles):
                axx, ayy, azz, axy, axz, ayz = [
                    self.factors[factor, x - 1 + i, tile] for factor in range(3, 9)
                ]
                double = now[tile] + now[tile]
                sum_x = after[tile] + before[tile]
                sum_y, sum_z = sums_y[tile], sums_z[tile]
                straight = ((axx * sum_x + ayy * sum_y) + azz * sum_z) - double
                mixed = (axy * slope_xy[tile] + axz * slope_xz[tile]) + ayz * (
                    next_z[tile] - previous_z[tile]
                )
                axis.append(straight + mixed)
                if full:
                    laplace.append(((sum_x + sum_y) + sum_z) - 3.0 * double)
            result.append((now, axis, laplace))
        return result

    def step(self, turn, x, count):
        tiles, factors = range(self.tiles), self.factors
        for pair in range(2):
            p_number, q_number = 2 * pair, 2 * pair + 1
            stencil = self.stencil if count > RIM else self.short_stencil
            of_q = stencil(q_number, turn, x, count, False)
            of_p = stencil(p_number, turn, x, count, True)
            for i in range(count):
                now = x + i
                q, q_axis, _ = of_q[i]
                p, p_axis, p_laplace = of_p[i]
                p_held = self.wave_tiles(p_number, turn, now)
                q_held = self.wave_tiles(q_number, turn, now)
                for tile in tiles:
                    velocity, with_e, with_d = [factors[number, now, tile] for number in range(3)]
                    across = p_laplace[tile] - p_axis[tile]
                    p_next = ((p[tile] + p[tile]) - p_held[tile]) + (
                        with_e * across + with_d * q_axis[tile]
                    )
                    q_next = ((q[tile] + q[tile]) - q_held[tile]) + (
                        with_d * across + velocity * q_axis[tile]
                    )
                    if pair == 1:
                        shift = lax.rem(REC_DEPTH - now + self.depth, self.depth)
                        moved = pltpu.roll(self.planes[STEPS - 1 - turn, tile], shift, 1)
                        p_next = p_next + jnp.where(self.at_depth, moved, 0.0)
                    self.waves[turn][p_number, now, tile] = p_next
                    if pair == 1 or turn < STEPS - 1:
                        self.waves[turn][q_number, now, tile] = q_next


def repeat(count, body):
    def run(i, carry):
        body(i)
        return carry

    lax.fori_loop(0, count, run, 0)


def inner_kernel(wide, planes, _, *refs):
    steps = Steps(wide, planes, refs[:STEPS], refs[STEPS])
    natural = refs[STEPS + 1]
    cells_x, cells_y, tiles = steps.cells_x, natural.shape[2] - 2 * RIM, steps.tiles

    def rim_rows(i):
        for x in [4 * i + k for k in range(4)]:
            raw = [wide[FIELDS + number, RIM + x, cells_y:, :] for number in range(5)]
            for number, value in enumerate(factors_of(*raw)):
                natural[number, x, cells_y:, :] = value

    def in_step_order(i):
        for x in [2 * i + k for k in range(2)]:
            for number in range(FACTORS):
                for tile in range(tiles):
                    steps.factors[number, RIM + x, tile] = natural[
                        number, x, pl.ds(tile, SUBLANES, stride=tiles), :
                    ]

    repeat(cells_x // 4, rim_rows)
    repeat(cells_x // 2, in_step_order)
    for turn in range(STEPS):
        first, last = RIM + 1 + turn, RIM + cells_x - 1 - turn
        half = (last - first) // 2
        steps.step(turn, first, half)
        steps.step(turn, first + half, half)


def outer_kernel(*refs):
    x_a, x_b, c_a, c_b, planes = refs[1:6]
    refs = refs[6 + STEPS + 1 :]
    wide, waves, factors = refs[0], refs[1 : 1 + STEPS], refs[1 + STEPS]
    outputs, sems = refs[-4:-1], refs[-1]
    cells_x, cells_y, depth = outputs[0].shape
    odd_x = is_odd("gx")
    for number, width, place in x_parts()[0]:
        low, high = RIM - width, RIM + cells_x
        for begin, side, corner in (
            (jnp.where(odd_x, low, high), x_a, c_a),
            (jnp.where(odd_x, high, low), x_b, c_b),
        ):
            wide[number, pl.ds(begin, width), :cells_y, :] = side[place : place + width]
            wide[number, pl.ds(begin, width), cells_y:, :] = corner[place : place + width]

    steps = Steps(wide, planes, waves, factors)

    for x in range(SLIM):
        steps.make_factors(RIM - SLIM + x)
        steps.make_factors(RIM + cells_x + x)
    for turn in range(STEPS):
        steps.step(turn, turn + 1, RIM)
        steps.step(turn, RIM + cells_x - 1 - turn, RIM)

    tiles = steps.tiles

    def finish(i):
        x = RIM + i
        total = None
        for back in range(STEPS + 1):
            source = steps.wave_tiles(0, 1 + STEPS - back, x)
            receiver = steps.wave_tiles(2, 1 + back, x)
            product = [a * b for a, b in zip(source, receiver)]
            total = product if total is None else [a + b for a, b in zip(total, product)]
        for out, value in (
            (0, total),
            (1, steps.wave_tiles(2, 1 + STEPS, x)),
            (2, steps.wave_tiles(3, 1 + STEPS, x)),
        ):
            for tile in range(tiles):
                wide[out, x, pl.ds(tile, SUBLANES, stride=tiles), :] = value[tile]

    moves = []
    quarter = cells_x // QUARTERS
    for part in range(QUARTERS):
        begin = part * quarter
        repeat(quarter, lambda i, begin=begin: finish(begin + i))
        for out, ref in enumerate(outputs):
            source = wide.at[out, pl.ds(RIM + begin, quarter), pl.ds(0, cells_y)]
            move = pltpu.make_async_copy(source, ref.at[pl.ds(begin, quarter)], sems.at[out, part])
            move.start()
            moves.append(move)
    for move in moves:
        move.wait()


def inner(wide, planes, own):
    _, planes_x, rows, depth = wide.shape
    tile = (planes_x, rows // SUBLANES, SUBLANES, depth)
    return pl.pallas_call(
        inner_kernel,
        out_shape=[vmem_out(4, *tile)] * STEPS
        + [vmem_out(FACTORS, *tile), vmem_out(*own.shape)],
        in_specs=in_vmem(3),
        out_specs=in_vmem(STEPS + 2),
        input_output_aliases={2: STEPS + 1},
        compiler_params=PARAMS,
        name="inner_steps",
    )(pinned(wide, pltpu.VMEM), planes, pinned(own, pltpu.VMEM))[:-1]


def outer(wide, rims, planes, state, cells_x, cells_y):
    out = pltpu.HBM((cells_x, cells_y, wide.shape[-1]), jnp.float32)
    kept = [vmem_out(*wide.shape)] + [vmem_out(*value.shape) for value in state]
    first = len(rims) + 2
    aliases = {0: 0} | {first + number: 1 + number for number in range(len(state))}
    return pl.pallas_call(
        outer_kernel,
        out_shape=kept + [out] * 3,
        in_specs=in_vmem(first + len(state)),
        out_specs=in_vmem(len(kept)) + [pl.BlockSpec(memory_space=pltpu.HBM)] * 3,
        input_output_aliases=aliases,
        scratch_shapes=[pltpu.SemaphoreType.DMA((3, QUARTERS))],
        compiler_params=PARAMS,
        name="outer_steps",
    )(
        pinned(wide, pltpu.VMEM),
        *rims,
        planes,
        *(pinned(value, pltpu.VMEM) for value in state),
    )[-3:]


def bits_of(axis):
    size = lax.axis_size(axis)
    return [1 << bit for bit in range(size.bit_length() - 1)] if size & (size - 1) == 0 else None


def doubled(windows, axis, bit):
    pairs = [(i, i ^ bit) for i in range(lax.axis_size(axis))]
    return jnp.concatenate([windows, lax.ppermute(windows, axis, pairs)], axis=0)


def table_kernel(samples, cells_x, table_x, table_y, picks, rows_y):
    size_y = lax.axis_size("gy")
    own_x, own_y = lax.axis_index("gx"), lax.axis_index("gy")
    wide_x = picks.shape[0]
    in_row = LANES // samples
    x_global = own_x * cells_x - RIM + lax.broadcasted_iota(jnp.int32, (wide_x, LANES), 0)
    lane = lax.broadcasted_iota(jnp.int32, (1, LANES), 1)
    bits_x, bits_y = bits_of("gx"), bits_of("gy")

    def source(place):
        device_x, device_y = own_x, own_y
        for number, bit in enumerate(bits_x):
            if place >> number & 1:
                device_x = jnp.bitwise_xor(device_x, bit)
        for number, bit in enumerate(bits_y):
            if place >> (len(bits_x) + number) & 1:
                device_y = jnp.bitwise_xor(device_y, bit)
        return device_x * size_y + device_y

    for group in range(rows_y.shape[0]):
        at_x = at_y = jnp.zeros((1, LANES), jnp.int32)
        for part in range(in_row):
            device = source(group * in_row + part)
            here = (lane >= part * samples) & (lane < (part + 1) * samples)
            shift = lax.rem((part - lax.rem(device, in_row)) * samples + LANES, LANES)
            table_row = pl.ds(lax.div(device, in_row), 1)
            at_x = jnp.where(here, pltpu.roll(table_x[table_row, :], shift, 1), at_x)
            at_y = jnp.where(here, pltpu.roll(table_y[table_row, :], shift, 1), at_y)
        span = slice(group * LANES, (group + 1) * LANES)
        picks[:, span] = (at_x == x_global).astype(jnp.float32)
        rows_y[group : group + 1, :] = at_y


def receiver_tables(receiver_x, receiver_y, samples, cells_x):
    receivers = receiver_x.shape[0]
    wide_x = -(-(cells_x + 2 * RIM) // 32) * 32
    return pl.pallas_call(
        functools.partial(table_kernel, samples, cells_x),
        out_shape=[
            vmem_out(wide_x, receivers),
            pltpu.VMEM((receivers // LANES, LANES), jnp.int32),
        ],
        in_specs=in_vmem(2),
        out_specs=in_vmem(2),
        compiler_params=PARAMS,
        name="receiver_tables",
    )(receiver_x.reshape(-1, LANES), receiver_y.reshape(-1, LANES))


def inject_kernel(samples, cells_y, gathered, picks, rows_y, planes, weights):
    own_y = lax.axis_index("gy")
    rows = cells_y + 2 * RIM
    tiles = rows // SUBLANES
    wide_x = picks.shape[0]
    in_row = LANES // samples
    place = lax.broadcasted_iota(jnp.int32, (rows, LANES), 0)
    row = tiles * lax.rem(place, SUBLANES) + lax.div(place, SUBLANES)
    y_global = own_y * cells_y + jnp.where(row < cells_y + RIM, row, row - rows)
    lane = lax.broadcasted_iota(jnp.int32, (1, LANES), 1)
    for group in range(rows_y.shape[0]):
        window = gathered[group * in_row]
        for part in range(1, in_row):
            here = (lane >= part * samples) & (lane < (part + 1) * samples)
            moved = pltpu.roll(gathered[group * in_row + part], part * samples, 1)
            window = jnp.where(here, moved, window)
        span = slice(group * LANES, (group + 1) * LANES)
        is_y = rows_y[group : group + 1, :] == y_global
        for sample in range(STEPS):
            weights[sample * rows : (sample + 1) * rows, span] = jnp.where(
                is_y, window[sample : sample + 1], 0.0
            )
    rest = weights[...]
    pick = picks[...].astype(jnp.bfloat16)
    total = None
    for _ in range(3):
        part = rest.astype(jnp.bfloat16)
        rest = rest - part.astype(jnp.float32)
        product = lax.dot_general(
            part, pick, (((1,), (1,)), ((), ())), preferred_element_type=jnp.float32
        )
        total = product if total is None else total + product
    planes[...] = jnp.zeros_like(planes)
    for sample in range(STEPS):
        for tile in range(tiles):
            begin = sample * rows + tile * SUBLANES
            planes[sample, tile, :, :wide_x] = total[begin : begin + SUBLANES]


def injected(gathered, picks, rows_y, samples, cells_y, depth):
    rows = cells_y + 2 * RIM
    return pl.pallas_call(
        functools.partial(inject_kernel, samples, cells_y),
        out_shape=vmem_out(STEPS, rows // SUBLANES, SUBLANES, depth),
        in_specs=in_vmem(3),
        out_specs=in_vmem(1)[0],
        scratch_shapes=[pltpu.VMEM((STEPS * rows, picks.shape[1]), jnp.float32)],
        compiler_params=PARAMS,
        name="inject",
    )(gathered, pinned(picks, pltpu.VMEM), pinned(rows_y, pltpu.VMEM))


def per_device(
    src_p_prev,
    src_p_now,
    src_q_prev,
    src_q_now,
    rec_p_next,
    rec_p_now,
    rec_q_next,
    rec_q_now,
    velocity_term,
    epsilon,
    delta,
    tilt,
    azimuth,
    traces,
    receiver_x,
    receiver_y,
    segment_start,
):
    blocks = (
        src_p_prev,
        src_p_now,
        src_q_prev,
        src_q_now,
        rec_p_next,
        rec_p_now,
        rec_q_next,
        rec_q_now,
        velocity_term,
        epsilon,
        delta,
        tilt,
        azimuth,
    )
    cells_x, cells_y, depth = src_p_now.shape
    wide, y_a, y_b, window = pack(blocks, traces, segment_start)
    y_a, y_b = swap(y_a, "gy", 0), swap(y_b, "gy", 1)
    wide, x_a, x_b = pack_x(wide, window)
    x_a, x_b = swap(x_a, "gx", 0), swap(x_b, "gx", 1)
    windows = jnp.concatenate([window, x_a[x_parts()[1] :, :STEPS, :]], axis=0)
    for bit in bits_of("gx")[1:]:
        windows = doubled(windows, "gx", bit)
    own = own_factors(wide, windows)
    for bit in bits_of("gy")[:-1]:
        windows = doubled(windows, "gy", bit)
    picks, rows_y = receiver_tables(receiver_x, receiver_y, traces.shape[1], cells_x)
    wide, c_a, c_b = corners(
        wide, y_a, y_b, windows, pinned(own, pltpu.VMEM), pinned(rows_y, pltpu.VMEM)
    )
    for bit in bits_of("gy")[-1:]:
        windows = doubled(windows, "gy", bit)
    c_a, c_b = swap(c_a, "gx", 0), swap(c_b, "gx", 1)
    planes = injected(windows, picks, rows_y, traces.shape[1], cells_y, depth)
    state = inner(wide, planes, own)
    return tuple(outer(wide, (x_a, x_b, c_a, c_b), planes, state, cells_x, cells_y))


def solution(mesh):
    state = P(("shot", "gx"), "gy", None)
    earth = P("gx", "gy", None)
    return jax.shard_map(
        per_device,
        mesh=mesh,
        in_specs=(state,) * FIELDS + (earth,) * 5 + (P("shot", ("gx", "gy")), P(), P(), P()),
        out_specs=(state,) * 3,
        check_vma=False,
    )
```
